32 devices in a mesh: row: 2 (over y), col: 4 (over z), own: 4 (over x, core).
Axes of the slice: x: 2, y: 2, z: 4, core: 2. Of those that a mesh axis runs over, the one named last changes fastest.
Arguments:
- viscosity: float32 [2048, 512], P(('row', 'own'), 'col'), may hold values from 0.5 to 8
- friction: float32 [2048, 512], P(('row', 'own'), 'col'), may hold values from 0.3 to 6
- driving: float32 [2, 2048, 512], P(None, ('row', 'own'), 'col'), may hold values from -32 to 32
- observed: float32 [2, 2048, 512], P(None, ('row', 'own'), 'col'), may hold values from -6 to 6
- ice_mask: int32 [2048, 512], P(('row', 'own'), 'col'), may hold values 0 or 1
- tile_block: int32 [16, 4], P(('row', 'own'), 'col'), may hold values from 0 to 15, as said below
- owner_list: int32 [16], replicated, may hold values from 0 to 15, each once
Outputs:
- velocity: float32 [2, 2048, 512], P(None, ('row', 'own'), 'col')
- block_gradient: float32 [4, 4, 1024], P('own')
The draws below stay inside these ranges and needn't reach their ends.
Inputs may be any that keep to these rules, and one draw needn't show every extreme that they name: `tile_block`: tile rows 2r and 2r+1 carry the same ids; along the tile columns they run through r*2 to r*2 + 1 in order, each id on one run of consecutive tile columns of ragged length. `owner_list`: every block appears once.
All inputs are finite; a program needn't handle non-finite values. No bound on the sum of `ice_mask` on one device may be relied on, other than what follows from the above.
Results may differ from the reference program's by a relative error of at most 0.000088.
Values sent between devices are 32-bit elements; how exact they have to be, the bound alone decides.
No kernel may reach another device: no remote copies, remote signals or barrier semaphores. Data moves between devices by JAX's collectives and lax.ppermute only.
A program may use at most 64 MiB of HBM per device.

```python
import math
import jax
import jax.numpy as jnp
from jax import lax

TILE = 128
MODES = 32
NX = 2048
NY = 512
GROUPS = 2
NB = 16
N_OWN = 4


def draw_tile_block(key, part):
    tile_rows = NX // TILE
    tile_cols = NY // TILE
    pairs = tile_rows // 2

    def one_pair(pair_index):
        sub_key = jax.random.fold_in(key, pair_index)
        cuts = jax.random.permutation(sub_key, tile_cols - 1)[:GROUPS - 1] + 1
        columns = jnp.arange(tile_cols)
        group = jnp.sum((cuts[:, None] <= columns[None, :]).astype(jnp.int32), axis=0)
        return pair_index * GROUPS + group
    labels = jax.vmap(one_pair)(jnp.arange(pairs))
    return jnp.repeat(labels, 2, axis=0).astype(jnp.int32)


def plant(drawn, stream_key, smallest, largest):
    index_at = [jax.random.randint(jax.random.fold_in(stream_key, axis), (), 0, length) for axis, length in enumerate(drawn.shape)]
    main_axis = drawn.shape.index(max(drawn.shape))
    beside = index_at[:main_axis] + [(index_at[main_axis] + 1) % drawn.shape[main_axis]] + index_at[main_axis + 1:]
    return drawn.at[tuple(index_at)].set(smallest).at[tuple(beside)].set(largest)


def level_of(own_key, dims, shards, low, top_value):
    level, own = 1.0, jax.random.fold_in(own_key, 6)
    for position, parts in shards:
        steps = jnp.exp(jax.random.uniform(jax.random.fold_in(own, position), (parts,), jnp.float32, low / len(shards), top_value / len(shards)))
        level = level * jnp.repeat(steps, dims[position] // parts).reshape([-1 if axis == position else 1 for axis in range(len(dims))])
    return level


def gaussian(stream_key, extent, width, limit, pieces=(), kind=jnp.bfloat16):
    gain = level_of(stream_key, extent, pieces, -0.22, 0.18) if pieces else 1.0
    array = jax.random.normal(stream_key, extent, jnp.float32) * width * gain
    return jnp.minimum(jnp.maximum(array, -limit), limit).astype(kind)


def setup_inputs(seed: int = 0) -> dict:
    streams_of = jax.random.split(jax.random.key(seed), 8)
    viscosity = jnp.clip(jnp.exp(math.log(8.0) - 2.7725887 * jax.random.uniform(streams_of[0], (NX, NY), jnp.float32) ** level_of(streams_of[0], (NX, NY), ((0, 8), (1, 4)), -0.2, 0.2)), 0.5, 8.0)
    friction = jnp.clip(jnp.exp(math.log(6.0) - 2.9957322 * jax.random.uniform(streams_of[1], (NX, NY), jnp.float32) ** level_of(streams_of[1], (NX, NY), ((0, 8), (1, 4)), -0.2, 0.2)), 0.3, 6.0)
    driving = gaussian(streams_of[2], (2, NX, NY), 6.0, 32.0, ((1, 8), (2, 4)), jnp.float32)
    observed = gaussian(streams_of[3], (2, NX, NY), 1.0, 6.0, ((1, 8), (2, 4)), jnp.float32)
    ice_mask = plant((jax.random.randint(streams_of[4], (NX, NY), 0, 8) < 7).astype(jnp.int32), jax.random.fold_in(streams_of[4], 1), 0, 1)
    tile_block = draw_tile_block(jax.random.fold_in(streams_of[7], 71), 0)
    owner_list = jax.random.permutation(streams_of[6], NB).astype(jnp.int32)
    return dict(viscosity=viscosity, friction=friction, driving=driving, observed=observed, ice_mask=ice_mask, tile_block=tile_block, owner_list=owner_list)


damping = 0.5


def along_x(field):
    return 0.5 * ((field[1:, :-1] - field[:-1, :-1]) + (field[1:, 1:] - field[:-1, 1:]))


def along_y(field):
    return 0.5 * ((field[:-1, 1:] - field[:-1, :-1]) + (field[1:, 1:] - field[1:, :-1]))


def back_x(corner):
    return 0.5 * ((corner[:-1, :-1] + corner[:-1, 1:]) - (corner[1:, :-1] + corner[1:, 1:]))


def back_y(corner):
    return 0.5 * ((corner[:-1, :-1] + corner[1:, :-1]) - (corner[:-1, 1:] + corner[1:, 1:]))


def apply_operator(state, viscous, friction_in):
    first_x = along_x(state[0])
    first_y = along_y(state[0])
    second_x = along_x(state[1])
    second_y = along_y(state[1])
    corner_visc = viscous[:-1, :-1]
    normal_one = corner_visc * (4.0 * first_x + 2.0 * second_y)
    shear = corner_visc * (first_y + second_x)
    normal_two = corner_visc * (4.0 * second_y + 2.0 * first_x)
    inner = state[:, 1:-1, 1:-1]
    out_first = back_x(normal_one) + back_y(shear) + friction_in * inner[0]
    out_second = back_y(normal_two) + back_x(shear) + friction_in * inner[1]
    return jnp.stack([out_first, out_second])


def diagonal_of(viscous, friction_in):
    corner = viscous[:-1, :-1]
    return 1.25 * (corner[:-1, :-1] + corner[:-1, 1:] + corner[1:, :-1] + corner[1:, 1:]) + friction_in


def relax(state, viscous, friction_in, target, safe_diag, keep):
    inner = state[:, 1:-1, 1:-1]
    image = apply_operator(state, viscous, friction_in)
    return jnp.where(keep, inner + damping * (target - image) / safe_diag, 0.0)


def cosine_basis():
    places = jnp.arange(TILE, dtype=jnp.float32) + 0.5
    orders = jnp.arange(MODES, dtype=jnp.float32)
    return jnp.cos(math.pi * places[:, None] * orders[None, :] / TILE)


def reference(viscosity, friction, driving, observed, ice_mask, tile_block, owner_list):
    keep = ice_mask > 0
    visc_pad = jnp.pad(viscosity, 1)
    safe_diag = jnp.where(keep, diagonal_of(visc_pad, friction), 1.0)
    state = jnp.where(keep, driving / safe_diag, 0.0)
    for sweep_index in range(3):
        state = relax(jnp.pad(state, ((0, 0), (1, 1), (1, 1))), visc_pad, friction, driving, safe_diag, keep)
    misfit = jnp.where(keep, state - observed, 0.0)
    adjoint = jnp.where(keep, misfit / safe_diag, 0.0)
    for sweep_index in range(3):
        adjoint = relax(jnp.pad(adjoint, ((0, 0), (1, 1), (1, 1))), visc_pad, friction, misfit, safe_diag, keep)
    density = -friction * (adjoint[0] * state[0] + adjoint[1] * state[1])
    tiles = density.reshape(NX // TILE, TILE, NY // TILE, TILE)
    basis = cosine_basis()
    projected = jnp.einsum("ip,aicj,jq->acpq", basis, tiles, basis, precision=lax.Precision.HIGHEST) / TILE
    flat = projected.reshape(-1, MODES * MODES)
    sums = jax.ops.segment_sum(flat, tile_block.reshape(-1).astype(jnp.int32), num_segments=NB)
    picked = sums[owner_list.astype(jnp.int32)]
    return state, picked.reshape(N_OWN, NB // N_OWN, MODES * MODES)
```

```python
import functools
import math

import jax
import jax.numpy as jnp
import numpy as np
from jax import lax
from jax.experimental import pallas as pl
from jax.experimental.pallas import tpu as pltpu
from jax.sharding import PartitionSpec as P

TILE = 128
MODES = 32
SWEEPS = 3
HALO = 8
ARRAYS = 7
EDGE = ARRAYS * HALO
ROW_AXES = ("row", "own")
COL_AXES = ("col",)
PARAMS = pltpu.CompilerParams(vmem_limit_bytes=40 * 1024 * 1024)


def swap(x, axes, first):
    size = lax.axis_size(axes)
    pairs = []
    for i in range(first, size - 1, 2):
        pairs += [(i, i + 1), (i + 1, i)]
    return lax.ppermute(x, axes, pairs)


def is_even(axes):
    index = 0
    for axis in axes:
        index = index * lax.axis_size(axis) + lax.axis_index(axis)
    return lax.rem(index, 2) == 0


def pack_rows_kernel(*refs):
    ins, (to_a, to_b) = refs[:-2], refs[-2:]
    even = is_even(ROW_AXES)
    heads, tails = ins[:5], ins[5:]

    def rows(refs5):
        visc, fric, driv, mask, obs = refs5
        return [visc[...], fric[...], driv[0], driv[1], mask[...].astype(jnp.float32), obs[0], obs[1]]

    for a, (head, tail) in enumerate(zip(rows(heads), rows(tails))):
        at = slice(HALO * a, HALO * (a + 1))
        to_a[at, :] = jnp.where(even, tail, head)
        to_b[at, :] = jnp.where(even, head, tail)


def pack_rows(visc, fric, driv, mask, obs):
    rows, cols = visc.shape
    last = rows // HALO - 1
    flat = lambda block: pl.BlockSpec((HALO, cols), lambda i: (block, 0))
    pair = lambda block: pl.BlockSpec((2, HALO, cols), lambda i: (0, block, 0))
    specs = []
    for block in (0, last):
        specs += [flat(block), flat(block), pair(block), flat(block), pair(block)]
    out = jax.ShapeDtypeStruct((EDGE, cols), jnp.float32)
    whole = pl.BlockSpec((EDGE, cols), lambda i: (0, 0))
    return pl.pallas_call(
        pack_rows_kernel,
        grid=(1,),
        in_specs=specs,
        out_specs=(whole, whole),
        out_shape=(out, out),
        compiler_params=PARAMS,
        name="pack_rows",
    )(visc, fric, driv, mask, obs, visc, fric, driv, mask, obs)


def pack_cols_kernel(visc, fric, driv, mask, obs, from_a, from_b, to_a, to_b):
    rows, cols = visc.shape
    lane = lax.broadcasted_iota(jnp.int32, (TILE, cols), 1)
    even = is_even(COL_AXES)
    for t in range(rows // TILE):
        at = slice(TILE * t, TILE * (t + 1))
        fields = [
            visc[at, :],
            fric[at, :],
            driv[0, at, :],
            driv[1, at, :],
            mask[at, :].astype(jnp.float32),
            obs[0, at, :],
            obs[1, at, :],
        ]
        packed = jnp.zeros((TILE, cols), jnp.float32)
        for a, field in enumerate(fields):
            here = lax.div(lane, 2 * HALO) == a
            packed = jnp.where(here, pltpu.roll(field, (2 * HALO * a + HALO) % cols, 1), packed)
        turned = packed.T
        for a in range(ARRAYS):
            right = turned[2 * HALO * a : 2 * HALO * a + HALO]
            left = turned[2 * HALO * a + HALO : 2 * HALO * (a + 1)]
            out = slice(EDGE * t + HALO * a, EDGE * t + HALO * (a + 1))
            to_a[out, :] = jnp.where(even, right, left)
            to_b[out, :] = jnp.where(even, left, right)
    row_even = is_even(ROW_AXES)
    above = jnp.where(row_even, from_b[...], from_a[...])
    below = jnp.where(row_even, from_a[...], from_b[...])
    halo = jnp.concatenate([above, below, jnp.zeros((TILE - 2 * EDGE, cols), jnp.float32)], axis=0).T
    left, right = halo[:HALO], halo[cols - HALO :]
    out = slice(EDGE * (rows // TILE), EDGE * (rows // TILE) + HALO)
    to_a[out, :] = jnp.where(even, right, left)
    to_b[out, :] = jnp.where(even, left, right)


def pack_cols(visc, fric, driv, mask, obs, from_a, from_b):
    rows, cols = visc.shape
    out = jax.ShapeDtypeStruct((EDGE * (rows // TILE) + HALO, TILE), jnp.float32)
    return pl.pallas_call(
        pack_cols_kernel,
        out_shape=(out, out),
        compiler_params=PARAMS,
        name="pack_cols",
    )(visc, fric, driv, mask, obs, from_a, from_b)


def main_kernel(
    visc, fric, driv, mask, obs, row_a, row_b, col_a, col_b, block, basis_p, basis_q,
    vel, coef,
    turned, w0m, w0s, w1m, w1s, n2m, n2s, cm, cs, im, is_, b0m, b0s, b1m, b1s, dens,
):
    rows, cols = visc.shape
    strips = rows // HALO + 2
    f32 = jnp.float32
    lane = lax.broadcasted_iota(jnp.int32, (HALO, cols), 1)
    sub = lax.broadcasted_iota(jnp.int32, (HALO, cols), 0)
    lane_last = lane == cols - 1
    lane_first = lane == 0
    sub_first = sub == 0
    beside = (lane < HALO) | (lane >= cols - HALO)
    row_even = is_even(ROW_AXES)
    col_even = is_even(COL_AXES)
    body = rows // TILE
    zero = jnp.zeros((HALO, cols), f32)

    for t in range(body):
        parts = []
        for a in range(ARRAYS):
            at = slice(EDGE * t + HALO * a, EDGE * t + HALO * (a + 1))
            got_a, got_b = col_a[at, :], col_b[at, :]
            parts += [jnp.where(col_even, got_b, got_a), jnp.where(col_even, got_a, got_b)]
        parts.append(jnp.zeros((TILE - 2 * EDGE, TILE), f32))
        turned[TILE * t : TILE * (t + 1), :] = jnp.concatenate(parts, axis=0).T
    at = slice(EDGE * body, EDGE * body + HALO)
    got_a, got_b = col_a[at, :], col_b[at, :]
    corner_right = jnp.where(col_even, got_a, got_b)
    corner_left = jnp.where(col_even, got_b, got_a)
    turned[TILE * body :, :] = jnp.concatenate(
        [corner_right, jnp.zeros((cols - 2 * HALO, TILE), f32), corner_left], axis=0
    ).T

    def own(a, at):
        if a == 0:
            return visc[at, :]
        if a == 1:
            return fric[at, :]
        if a in (2, 3):
            return driv[a - 2, at, :]
        if a == 4:
            return mask[at, :].astype(f32)
        return obs[a - 5, at, :]

    def fetch(a, s):
        if s in (0, strips - 1):
            at = slice(HALO * a, HALO * (a + 1))
            got_a, got_b = row_a[at, :], row_b[at, :]
            base = TILE * body + (0 if s == 0 else EDGE) + HALO * a
            side = turned[base : base + HALO, :]
            if s == 0:
                return jnp.where(row_even, got_b, got_a), side
            return jnp.where(row_even, got_a, got_b), side
        at = slice(HALO * (s - 1), HALO * s)
        side = pltpu.roll(turned[at, :], (cols - HALO - 2 * HALO * a) % cols, 1)
        return own(a, at), jnp.where(beside, side, 0.0)

    def next_col(m, s):
        m, s = pltpu.roll(m, cols - 1, 1), pltpu.roll(s, cols - 1, 1)
        return jnp.where(lane_last, s, m), jnp.where(lane_last, m, s)

    def prev_col(m, s):
        m, s = pltpu.roll(m, 1, 1), pltpu.roll(s, 1, 1)
        return jnp.where(lane_first, s, m), jnp.where(lane_first, m, s)

    carried = [zero, zero]
    for s in range(strips):
        at = slice(HALO * s, HALO * (s + 1))
        n = fetch(0, s)
        pairs = []
        for k in range(2):
            shifted = pltpu.roll(n[k], 1, 0)
            pairs.append(n[k] + jnp.where(sub_first, carried[k], shifted))
            carried[k] = shifted
        before = prev_col(*pairs)
        fr = fetch(1, s)
        keep = fetch(4, s)
        d0, d1 = fetch(2, s), fetch(3, s)
        for k, (n2, c, i, b0, b1, w0, w1) in enumerate(
            ((n2m, cm, im, b0m, b1m, w0m, w1m), (n2s, cs, is_, b0s, b1s, w0s, w1s))
        ):
            diag = 1.25 * (pairs[k] + before[k]) + fr[k]
            on = keep[k] > 0.0
            inv = jnp.where(on, 0.5 / jnp.where(on, diag, 1.0), 0.0)
            n2[at, :] = 0.5 * n[k]
            c[at, :] = 1.0 - fr[k] * inv
            i[at, :] = inv
            t0, t1 = inv * d0[k], inv * d1[k]
            b0[at, :] = t0
            b1[at, :] = t1
            w0[at, :] = t0 + t0
            w1[at, :] = t1 + t1
    for w in (w0m, w0s, w1m, w1s):
        w[HALO * strips :, :] = zero

    def sweep(_, carry):
        old = [zero] * 6
        for s in range(strips):
            at = slice(HALO * s, HALO * (s + 1))
            down = slice(HALO * s + 1, HALO * (s + 1) + 1)
            here = ((w0m[at, :], w1m[at, :]), (w0s[at, :], w1s[at, :]))
            below = ((w0m[down, :], w1m[down, :]), (w0s[down, :], w1s[down, :]))
            diff0, diff1, sum0, sum1 = [], [], [], []
            for k in range(2):
                diff0.append(below[k][0] - here[k][0])
                diff1.append(below[k][1] - here[k][1])
                sum0.append(below[k][0] + here[k][0])
                sum1.append(below[k][1] + here[k][1])
            r_diff0 = next_col(*diff0)
            r_sum1 = next_col(*sum1)
            r_mix = next_col(sum0[0] + diff1[0], sum0[1] + diff1[1])
            one, two = [], []
            one_r, two_r = [], []
            for k, n2_ref in enumerate((n2m, n2s)):
                n2 = n2_ref[at, :]
                x = diff0[k] + r_diff0[k]
                y = r_sum1[k] - sum1[k]
                both = x + y
                p = n2 * (both + x)
                r = n2 * (both + y)
                q = (0.5 * n2) * (r_mix[k] + (diff1[k] - sum0[k]))
                ups = []
                for j, v in enumerate((p, q, r)):
                    shifted = pltpu.roll(v, 1, 0)
                    ups.append(jnp.where(sub_first, old[3 * k + j], shifted))
                    old[3 * k + j] = shifted
                g, t = ups[0] - p, ups[1] + q
                gq, tr = ups[1] - q, ups[2] + r
                one.append(g - t)
                one_r.append(g + t)
                two.append(gq - tr)
                two_r.append(gq + tr)
            one_r = prev_col(*one_r)
            two_r = prev_col(*two_r)
            for k, (c, i, b0, b1, w0, w1) in enumerate(
                ((cm, im, b0m, b1m, w0m, w1m), (cs, is_, b0s, b1s, w0s, w1s))
            ):
                cv, iv = c[at, :], i[at, :]
                w0[at, :] = (cv * here[k][0] + b0[at, :]) - iv * (one[k] + one_r[k])
                w1[at, :] = (cv * here[k][1] + b1[at, :]) - iv * (two[k] + two_r[k])
        return carry

    lax.fori_loop(0, SWEEPS, sweep, 0)

    for s in range(strips):
        at = slice(HALO * s, HALO * (s + 1))
        o0, o1 = fetch(5, s), fetch(6, s)
        if 0 < s < strips - 1:
            out = slice(HALO * (s - 1), HALO * s)
            vel[0, out, :] = w0m[at, :]
            vel[1, out, :] = w1m[at, :]
        for k, (i, b0, b1, w0, w1) in enumerate(
            ((im, b0m, b1m, w0m, w1m), (is_, b0s, b1s, w0s, w1s))
        ):
            inv = i[at, :]
            t0, t1 = inv * (w0[at, :] - o0[k]), inv * (w1[at, :] - o1[k])
            b0[at, :] = t0
            b1[at, :] = t1
            w0[at, :] = t0 + t0
            w1[at, :] = t1 + t1

    lax.fori_loop(0, SWEEPS, sweep, 0)

    for s in range(TILE // HALO):
        total = zero
        for t in range(body):
            out = slice(TILE * t + HALO * s, TILE * t + HALO * (s + 1))
            at = slice(TILE * t + HALO * (s + 1), TILE * t + HALO * (s + 2))
            total -= fric[out, :] * (w0m[at, :] * vel[0, out, :] + w1m[at, :] * vel[1, out, :])
        dens[HALO * s : HALO * (s + 1), :] = total
    exact = dict(precision=lax.Precision.HIGHEST, preferred_element_type=f32)
    half = jnp.dot(basis_p[...], dens[...], **exact)
    full = jnp.dot(half, basis_q[...], **exact)
    groups = MODES // HALO
    which = lax.div(lane, MODES)
    flat = full[:HALO]
    for j in range(1, groups):
        flat = jnp.where(which == j, full[HALO * j : HALO * (j + 1)], flat)
    count = coef.shape[0]
    first = (lax.axis_index("row") * lax.axis_size("own") + lax.axis_index("own")) * count
    for g in range(count):
        coef[g] = jnp.where(block[0, 0] - first == g, flat, 0.0)


def bases():
    places = np.arange(TILE) + 0.5
    basis = np.cos(math.pi * places[:, None] * np.arange(MODES)[None, :] / TILE)
    groups = MODES // HALO
    order = np.arange(MODES).reshape(HALO, groups).T.reshape(-1)
    first = basis.T[order] / TILE
    second = np.tile(basis, (1, groups))
    return jnp.asarray(first, jnp.float32), jnp.asarray(second, jnp.float32)


def main(visc, fric, driv, mask, obs, row_a, row_b, col_a, col_b, block, groups):
    rows, cols = visc.shape
    f32 = jnp.float32
    deep = rows + 2 * HALO
    field = pltpu.VMEM((deep, cols), f32)
    swept = pltpu.VMEM((deep + HALO, cols), f32)
    vmem = pl.BlockSpec(memory_space=pltpu.VMEM)
    smem = pl.BlockSpec(memory_space=pltpu.SMEM)
    basis_p, basis_q = bases()
    return pl.pallas_call(
        main_kernel,
        in_specs=[vmem] * 9 + [smem] + [vmem] * 2,
        out_specs=(vmem, vmem),
        out_shape=(
            jax.ShapeDtypeStruct((2, rows, cols), f32),
            jax.ShapeDtypeStruct((groups, HALO, TILE), f32),
        ),
        scratch_shapes=[pltpu.VMEM((rows + TILE, cols), f32)]
        + [swept] * 4
        + [field] * 10
        + [pltpu.VMEM((TILE, TILE), f32)],
        compiler_params=PARAMS,
        name="sweeps",
    )(visc, fric, driv, mask, obs, row_a, row_b, col_a, col_b, block, basis_p, basis_q)


def local(viscosity, friction, driving, observed, ice_mask, tile_block, owner_list):
    fields = (viscosity, friction, driving, ice_mask, observed)
    to_a, to_b = pack_rows(*fields)
    row_a = swap(to_a, ROW_AXES, 0)
    row_b = swap(to_b, ROW_AXES, 1)
    to_a, to_b = pack_cols(*fields, row_a, row_b)
    col_a = swap(to_a, COL_AXES, 0)
    col_b = swap(to_b, COL_AXES, 1)
    groups = owner_list.shape[0] // lax.axis_size(ROW_AXES)
    state, coef = main(*fields, row_a, row_b, col_a, col_b, tile_block, groups)
    every = lax.all_gather(coef, ROW_AXES + COL_AXES, axis=0)
    every = every.reshape(-1, lax.axis_size(COL_AXES), groups, HALO, TILE)
    owner_rows = owner_list.reshape(lax.axis_size("own"), -1)
    mine = lax.dynamic_index_in_dim(owner_rows, lax.axis_index("own"), 0, keepdims=False)
    summed = jnp.sum(every, axis=1).reshape(-1, MODES * MODES)
    picked = jnp.take(summed, mine, axis=0)
    return (state, picked[None])


def solution(mesh):
    return jax.shard_map(
        local,
        mesh=mesh,
        in_specs=(
            P(("row", "own"), "col"),
            P(("row", "own"), "col"),
            P(None, ("row", "own"), "col"),
            P(None, ("row", "own"), "col"),
            P(("row", "own"), "col"),
            P(("row", "own"), "col"),
            P(),
        ),
        out_specs=(P(None, ("row", "own"), "col"), P("own", None, None)),
        check_vma=False,
    )
```

```python
import functools
import math

import jax
import jax.numpy as jnp
import numpy as np
from jax import lax
from jax.experimental import pallas as pl
from jax.experimental.pallas import tpu as pltpu
from jax.sharding import PartitionSpec as P

TILE = 128
MODES = 32
SWEEPS = 3
HALO = 8
ARRAYS = 7
EDGE = ARRAYS * HALO
ROW_AXES = ("row", "own")
COL_AXES = ("col",)
PARAMS = pltpu.CompilerParams(vmem_limit_bytes=40 * 1024 * 1024)


def swap(x, axes, first):
    size = lax.axis_size(axes)
    pairs = []
    for i in range(first, size - 1, 2):
        pairs += [(i, i + 1), (i + 1, i)]
    return lax.ppermute(x, axes, pairs)


def is_even(axes):
    index = 0
    for axis in axes:
        index = index * lax.axis_size(axis) + lax.axis_index(axis)
    return lax.rem(index, 2) == 0


def pack_rows_kernel(visc, fric, driv, mask, obs, to_a, to_b, head, tail, mask_head, mask_tail, sems):
    rows = visc.shape[0]
    copies = []
    for e, (place, flags, first) in enumerate(((head, mask_head, 0), (tail, mask_tail, rows - HALO))):
        at = pl.ds(first, HALO)
        parts = [visc.at[at], fric.at[at], driv.at[0, at], driv.at[1, at], None, obs.at[0, at], obs.at[1, at]]
        for a, part in enumerate(parts):
            if a == 4:
                copies.append(pltpu.make_async_copy(mask.at[at], flags, sems.at[e, a]))
            else:
                copies.append(pltpu.make_async_copy(part, place.at[pl.ds(HALO * a, HALO)], sems.at[e, a]))
    for copy in copies:
        copy.start()
    for copy in copies:
        copy.wait()
    at = slice(4 * HALO, 5 * HALO)
    head[at, :] = mask_head[...].astype(jnp.float32)
    tail[at, :] = mask_tail[...].astype(jnp.float32)
    even = is_even(ROW_AXES)
    to_a[...] = jnp.where(even, tail[...], head[...])
    to_b[...] = jnp.where(even, head[...], tail[...])


def pack_rows(visc, fric, driv, mask, obs):
    cols = visc.shape[1]
    out = jax.ShapeDtypeStruct((EDGE, cols), jnp.float32)
    return pl.pallas_call(
        pack_rows_kernel,
        in_specs=[pl.BlockSpec(memory_space=pltpu.HBM)] * 5,
        out_shape=(out, out),
        scratch_shapes=[pltpu.VMEM((EDGE, cols), jnp.float32)] * 2
        + [pltpu.VMEM((HALO, cols), jnp.int32)] * 2
        + [pltpu.SemaphoreType.DMA((2, ARRAYS))],
        compiler_params=PARAMS,
        name="pack_rows",
    )(visc, fric, driv, mask, obs)


def pack_cols_kernel(visc, fric, driv, mask, obs, from_a, from_b, to_a, to_b):
    rows, cols = visc.shape
    lane = lax.broadcasted_iota(jnp.int32, (TILE, cols), 1)
    even = is_even(COL_AXES)
    for t in range(rows // TILE):
        at = slice(TILE * t, TILE * (t + 1))
        fields = [
            visc[at, :],
            fric[at, :],
            driv[0, at, :],
            driv[1, at, :],
            mask[at, :].astype(jnp.float32),
            obs[0, at, :],
            obs[1, at, :],
        ]
        packed = jnp.zeros((TILE, cols), jnp.float32)
        for a, field in enumerate(fields):
            here = lax.div(lane, 2 * HALO) == a
            packed = jnp.where(here, pltpu.roll(field, (2 * HALO * a + HALO) % cols, 1), packed)
        turned = packed.T
        for a in range(ARRAYS):
            right = turned[2 * HALO * a : 2 * HALO * a + HALO]
            left = turned[2 * HALO * a + HALO : 2 * HALO * (a + 1)]
            out = slice(EDGE * t + HALO * a, EDGE * t + HALO * (a + 1))
            to_a[out, :] = jnp.where(even, right, left)
            to_b[out, :] = jnp.where(even, left, right)
    row_even = is_even(ROW_AXES)
    above = jnp.where(row_even, from_b[...], from_a[...])
    below = jnp.where(row_even, from_a[...], from_b[...])
    halo = jnp.concatenate([above, below, jnp.zeros((TILE - 2 * EDGE, cols), jnp.float32)], axis=0).T
    left, right = halo[:HALO], halo[cols - HALO :]
    out = slice(EDGE * (rows // TILE), EDGE * (rows // TILE) + HALO)
    to_a[out, :] = jnp.where(even, right, left)
    to_b[out, :] = jnp.where(even, left, right)


def pack_cols(visc, fric, driv, mask, obs, from_a, from_b):
    rows, cols = visc.shape
    out = jax.ShapeDtypeStruct((EDGE * (rows // TILE) + HALO, TILE), jnp.float32)
    return pl.pallas_call(
        pack_cols_kernel,
        out_shape=(out, out),
        compiler_params=PARAMS,
        name="pack_cols",
    )(visc, fric, driv, mask, obs, from_a, from_b)


def main_kernel(
    visc, fric, driv, mask, obs, row_a, row_b, col_a, col_b, block, basis_p, basis_q,
    vel, coef,
    turned, w0m, w0s, w1m, w1s, n2m, n2s, cm, cs, im, is_, b0m, b0s, b1m, b1s, dens,
):
    rows, cols = visc.shape
    strips = rows // HALO + 2
    f32 = jnp.float32
    lane = lax.broadcasted_iota(jnp.int32, (HALO, cols), 1)
    sub = lax.broadcasted_iota(jnp.int32, (HALO, cols), 0)
    lane_last = lane == cols - 1
    lane_first = lane == 0
    sub_first = sub == 0
    beside = (lane < HALO) | (lane >= cols - HALO)
    row_even = is_even(ROW_AXES)
    col_even = is_even(COL_AXES)
    body = rows // TILE
    zero = jnp.zeros((HALO, cols), f32)

    for t in range(body):
        parts = []
        for a in range(ARRAYS):
            at = slice(EDGE * t + HALO * a, EDGE * t + HALO * (a + 1))
            got_a, got_b = col_a[at, :], col_b[at, :]
            parts += [jnp.where(col_even, got_b, got_a), jnp.where(col_even, got_a, got_b)]
        parts.append(jnp.zeros((TILE - 2 * EDGE, TILE), f32))
        turned[TILE * t : TILE * (t + 1), :] = jnp.concatenate(parts, axis=0).T
    at = slice(EDGE * body, EDGE * body + HALO)
    got_a, got_b = col_a[at, :], col_b[at, :]
    corner_right = jnp.where(col_even, got_a, got_b)
    corner_left = jnp.where(col_even, got_b, got_a)
    turned[TILE * body :, :] = jnp.concatenate(
        [corner_right, jnp.zeros((cols - 2 * HALO, TILE), f32), corner_left], axis=0
    ).T

    def own(a, at):
        if a == 0:
            return visc[at, :]
        if a == 1:
            return fric[at, :]
        if a in (2, 3):
            return driv[a - 2, at, :]
        if a == 4:
            return mask[at, :].astype(f32)
        return obs[a - 5, at, :]

    def fetch(a, s):
        if s in (0, strips - 1):
            at = slice(HALO * a, HALO * (a + 1))
            got_a, got_b = row_a[at, :], row_b[at, :]
            base = TILE * body + (0 if s == 0 else EDGE) + HALO * a
            side = turned[base : base + HALO, :]
            if s == 0:
                return jnp.where(row_even, got_b, got_a), side
            return jnp.where(row_even, got_a, got_b), side
        at = slice(HALO * (s - 1), HALO * s)
        side = pltpu.roll(turned[at, :], (cols - HALO - 2 * HALO * a) % cols, 1)
        return own(a, at), jnp.where(beside, side, 0.0)

    def next_col(m, s):
        m, s = pltpu.roll(m, cols - 1, 1), pltpu.roll(s, cols - 1, 1)
        return jnp.where(lane_last, s, m), jnp.where(lane_last, m, s)

    def prev_col(m, s):
        m, s = pltpu.roll(m, 1, 1), pltpu.roll(s, 1, 1)
        return jnp.where(lane_first, s, m), jnp.where(lane_first, m, s)

    carried = [zero, zero]
    for s in range(strips):
        at = slice(HALO * s, HALO * (s + 1))
        n = fetch(0, s)
        pairs = []
        for k in range(2):
            shifted = pltpu.roll(n[k], 1, 0)
            pairs.append(n[k] + jnp.where(sub_first, carried[k], shifted))
            carried[k] = shifted
        before = prev_col(*pairs)
        fr = fetch(1, s)
        keep = fetch(4, s)
        d0, d1 = fetch(2, s), fetch(3, s)
        for k, (n2, c, i, b0, b1, w0, w1) in enumerate(
            ((n2m, cm, im, b0m, b1m, w0m, w1m), (n2s, cs, is_, b0s, b1s, w0s, w1s))
        ):
            diag = 1.25 * (pairs[k] + before[k]) + fr[k]
            on = keep[k] > 0.0
            inv = jnp.where(on, 0.5 / jnp.where(on, diag, 1.0), 0.0)
            n2[at, :] = 0.5 * n[k]
            c[at, :] = 1.0 - fr[k] * inv
            i[at, :] = inv
            t0, t1 = inv * d0[k], inv * d1[k]
            b0[at, :] = t0
            b1[at, :] = t1
            w0[at, :] = t0 + t0
            w1[at, :] = t1 + t1
    for w in (w0m, w0s, w1m, w1s):
        w[HALO * strips :, :] = zero

    def sweep(_, carry):
        old = [zero] * 6
        for s in range(strips):
            at = slice(HALO * s, HALO * (s + 1))
            down = slice(HALO * s + 1, HALO * (s + 1) + 1)
            here = ((w0m[at, :], w1m[at, :]), (w0s[at, :], w1s[at, :]))
            below = ((w0m[down, :], w1m[down, :]), (w0s[down, :], w1s[down, :]))
            diff0, diff1, sum0, sum1 = [], [], [], []
            for k in range(2):
                diff0.append(below[k][0] - here[k][0])
                diff1.append(below[k][1] - here[k][1])
                sum0.append(below[k][0] + here[k][0])
                sum1.append(below[k][1] + here[k][1])
            r_diff0 = next_col(*diff0)
            r_sum1 = next_col(*sum1)
            r_mix = next_col(sum0[0] + diff1[0], sum0[1] + diff1[1])
            one, two = [], []
            one_r, two_r = [], []
            for k, n2_ref in enumerate((n2m, n2s)):
                n2 = n2_ref[at, :]
                x = diff0[k] + r_diff0[k]
                y = r_sum1[k] - sum1[k]
                both = x + y
                p = n2 * (both + x)
                r = n2 * (both + y)
                q = (0.5 * n2) * (r_mix[k] + (diff1[k] - sum0[k]))
                ups = []
                for j, v in enumerate((p, q, r)):
                    shifted = pltpu.roll(v, 1, 0)
                    ups.append(jnp.where(sub_first, old[3 * k + j], shifted))
                    old[3 * k + j] = shifted
                g, t = ups[0] - p, ups[1] + q
                gq, tr = ups[1] - q, ups[2] + r
                one.append(g - t)
                one_r.append(g + t)
                two.append(gq - tr)
                two_r.append(gq + tr)
            one_r = prev_col(*one_r)
            two_r = prev_col(*two_r)
            for k, (c, i, b0, b1, w0, w1) in enumerate(
                ((cm, im, b0m, b1m, w0m, w1m), (cs, is_, b0s, b1s, w0s, w1s))
            ):
                cv, iv = c[at, :], i[at, :]
                w0[at, :] = (cv * here[k][0] + b0[at, :]) - iv * (one[k] + one_r[k])
                w1[at, :] = (cv * here[k][1] + b1[at, :]) - iv * (two[k] + two_r[k])
        return carry

    lax.fori_loop(0, SWEEPS, sweep, 0)

    for s in range(strips):
        at = slice(HALO * s, HALO * (s + 1))
        o0, o1 = fetch(5, s), fetch(6, s)
        if 0 < s < strips - 1:
            out = slice(HALO * (s - 1), HALO * s)
            vel[0, out, :] = w0m[at, :]
            vel[1, out, :] = w1m[at, :]
        for k, (i, b0, b1, w0, w1) in enumerate(
            ((im, b0m, b1m, w0m, w1m), (is_, b0s, b1s, w0s, w1s))
        ):
            inv = i[at, :]
            t0, t1 = inv * (w0[at, :] - o0[k]), inv * (w1[at, :] - o1[k])
            b0[at, :] = t0
            b1[at, :] = t1
            w0[at, :] = t0 + t0
            w1[at, :] = t1 + t1

    lax.fori_loop(0, SWEEPS, sweep, 0)

    for s in range(TILE // HALO):
        total = zero
        for t in range(body):
            out = slice(TILE * t + HALO * s, TILE * t + HALO * (s + 1))
            at = slice(TILE * t + HALO * (s + 1), TILE * t + HALO * (s + 2))
            total -= fric[out, :] * (w0m[at, :] * vel[0, out, :] + w1m[at, :] * vel[1, out, :])
        dens[HALO * s : HALO * (s + 1), :] = total
    exact = dict(precision=lax.Precision.HIGHEST, preferred_element_type=f32)
    half = jnp.dot(basis_p[...], dens[...], **exact)
    full = jnp.dot(half, basis_q[...], **exact)
    groups = MODES // HALO
    which = lax.div(lane, MODES)
    flat = full[:HALO]
    for j in range(1, groups):
        flat = jnp.where(which == j, full[HALO * j : HALO * (j + 1)], flat)
    count = coef.shape[0]
    first = (lax.axis_index("row") * lax.axis_size("own") + lax.axis_index("own")) * count
    for g in range(count):
        coef[g] = jnp.where(block[0, 0] - first == g, flat, 0.0)


def bases():
    places = np.arange(TILE) + 0.5
    basis = np.cos(math.pi * places[:, None] * np.arange(MODES)[None, :] / TILE)
    groups = MODES // HALO
    order = np.arange(MODES).reshape(HALO, groups).T.reshape(-1)
    first = basis.T[order] / TILE
    second = np.tile(basis, (1, groups))
    return jnp.asarray(first, jnp.float32), jnp.asarray(second, jnp.float32)


def main(visc, fric, driv, mask, obs, row_a, row_b, col_a, col_b, block, groups):
    rows, cols = visc.shape
    f32 = jnp.float32
    deep = rows + 2 * HALO
    field = pltpu.VMEM((deep, cols), f32)
    swept = pltpu.VMEM((deep + HALO, cols), f32)
    vmem = pl.BlockSpec(memory_space=pltpu.VMEM)
    smem = pl.BlockSpec(memory_space=pltpu.SMEM)
    basis_p, basis_q = bases()
    return pl.pallas_call(
        main_kernel,
        in_specs=[vmem] * 9 + [smem] + [vmem] * 2,
        out_specs=(vmem, vmem),
        out_shape=(
            jax.ShapeDtypeStruct((2, rows, cols), f32),
            jax.ShapeDtypeStruct((groups, HALO, TILE), f32),
        ),
        scratch_shapes=[pltpu.VMEM((rows + TILE, cols), f32)]
        + [swept] * 4
        + [field] * 10
        + [pltpu.VMEM((TILE, TILE), f32)],
        compiler_params=PARAMS,
        name="sweeps",
    )(visc, fric, driv, mask, obs, row_a, row_b, col_a, col_b, block, basis_p, basis_q)


def exchange(x, axes, bit):
    size = lax.axis_size(axes)
    return lax.ppermute(x, axes, [(i, i ^ bit) for i in range(size)])


def pick_kernel(owners, every, out):
    mine = out.shape[1]
    groups, tiles = every.shape[1:3]
    me = lax.axis_index("row") * lax.axis_size("own") + lax.axis_index("own")
    first = lax.axis_index("own") * mine
    for k in range(mine):
        block = owners[first + k]
        chosen = every[lax.div(block, groups) ^ me, lax.rem(block, groups)]
        for r in range(tiles):
            out[0, k : k + 1, TILE * r : TILE * (r + 1)] = chosen[r : r + 1]


def pick(owners, every, mine):
    return pl.pallas_call(
        pick_kernel,
        in_specs=[pl.BlockSpec(memory_space=pltpu.SMEM), pl.BlockSpec(memory_space=pltpu.VMEM)],
        out_shape=jax.ShapeDtypeStruct((1, mine, MODES * MODES), jnp.float32),
        compiler_params=PARAMS,
        name="pick",
    )(owners, every)


def local(viscosity, friction, driving, observed, ice_mask, tile_block, owner_list):
    fields = (viscosity, friction, driving, ice_mask, observed)
    to_a, to_b = pack_rows(*fields)
    row_a = swap(to_a, ROW_AXES, 0)
    row_b = swap(to_b, ROW_AXES, 1)
    to_a, to_b = pack_cols(*fields, row_a, row_b)
    col_a = swap(to_a, COL_AXES, 0)
    col_b = swap(to_b, COL_AXES, 1)
    groups = owner_list.shape[0] // lax.axis_size(ROW_AXES)
    state, coef = main(*fields, row_a, row_b, col_a, col_b, tile_block, groups)
    bit = 1
    while bit < lax.axis_size(COL_AXES):
        coef = coef + exchange(coef, COL_AXES, bit)
        bit *= 2
    every = coef[None]
    bit = 1
    while bit < lax.axis_size(ROW_AXES):
        every = jnp.concatenate([every, exchange(every, ROW_AXES, bit)], axis=0)
        bit *= 2
    picked = pick(owner_list, every, owner_list.shape[0] // lax.axis_size("own"))
    return (state, picked)


def solution(mesh):
    return jax.shard_map(
        local,
        mesh=mesh,
        in_specs=(
            P(("row", "own"), "col"),
            P(("row", "own"), "col"),
            P(None, ("row", "own"), "col"),
            P(None, ("row", "own"), "col"),
            P(("row", "own"), "col"),
            P(("row", "own"), "col"),
            P(),
        ),
        out_specs=(P(None, ("row", "own"), "col"), P("own", None, None)),
        check_vma=False,
    )
```

```python
import functools
import math

import jax
import jax.numpy as jnp
import numpy as np
from jax import lax
from jax.experimental import pallas as pl
from jax.experimental.pallas import tpu as pltpu
from jax.sharding import PartitionSpec as P

TILE = 128
MODES = 32
SWEEPS = 3
HALO = 8
ARRAYS = 7
EDGE = ARRAYS * HALO
ROW_AXES = ("row", "own")
COL_AXES = ("col",)
PARAMS = pltpu.CompilerParams(vmem_limit_bytes=40 * 1024 * 1024)
EDGE_PARAMS = pltpu.CompilerParams(vmem_limit_bytes=64 * 1024 * 1024 - 150 * 1024)


def swap(x, axes, first):
    size = lax.axis_size(axes)
    pairs = []
    for i in range(first, size - 1, 2):
        pairs += [(i, i + 1), (i + 1, i)]
    return lax.ppermute(x, axes, pairs)


def is_even(axes):
    index = 0
    for axis in axes:
        index = index * lax.axis_size(axis) + lax.axis_index(axis)
    return lax.rem(index, 2) == 0


def pack_rows_kernel(visc, fric, driv, mask, obs, to_a, to_b, head, tail, mask_head, mask_tail, sems):
    rows = visc.shape[0]
    copies = []
    for e, (place, flags, first) in enumerate(((head, mask_head, 0), (tail, mask_tail, rows - HALO))):
        at = pl.ds(first, HALO)
        parts = [visc.at[at], fric.at[at], driv.at[0, at], driv.at[1, at], None, obs.at[0, at], obs.at[1, at]]
        for a, part in enumerate(parts):
            if a == 4:
                copies.append(pltpu.make_async_copy(mask.at[at], flags, sems.at[e, a]))
            else:
                copies.append(pltpu.make_async_copy(part, place.at[pl.ds(HALO * a, HALO)], sems.at[e, a]))
    for copy in copies:
        copy.start()
    for copy in copies:
        copy.wait()
    at = slice(4 * HALO, 5 * HALO)
    head[at, :] = mask_head[...].astype(jnp.float32)
    tail[at, :] = mask_tail[...].astype(jnp.float32)
    even = is_even(ROW_AXES)
    to_a[...] = jnp.where(even, tail[...], head[...])
    to_b[...] = jnp.where(even, head[...], tail[...])


def pack_rows(visc, fric, driv, mask, obs):
    cols = visc.shape[1]
    out = jax.ShapeDtypeStruct((EDGE, cols), jnp.float32)
    return pl.pallas_call(
        pack_rows_kernel,
        in_specs=[pl.BlockSpec(memory_space=pltpu.HBM)] * 5,
        out_shape=(out, out),
        scratch_shapes=[pltpu.VMEM((EDGE, cols), jnp.float32)] * 2
        + [pltpu.VMEM((HALO, cols), jnp.int32)] * 2
        + [pltpu.SemaphoreType.DMA((2, ARRAYS))],
        compiler_params=EDGE_PARAMS,
        name="pack_rows",
    )(visc, fric, driv, mask, obs)


def pack_cols_kernel(visc, fric, driv, mask, obs, from_a, from_b, to_a, to_b):
    rows, cols = visc.shape
    lane = lax.broadcasted_iota(jnp.int32, (TILE, cols), 1)
    even = is_even(COL_AXES)
    for t in range(rows // TILE):
        at = slice(TILE * t, TILE * (t + 1))
        fields = [
            visc[at, :],
            fric[at, :],
            driv[0, at, :],
            driv[1, at, :],
            mask[at, :].astype(jnp.float32),
            obs[0, at, :],
            obs[1, at, :],
        ]
        packed = jnp.zeros((TILE, cols), jnp.float32)
        for a, field in enumerate(fields):
            here = lax.div(lane, 2 * HALO) == a
            packed = jnp.where(here, pltpu.roll(field, (2 * HALO * a + HALO) % cols, 1), packed)
        turned = packed.T
        for a in range(ARRAYS):
            right = turned[2 * HALO * a : 2 * HALO * a + HALO]
            left = turned[2 * HALO * a + HALO : 2 * HALO * (a + 1)]
            out = slice(EDGE * t + HALO * a, EDGE * t + HALO * (a + 1))
            to_a[out, :] = jnp.where(even, right, left)
            to_b[out, :] = jnp.where(even, left, right)
    row_even = is_even(ROW_AXES)
    above = jnp.where(row_even, from_b[...], from_a[...])
    below = jnp.where(row_even, from_a[...], from_b[...])
    halo = jnp.concatenate([above, below, jnp.zeros((TILE - 2 * EDGE, cols), jnp.float32)], axis=0).T
    left, right = halo[:HALO], halo[cols - HALO :]
    out = slice(EDGE * (rows // TILE), EDGE * (rows // TILE) + HALO)
    to_a[out, :] = jnp.where(even, right, left)
    to_b[out, :] = jnp.where(even, left, right)


def pack_cols(visc, fric, driv, mask, obs, from_a, from_b):
    rows, cols = visc.shape
    out = jax.ShapeDtypeStruct((EDGE * (rows // TILE) + HALO, TILE), jnp.float32)
    return pl.pallas_call(
        pack_cols_kernel,
        out_shape=(out, out),
        compiler_params=PARAMS,
        name="pack_cols",
    )(visc, fric, driv, mask, obs, from_a, from_b)


def main_kernel(
    visc, fric, driv, mask, obs, row_a, row_b, col_a, col_b, block, basis_p, basis_q,
    vel, coef,
    turned, w0m, w0s, w1m, w1s, n2m, n2s, cm, cs, im, is_, b0m, b0s, b1m, b1s, dens,
):
    rows, cols = visc.shape
    strips = rows // HALO + 2
    f32 = jnp.float32
    lane = lax.broadcasted_iota(jnp.int32, (HALO, cols), 1)
    sub = lax.broadcasted_iota(jnp.int32, (HALO, cols), 0)
    lane_last = lane == cols - 1
    lane_first = lane == 0
    sub_first = sub == 0
    beside = (lane < HALO) | (lane >= cols - HALO)
    row_even = is_even(ROW_AXES)
    col_even = is_even(COL_AXES)
    body = rows // TILE
    zero = jnp.zeros((HALO, cols), f32)

    for t in range(body):
        parts = []
        for a in range(ARRAYS):
            at = slice(EDGE * t + HALO * a, EDGE * t + HALO * (a + 1))
            got_a, got_b = col_a[at, :], col_b[at, :]
            parts += [jnp.where(col_even, got_b, got_a), jnp.where(col_even, got_a, got_b)]
        parts.append(jnp.zeros((TILE - 2 * EDGE, TILE), f32))
        turned[TILE * t : TILE * (t + 1), :] = jnp.concatenate(parts, axis=0).T
    at = slice(EDGE * body, EDGE * body + HALO)
    got_a, got_b = col_a[at, :], col_b[at, :]
    corner_right = jnp.where(col_even, got_a, got_b)
    corner_left = jnp.where(col_even, got_b, got_a)
    turned[TILE * body :, :] = jnp.concatenate(
        [corner_right, jnp.zeros((cols - 2 * HALO, TILE), f32), corner_left], axis=0
    ).T

    def own(a, at):
        if a == 0:
            return visc[at, :]
        if a == 1:
            return fric[at, :]
        if a in (2, 3):
            return driv[a - 2, at, :]
        if a == 4:
            return mask[at, :].astype(f32)
        return obs[a - 5, at, :]

    def fetch(a, s):
        if s in (0, strips - 1):
            at = slice(HALO * a, HALO * (a + 1))
            got_a, got_b = row_a[at, :], row_b[at, :]
            base = TILE * body + (0 if s == 0 else EDGE) + HALO * a
            side = turned[base : base + HALO, :]
            if s == 0:
                return jnp.where(row_even, got_b, got_a), side
            return jnp.where(row_even, got_a, got_b), side
        at = slice(HALO * (s - 1), HALO * s)
        side = pltpu.roll(turned[at, :], (cols - HALO - 2 * HALO * a) % cols, 1)
        return own(a, at), jnp.where(beside, side, 0.0)

    def next_col(m, s):
        m, s = pltpu.roll(m, cols - 1, 1), pltpu.roll(s, cols - 1, 1)
        return jnp.where(lane_last, s, m), jnp.where(lane_last, m, s)

    def prev_col(m, s):
        m, s = pltpu.roll(m, 1, 1), pltpu.roll(s, 1, 1)
        return jnp.where(lane_first, s, m), jnp.where(lane_first, m, s)

    carried = [zero, zero]
    for s in range(strips):
        at = slice(HALO * s, HALO * (s + 1))
        n = fetch(0, s)
        pairs = []
        for k in range(2):
            shifted = pltpu.roll(n[k], 1, 0)
            pairs.append(n[k] + jnp.where(sub_first, carried[k], shifted))
            carried[k] = shifted
        before = prev_col(*pairs)
        fr = fetch(1, s)
        keep = fetch(4, s)
        d0, d1 = fetch(2, s), fetch(3, s)
        for k, (n2, c, i, b0, b1, w0, w1) in enumerate(
            ((n2m, cm, im, b0m, b1m, w0m, w1m), (n2s, cs, is_, b0s, b1s, w0s, w1s))
        ):
            diag = 1.25 * (pairs[k] + before[k]) + fr[k]
            on = keep[k] > 0.0
            inv = jnp.where(on, 0.5 / jnp.where(on, diag, 1.0), 0.0)
            n2[at, :] = 0.5 * n[k]
            c[at, :] = 1.0 - fr[k] * inv
            i[at, :] = inv
            t0, t1 = inv * d0[k], inv * d1[k]
            b0[at, :] = t0
            b1[at, :] = t1
            w0[at, :] = t0 + t0
            w1[at, :] = t1 + t1
    for w in (w0m, w0s, w1m, w1s):
        w[HALO * strips :, :] = zero

    def sweep(_, carry):
        old = [zero] * 6
        for s in range(strips):
            at = slice(HALO * s, HALO * (s + 1))
            down = slice(HALO * s + 1, HALO * (s + 1) + 1)
            here = ((w0m[at, :], w1m[at, :]), (w0s[at, :], w1s[at, :]))
            below = ((w0m[down, :], w1m[down, :]), (w0s[down, :], w1s[down, :]))
            diff0, diff1, sum0, sum1 = [], [], [], []
            for k in range(2):
                diff0.append(below[k][0] - here[k][0])
                diff1.append(below[k][1] - here[k][1])
                sum0.append(below[k][0] + here[k][0])
                sum1.append(below[k][1] + here[k][1])
            r_diff0 = next_col(*diff0)
            r_sum1 = next_col(*sum1)
            r_mix = next_col(sum0[0] + diff1[0], sum0[1] + diff1[1])
            one, two = [], []
            one_r, two_r = [], []
            for k, n2_ref in enumerate((n2m, n2s)):
                n2 = n2_ref[at, :]
                x = diff0[k] + r_diff0[k]
                y = r_sum1[k] - sum1[k]
                both = x + y
                p = n2 * (both + x)
                r = n2 * (both + y)
                q = (0.5 * n2) * (r_mix[k] + (diff1[k] - sum0[k]))
                ups = []
                for j, v in enumerate((p, q, r)):
                    shifted = pltpu.roll(v, 1, 0)
                    ups.append(jnp.where(sub_first, old[3 * k + j], shifted))
                    old[3 * k + j] = shifted
                g, t = ups[0] - p, ups[1] + q
                gq, tr = ups[1] - q, ups[2] + r
                one.append(g - t)
                one_r.append(g + t)
                two.append(gq - tr)
                two_r.append(gq + tr)
            one_r = prev_col(*one_r)
            two_r = prev_col(*two_r)
            for k, (c, i, b0, b1, w0, w1) in enumerate(
                ((cm, im, b0m, b1m, w0m, w1m), (cs, is_, b0s, b1s, w0s, w1s))
            ):
                cv, iv = c[at, :], i[at, :]
                w0[at, :] = (cv * here[k][0] + b0[at, :]) - iv * (one[k] + one_r[k])
                w1[at, :] = (cv * here[k][1] + b1[at, :]) - iv * (two[k] + two_r[k])
        return carry

    lax.fori_loop(0, SWEEPS, sweep, 0)

    for s in range(strips):
        at = slice(HALO * s, HALO * (s + 1))
        o0, o1 = fetch(5, s), fetch(6, s)
        if 0 < s < strips - 1:
            out = slice(HALO * (s - 1), HALO * s)
            vel[0, out, :] = w0m[at, :]
            vel[1, out, :] = w1m[at, :]
        for k, (i, b0, b1, w0, w1) in enumerate(
            ((im, b0m, b1m, w0m, w1m), (is_, b0s, b1s, w0s, w1s))
        ):
            inv = i[at, :]
            t0, t1 = inv * (w0[at, :] - o0[k]), inv * (w1[at, :] - o1[k])
            b0[at, :] = t0
            b1[at, :] = t1
            w0[at, :] = t0 + t0
            w1[at, :] = t1 + t1

    lax.fori_loop(0, SWEEPS, sweep, 0)

    for s in range(TILE // HALO):
        total = zero
        for t in range(body):
            out = slice(TILE * t + HALO * s, TILE * t + HALO * (s + 1))
            at = slice(TILE * t + HALO * (s + 1), TILE * t + HALO * (s + 2))
            total -= fric[out, :] * (w0m[at, :] * vel[0, out, :] + w1m[at, :] * vel[1, out, :])
        dens[HALO * s : HALO * (s + 1), :] = total
    exact = dict(precision=lax.Precision.HIGHEST, preferred_element_type=f32)
    half = jnp.dot(basis_p[...], dens[...], **exact)
    full = jnp.dot(half, basis_q[...], **exact)
    groups = MODES // HALO
    which = lax.div(lane, MODES)
    flat = full[:HALO]
    for j in range(1, groups):
        flat = jnp.where(which == j, full[HALO * j : HALO * (j + 1)], flat)
    count = coef.shape[0]
    first = (lax.axis_index("row") * lax.axis_size("own") + lax.axis_index("own")) * count
    for g in range(count):
        coef[g] = jnp.where(block[0, 0] - first == g, flat, 0.0)


def bases():
    places = np.arange(TILE) + 0.5
    basis = np.cos(math.pi * places[:, None] * np.arange(MODES)[None, :] / TILE)
    groups = MODES // HALO
    order = np.arange(MODES).reshape(HALO, groups).T.reshape(-1)
    first = basis.T[order] / TILE
    second = np.tile(basis, (1, groups))
    return jnp.asarray(first, jnp.float32), jnp.asarray(second, jnp.float32)


def main(visc, fric, driv, mask, obs, row_a, row_b, col_a, col_b, block, groups):
    rows, cols = visc.shape
    f32 = jnp.float32
    deep = rows + 2 * HALO
    field = pltpu.VMEM((deep, cols), f32)
    swept = pltpu.VMEM((deep + HALO, cols), f32)
    vmem = pl.BlockSpec(memory_space=pltpu.VMEM)
    smem = pl.BlockSpec(memory_space=pltpu.SMEM)
    basis_p, basis_q = bases()
    return pl.pallas_call(
        main_kernel,
        in_specs=[vmem] * 9 + [smem] + [vmem] * 2,
        out_specs=(vmem, vmem),
        out_shape=(
            jax.ShapeDtypeStruct((2, rows, cols), f32),
            jax.ShapeDtypeStruct((groups, HALO, TILE), f32),
        ),
        scratch_shapes=[pltpu.VMEM((rows + TILE, cols), f32)]
        + [swept] * 4
        + [field] * 10
        + [pltpu.VMEM((TILE, TILE), f32)],
        compiler_params=PARAMS,
        name="sweeps",
    )(visc, fric, driv, mask, obs, row_a, row_b, col_a, col_b, block, basis_p, basis_q)


def pick_kernel(owners, every, out):
    mine = out.shape[1]
    members, groups, tiles = every.shape[1:4]
    own = lax.axis_index("own")
    wanted = [owners[pl.ds(own, 1), k : k + 1] for k in range(mine)]
    chosen = [jnp.zeros((tiles, TILE), jnp.float32)] * mine
    for r in range(every.shape[0]):
        for g in range(groups):
            total = every[r, 0, g]
            for c in range(1, members):
                total += every[r, c, g]
            for k in range(mine):
                chosen[k] = jnp.where(wanted[k] == r * groups + g, total, chosen[k])
    for k in range(mine):
        for t in range(tiles):
            out[0, k : k + 1, TILE * t : TILE * (t + 1)] = chosen[k][t : t + 1]


def pick(owners, every):
    mine = owners.shape[1]
    return pl.pallas_call(
        pick_kernel,
        out_shape=jax.ShapeDtypeStruct((1, mine, MODES * MODES), jnp.float32),
        compiler_params=PARAMS,
        name="pick",
    )(owners, every)


def local(viscosity, friction, driving, observed, ice_mask, tile_block, owner_list):
    fields = (viscosity, friction, driving, ice_mask, observed)
    to_a, to_b = pack_rows(*fields)
    row_a = swap(to_a, ROW_AXES, 0)
    row_b = swap(to_b, ROW_AXES, 1)
    to_a, to_b = pack_cols(*fields, row_a, row_b)
    col_a = swap(to_a, COL_AXES, 0)
    col_b = swap(to_b, COL_AXES, 1)
    groups = owner_list.shape[0] // lax.axis_size(ROW_AXES)
    state, coef = main(*fields, row_a, row_b, col_a, col_b, tile_block, groups)
    rows, cols = lax.axis_size(ROW_AXES), lax.axis_size(COL_AXES)
    every = jnp.broadcast_to(coef[None], (rows * cols,) + coef.shape)
    every = lax.all_to_all(every, ROW_AXES + COL_AXES, 0, 0, tiled=True)
    every = every.reshape((rows, cols) + coef.shape)
    picked = pick(owner_list.reshape(lax.axis_size("own"), -1), every)
    return (state, picked)


def solution(mesh):
    return jax.shard_map(
        local,
        mesh=mesh,
        in_specs=(
            P(("row", "own"), "col"),
            P(("row", "own"), "col"),
            P(None, ("row", "own"), "col"),
            P(None, ("row", "own"), "col"),
            P(("row", "own"), "col"),
            P(("row", "own"), "col"),
            P(),
        ),
        out_specs=(P(None, ("row", "own"), "col"), P("own", None, None)),
        check_vma=False,
    )
```

```python
import math

import jax
import jax.numpy as jnp
import numpy as np
from jax import lax
from jax.experimental import pallas as pl
from jax.experimental.pallas import tpu as pltpu
from jax.sharding import PartitionSpec as P

TILE = 128
MODES = 32
SWEEPS = 3
SUB = 8
HALO = 8
INNER = 2 * HALO
STRIP = 2 * (HALO + INNER)
ARRAYS = 7
VISC, FRIC, DRIV, MASK, OBS = 0, 1, 2, 4, 5
EDGE = ARRAYS * HALO
SLOT = 2 * INNER
PER = TILE // SLOT
PARTS = 3
ROW_AXES = ("row", "own")
COL_AXES = ("col",)
F32 = jnp.float32
LIMIT = 40 * 1024 * 1024


def swap(x, axes, first):
    size = lax.axis_size(axes)
    pairs = []
    for i in range(first, size - 1, 2):
        pairs += [(i, i + 1), (i + 1, i)]
    return lax.ppermute(x, axes, pairs)


def is_even(axes):
    index = 0
    for axis in axes:
        index = index * lax.axis_size(axis) + lax.axis_index(axis)
    return lax.rem(index, 2) == 0


def lanes():
    return lax.broadcasted_iota(jnp.int32, (SUB, TILE), 1)


def call(kernel, name, outs, scratch, cost, *args):
    return pl.pallas_call(
        kernel,
        out_shape=outs,
        scratch_shapes=scratch,
        compiler_params=pltpu.CompilerParams(vmem_limit_bytes=LIMIT),
        cost_estimate=pl.CostEstimate(flops=cost, bytes_accessed=cost, transcendentals=0),
        name=name,
    )(*args)


def vmem(*shape):
    return pltpu.VMEM(shape, F32)


class Domain:
    def __init__(self, refs, base, span, source):
        self.refs, self.base, self.span, self.source = refs, base, span, source

    def at(self, j):
        return pl.ds(self.base + SUB * j, SUB)

    def prepare(self, flipped):
        n2, n4, c, i, b0, b1, w0, w1 = self.refs
        visc = [self.source(VISC, j) for j in range(self.span)]
        for j in range(self.span):
            at = self.at(j)
            before = visc[j - 1] if j else pltpu.roll(visc[-1], 1, 0)
            pair = visc[j] + before
            fric = self.source(FRIC, j)
            diag = 1.25 * (pair + pltpu.roll(pair, 1, 1)) + fric
            on = self.source(MASK, j) > 0.0
            inv = jnp.where(on, 0.5 / jnp.where(on, diag, 1.0), 0.0)
            half = 0.5 * visc[j]
            n2[at, :] = half
            n4[at, :] = 0.5 * half
            c[at, :] = 1.0 - fric * inv
            i[at, :] = inv
            for k, (b, w) in enumerate(((b0, w0), (b1, w1))):
                value = inv * self.source(DRIV + (1 - k if flipped else k), j)
                b[at, :] = value
                w[at, :] = value + value

    def retarget(self, flipped):
        _, _, _, i, b0, b1, w0, w1 = self.refs
        for j in range(self.span):
            at = self.at(j)
            for k, (b, w) in enumerate(((b0, w0), (b1, w1))):
                value = i[at, :] * (w[at, :] - self.source(OBS + (1 - k if flipped else k), j))
                b[at, :] = value
                w[at, :] = value + value

    def sweep(self):
        n2, n4, c, i, b0, b1, w0, w1 = self.refs

        def corners(j, here, below):
            at = self.at(j)
            diff0, diff1 = below[0] - here[0], below[1] - here[1]
            sum0, sum1 = below[0] + here[0], below[1] + here[1]
            x = diff0 + pltpu.roll(diff0, TILE - 1, 1)
            y = pltpu.roll(sum1, TILE - 1, 1) - sum1
            q = pltpu.roll(sum0 + diff1, TILE - 1, 1) + (diff1 - sum0)
            both = x + y
            half = n2[at, :]
            return half * (both + x), n4[at, :] * q, half * (both + y)

        def load(j):
            at = self.at(j)
            return w0[at, :], w1[at, :]

        top = load(0)
        end = load(self.span - 1)
        last = corners(self.span - 1, end, [pltpu.roll(v, SUB - 1, 0) for v in top])
        up = [pltpu.roll(v, 1, 0) for v in last]
        here = top
        for j in range(self.span):
            at = self.at(j)
            if j < self.span - 1:
                below = load(j + 1)
                p, q, r = corners(j, here, below)
            else:
                below, (p, q, r) = None, last
            g, t = up[0] - p, up[1] + q
            gq, tr = up[1] - q, up[2] + r
            one = (g - t) + pltpu.roll(g + t, 1, 1)
            two = (gq - tr) + pltpu.roll(gq + tr, 1, 1)
            cv, iv = c[at, :], i[at, :]
            w0[at, :] = (cv * here[0] + b0[at, :]) - iv * one
            w1[at, :] = (cv * here[1] + b1[at, :]) - iv * two
            up, here = (p, q, r), below


def run(domains):
    def body(_, carry):
        for domain in domains:
            domain.sweep()
        return carry

    lax.fori_loop(0, SWEEPS, body, 0)


def load_kernel(visc, fric, driv, mask, obs, every, to_a, to_b, flags, sems):
    rows = visc.shape[0]

    def place(a):
        return every.at[pl.ds(rows * a, rows)]

    copies = [
        pltpu.make_async_copy(visc, place(VISC), sems.at[VISC]),
        pltpu.make_async_copy(fric, place(FRIC), sems.at[FRIC]),
        pltpu.make_async_copy(driv.at[0], place(DRIV), sems.at[DRIV]),
        pltpu.make_async_copy(driv.at[1], place(DRIV + 1), sems.at[DRIV + 1]),
        pltpu.make_async_copy(mask, flags, sems.at[MASK]),
        pltpu.make_async_copy(obs.at[0], place(OBS), sems.at[OBS]),
        pltpu.make_async_copy(obs.at[1], place(OBS + 1), sems.at[OBS + 1]),
    ]
    for copy in copies:
        copy.start()
    for copy in copies:
        copy.wait()
    every[MASK * rows : (MASK + 1) * rows, :] = flags[...].astype(F32)
    even = is_even(ROW_AXES)
    for a in range(ARRAYS):
        head = every[rows * a : rows * a + HALO, :]
        tail = every[rows * (a + 1) - HALO : rows * (a + 1), :]
        at = slice(HALO * a, HALO * (a + 1))
        to_a[at, :] = jnp.where(even, tail, head)
        to_b[at, :] = jnp.where(even, head, tail)


def interior_kernel(every, vel, dens, edge, *refs):
    rows = every.shape[0] // ARRAYS
    span = rows // SUB

    def source(a, j):
        return every[pl.ds(rows * a + j, SUB, stride=span), :]

    lane = lanes()
    for part in range(PARTS):
        first = part_start(part, rows)
        for m in range(-(-ARRAYS // PER)):
            strips = []
            for s in range(TILE // SUB):
                row = first + SUB * s
                packed = jnp.zeros((SUB, TILE), F32)
                if 0 <= row < rows:
                    for k in range(min(PER, ARRAYS - PER * m)):
                        base = rows * (PER * m + k) + row
                        moved = pltpu.roll(every[base : base + SUB, :], (SLOT * k + INNER) % TILE, 1)
                        packed = jnp.where(lax.div(lane, SLOT) == k, moved, packed)
                strips.append(packed)
            base = TILE * (2 * part + m)
            edge[base : base + TILE, :] = jnp.concatenate(strips, axis=0).T

    domain = Domain(refs, 0, span, source)
    domain.prepare(False)
    run([domain])
    w0, w1 = refs[-2:]
    for j in range(span):
        at = domain.at(j)
        vel[pl.ds(j, SUB, stride=span), :] = w0[at, :]
        vel[pl.ds(rows + j, SUB, stride=span), :] = w1[at, :]
    domain.retarget(False)
    run([domain])
    for j in range(span):
        at = domain.at(j)
        here = pl.ds(j, SUB, stride=span)
        there = pl.ds(rows + j, SUB, stride=span)
        dens[here, :] = -source(FRIC, j) * (w0[at, :] * vel[here, :] + w1[at, :] * vel[there, :])


def part_start(part, rows):
    return (-HALO, rows // 2 - TILE // 2, rows + HALO - TILE)[part]


def slot(part, a):
    return TILE * (2 * part + a // PER) + SLOT * (a % PER)


def columns_kernel(row_a, row_b, edge, to_a, to_b, full):
    even = is_even(ROW_AXES)
    above = jnp.where(even, row_b[...], row_a[...])
    below = jnp.where(even, row_a[...], row_b[...])
    turned = jnp.concatenate([above, below, jnp.zeros((TILE - 2 * EDGE, TILE), F32)], axis=0).T
    turned = jnp.concatenate([turned[TILE - INNER :], turned[:INNER]], axis=0)
    lane = lax.broadcasted_iota(jnp.int32, (SLOT, TILE), 1)
    even = is_even(COL_AXES)
    for part in range(PARTS):
        for a in range(ARRAYS):
            at = slot(part, a)
            value = edge[at : at + SLOT, :]
            if part == 0:
                value = jnp.where(lane < HALO, pltpu.roll(turned, (TILE - HALO * a) % TILE, 1), value)
            if part == PARTS - 1:
                moved = pltpu.roll(turned, (2 * TILE - HALO - EDGE - HALO * a) % TILE, 1)
                value = jnp.where(lane >= TILE - HALO, moved, value)
            full[at : at + SLOT, :] = value
            right, left = value[INNER - HALO : INNER], value[INNER : INNER + HALO]
            out = slice(EDGE * part + HALO * a, EDGE * part + HALO * (a + 1))
            to_a[out, :] = jnp.where(even, right, left)
            to_b[out, :] = jnp.where(even, left, right)


def strided(stack, base):
    span = STRIP // SUB
    return lambda a, j: stack[pl.ds(base + STRIP * a + j, SUB, stride=span), :]


def top_bottom_kernel(every, row_a, row_b, vel, dens, stack, plain, *refs):
    rows = every.shape[0] // ARRAYS
    even = is_even(ROW_AXES)
    for a in range(ARRAYS):
        at = slice(HALO * a, HALO * (a + 1))
        got_a, got_b = row_a[at, :], row_b[at, :]
        base = STRIP * a
        stack[base : base + HALO, :] = jnp.where(even, got_b, got_a)
        stack[base + HALO : base + HALO + INNER, :] = every[rows * a : rows * a + INNER, :]
        stack[base + HALO + INNER : base + HALO + 2 * INNER, :] = every[
            rows * (a + 1) - INNER : rows * (a + 1), :
        ]
        stack[base + HALO + 2 * INNER : base + STRIP, :] = jnp.where(even, got_a, got_b)
    source = strided(stack, 0)
    domain = Domain(refs, 0, STRIP // SUB, source)
    domain.prepare(False)
    run([domain])
    held = velocity(domain, plain, 0)
    for k in range(2):
        for e in range(2):
            at = STRIP * k + HALO + 2 * INNER * e - HALO * e
            out = 2 * HALO * k + HALO * e
            vel[out : out + HALO, :] = plain[at : at + HALO, :]
    domain.retarget(False)
    run([domain])
    density(domain, held, plain, 0)
    for e in range(2):
        at = HALO + 2 * INNER * e - HALO * e
        dens[HALO * e : HALO * (e + 1), :] = plain[at : at + HALO, :]


def velocity(domain, plain, base):
    w0, w1 = domain.refs[-2:]
    held = []
    for j in range(domain.span):
        at = domain.at(j)
        held.append((w0[at, :], w1[at, :]))
        plain[pl.ds(base + j, SUB, stride=domain.span), :] = held[-1][0]
        plain[pl.ds(base + STRIP + j, SUB, stride=domain.span), :] = held[-1][1]
    return held


def density(domain, held, plain, base):
    w0, w1 = domain.refs[-2:]
    for j in range(domain.span):
        at = domain.at(j)
        value = -domain.source(FRIC, j) * (w0[at, :] * held[j][0] + w1[at, :] * held[j][1])
        plain[pl.ds(base + j, SUB, stride=domain.span), :] = value


def left_right_kernel(
    full, col_a, col_b, vel_in, dens_in, vel_ends, dens_ends, block, basis_p, basis_q,
    vel, coef,
    stack, plain, turned, total, vel_out, sem, *refs,
):
    rows = dens_in.shape[0]
    even = is_even(COL_AXES)
    span = STRIP // SUB
    domains = []
    for part in range(PARTS):
        for a in range(ARRAYS):
            at = slice(EDGE * part + HALO * a, EDGE * part + HALO * (a + 1))
            got_a, got_b = col_a[at, :], col_b[at, :]
            base = STRIP * (ARRAYS * part + a)
            own = slot(part, a)
            stack[base : base + HALO, :] = jnp.where(even, got_b, got_a)
            stack[base + HALO : base + HALO + INNER, :] = full[own + INNER : own + SLOT, :]
            stack[base + HALO + INNER : base + HALO + 2 * INNER, :] = full[own : own + INNER, :]
            stack[base + HALO + 2 * INNER : base + STRIP, :] = jnp.where(even, got_a, got_b)
        source = strided(stack, STRIP * ARRAYS * part)
        domains.append(Domain(refs, STRIP * part, span, source))
    lane = lanes()
    side = (lane < HALO) | (lane >= TILE - HALO)
    middle = jnp.zeros((TILE - 2 * HALO, TILE), F32)

    def turn(base):
        first = plain[base + HALO : base + 2 * HALO, :]
        last = plain[base + STRIP - 2 * HALO : base + STRIP - HALO, :]
        return jnp.concatenate([first, middle, last], axis=0).T

    def from_part(row):
        part = 0 if row < rows // 2 - TILE // 4 else 1 if row < rows // 2 + TILE // 4 else 2
        return part, row - part_start(part, rows)

    for domain in domains:
        domain.prepare(True)
    run(domains)
    held = []
    for part, domain in enumerate(domains):
        base = 2 * STRIP * part
        held.append(velocity(domain, plain, base))
        for k in range(2):
            at = TILE * (2 * part + k)
            turned[at : at + TILE, :] = turn(base + STRIP * (1 - k))
    for k in range(2):
        for row in range(0, rows, SUB):
            if row == 0:
                value = vel_ends[2 * HALO * k : 2 * HALO * k + HALO, :]
            elif row == rows - SUB:
                value = vel_ends[2 * HALO * k + HALO : 2 * HALO * (k + 1), :]
            else:
                value = vel_in[rows * k + row : rows * k + row + SUB, :]
            part, place = from_part(row)
            at = TILE * (2 * part + k) + place
            vel_out[k, row : row + SUB, :] = jnp.where(side, turned[at : at + SUB, :], value)
    copy = pltpu.make_async_copy(vel_out, vel, sem)
    copy.start()

    for domain in domains:
        domain.retarget(True)
    run(domains)
    for part, domain in enumerate(domains):
        base = 2 * STRIP * part
        density(domain, held[part], plain, base)
        at = TILE * 2 * part
        turned[at : at + TILE, :] = turn(base)

    for s in range(TILE // SUB):
        summed = jnp.zeros((SUB, TILE), F32)
        for row in range(SUB * s, rows, TILE):
            if row == 0:
                value = dens_ends[:HALO, :]
            elif row == rows - SUB:
                value = dens_ends[HALO:, :]
            else:
                value = dens_in[row : row + SUB, :]
            part, place = from_part(row)
            at = TILE * 2 * part + place
            summed += jnp.where(side, turned[at : at + SUB, :], value)
        total[SUB * s : SUB * (s + 1), :] = summed
    exact = dict(precision=lax.Precision.HIGHEST, preferred_element_type=F32)
    half = jnp.dot(basis_p[...], total[...], **exact)
    wide = jnp.dot(half, basis_q[...], **exact)
    which = lax.div(lane, MODES)
    flat = wide[:SUB]
    for j in range(1, MODES // SUB):
        flat = jnp.where(which == j, wide[SUB * j : SUB * (j + 1)], flat)
    mark = jnp.broadcast_to(block[:1, :].astype(F32), (1, TILE))
    pieces = [flat[r : r + 1] for r in range(SUB)] + [mark]
    chunk = min(32, coef.shape[0])

    def spread(d, carry):
        for e in range(chunk):
            for r, piece in enumerate(pieces):
                coef[d * chunk + e, :, TILE * r : TILE * (r + 1)] = piece
        return carry

    lax.fori_loop(0, coef.shape[0] // chunk, spread, 0)
    copy.wait()


def bases():
    places = np.arange(TILE) + 0.5
    basis = np.cos(math.pi * places[:, None] * np.arange(MODES)[None, :] / TILE)
    groups = MODES // SUB
    order = np.arange(MODES).reshape(SUB, groups).T.reshape(-1)
    first = basis.T[order] / TILE
    second = np.tile(basis, (1, groups))
    return jnp.asarray(first, F32), jnp.asarray(second, F32)


def pick_kernel(owners, every, out):
    count, mine = every.shape[0], out.shape[1]
    own = lax.axis_index("own")
    wanted = [owners[pl.ds(own, 1), k : k + 1].astype(F32) for k in range(mine)]
    chunk = min(32, count)

    def body(d, sums):
        sums = list(sums)
        for e in range(chunk):
            mark = every[d * chunk + e, :, SUB * TILE :]
            part = every[d * chunk + e, :, : SUB * TILE]
            for k in range(mine):
                hit = jnp.where(mark == wanted[k], 1.0, 0.0)[:, :1] > 0.0
                sums[k] = jnp.where(hit, sums[k] + part, sums[k])
        return tuple(sums)

    sums = lax.fori_loop(0, count // chunk, body, (jnp.zeros((1, SUB * TILE), F32),) * mine)
    for k in range(mine):
        out[0, k : k + 1, :] = sums[k]


def local(viscosity, friction, driving, observed, ice_mask, tile_block, owner_list):
    rows, cols = viscosity.shape
    inputs = [
        pltpu.with_memory_space_constraint(x, pltpu.HBM)
        for x in (viscosity, friction, driving, ice_mask, observed)
    ]
    every, to_a, to_b = call(
        load_kernel,
        "load",
        (vmem(ARRAYS * rows, cols), vmem(EDGE, cols), vmem(EDGE, cols)),
        [pltpu.VMEM((rows, cols), jnp.int32), pltpu.SemaphoreType.DMA((ARRAYS,))],
        10**6,
        *inputs,
    )
    row_a = swap(to_a, ROW_AXES, 0)
    row_b = swap(to_b, ROW_AXES, 1)
    vel_in, dens_in, edge = call(
        interior_kernel,
        "interior",
        (vmem(2 * rows, cols), vmem(rows, cols), vmem(2 * PARTS * TILE, TILE)),
        [vmem(rows, cols)] * 8,
        8 * 10**6,
        every,
    )
    to_a, to_b, full = call(
        columns_kernel,
        "columns",
        (vmem(PARTS * EDGE, TILE), vmem(PARTS * EDGE, TILE), vmem(2 * PARTS * TILE, TILE)),
        [],
        10**5,
        row_a,
        row_b,
        edge,
    )
    col_a = swap(to_a, COL_AXES, 0)
    col_b = swap(to_b, COL_AXES, 1)
    vel_ends, dens_ends = call(
        top_bottom_kernel,
        "top_bottom",
        (vmem(4 * HALO, cols), vmem(2 * HALO, cols)),
        [vmem(ARRAYS * STRIP, cols), vmem(2 * STRIP, cols)] + [vmem(STRIP, cols)] * 8,
        2 * 10**6,
        every,
        row_a,
        row_b,
    )
    devices = lax.axis_size(ROW_AXES + COL_AXES)
    state, coef = call(
        left_right_kernel,
        "left_right",
        (pltpu.HBM((2, rows, cols), F32), vmem(devices, 1, SUB * TILE + TILE)),
        [
            vmem(PARTS * ARRAYS * STRIP, TILE),
            vmem(PARTS * 2 * STRIP, TILE),
            vmem(PARTS * 2 * TILE, TILE),
            vmem(TILE, TILE),
            vmem(2, rows, cols),
            pltpu.SemaphoreType.DMA,
        ]
        + [vmem(PARTS * STRIP, TILE)] * 8,
        4 * 10**6,
        full,
        col_a,
        col_b,
        vel_in,
        dens_in,
        vel_ends,
        dens_ends,
        tile_block,
        *bases(),
    )
    parts = lax.all_to_all(coef, ROW_AXES + COL_AXES, 0, 0, tiled=True)
    owners = owner_list.reshape(lax.axis_size("own"), -1)
    picked = call(
        pick_kernel,
        "pick",
        jax.ShapeDtypeStruct((1, owners.shape[1], MODES * MODES), F32),
        [],
        10**5,
        owners,
        parts,
    )
    return (state, picked)


def solution(mesh):
    return jax.shard_map(
        local,
        mesh=mesh,
        in_specs=(
            P(("row", "own"), "col"),
            P(("row", "own"), "col"),
            P(None, ("row", "own"), "col"),
            P(None, ("row", "own"), "col"),
            P(("row", "own"), "col"),
            P(("row", "own"), "col"),
            P(),
        ),
        out_specs=(P(None, ("row", "own"), "col"), P("own", None, None)),
        check_vma=False,
    )
```

```python
import math

import jax
import jax.numpy as jnp
import numpy as np
from jax import lax
from jax.experimental import pallas as pl
from jax.experimental.pallas import tpu as pltpu
from jax.sharding import PartitionSpec as P

TILE = 128
MODES = 32
SWEEPS = 3
SUB = 8
HALO = 8
INNER = 2 * HALO
STRIP = 2 * (HALO + INNER)
ARRAYS = 7
VISC, FRIC, DRIV, MASK, OBS = 0, 1, 2, 4, 5
EDGE = ARRAYS * HALO
SLOT = 2 * INNER
PER = TILE // SLOT
PARTS = 3
ROW_AXES = ("row", "own")
COL_AXES = ("col",)
F32 = jnp.float32
LIMIT = 40 * 1024 * 1024


def swap(x, axes, first):
    size = lax.axis_size(axes)
    pairs = []
    for i in range(first, size - 1, 2):
        pairs += [(i, i + 1), (i + 1, i)]
    return lax.ppermute(x, axes, pairs)


def is_even(axes):
    index = 0
    for axis in axes:
        index = index * lax.axis_size(axis) + lax.axis_index(axis)
    return lax.rem(index, 2) == 0


def lanes():
    return lax.broadcasted_iota(jnp.int32, (SUB, TILE), 1)


def call(kernel, name, outs, scratch, cost, *args):
    return pl.pallas_call(
        kernel,
        out_shape=outs,
        scratch_shapes=scratch,
        compiler_params=pltpu.CompilerParams(vmem_limit_bytes=LIMIT),
        cost_estimate=pl.CostEstimate(flops=cost, bytes_accessed=cost, transcendentals=0),
        name=name,
    )(*args)


def vmem(*shape):
    return pltpu.VMEM(shape, F32)


FIELDS = 14


class Domain:
    def __init__(self, refs, base, span, source):
        self.refs, self.base, self.span, self.source = refs, base, span, source

    def at(self, j):
        return pl.ds(self.base + SUB * j, SUB)

    def prepare(self, flipped):
        n2, n4, c, i, b0, b1 = self.refs[:6]
        visc = [self.source(VISC, j) for j in range(self.span)]
        for j in range(self.span):
            at = self.at(j)
            before = visc[j - 1] if j else pltpu.roll(visc[-1], 1, 0)
            pair = visc[j] + before
            fric = self.source(FRIC, j)
            diag = 1.25 * (pair + pltpu.roll(pair, 1, 1)) + fric
            on = self.source(MASK, j) > 0.0
            inv = jnp.where(on, 0.5 / jnp.where(on, diag, 1.0), 0.0)
            half = 0.5 * visc[j]
            n2[at, :] = half
            n4[at, :] = 0.5 * half
            c[at, :] = 1.0 - fric * inv
            i[at, :] = inv
            for k, b in enumerate((b0, b1)):
                value = inv * self.source(DRIV + (1 - k if flipped else k), j)
                b[at, :] = value
                self.write(k, at, value + value)

    def write(self, k, at, value):
        self.refs[6 + k][at, :] = value
        self.refs[8 + k][at, :] = pltpu.roll(value, TILE - 1, 1)

    def retarget(self, flipped):
        i, b0, b1, w0, w1 = self.refs[3:8]
        for j in range(self.span):
            at = self.at(j)
            for k, (b, w) in enumerate(((b0, w0), (b1, w1))):
                value = i[at, :] * (w[at, :] - self.source(OBS + (1 - k if flipped else k), j))
                b[at, :] = value
                self.write(k, at, value + value)

    def differences(self):
        n2, n4 = self.refs[:2]
        fields = self.refs[6:10]
        parts = self.refs[10:14]

        def corners(j, here, below):
            w0, w1, r0, r1 = here
            v0, v1, s0, s1 = below
            a1, a2 = s0 - w0, v0 - r0
            e1, e2 = s1 - w1, v1 - r1
            x, y = a1 + a2, e1 - e2
            q = (a1 - a2) + (e1 + e2)
            both = x + y
            at = self.at(j)
            half = n2[at, :]
            return half * (both + x), n4[at, :] * q, half * (both + y)

        def load(j):
            at = self.at(j)
            return [field[at, :] for field in fields]

        top = load(0)
        last = corners(self.span - 1, load(self.span - 1), [pltpu.roll(v, SUB - 1, 0) for v in top])
        up = [pltpu.roll(v, 1, 0) for v in last]
        here = top
        for j in range(self.span):
            at = self.at(j)
            if j < self.span - 1:
                below = load(j + 1)
                p, q, r = corners(j, here, below)
                here = below
            else:
                p, q, r = last
            g, t = up[0] - p, up[1] + q
            gq, tr = up[1] - q, up[2] + r
            parts[0][at, :] = g - t
            parts[1][at, :] = gq - tr
            parts[2][at, :] = pltpu.roll(g + t, 1, 1)
            parts[3][at, :] = pltpu.roll(gq + tr, 1, 1)
            up = (p, q, r)

    def update(self):
        c, i, b0, b1, w0, w1 = self.refs[2:8]
        parts = self.refs[10:14]
        for j in range(self.span):
            at = self.at(j)
            cv, iv = c[at, :], i[at, :]
            for k, (b, w) in enumerate(((b0, w0), (b1, w1))):
                value = (cv * w[at, :] + b[at, :]) - iv * (parts[k][at, :] + parts[k + 2][at, :])
                self.write(k, at, value)


def run(domains):
    def body(_, carry):
        for domain in domains:
            domain.differences()
        for domain in domains:
            domain.update()
        return carry

    lax.fori_loop(0, SWEEPS, body, 0)


def ends_kernel(visc, fric, driv, mask, obs, ends, to_a, to_b, flags, sems):
    rows = visc.shape[0]
    copies = []
    for e, first in enumerate((0, rows - INNER)):
        at = pl.ds(first, INNER)
        parts = [visc.at[at], fric.at[at], driv.at[0, at], driv.at[1, at], None, obs.at[0, at], obs.at[1, at]]
        for a, part in enumerate(parts):
            if a == MASK:
                copies.append(pltpu.make_async_copy(mask.at[at], flags.at[e], sems.at[e, a]))
            else:
                place = ends.at[pl.ds(SLOT * a + INNER * e, INNER)]
                copies.append(pltpu.make_async_copy(part, place, sems.at[e, a]))
    for copy in copies:
        copy.start()
    for copy in copies:
        copy.wait()
    for e in range(2):
        at = SLOT * MASK + INNER * e
        ends[at : at + INNER, :] = flags[e].astype(F32)
    even = is_even(ROW_AXES)
    for a in range(ARRAYS):
        head = ends[SLOT * a : SLOT * a + HALO, :]
        tail = ends[SLOT * (a + 1) - HALO : SLOT * (a + 1), :]
        at = slice(HALO * a, HALO * (a + 1))
        to_a[at, :] = jnp.where(even, tail, head)
        to_b[at, :] = jnp.where(even, head, tail)


def interior_kernel(visc, fric, driv, mask, obs, vel, dens, edge, *refs):
    rows = visc.shape[0]
    span = rows // SUB

    def field(a, at):
        if a == MASK:
            return mask[at, :].astype(F32)
        if a >= OBS:
            return obs[a - OBS, at, :]
        if a >= DRIV:
            return driv[a - DRIV, at, :]
        return (visc, fric)[a][at, :]

    def source(a, j):
        return field(a, pl.ds(j, SUB, stride=span))

    lane = lanes()
    for part in range(PARTS):
        first = part_start(part, rows)
        for m in range(-(-ARRAYS // PER)):
            strips = []
            for s in range(TILE // SUB):
                row = first + SUB * s
                packed = jnp.zeros((SUB, TILE), F32)
                if 0 <= row < rows:
                    for k in range(min(PER, ARRAYS - PER * m)):
                        value = field(PER * m + k, slice(row, row + SUB))
                        moved = pltpu.roll(value, (SLOT * k + INNER) % TILE, 1)
                        packed = jnp.where(lax.div(lane, SLOT) == k, moved, packed)
                strips.append(packed)
            base = TILE * (2 * part + m)
            edge[base : base + TILE, :] = jnp.concatenate(strips, axis=0).T

    domain = Domain(refs, 0, span, source)
    domain.prepare(False)
    run([domain])
    w0, w1 = refs[6:8]
    for j in range(span):
        at = domain.at(j)
        vel[pl.ds(j, SUB, stride=span), :] = w0[at, :]
        vel[pl.ds(rows + j, SUB, stride=span), :] = w1[at, :]
    domain.retarget(False)
    run([domain])
    for j in range(span):
        at = domain.at(j)
        here = pl.ds(j, SUB, stride=span)
        there = pl.ds(rows + j, SUB, stride=span)
        dens[here, :] = -source(FRIC, j) * (w0[at, :] * vel[here, :] + w1[at, :] * vel[there, :])


def part_start(part, rows):
    return (-HALO, rows // 2 - TILE // 2, rows + HALO - TILE)[part]


def slot(part, a):
    return TILE * (2 * part + a // PER) + SLOT * (a % PER)


def columns_kernel(row_a, row_b, edge, to_a, to_b, full):
    even = is_even(ROW_AXES)
    above = jnp.where(even, row_b[...], row_a[...])
    below = jnp.where(even, row_a[...], row_b[...])
    turned = jnp.concatenate([above, below, jnp.zeros((TILE - 2 * EDGE, TILE), F32)], axis=0).T
    turned = jnp.concatenate([turned[TILE - INNER :], turned[:INNER]], axis=0)
    lane = lax.broadcasted_iota(jnp.int32, (SLOT, TILE), 1)
    even = is_even(COL_AXES)
    for part in range(PARTS):
        for a in range(ARRAYS):
            at = slot(part, a)
            value = edge[at : at + SLOT, :]
            if part == 0:
                value = jnp.where(lane < HALO, pltpu.roll(turned, (TILE - HALO * a) % TILE, 1), value)
            if part == PARTS - 1:
                moved = pltpu.roll(turned, (2 * TILE - HALO - EDGE - HALO * a) % TILE, 1)
                value = jnp.where(lane >= TILE - HALO, moved, value)
            full[at : at + SLOT, :] = value
            right, left = value[INNER - HALO : INNER], value[INNER : INNER + HALO]
            out = slice(EDGE * part + HALO * a, EDGE * part + HALO * (a + 1))
            to_a[out, :] = jnp.where(even, right, left)
            to_b[out, :] = jnp.where(even, left, right)


def strided(stack, base):
    span = STRIP // SUB
    return lambda a, j: stack[pl.ds(base + STRIP * a + j, SUB, stride=span), :]


def top_bottom_kernel(ends, row_a, row_b, vel, dens, stack, plain, *refs):
    even = is_even(ROW_AXES)
    for a in range(ARRAYS):
        at = slice(HALO * a, HALO * (a + 1))
        got_a, got_b = row_a[at, :], row_b[at, :]
        base = STRIP * a
        stack[base : base + HALO, :] = jnp.where(even, got_b, got_a)
        stack[base + HALO : base + HALO + SLOT, :] = ends[SLOT * a : SLOT * (a + 1), :]
        stack[base + HALO + 2 * INNER : base + STRIP, :] = jnp.where(even, got_a, got_b)
    source = strided(stack, 0)
    domain = Domain(refs, 0, STRIP // SUB, source)
    domain.prepare(False)
    run([domain])
    held = velocity(domain, plain, 0)
    for k in range(2):
        for e in range(2):
            at = STRIP * k + HALO + 2 * INNER * e - HALO * e
            out = 2 * HALO * k + HALO * e
            vel[out : out + HALO, :] = plain[at : at + HALO, :]
    domain.retarget(False)
    run([domain])
    density(domain, held, plain, 0)
    for e in range(2):
        at = HALO + 2 * INNER * e - HALO * e
        dens[HALO * e : HALO * (e + 1), :] = plain[at : at + HALO, :]


def velocity(domain, plain, base):
    w0, w1 = domain.refs[6:8]
    held = []
    for j in range(domain.span):
        at = domain.at(j)
        held.append((w0[at, :], w1[at, :]))
        plain[pl.ds(base + j, SUB, stride=domain.span), :] = held[-1][0]
        plain[pl.ds(base + STRIP + j, SUB, stride=domain.span), :] = held[-1][1]
    return held


def density(domain, held, plain, base):
    w0, w1 = domain.refs[6:8]
    for j in range(domain.span):
        at = domain.at(j)
        value = -domain.source(FRIC, j) * (w0[at, :] * held[j][0] + w1[at, :] * held[j][1])
        plain[pl.ds(base + j, SUB, stride=domain.span), :] = value


def left_right_kernel(
    full, col_a, col_b, vel_in, dens_in, vel_ends, dens_ends, block, basis_p, basis_q,
    vel, coef,
    stack, plain, turned, total, vel_out, sem, *refs,
):
    rows = dens_in.shape[0]
    even = is_even(COL_AXES)
    span = STRIP // SUB
    domains = []
    for part in range(PARTS):
        for a in range(ARRAYS):
            at = slice(EDGE * part + HALO * a, EDGE * part + HALO * (a + 1))
            got_a, got_b = col_a[at, :], col_b[at, :]
            base = STRIP * (ARRAYS * part + a)
            own = slot(part, a)
            stack[base : base + HALO, :] = jnp.where(even, got_b, got_a)
            stack[base + HALO : base + HALO + INNER, :] = full[own + INNER : own + SLOT, :]
            stack[base + HALO + INNER : base + HALO + 2 * INNER, :] = full[own : own + INNER, :]
            stack[base + HALO + 2 * INNER : base + STRIP, :] = jnp.where(even, got_a, got_b)
        source = strided(stack, STRIP * ARRAYS * part)
        domains.append(Domain(refs, STRIP * part, span, source))
    lane = lanes()
    side = (lane < HALO) | (lane >= TILE - HALO)
    middle = jnp.zeros((TILE - 2 * HALO, TILE), F32)

    def turn(base):
        first = plain[base + HALO : base + 2 * HALO, :]
        last = plain[base + STRIP - 2 * HALO : base + STRIP - HALO, :]
        return jnp.concatenate([first, middle, last], axis=0).T

    def from_part(row):
        part = 0 if row < rows // 2 - TILE // 4 else 1 if row < rows // 2 + TILE // 4 else 2
        return part, row - part_start(part, rows)

    for domain in domains:
        domain.prepare(True)
    run(domains)
    held = []
    for part, domain in enumerate(domains):
        base = 2 * STRIP * part
        held.append(velocity(domain, plain, base))
        for k in range(2):
            at = TILE * (2 * part + k)
            turned[at : at + TILE, :] = turn(base + STRIP * (1 - k))
    for k in range(2):
        for row in range(0, rows, SUB):
            if row == 0:
                value = vel_ends[2 * HALO * k : 2 * HALO * k + HALO, :]
            elif row == rows - SUB:
                value = vel_ends[2 * HALO * k + HALO : 2 * HALO * (k + 1), :]
            else:
                value = vel_in[rows * k + row : rows * k + row + SUB, :]
            part, place = from_part(row)
            at = TILE * (2 * part + k) + place
            vel_out[k, row : row + SUB, :] = jnp.where(side, turned[at : at + SUB, :], value)
    copy = pltpu.make_async_copy(vel_out, vel, sem)
    copy.start()

    for domain in domains:
        domain.retarget(True)
    run(domains)
    for part, domain in enumerate(domains):
        base = 2 * STRIP * part
        density(domain, held[part], plain, base)
        at = TILE * 2 * part
        turned[at : at + TILE, :] = turn(base)

    for s in range(TILE // SUB):
        summed = jnp.zeros((SUB, TILE), F32)
        for row in range(SUB * s, rows, TILE):
            if row == 0:
                value = dens_ends[:HALO, :]
            elif row == rows - SUB:
                value = dens_ends[HALO:, :]
            else:
                value = dens_in[row : row + SUB, :]
            part, place = from_part(row)
            at = TILE * 2 * part + place
            summed += jnp.where(side, turned[at : at + SUB, :], value)
        total[SUB * s : SUB * (s + 1), :] = summed
    exact = dict(precision=lax.Precision.HIGHEST, preferred_element_type=F32)
    half = jnp.dot(basis_p[...], total[...], **exact)
    wide = jnp.dot(half, basis_q[...], **exact)
    which = lax.div(lane, MODES)
    flat = wide[:SUB]
    for j in range(1, MODES // SUB):
        flat = jnp.where(which == j, wide[SUB * j : SUB * (j + 1)], flat)
    mark = jnp.broadcast_to(block[:1, :].astype(F32), (1, TILE))
    pieces = [flat[r : r + 1] for r in range(SUB)] + [mark]
    chunk = min(32, coef.shape[0])

    def spread(d, carry):
        for e in range(chunk):
            for r, piece in enumerate(pieces):
                coef[d * chunk + e, :, TILE * r : TILE * (r + 1)] = piece
        return carry

    lax.fori_loop(0, coef.shape[0] // chunk, spread, 0)
    copy.wait()


def bases():
    places = np.arange(TILE) + 0.5
    basis = np.cos(math.pi * places[:, None] * np.arange(MODES)[None, :] / TILE)
    groups = MODES // SUB
    order = np.arange(MODES).reshape(SUB, groups).T.reshape(-1)
    first = basis.T[order] / TILE
    second = np.tile(basis, (1, groups))
    return jnp.asarray(first, F32), jnp.asarray(second, F32)


def pick_kernel(owners, every, out):
    count, mine = every.shape[0], out.shape[1]
    own = lax.axis_index("own")
    wanted = [owners[pl.ds(own, 1), k : k + 1].astype(F32) for k in range(mine)]
    chunk = min(32, count)

    def body(d, sums):
        sums = list(sums)
        for e in range(chunk):
            mark = every[d * chunk + e, :, SUB * TILE :]
            part = every[d * chunk + e, :, : SUB * TILE]
            for k in range(mine):
                hit = jnp.concatenate([mark == wanted[k]] * SUB, axis=1)
                sums[k] = jnp.where(hit, sums[k] + part, sums[k])
        return tuple(sums)

    sums = lax.fori_loop(0, count // chunk, body, (jnp.zeros((1, SUB * TILE), F32),) * mine)
    for k in range(mine):
        out[0, k : k + 1, :] = sums[k]


def local(viscosity, friction, driving, observed, ice_mask, tile_block, owner_list):
    rows, cols = viscosity.shape
    inputs = (viscosity, friction, driving, ice_mask, observed)
    ends, to_a, to_b = call(
        ends_kernel,
        "ends",
        (vmem(ARRAYS * SLOT, cols), vmem(EDGE, cols), vmem(EDGE, cols)),
        [pltpu.VMEM((2, INNER, cols), jnp.int32), pltpu.SemaphoreType.DMA((2, ARRAYS))],
        10**6,
        *(pltpu.with_memory_space_constraint(x, pltpu.HBM) for x in inputs),
    )
    row_a = swap(to_a, ROW_AXES, 0)
    row_b = swap(to_b, ROW_AXES, 1)
    vel_in, dens_in, edge = call(
        interior_kernel,
        "interior",
        (vmem(2 * rows, cols), vmem(rows, cols), vmem(2 * PARTS * TILE, TILE)),
        [vmem(rows, cols)] * FIELDS,
        8 * 10**6,
        *(pltpu.with_memory_space_constraint(x, pltpu.VMEM) for x in inputs),
    )
    to_a, to_b, full = call(
        columns_kernel,
        "columns",
        (vmem(PARTS * EDGE, TILE), vmem(PARTS * EDGE, TILE), vmem(2 * PARTS * TILE, TILE)),
        [],
        10**5,
        row_a,
        row_b,
        edge,
    )
    col_a = swap(to_a, COL_AXES, 0)
    col_b = swap(to_b, COL_AXES, 1)
    vel_ends, dens_ends = call(
        top_bottom_kernel,
        "top_bottom",
        (vmem(4 * HALO, cols), vmem(2 * HALO, cols)),
        [vmem(ARRAYS * STRIP, cols), vmem(2 * STRIP, cols)] + [vmem(STRIP, cols)] * FIELDS,
        2 * 10**6,
        ends,
        row_a,
        row_b,
    )
    devices = lax.axis_size(ROW_AXES + COL_AXES)
    state, coef = call(
        left_right_kernel,
        "left_right",
        (pltpu.HBM((2, rows, cols), F32), vmem(devices, 1, SUB * TILE + TILE)),
        [
            vmem(PARTS * ARRAYS * STRIP, TILE),
            vmem(PARTS * 2 * STRIP, TILE),
            vmem(PARTS * 2 * TILE, TILE),
            vmem(TILE, TILE),
            vmem(2, rows, cols),
            pltpu.SemaphoreType.DMA,
        ]
        + [vmem(PARTS * STRIP, TILE)] * FIELDS,
        4 * 10**6,
        full,
        col_a,
        col_b,
        vel_in,
        dens_in,
        vel_ends,
        dens_ends,
        tile_block,
        *bases(),
    )
    parts = lax.all_to_all(coef, ROW_AXES + COL_AXES, 0, 0, tiled=True)
    owners = owner_list.reshape(lax.axis_size("own"), -1)
    picked = call(
        pick_kernel,
        "pick",
        jax.ShapeDtypeStruct((1, owners.shape[1], MODES * MODES), F32),
        [],
        10**5,
        owners,
        parts,
    )
    return (state, picked)


def solution(mesh):
    return jax.shard_map(
        local,
        mesh=mesh,
        in_specs=(
            P(("row", "own"), "col"),
            P(("row", "own"), "col"),
            P(None, ("row", "own"), "col"),
            P(None, ("row", "own"), "col"),
            P(("row", "own"), "col"),
            P(("row", "own"), "col"),
            P(),
        ),
        out_specs=(P(None, ("row", "own"), "col"), P("own", None, None)),
        check_vma=False,
    )
```

```python
import math

import jax
import jax.numpy as jnp
import numpy as np
from jax import lax
from jax.experimental import pallas as pl
from jax.experimental.pallas import tpu as pltpu
from jax.sharding import PartitionSpec as P

TILE = 128
MODES = 32
SWEEPS = 3
SUB = 8
HALO = 8
INNER = 2 * HALO
STRIP = 2 * (HALO + INNER)
ARRAYS = 7
VISC, FRIC, DRIV, MASK, OBS = 0, 1, 2, 4, 5
EDGE = ARRAYS * HALO
SLOT = 2 * INNER
PER = TILE // SLOT
GROUPS = 5
SENT = 2 * GROUPS * HALO + HALO
PARTS = 3
UPPER, LOWER = 32, 64
ROW_AXES = ("row", "own")
COL_AXES = ("col",)
F32 = jnp.float32
LIMIT = 40 * 1024 * 1024


def swap(x, axes, first):
    size = lax.axis_size(axes)
    pairs = []
    for i in range(first, size - 1, 2):
        pairs += [(i, i + 1), (i + 1, i)]
    return lax.ppermute(x, axes, pairs)


def is_even(axes):
    index = 0
    for axis in axes:
        index = index * lax.axis_size(axis) + lax.axis_index(axis)
    return lax.rem(index, 2) == 0


def lanes():
    return lax.broadcasted_iota(jnp.int32, (SUB, TILE), 1)


def call(kernel, name, outs, scratch, cost, *args):
    return pl.pallas_call(
        kernel,
        out_shape=outs,
        scratch_shapes=scratch,
        compiler_params=pltpu.CompilerParams(vmem_limit_bytes=LIMIT),
        cost_estimate=pl.CostEstimate(flops=cost, bytes_accessed=cost, transcendentals=0),
        name=name,
    )(*args)


def vmem(*shape):
    return pltpu.VMEM(shape, F32)


FIELDS = 14


class Domain:
    def __init__(self, refs, base, span, source):
        self.refs, self.base, self.span, self.source = refs, base, span, source

    def at(self, j):
        return pl.ds(self.base + SUB * j, SUB)

    def prepare(self, flipped):
        n2, n4, c, i, b0, b1 = self.refs[:6]
        visc = [self.source(VISC, j) for j in range(self.span)]
        for j in range(self.span):
            at = self.at(j)
            before = visc[j - 1] if j else pltpu.roll(visc[-1], 1, 0)
            pair = visc[j] + before
            fric = self.source(FRIC, j)
            diag = 1.25 * (pair + pltpu.roll(pair, 1, 1)) + fric
            on = self.source(MASK, j) > 0.0
            inv = jnp.where(on, 0.5 / jnp.where(on, diag, 1.0), 0.0)
            half = 0.5 * visc[j]
            n2[at, :] = half
            n4[at, :] = 0.5 * half
            c[at, :] = 1.0 - fric * inv
            i[at, :] = inv
            for k, b in enumerate((b0, b1)):
                value = inv * self.source(DRIV + (1 - k if flipped else k), j)
                b[at, :] = value
                self.write(k, at, value + value)

    def write(self, k, at, value):
        self.refs[6 + k][at, :] = value
        self.refs[8 + k][at, :] = pltpu.roll(value, TILE - 1, 1)

    def retarget(self, flipped, velocity=None):
        i, b0, b1 = self.refs[3:6]
        w0, w1 = velocity or self.refs[6:8]
        for j in range(self.span):
            at = self.at(j)
            for k, (b, w) in enumerate(((b0, w0), (b1, w1))):
                value = i[at, :] * (w[at, :] - self.source(OBS + (1 - k if flipped else k), j))
                b[at, :] = value
                self.write(k, at, value + value)

    def differences(self):
        n2, n4 = self.refs[:2]
        fields = self.refs[6:10]
        parts = self.refs[10:14]

        def corners(j, here, below):
            w0, w1, r0, r1 = here
            v0, v1, s0, s1 = below
            a1, a2 = s0 - w0, v0 - r0
            e1, e2 = s1 - w1, v1 - r1
            x, y = a1 + a2, e1 - e2
            q = (a1 - a2) + (e1 + e2)
            both = x + y
            at = self.at(j)
            half = n2[at, :]
            return half * (both + x), n4[at, :] * q, half * (both + y)

        def load(j):
            at = self.at(j)
            return [field[at, :] for field in fields]

        top = load(0)
        last = corners(self.span - 1, load(self.span - 1), [pltpu.roll(v, SUB - 1, 0) for v in top])
        up = [pltpu.roll(v, 1, 0) for v in last]
        here = top
        for j in range(self.span):
            at = self.at(j)
            if j < self.span - 1:
                below = load(j + 1)
                p, q, r = corners(j, here, below)
                here = below
            else:
                p, q, r = last
            g, t = up[0] - p, up[1] + q
            gq, tr = up[1] - q, up[2] + r
            parts[0][at, :] = g - t
            parts[1][at, :] = gq - tr
            parts[2][at, :] = pltpu.roll(g + t, 1, 1)
            parts[3][at, :] = pltpu.roll(gq + tr, 1, 1)
            up = (p, q, r)

    def update(self):
        c, i, b0, b1, w0, w1 = self.refs[2:8]
        parts = self.refs[10:14]
        for j in range(self.span):
            at = self.at(j)
            cv, iv = c[at, :], i[at, :]
            for k, (b, w) in enumerate(((b0, w0), (b1, w1))):
                value = (cv * w[at, :] + b[at, :]) - iv * (parts[k][at, :] + parts[k + 2][at, :])
                self.write(k, at, value)


def run(domains):
    def body(_, carry):
        for domain in domains:
            domain.differences()
        for domain in domains:
            domain.update()
        return carry

    lax.fori_loop(0, SWEEPS, body, 0)


def ends_kernel(visc, fric, driv, mask, obs, ends, to_a, to_b, flags, sems):
    rows = visc.shape[0]
    copies = []
    for e, first in enumerate((0, rows - INNER)):
        at = pl.ds(first, INNER)
        parts = [visc.at[at], fric.at[at], driv.at[0, at], driv.at[1, at], None, obs.at[0, at], obs.at[1, at]]
        for a, part in enumerate(parts):
            if a == MASK:
                copies.append(pltpu.make_async_copy(mask.at[at], flags.at[e], sems.at[e, a]))
            else:
                place = ends.at[pl.ds(SLOT * a + INNER * e, INNER)]
                copies.append(pltpu.make_async_copy(part, place, sems.at[e, a]))
    for copy in copies:
        copy.start()
    for copy in copies:
        copy.wait()
    for e in range(2):
        at = SLOT * MASK + INNER * e
        ends[at : at + INNER, :] = flags[e].astype(F32)
    even = is_even(ROW_AXES)
    for a in range(ARRAYS):
        head = ends[SLOT * a : SLOT * a + HALO, :]
        tail = ends[SLOT * (a + 1) - HALO : SLOT * (a + 1), :]
        at = slice(HALO * a, HALO * (a + 1))
        to_a[at, :] = jnp.where(even, tail, head)
        to_b[at, :] = jnp.where(even, head, tail)


def field_of(visc, fric, driv, mask, obs):
    def field(a, at):
        if a == MASK:
            return mask[at, :].astype(F32)
        if a >= OBS:
            return obs[a - OBS, at, :]
        if a >= DRIV:
            return driv[a - DRIV, at, :]
        return (visc, fric)[a][at, :]

    return field


def first_row(part, lane):
    if part < 2:
        return TILE * part + lane
    if lane < INNER + HALO:
        return TILE + lane
    if lane >= TILE - INNER - HALO:
        return lane
    if UPPER + HALO <= lane < UPPER + SLOT:
        return lane - UPPER - HALO
    if LOWER <= lane < LOWER + INNER + HALO:
        return 2 * TILE - INNER - HALO + lane - LOWER
    return None


def right_part(row):
    seam = TILE - HALO <= row < TILE + HALO
    part = 2 if seam or row == 0 or row == 2 * TILE - HALO else row // TILE
    return part, [lane for lane in range(0, TILE, SUB) if first_row(part, lane) == row][-1]


def slot(part, a):
    return TILE * (2 * part + a // PER) + SLOT * (a % PER)


def interior_kernel(visc, fric, driv, mask, obs, edge, n2, n4, c, i, v0, v1, *refs):
    span = visc.shape[0] // SUB
    field = field_of(visc, fric, driv, mask, obs)
    lane = lanes()
    for part in range(PARTS):
        for m in range(-(-ARRAYS // PER)):
            strips = []
            for at in range(0, TILE, SUB):
                row = first_row(part, at)
                packed = jnp.zeros((SUB, TILE), F32)
                if row is not None:
                    for k in range(min(PER, ARRAYS - PER * m)):
                        value = field(PER * m + k, slice(row, row + SUB))
                        moved = pltpu.roll(value, (SLOT * k + INNER) % TILE, 1)
                        packed = jnp.where(lax.div(lane, SLOT) == k, moved, packed)
                strips.append(packed)
            base = TILE * (2 * part + m)
            edge[base : base + TILE, :] = jnp.concatenate(strips, axis=0).T
    refs = (n2, n4, c, i, *refs[:2], v0, v1, *refs[2:])
    domain = Domain(refs, 0, span, lambda a, j: field(a, pl.ds(j, SUB, stride=span)))
    domain.prepare(False)
    run([domain])


def columns_kernel(row_a, row_b, edge, to_a, to_b, turned):
    even = is_even(ROW_AXES)
    above = jnp.where(even, row_b[...], row_a[...])
    below = jnp.where(even, row_a[...], row_b[...])
    halo = jnp.concatenate([above, below, jnp.zeros((TILE - 2 * EDGE, TILE), F32)], axis=0).T
    turned[:INNER, :] = halo[TILE - INNER :]
    turned[INNER:, :] = halo[:INNER]
    even = is_even(COL_AXES)
    row = lax.broadcasted_iota(jnp.int32, (SUB, TILE), 0)

    def put(out, right, left):
        to_a[out : out + HALO, :] = jnp.where(even, right, left)
        to_b[out : out + HALO, :] = jnp.where(even, left, right)

    for part in range(2):
        right, left = [], []
        for a in range(ARRAYS):
            at = slot(part, a) + INNER
            right.append(edge[at - HALO : at, :])
            left.append(edge[at : at + HALO, :])
        for k in range(2):
            seen_r, seen_l = right[OBS + k], left[OBS + k]
            g = 1 + 2 * k
            right[g] = jnp.where(row < 2, pltpu.roll(seen_r, 2, 0), right[g])
            right[g + 1] = jnp.where(row < 2, pltpu.roll(seen_r, 4, 0), right[g + 1])
            left[g] = jnp.where(row >= 6, pltpu.roll(seen_l, 6, 0), left[g])
            left[g + 1] = jnp.where(row >= 6, pltpu.roll(seen_l, 4, 0), left[g + 1])
        for g in range(GROUPS):
            put(HALO * (GROUPS * part + g), right[g], left[g])
    put(2 * GROUPS * HALO, halo[TILE - HALO :], halo[:HALO])


def strided(stack, base):
    span = STRIP // SUB
    return lambda a, j: stack[pl.ds(base + STRIP * a + j, SUB, stride=span), :]


def velocity(domain, plain, base):
    for j in range(domain.span):
        at = domain.at(j)
        for k in range(2):
            plain[pl.ds(base + STRIP * k + j, SUB, stride=domain.span), :] = domain.refs[6 + k][at, :]


def density(domain, plain, base, out, place):
    w0, w1 = domain.refs[6:8]
    for j in range(domain.span):
        at = domain.at(j)
        v0, v1 = (plain[pl.ds(base + STRIP * k + j, SUB, stride=domain.span), :] for k in range(2))
        value = -domain.source(FRIC, j) * (w0[at, :] * v0 + w1[at, :] * v1)
        out[pl.ds(place + j, SUB, stride=domain.span), :] = value


def beside():
    lane = lanes()
    return (lane < HALO) | (lane >= TILE - HALO)


def adjoint_kernel(
    ends, row_a, row_b, visc, fric, driv, mask, obs, n2, n4, c, i, v0, v1, basis_p, basis_q,
    vel, wide,
    stack, plain, dens, total, *refs,
):
    rows = visc.shape[0]
    span = rows // SUB
    even = is_even(ROW_AXES)
    for a in range(ARRAYS):
        at = slice(HALO * a, HALO * (a + 1))
        got_a, got_b = row_a[at, :], row_b[at, :]
        base = STRIP * a
        stack[base : base + HALO, :] = jnp.where(even, got_b, got_a)
        stack[base + HALO : base + HALO + SLOT, :] = ends[SLOT * a : SLOT * (a + 1), :]
        stack[base + HALO + SLOT : base + STRIP, :] = jnp.where(even, got_a, got_b)
    strips = Domain(refs[:FIELDS], 0, STRIP // SUB, strided(stack, 0))
    strips.prepare(False)
    run([strips])
    velocity(strips, plain, 0)
    outer = (HALO, SLOT)
    for k in range(2):
        for e in range(2):
            out = HALO * (2 * k + e)
            vel[out : out + HALO, :] = plain[STRIP * k + outer[e] : STRIP * k + outer[e] + HALO, :]
    field = field_of(visc, fric, driv, mask, obs)
    interior = Domain(
        (n2, n4, c, i, *refs[FIELDS:]), 0, span, lambda a, j: field(a, pl.ds(j, SUB, stride=span))
    )
    strips.retarget(False)
    interior.retarget(False, (v0, v1))
    run([interior, strips])
    w0, w1 = interior.refs[6:8]
    for j in range(span):
        at = interior.at(j)
        value = -interior.source(FRIC, j) * (w0[at, :] * v0[at, :] + w1[at, :] * v1[at, :])
        dens[pl.ds(j, SUB, stride=span), :] = value
    density(strips, plain, 0, dens, rows)

    side = beside()
    for s in range(0, TILE, SUB):
        summed = jnp.zeros((SUB, TILE), F32)
        for row in range(s, rows, TILE):
            at = rows + outer[0] if row == 0 else rows + outer[1] if row == rows - SUB else row
            summed += dens[at : at + SUB, :]
        total[s : s + SUB, :] = jnp.where(side, 0.0, summed)
    exact = dict(precision=lax.Precision.HIGHEST, preferred_element_type=F32)
    half = jnp.dot(basis_p[...], total[...], **exact)
    wide[...] = jnp.dot(half, basis_q[...], **exact)


def left_right_kernel(
    edge, turned, col_a, col_b, wide_in, block, basis_rows, basis_cols,
    strips, coef,
    stack, plain, *refs,
):
    even = is_even(COL_AXES)
    lane = lanes()
    row = lax.broadcasted_iota(jnp.int32, (SUB, TILE), 0)
    upper = (lane >= UPPER + HALO) & (lane < UPPER + SLOT)
    lower = (lane >= LOWER) & (lane < LOWER + INNER + HALO)
    seam_t0 = lane >= TILE - INNER - HALO
    seam_t1 = lane < INNER + HALO
    corner = ((lane >= UPPER) & (lane < UPPER + HALO)) | ((lane >= LOWER + INNER + HALO) & (lane < LOWER + SLOT))

    def place(part, a):
        return STRIP * (ARRAYS * part + a)

    for from_left in (True, False):
        groups = []
        for g in range(2 * GROUPS + 1):
            got_a, got_b = col_a[HALO * g : HALO * (g + 1), :], col_b[HALO * g : HALO * (g + 1), :]
            groups.append(jnp.where(even, got_b, got_a) if from_left else jnp.where(even, got_a, got_b))
        tiles = []
        for part in range(2):
            tile = groups[GROUPS * part : GROUPS * (part + 1)]
            for k in range(2):
                g, h = tile[1 + 2 * k], tile[2 + 2 * k]
                if from_left:
                    tile.append(jnp.where(row >= 6, pltpu.roll(g, 6, 0), pltpu.roll(h, 4, 0)))
                else:
                    tile.append(jnp.where(row < 2, pltpu.roll(g, 2, 0), pltpu.roll(h, 4, 0)))
            tiles.append(tile)
        for a in range(ARRAYS):
            t0, t1 = tiles[0][a], tiles[1][a]
            third = jnp.where(corner, pltpu.roll(groups[-1], (UPPER - HALO * a) % TILE, 1), 0.0)
            third = jnp.where(upper, pltpu.roll(t0, UPPER + HALO, 1), third)
            third = jnp.where(lower, pltpu.roll(t1, LOWER + INNER + HALO, 1), third)
            third = jnp.where(seam_t0, t0, jnp.where(seam_t1, t1, third))
            for part, value in enumerate((t0, t1, third)):
                base = place(part, a) + (0 if from_left else HALO + SLOT)
                stack[base : base + HALO, :] = value
    for a in range(ARRAYS):
        for part in range(PARTS):
            base = place(part, a) + HALO
            for r in range(0, SLOT, SUB):
                value = edge[slot(part, a) + r : slot(part, a) + r + SUB, :]
                if part == 2:
                    moved = pltpu.roll(turned[r : r + SUB, :], (UPPER - HALO * a) % TILE, 1)
                    value = jnp.where(corner, moved, value)
                to = base + (r + INNER) % SLOT
                stack[to : to + SUB, :] = value

    domains = [
        Domain(refs, STRIP * part, STRIP // SUB, strided(stack, place(part, 0))) for part in range(PARTS)
    ]
    for domain in domains:
        domain.prepare(True)
    run(domains)
    for part, domain in enumerate(domains):
        velocity(domain, strips, 2 * STRIP * part)
        domain.retarget(True)
    run(domains)
    for part, domain in enumerate(domains):
        density(domain, strips, 2 * STRIP * part, plain, STRIP * part)

    def side(part):
        base = STRIP * part
        return jnp.concatenate(
            [plain[base + HALO : base + 2 * HALO, :], plain[base + SLOT : base + SLOT + HALO, :]], axis=0
        )

    lane = lax.broadcasted_iota(jnp.int32, (2 * HALO, TILE), 1)
    straight = (lane >= HALO) & (lane < TILE - HALO)
    seam = (lane < HALO) | (lane >= TILE - HALO)
    top = (lane >= UPPER + HALO) & (lane < UPPER + 2 * HALO)
    bottom = (lane >= LOWER + INNER) & (lane < LOWER + INNER + HALO)
    dens = jnp.concatenate(
        [jnp.where(straight, side(0) + side(1), 0.0), jnp.where(seam | top | bottom, side(2), 0.0)], axis=1
    )
    exact = dict(precision=lax.Precision.HIGHEST, preferred_element_type=F32)
    half = jnp.dot(dens, basis_rows[...], **exact)
    wide = wide_in[...] + lax.dot_general(half, basis_cols[...], (((0,), (0,)), ((), ())), **exact)
    lane = lanes()
    which = lax.div(lane, MODES)
    flat = wide[:SUB]
    for j in range(1, MODES // SUB):
        flat = jnp.where(which == j, wide[SUB * j : SUB * (j + 1)], flat)
    mark = jnp.broadcast_to(block[:1, :].astype(F32), (1, TILE))
    pieces = [flat[r : r + 1] for r in range(SUB)] + [mark]
    chunk = min(32, coef.shape[0])

    def spread(d, carry):
        for e in range(chunk):
            for r, piece in enumerate(pieces):
                coef[d * chunk + e, :, TILE * r : TILE * (r + 1)] = piece
        return carry

    lax.fori_loop(0, coef.shape[0] // chunk, spread, 0)


def join_kernel(v0, v1, ends, strips, vel, turned):
    rows = vel.shape[1]
    span = rows // SUB
    middle = jnp.zeros((TILE - 2 * HALO, TILE), F32)
    side = beside()
    for k, v in enumerate((v0, v1)):
        for part in range(PARTS):
            base = STRIP * (2 * part + 1 - k)
            first = strips[base + HALO : base + 2 * HALO, :]
            last = strips[base + SLOT : base + SLOT + HALO, :]
            at = TILE * (2 * part + k)
            turned[at : at + TILE, :] = jnp.concatenate([first, middle, last], axis=0).T
        for row in range(0, rows, SUB):
            if row == 0:
                value = ends[2 * HALO * k : 2 * HALO * k + HALO, :]
            elif row == rows - SUB:
                value = ends[2 * HALO * k + HALO : 2 * HALO * (k + 1), :]
            else:
                value = v[pl.ds(SUB * (row % span) + row // span, SUB, stride=SUB), :]
            part, lane = right_part(row)
            at = TILE * (2 * part + k) + lane
            vel[k, row : row + SUB, :] = jnp.where(side, turned[at : at + SUB, :], value)


def bases():
    places = np.arange(TILE) + 0.5
    basis = np.cos(math.pi * places[:, None] * np.arange(MODES)[None, :] / TILE)
    groups = MODES // SUB
    order = np.arange(MODES).reshape(SUB, groups).T.reshape(-1)
    rows = basis[:, order] / TILE
    cols = np.tile(basis, (1, groups))
    placed = np.zeros((2 * TILE, MODES))
    for row in range(0, 2 * TILE, SUB):
        part, lane = right_part(row)
        at = lane + (TILE if part == 2 else 0)
        placed[at : at + SUB] = rows[row % TILE : row % TILE + SUB]
    outer = np.concatenate([cols[:HALO], cols[TILE - HALO :]])
    return [jnp.asarray(x, F32) for x in (rows.T, cols, placed, outer)]


def pick_kernel(owners, every, out):
    mine = out.shape[1]
    own = lax.axis_index("own")
    wanted = [owners[pl.ds(own, 1), k : k + 1].astype(F32) for k in range(mine)]
    lines = SUB + 1
    devices = every.shape[0] // lines
    chunk = min(4, devices // SUB)

    def body(d, sums):
        sums = list(sums)
        for e in range(chunk):
            base = (d * chunk + e) * SUB * lines
            mark = every[pl.ds(base + SUB, SUB, stride=lines), :]
            hits = [mark == wanted[k] for k in range(mine)]
            for r in range(SUB):
                part = every[pl.ds(base + r, SUB, stride=lines), :]
                for k in range(mine):
                    sums[SUB * k + r] += jnp.where(hits[k], part, 0.0)
        return tuple(sums)

    start = (jnp.zeros((SUB, TILE), F32),) * (mine * SUB)
    sums = lax.fori_loop(0, devices // SUB // chunk, body, start)
    for k in range(mine):
        for r in range(SUB):
            total = jnp.sum(sums[SUB * k + r], axis=0, keepdims=True)
            out[0, k : k + 1, TILE * r : TILE * (r + 1)] = total


def local(viscosity, friction, driving, observed, ice_mask, tile_block, owner_list):
    rows, cols = viscosity.shape
    assert (rows, cols) == (2 * TILE, TILE)
    inputs = (viscosity, friction, driving, ice_mask, observed)
    near = [pltpu.with_memory_space_constraint(x, pltpu.VMEM) for x in inputs]
    basis_p, basis_q, basis_rows, basis_cols = bases()
    ends, to_a, to_b = call(
        ends_kernel,
        "ends",
        (vmem(ARRAYS * SLOT, cols), vmem(EDGE, cols), vmem(EDGE, cols)),
        [pltpu.VMEM((2, INNER, cols), jnp.int32), pltpu.SemaphoreType.DMA((2, ARRAYS))],
        10**6,
        *(pltpu.with_memory_space_constraint(x, pltpu.HBM) for x in inputs),
    )
    row_b = swap(to_b, ROW_AXES, 1)
    row_a = swap(to_a, ROW_AXES, 0)
    edge, *forward = call(
        interior_kernel,
        "interior",
        (vmem(2 * PARTS * TILE, TILE),) + (vmem(rows, cols),) * 6,
        [vmem(rows, cols)] * (FIELDS - 6),
        8 * 10**6,
        *near,
    )
    to_a, to_b, turned = call(
        columns_kernel,
        "columns",
        (vmem(SENT, TILE), vmem(SENT, TILE), vmem(SLOT, TILE)),
        [],
        10**5,
        row_a,
        row_b,
        edge,
    )
    col_a = swap(to_a, COL_AXES, 0)
    col_b = swap(to_b, COL_AXES, 1)
    vel_ends, wide = call(
        adjoint_kernel,
        "adjoint",
        (vmem(4 * HALO, cols), vmem(MODES, TILE)),
        [vmem(ARRAYS * STRIP, cols), vmem(2 * STRIP, cols), vmem(rows + STRIP, cols), vmem(TILE, cols)]
        + [vmem(STRIP, cols)] * FIELDS
        + [vmem(rows, cols)] * (FIELDS - 4),
        8 * 10**6,
        ends,
        row_a,
        row_b,
        *near,
        *forward,
        basis_p,
        basis_q,
    )
    devices = lax.axis_size(ROW_AXES + COL_AXES)
    strips, coef = call(
        left_right_kernel,
        "left_right",
        (vmem(PARTS * 2 * STRIP, TILE), vmem(devices, 1, SUB * TILE + TILE)),
        [vmem(PARTS * ARRAYS * STRIP, TILE), vmem(PARTS * STRIP, TILE)]
        + [vmem(PARTS * STRIP, TILE)] * FIELDS,
        4 * 10**6,
        edge,
        turned,
        col_a,
        col_b,
        wide,
        tile_block,
        basis_rows,
        basis_cols,
    )
    parts = lax.all_to_all(coef, ROW_AXES + COL_AXES, 0, 0, tiled=True)
    state = call(
        join_kernel,
        "join",
        jax.ShapeDtypeStruct((2, rows, cols), F32),
        [vmem(2 * PARTS * TILE, TILE)],
        4 * 10**6,
        *forward[4:],
        vel_ends,
        strips,
    )
    owners = owner_list.reshape(lax.axis_size("own"), -1)
    picked = call(
        pick_kernel,
        "pick",
        jax.ShapeDtypeStruct((1, owners.shape[1], MODES * MODES), F32),
        [],
        10**5,
        owners,
        parts.reshape(-1, TILE),
    )
    return (state, picked)


def solution(mesh):
    return jax.shard_map(
        local,
        mesh=mesh,
        in_specs=(
            P(("row", "own"), "col"),
            P(("row", "own"), "col"),
            P(None, ("row", "own"), "col"),
            P(None, ("row", "own"), "col"),
            P(("row", "own"), "col"),
            P(("row", "own"), "col"),
            P(),
        ),
        out_specs=(P(None, ("row", "own"), "col"), P("own", None, None)),
        check_vma=False,
    )
```

```python
import math

import jax
import jax.numpy as jnp
import numpy as np
from jax import lax
from jax.experimental import pallas as pl
from jax.experimental.pallas import tpu as pltpu
from jax.sharding import PartitionSpec as P

TILE = 128
MODES = 32
SWEEPS = 3
SUB = 8
HALO = 8
INNER = 2 * HALO
STRIP = 2 * (HALO + INNER)
ARRAYS = 7
VISC, FRIC, DRIV, MASK, OBS = 0, 1, 2, 4, 5
EDGE = ARRAYS * HALO
SLOT = 2 * INNER
PER = TILE // SLOT
GROUPS = 5
SENT = 2 * GROUPS * HALO + HALO
PARTS = 3
UPPER, LOWER = 32, 64
ROW_AXES = ("row", "own")
COL_AXES = ("col",)
F32 = jnp.float32
LIMIT = 40 * 1024 * 1024


def swap(x, axes, first):
    size = lax.axis_size(axes)
    pairs = [(i, i) for i in (0, size - 1) if first]
    for i in range(first, size - 1, 2):
        pairs += [(i, i + 1), (i + 1, i)]
    return lax.ppermute(x, axes, pairs)


def position(axes):
    index, size = 0, 1
    for axis in axes:
        index = index * lax.axis_size(axis) + lax.axis_index(axis)
        size *= lax.axis_size(axis)
    assert size % 2 == 0
    return lax.rem(index, 2) == 0, (index == 0) | (index == size - 1)


def is_even(axes):
    return position(axes)[0]


def lanes():
    return lax.broadcasted_iota(jnp.int32, (SUB, TILE), 1)


def call(kernel, name, outs, scratch, cost, *args):
    return pl.pallas_call(
        kernel,
        out_shape=outs,
        scratch_shapes=scratch,
        compiler_params=pltpu.CompilerParams(vmem_limit_bytes=LIMIT),
        cost_estimate=pl.CostEstimate(flops=cost, bytes_accessed=cost, transcendentals=0),
        name=name,
    )(*args)


def vmem(*shape):
    return pltpu.VMEM(shape, F32)


FIELDS = 14


class Domain:
    def __init__(self, refs, base, span, source):
        self.refs, self.base, self.span, self.source = refs, base, span, source

    def at(self, j):
        return pl.ds(self.base + SUB * j, SUB)

    def prepare(self, flipped):
        n2, n4, c, i, b0, b1 = self.refs[:6]
        visc = [self.source(VISC, j) for j in range(self.span)]
        for j in range(self.span):
            at = self.at(j)
            before = visc[j - 1] if j else pltpu.roll(visc[-1], 1, 0)
            pair = visc[j] + before
            fric = self.source(FRIC, j)
            diag = 1.25 * (pair + pltpu.roll(pair, 1, 1)) + fric
            on = self.source(MASK, j) > 0.0
            inv = jnp.where(on, 0.5 / jnp.where(on, diag, 1.0), 0.0)
            half = 0.5 * visc[j]
            n2[at, :] = half
            n4[at, :] = 0.5 * half
            c[at, :] = 1.0 - fric * inv
            i[at, :] = inv
            for k, b in enumerate((b0, b1)):
                value = inv * self.source(DRIV + (1 - k if flipped else k), j)
                b[at, :] = value
                self.write(k, at, value + value)

    def write(self, k, at, value):
        self.refs[6 + k][at, :] = value
        self.refs[8 + k][at, :] = pltpu.roll(value, TILE - 1, 1)

    def retarget(self, flipped, velocity=None):
        i, b0, b1 = self.refs[3:6]
        w0, w1 = velocity or self.refs[6:8]
        for j in range(self.span):
            at = self.at(j)
            for k, (b, w) in enumerate(((b0, w0), (b1, w1))):
                value = i[at, :] * (w[at, :] - self.source(OBS + (1 - k if flipped else k), j))
                b[at, :] = value
                self.write(k, at, value + value)

    def differences(self):
        n2, n4 = self.refs[:2]
        fields = self.refs[6:10]
        parts = self.refs[10:14]

        def corners(j, here, below):
            w0, w1, r0, r1 = here
            v0, v1, s0, s1 = below
            a1, a2 = s0 - w0, v0 - r0
            e1, e2 = s1 - w1, v1 - r1
            x, y = a1 + a2, e1 - e2
            q = (a1 - a2) + (e1 + e2)
            both = x + y
            at = self.at(j)
            half = n2[at, :]
            return half * (both + x), n4[at, :] * q, half * (both + y)

        def load(j):
            at = self.at(j)
            return [field[at, :] for field in fields]

        top = load(0)
        last = corners(self.span - 1, load(self.span - 1), [pltpu.roll(v, SUB - 1, 0) for v in top])
        up = [pltpu.roll(v, 1, 0) for v in last]
        here = top
        for j in range(self.span):
            at = self.at(j)
            if j < self.span - 1:
                below = load(j + 1)
                p, q, r = corners(j, here, below)
                here = below
            else:
                p, q, r = last
            g, t = up[0] - p, up[1] + q
            gq, tr = up[1] - q, up[2] + r
            parts[0][at, :] = g - t
            parts[1][at, :] = gq - tr
            parts[2][at, :] = pltpu.roll(g + t, 1, 1)
            parts[3][at, :] = pltpu.roll(gq + tr, 1, 1)
            up = (p, q, r)

    def update(self):
        c, i, b0, b1, w0, w1 = self.refs[2:8]
        parts = self.refs[10:14]
        for j in range(self.span):
            at = self.at(j)
            cv, iv = c[at, :], i[at, :]
            for k, (b, w) in enumerate(((b0, w0), (b1, w1))):
                value = (cv * w[at, :] + b[at, :]) - iv * (parts[k][at, :] + parts[k + 2][at, :])
                self.write(k, at, value)


def run(domains):
    def body(_, carry):
        for domain in domains:
            domain.differences()
        for domain in domains:
            domain.update()
        return carry

    lax.fori_loop(0, SWEEPS, body, 0)


def ends_kernel(visc, fric, driv, mask, obs, to_a, to_b, one, two, flags, sems):
    rows = visc.shape[0]
    copies = []
    for e, first in enumerate((0, rows - HALO)):
        at = pl.ds(first, HALO)
        pieces = [
            (visc.at[at], one.at[e, 0]),
            (fric.at[at], one.at[e, 1]),
            (driv.at[:, at], two.at[e, 0]),
            (mask.at[at], flags.at[e]),
            (obs.at[:, at], two.at[e, 1]),
        ]
        for n, (source, place) in enumerate(pieces):
            copies.append(pltpu.make_async_copy(source, place, sems.at[e, n]))
    for copy in copies:
        copy.start()
    for copy in copies:
        copy.wait()
    even, at_end = position(ROW_AXES)

    def edge(e):
        return [one[e, 0], one[e, 1], two[e, 0, 0], two[e, 0, 1], flags[e].astype(F32), two[e, 1, 0], two[e, 1, 1]]

    for a, (head, tail) in enumerate(zip(edge(0), edge(1))):
        at = slice(HALO * a, HALO * (a + 1))
        to_a[at, :] = jnp.where(even, tail, head)
        to_b[at, :] = jnp.where(at_end, 0.0, jnp.where(even, head, tail))


def field_of(visc, fric, driv, mask, obs):
    def field(a, at):
        if a == MASK:
            return mask[at, :].astype(F32)
        if a >= OBS:
            return obs[a - OBS, at, :]
        if a >= DRIV:
            return driv[a - DRIV, at, :]
        return (visc, fric)[a][at, :]

    return field


def first_row(part, lane):
    if part < 2:
        return TILE * part + lane
    if lane < INNER + HALO:
        return TILE + lane
    if lane >= TILE - INNER - HALO:
        return lane
    if UPPER + HALO <= lane < UPPER + SLOT:
        return lane - UPPER - HALO
    if LOWER <= lane < LOWER + INNER + HALO:
        return 2 * TILE - INNER - HALO + lane - LOWER
    return None


def right_part(row):
    seam = TILE - HALO <= row < TILE + HALO
    part = 2 if seam or row == 0 or row == 2 * TILE - HALO else row // TILE
    return part, [lane for lane in range(0, TILE, SUB) if first_row(part, lane) == row][-1]


def slot(part, a):
    return TILE * (2 * part + a // PER) + SLOT * (a % PER)


def interior_kernel(visc, fric, driv, mask, obs, edge, n2, n4, c, i, v0, v1, *refs):
    span = visc.shape[0] // SUB
    field = field_of(visc, fric, driv, mask, obs)
    lane = lanes()
    for part in range(PARTS):
        for m in range(-(-ARRAYS // PER)):
            strips = []
            for at in range(0, TILE, SUB):
                row = first_row(part, at)
                packed = jnp.zeros((SUB, TILE), F32)
                if row is not None:
                    for k in range(min(PER, ARRAYS - PER * m)):
                        value = field(PER * m + k, slice(row, row + SUB))
                        moved = pltpu.roll(value, (SLOT * k + INNER) % TILE, 1)
                        packed = jnp.where(lax.div(lane, SLOT) == k, moved, packed)
                strips.append(packed)
            base = TILE * (2 * part + m)
            edge[base : base + TILE, :] = jnp.concatenate(strips, axis=0).T
    refs = (n2, n4, c, i, *refs[:2], v0, v1, *refs[2:])
    domain = Domain(refs, 0, span, lambda a, j: field(a, pl.ds(j, SUB, stride=span)))
    domain.prepare(False)
    run([domain])


def columns_kernel(row_a, row_b, edge, to_a, to_b, turned):
    even = is_even(ROW_AXES)
    above = jnp.where(even, row_b[...], row_a[...])
    below = jnp.where(even, row_a[...], row_b[...])
    halo = jnp.concatenate([above, below, jnp.zeros((TILE - 2 * EDGE, TILE), F32)], axis=0).T
    turned[:INNER, :] = halo[TILE - INNER :]
    turned[INNER:, :] = halo[:INNER]
    even, at_end = position(COL_AXES)
    row = lax.broadcasted_iota(jnp.int32, (SUB, TILE), 0)

    def put(out, right, left):
        to_a[out : out + HALO, :] = jnp.where(even, right, left)
        to_b[out : out + HALO, :] = jnp.where(at_end, 0.0, jnp.where(even, left, right))

    for part in range(2):
        right, left = [], []
        for a in range(ARRAYS):
            at = slot(part, a) + INNER
            right.append(edge[at - HALO : at, :])
            left.append(edge[at : at + HALO, :])
        for k in range(2):
            seen_r, seen_l = right[OBS + k], left[OBS + k]
            g = 1 + 2 * k
            right[g] = jnp.where(row < 2, pltpu.roll(seen_r, 2, 0), right[g])
            right[g + 1] = jnp.where(row < 2, pltpu.roll(seen_r, 4, 0), right[g + 1])
            left[g] = jnp.where(row >= 6, pltpu.roll(seen_l, 6, 0), left[g])
            left[g + 1] = jnp.where(row >= 6, pltpu.roll(seen_l, 4, 0), left[g + 1])
        for g in range(GROUPS):
            put(HALO * (GROUPS * part + g), right[g], left[g])
    put(2 * GROUPS * HALO, halo[TILE - HALO :], halo[:HALO])


def strided(stack, base):
    span = STRIP // SUB
    return lambda a, j: stack[pl.ds(base + STRIP * a + j, SUB, stride=span), :]


def velocity(domain, plain, base):
    for j in range(domain.span):
        at = domain.at(j)
        for k in range(2):
            plain[pl.ds(base + STRIP * k + j, SUB, stride=domain.span), :] = domain.refs[6 + k][at, :]


def density(domain, plain, base, out, place):
    w0, w1 = domain.refs[6:8]
    for j in range(domain.span):
        at = domain.at(j)
        v0, v1 = (plain[pl.ds(base + STRIP * k + j, SUB, stride=domain.span), :] for k in range(2))
        value = -domain.source(FRIC, j) * (w0[at, :] * v0 + w1[at, :] * v1)
        out[pl.ds(place + j, SUB, stride=domain.span), :] = value


def beside():
    lane = lanes()
    return (lane < HALO) | (lane >= TILE - HALO)


def adjoint_kernel(
    row_a, row_b, visc, fric, driv, mask, obs, n2, n4, c, i, v0, v1, basis_p, basis_q,
    vel, wide,
    stack, plain, dens, total, *refs,
):
    rows = visc.shape[0]
    span = rows // SUB
    even = is_even(ROW_AXES)
    field = field_of(visc, fric, driv, mask, obs)
    for a in range(ARRAYS):
        at = slice(HALO * a, HALO * (a + 1))
        got_a, got_b = row_a[at, :], row_b[at, :]
        base = STRIP * a
        stack[base : base + HALO, :] = jnp.where(even, got_b, got_a)
        stack[base + HALO : base + HALO + INNER, :] = field(a, slice(0, INNER))
        stack[base + HALO + INNER : base + HALO + SLOT, :] = field(a, slice(rows - INNER, rows))
        stack[base + HALO + SLOT : base + STRIP, :] = jnp.where(even, got_a, got_b)
    strips = Domain(refs[:FIELDS], 0, STRIP // SUB, strided(stack, 0))
    strips.prepare(False)
    run([strips])
    velocity(strips, plain, 0)
    outer = (HALO, SLOT)
    for k in range(2):
        for e in range(2):
            out = HALO * (2 * k + e)
            vel[out : out + HALO, :] = plain[STRIP * k + outer[e] : STRIP * k + outer[e] + HALO, :]
    interior = Domain(
        (n2, n4, c, i, *refs[FIELDS:]), 0, span, lambda a, j: field(a, pl.ds(j, SUB, stride=span))
    )
    strips.retarget(False)
    interior.retarget(False, (v0, v1))
    run([interior, strips])
    w0, w1 = interior.refs[6:8]
    for j in range(span):
        at = interior.at(j)
        value = -interior.source(FRIC, j) * (w0[at, :] * v0[at, :] + w1[at, :] * v1[at, :])
        dens[pl.ds(j, SUB, stride=span), :] = value
    density(strips, plain, 0, dens, rows)

    side = beside()
    for s in range(0, TILE, SUB):
        summed = jnp.zeros((SUB, TILE), F32)
        for row in range(s, rows, TILE):
            at = rows + outer[0] if row == 0 else rows + outer[1] if row == rows - SUB else row
            summed += dens[at : at + SUB, :]
        total[s : s + SUB, :] = jnp.where(side, 0.0, summed)
    exact = dict(precision=lax.Precision.HIGHEST, preferred_element_type=F32)
    half = jnp.dot(basis_p[...], total[...], **exact)
    wide[...] = jnp.dot(half, basis_q[...], **exact)


def left_right_kernel(
    edge, turned, col_a, col_b, wide_in, block, basis_rows, basis_cols,
    strips, coef,
    stack, plain, *refs,
):
    even = is_even(COL_AXES)
    lane = lanes()
    row = lax.broadcasted_iota(jnp.int32, (SUB, TILE), 0)
    upper = (lane >= UPPER + HALO) & (lane < UPPER + SLOT)
    lower = (lane >= LOWER) & (lane < LOWER + INNER + HALO)
    seam_t0 = lane >= TILE - INNER - HALO
    seam_t1 = lane < INNER + HALO
    corner = ((lane >= UPPER) & (lane < UPPER + HALO)) | ((lane >= LOWER + INNER + HALO) & (lane < LOWER + SLOT))

    def place(part, a):
        return STRIP * (ARRAYS * part + a)

    for from_left in (True, False):
        groups = []
        for g in range(2 * GROUPS + 1):
            got_a, got_b = col_a[HALO * g : HALO * (g + 1), :], col_b[HALO * g : HALO * (g + 1), :]
            groups.append(jnp.where(even, got_b, got_a) if from_left else jnp.where(even, got_a, got_b))
        tiles = []
        for part in range(2):
            tile = groups[GROUPS * part : GROUPS * (part + 1)]
            for k in range(2):
                g, h = tile[1 + 2 * k], tile[2 + 2 * k]
                if from_left:
                    tile.append(jnp.where(row >= 6, pltpu.roll(g, 6, 0), pltpu.roll(h, 4, 0)))
                else:
                    tile.append(jnp.where(row < 2, pltpu.roll(g, 2, 0), pltpu.roll(h, 4, 0)))
            tiles.append(tile)
        for a in range(ARRAYS):
            t0, t1 = tiles[0][a], tiles[1][a]
            third = jnp.where(corner, pltpu.roll(groups[-1], (UPPER - HALO * a) % TILE, 1), 0.0)
            third = jnp.where(upper, pltpu.roll(t0, UPPER + HALO, 1), third)
            third = jnp.where(lower, pltpu.roll(t1, LOWER + INNER + HALO, 1), third)
            third = jnp.where(seam_t0, t0, jnp.where(seam_t1, t1, third))
            for part, value in enumerate((t0, t1, third)):
                base = place(part, a) + (0 if from_left else HALO + SLOT)
                stack[base : base + HALO, :] = value
    for a in range(ARRAYS):
        for part in range(PARTS):
            base = place(part, a) + HALO
            for r in range(0, SLOT, SUB):
                value = edge[slot(part, a) + r : slot(part, a) + r + SUB, :]
                if part == 2:
                    moved = pltpu.roll(turned[r : r + SUB, :], (UPPER - HALO * a) % TILE, 1)
                    value = jnp.where(corner, moved, value)
                to = base + (r + INNER) % SLOT
                stack[to : to + SUB, :] = value

    domains = [
        Domain(refs, STRIP * part, STRIP // SUB, strided(stack, place(part, 0))) for part in range(PARTS)
    ]
    for domain in domains:
        domain.prepare(True)
    run(domains)
    for part, domain in enumerate(domains):
        velocity(domain, strips, 2 * STRIP * part)
        domain.retarget(True)
    run(domains)
    for part, domain in enumerate(domains):
        density(domain, strips, 2 * STRIP * part, plain, STRIP * part)

    def side(part):
        base = STRIP * part
        return jnp.concatenate(
            [plain[base + HALO : base + 2 * HALO, :], plain[base + SLOT : base + SLOT + HALO, :]], axis=0
        )

    lane = lax.broadcasted_iota(jnp.int32, (2 * HALO, TILE), 1)
    straight = (lane >= HALO) & (lane < TILE - HALO)
    seam = (lane < HALO) | (lane >= TILE - HALO)
    top = (lane >= UPPER + HALO) & (lane < UPPER + 2 * HALO)
    bottom = (lane >= LOWER + INNER) & (lane < LOWER + INNER + HALO)
    dens = jnp.concatenate(
        [jnp.where(straight, side(0) + side(1), 0.0), jnp.where(seam | top | bottom, side(2), 0.0)], axis=1
    )
    exact = dict(precision=lax.Precision.HIGHEST, preferred_element_type=F32)
    half = jnp.dot(dens, basis_rows[...], **exact)
    wide = wide_in[...] + lax.dot_general(half, basis_cols[...], (((0,), (0,)), ((), ())), **exact)
    lane = lanes()
    which = lax.div(lane, MODES)
    flat = wide[:SUB]
    for j in range(1, MODES // SUB):
        flat = jnp.where(which == j, wide[SUB * j : SUB * (j + 1)], flat)
    mark = jnp.broadcast_to(block[:1, :].astype(F32), (1, TILE))
    pieces = [flat[r : r + 1] for r in range(SUB)] + [mark]
    chunk = min(32, coef.shape[0])

    def spread(d, carry):
        for e in range(chunk):
            for r, piece in enumerate(pieces):
                coef[d * chunk + e, :, TILE * r : TILE * (r + 1)] = piece
        return carry

    lax.fori_loop(0, coef.shape[0] // chunk, spread, 0)


def join_kernel(v0, v1, ends, strips, vel, turned):
    rows = vel.shape[1]
    span = rows // SUB
    middle = jnp.zeros((TILE - 2 * HALO, TILE), F32)
    side = beside()
    for k, v in enumerate((v0, v1)):
        for part in range(PARTS):
            base = STRIP * (2 * part + 1 - k)
            first = strips[base + HALO : base + 2 * HALO, :]
            last = strips[base + SLOT : base + SLOT + HALO, :]
            at = TILE * (2 * part + k)
            turned[at : at + TILE, :] = jnp.concatenate([first, middle, last], axis=0).T
        for row in range(0, rows, SUB):
            if row == 0:
                value = ends[2 * HALO * k : 2 * HALO * k + HALO, :]
            elif row == rows - SUB:
                value = ends[2 * HALO * k + HALO : 2 * HALO * (k + 1), :]
            else:
                value = v[pl.ds(SUB * (row % span) + row // span, SUB, stride=SUB), :]
            part, lane = right_part(row)
            at = TILE * (2 * part + k) + lane
            vel[k, row : row + SUB, :] = jnp.where(side, turned[at : at + SUB, :], value)


def bases():
    places = np.arange(TILE) + 0.5
    basis = np.cos(math.pi * places[:, None] * np.arange(MODES)[None, :] / TILE)
    groups = MODES // SUB
    order = np.arange(MODES).reshape(SUB, groups).T.reshape(-1)
    rows = basis[:, order] / TILE
    cols = np.tile(basis, (1, groups))
    placed = np.zeros((2 * TILE, MODES))
    for row in range(0, 2 * TILE, SUB):
        part, lane = right_part(row)
        at = lane + (TILE if part == 2 else 0)
        placed[at : at + SUB] = rows[row % TILE : row % TILE + SUB]
    outer = np.concatenate([cols[:HALO], cols[TILE - HALO :]])
    return [jnp.asarray(x, F32) for x in (rows.T, cols, placed, outer)]


def pick_kernel(owners, every, out):
    mine = out.shape[1]
    own = lax.axis_index("own")
    wanted = [owners[pl.ds(own, 1), k : k + 1].astype(F32) for k in range(mine)]
    lines = SUB + 1
    devices = every.shape[0] // lines
    chunk = min(4, devices // SUB)

    def body(d, sums):
        sums = list(sums)
        for e in range(chunk):
            base = (d * chunk + e) * SUB * lines
            mark = every[pl.ds(base + SUB, SUB, stride=lines), :]
            hits = [mark == wanted[k] for k in range(mine)]
            for r in range(SUB):
                part = every[pl.ds(base + r, SUB, stride=lines), :]
                for k in range(mine):
                    sums[SUB * k + r] += jnp.where(hits[k], part, 0.0)
        return tuple(sums)

    start = (jnp.zeros((SUB, TILE), F32),) * (mine * SUB)
    sums = lax.fori_loop(0, devices // SUB // chunk, body, start)
    for k in range(mine):
        for r in range(SUB):
            total = jnp.sum(sums[SUB * k + r], axis=0, keepdims=True)
            out[0, k : k + 1, TILE * r : TILE * (r + 1)] = total


def local(viscosity, friction, driving, observed, ice_mask, tile_block, owner_list):
    rows, cols = viscosity.shape
    assert (rows, cols) == (2 * TILE, TILE)
    inputs = (viscosity, friction, driving, ice_mask, observed)
    near = [pltpu.with_memory_space_constraint(x, pltpu.VMEM) for x in inputs]
    basis_p, basis_q, basis_rows, basis_cols = bases()
    to_a, to_b = call(
        ends_kernel,
        "ends",
        (vmem(EDGE, cols), vmem(EDGE, cols)),
        [
            vmem(2, 2, HALO, cols),
            vmem(2, 2, 2, HALO, cols),
            pltpu.VMEM((2, HALO, cols), jnp.int32),
            pltpu.SemaphoreType.DMA((2, 5)),
        ],
        10**6,
        *(pltpu.with_memory_space_constraint(x, pltpu.HBM) for x in inputs),
    )
    row_b = swap(to_b, ROW_AXES, 1)
    row_a = swap(to_a, ROW_AXES, 0)
    edge, *forward = call(
        interior_kernel,
        "interior",
        (vmem(2 * PARTS * TILE, TILE),) + (vmem(rows, cols),) * 6,
        [vmem(rows, cols)] * (FIELDS - 6),
        8 * 10**6,
        *near,
    )
    to_a, to_b, turned = call(
        columns_kernel,
        "columns",
        (vmem(SENT, TILE), vmem(SENT, TILE), vmem(SLOT, TILE)),
        [],
        10**5,
        row_a,
        row_b,
        edge,
    )
    col_a = swap(to_a, COL_AXES, 0)
    col_b = swap(to_b, COL_AXES, 1)
    vel_ends, wide = call(
        adjoint_kernel,
        "adjoint",
        (vmem(4 * HALO, cols), vmem(MODES, TILE)),
        [vmem(ARRAYS * STRIP, cols), vmem(2 * STRIP, cols), vmem(rows + STRIP, cols), vmem(TILE, cols)]
        + [vmem(STRIP, cols)] * FIELDS
        + [vmem(rows, cols)] * (FIELDS - 4),
        8 * 10**6,
        row_a,
        row_b,
        *near,
        *forward,
        basis_p,
        basis_q,
    )
    devices = lax.axis_size(ROW_AXES + COL_AXES)
    strips, coef = call(
        left_right_kernel,
        "left_right",
        (vmem(PARTS * 2 * STRIP, TILE), vmem(devices, 1, SUB * TILE + TILE)),
        [vmem(PARTS * ARRAYS * STRIP, TILE), vmem(PARTS * STRIP, TILE)]
        + [vmem(PARTS * STRIP, TILE)] * FIELDS,
        4 * 10**6,
        edge,
        turned,
        col_a,
        col_b,
        wide,
        tile_block,
        basis_rows,
        basis_cols,
    )
    parts = lax.all_to_all(coef, ROW_AXES + COL_AXES, 0, 0, tiled=True)
    state = call(
        join_kernel,
        "join",
        jax.ShapeDtypeStruct((2, rows, cols), F32),
        [vmem(2 * PARTS * TILE, TILE)],
        4 * 10**6,
        *forward[4:],
        vel_ends,
        strips,
    )
    owners = owner_list.reshape(lax.axis_size("own"), -1)
    picked = call(
        pick_kernel,
        "pick",
        jax.ShapeDtypeStruct((1, owners.shape[1], MODES * MODES), F32),
        [],
        10**5,
        owners,
        parts.reshape(-1, TILE),
    )
    return (state, picked)


def solution(mesh):
    return jax.shard_map(
        local,
        mesh=mesh,
        in_specs=(
            P(("row", "own"), "col"),
            P(("row", "own"), "col"),
            P(None, ("row", "own"), "col"),
            P(None, ("row", "own"), "col"),
            P(("row", "own"), "col"),
            P(("row", "own"), "col"),
            P(),
        ),
        out_specs=(P(None, ("row", "own"), "col"), P("own", None, None)),
        check_vma=False,
    )
```

```python
import math

import jax
import jax.numpy as jnp
import numpy as np
from jax import lax
from jax.experimental import pallas as pl
from jax.experimental.pallas import tpu as pltpu
from jax.sharding import PartitionSpec as P

TILE = 128
MODES = 32
SWEEPS = 3
SUB = 8
HALO = 8
INNER = 2 * HALO
STRIP = 2 * (HALO + INNER)
ARRAYS = 7
VISC, FRIC, DRIV, MASK, OBS = 0, 1, 2, 4, 5
EDGE = ARRAYS * HALO
SLOT = 2 * INNER
PER = TILE // SLOT
GROUPS = 5
SENT = 2 * GROUPS * HALO + HALO
PARTS = 3
UPPER, LOWER = 32, 64
ROW_AXES = ("row", "own")
COL_AXES = ("col",)
F32 = jnp.float32
LIMIT = 40 * 1024 * 1024


def swap(x, axes, first):
    size = lax.axis_size(axes)
    pairs = [(i, i) for i in (0, size - 1) if first]
    for i in range(first, size - 1, 2):
        pairs += [(i, i + 1), (i + 1, i)]
    return lax.ppermute(x, axes, pairs)


def position(axes):
    index, size = 0, 1
    for axis in axes:
        index = index * lax.axis_size(axis) + lax.axis_index(axis)
        size *= lax.axis_size(axis)
    assert size % 2 == 0
    return lax.rem(index, 2) == 0, (index == 0) | (index == size - 1)


def is_even(axes):
    return position(axes)[0]


def lanes():
    return lax.broadcasted_iota(jnp.int32, (SUB, TILE), 1)


def call(kernel, name, outs, scratch, cost, *args):
    return pl.pallas_call(
        kernel,
        out_shape=outs,
        scratch_shapes=scratch,
        compiler_params=pltpu.CompilerParams(vmem_limit_bytes=LIMIT),
        cost_estimate=pl.CostEstimate(flops=cost, bytes_accessed=cost, transcendentals=0),
        name=name,
    )(*args)


def vmem(*shape):
    return pltpu.VMEM(shape, F32)


FIELDS = 14


class Domain:
    def __init__(self, refs, base, span, source):
        self.refs, self.base, self.span, self.source = refs, base, span, source

    def at(self, j):
        return pl.ds(self.base + SUB * j, SUB)

    def prepare(self, flipped):
        n2, n4, c, i, b0, b1 = self.refs[:6]
        visc = [self.source(VISC, j) for j in range(self.span)]
        for j in range(self.span):
            at = self.at(j)
            before = visc[j - 1] if j else pltpu.roll(visc[-1], 1, 0)
            pair = visc[j] + before
            fric = self.source(FRIC, j)
            diag = 1.25 * (pair + pltpu.roll(pair, 1, 1)) + fric
            on = self.source(MASK, j) > 0.0
            inv = jnp.where(on, 0.5 / jnp.where(on, diag, 1.0), 0.0)
            half = 0.5 * visc[j]
            n2[at, :] = half
            n4[at, :] = 0.5 * half
            c[at, :] = 1.0 - fric * inv
            i[at, :] = inv
            for k, b in enumerate((b0, b1)):
                value = inv * self.source(DRIV + (1 - k if flipped else k), j)
                b[at, :] = value
                self.write(k, at, value + value)

    def write(self, k, at, value):
        self.refs[6 + k][at, :] = value
        self.refs[8 + k][at, :] = pltpu.roll(value, TILE - 1, 1)

    def retarget(self, flipped, velocity=None):
        i, b0, b1 = self.refs[3:6]
        w = self.refs[6:8]
        for j in range(self.span):
            at = self.at(j)
            for k, b in enumerate((b0, b1)):
                now = velocity(k, j) if velocity else w[k][at, :]
                value = i[at, :] * (now - self.source(OBS + (1 - k if flipped else k), j))
                b[at, :] = value
                self.write(k, at, value + value)

    def differences(self):
        n2, n4 = self.refs[:2]
        fields = self.refs[6:10]
        parts = self.refs[10:14]

        def corners(j, here, below):
            w0, w1, r0, r1 = here
            v0, v1, s0, s1 = below
            a1, a2 = s0 - w0, v0 - r0
            e1, e2 = s1 - w1, v1 - r1
            x, y = a1 + a2, e1 - e2
            q = (a1 - a2) + (e1 + e2)
            both = x + y
            at = self.at(j)
            half = n2[at, :]
            return half * (both + x), n4[at, :] * q, half * (both + y)

        def load(j):
            at = self.at(j)
            return [field[at, :] for field in fields]

        top = load(0)
        last = corners(self.span - 1, load(self.span - 1), [pltpu.roll(v, SUB - 1, 0) for v in top])
        up = [pltpu.roll(v, 1, 0) for v in last]
        here = top
        for j in range(self.span):
            at = self.at(j)
            if j < self.span - 1:
                below = load(j + 1)
                p, q, r = corners(j, here, below)
                here = below
            else:
                p, q, r = last
            g, t = up[0] - p, up[1] + q
            gq, tr = up[1] - q, up[2] + r
            parts[0][at, :] = g - t
            parts[1][at, :] = gq - tr
            parts[2][at, :] = pltpu.roll(g + t, 1, 1)
            parts[3][at, :] = pltpu.roll(gq + tr, 1, 1)
            up = (p, q, r)

    def update(self):
        c, i, b0, b1, w0, w1 = self.refs[2:8]
        parts = self.refs[10:14]
        for j in range(self.span):
            at = self.at(j)
            cv, iv = c[at, :], i[at, :]
            for k, (b, w) in enumerate(((b0, w0), (b1, w1))):
                value = (cv * w[at, :] + b[at, :]) - iv * (parts[k][at, :] + parts[k + 2][at, :])
                self.write(k, at, value)


def run(domains):
    def body(_, carry):
        for domain in domains:
            domain.differences()
        for domain in domains:
            domain.update()
        return carry

    lax.fori_loop(0, SWEEPS, body, 0)


def hold_kernel(x, *refs):
    refs[-1][...] = x[...]


def hold(x, *after):
    anywhere = pl.BlockSpec(memory_space=pl.ANY)
    near = pl.BlockSpec(memory_space=pltpu.VMEM)
    return pl.pallas_call(
        hold_kernel,
        in_specs=[near] + [anywhere] * len(after),
        out_specs=near,
        out_shape=vmem(*x.shape),
        compiler_params=pltpu.CompilerParams(vmem_limit_bytes=LIMIT),
        name="hold",
    )(x, *after)


def ends_kernel(visc, fric, driv, mask, obs, to_a, to_b, one, two, flags, sems):
    rows = visc.shape[0]
    copies = []
    for e, first in enumerate((0, rows - HALO)):
        at = pl.ds(first, HALO)
        pieces = [
            (visc.at[at], one.at[e, 0]),
            (fric.at[at], one.at[e, 1]),
            (driv.at[:, at], two.at[e, 0]),
            (mask.at[at], flags.at[e]),
            (obs.at[:, at], two.at[e, 1]),
        ]
        for n, (source, place) in enumerate(pieces):
            copies.append(pltpu.make_async_copy(source, place, sems.at[e, n]))
    for copy in copies:
        copy.start()
    for copy in copies:
        copy.wait()
    even, at_end = position(ROW_AXES)

    def edge(e):
        return [one[e, 0], one[e, 1], two[e, 0, 0], two[e, 0, 1], flags[e].astype(F32), two[e, 1, 0], two[e, 1, 1]]

    for a, (head, tail) in enumerate(zip(edge(0), edge(1))):
        at = slice(HALO * a, HALO * (a + 1))
        to_a[at, :] = jnp.where(even, tail, head)
        to_b[at, :] = jnp.where(at_end, 0.0, jnp.where(even, head, tail))


def field_of(visc, fric, driv, mask, obs):
    def field(a, at):
        if a == MASK:
            return mask[at, :].astype(F32)
        if a >= OBS:
            return obs[a - OBS, at, :]
        if a >= DRIV:
            return driv[a - DRIV, at, :]
        return (visc, fric)[a][at, :]

    return field


def first_row(part, lane):
    if part < 2:
        return TILE * part + lane
    if lane < INNER + HALO:
        return TILE + lane
    if lane >= TILE - INNER - HALO:
        return lane
    if UPPER + HALO <= lane < UPPER + SLOT:
        return lane - UPPER - HALO
    if LOWER <= lane < LOWER + INNER + HALO:
        return 2 * TILE - INNER - HALO + lane - LOWER
    return None


def right_part(row):
    seam = TILE - HALO <= row < TILE + HALO
    part = 2 if seam or row == 0 or row == 2 * TILE - HALO else row // TILE
    return part, [lane for lane in range(0, TILE, SUB) if first_row(part, lane) == row][-1]


def slot(part, a):
    return TILE * (2 * part + a // PER) + SLOT * (a % PER)


def interior_kernel(visc, fric, driv, mask, obs, n2, n4, c, i, v0, v1, *refs):
    span = visc.shape[0] // SUB
    field = field_of(visc, fric, driv, mask, obs)
    refs = (n2, n4, c, i, *refs[:2], v0, v1, *refs[2:])
    domain = Domain(refs, 0, span, lambda a, j: field(a, pl.ds(j, SUB, stride=span)))
    domain.prepare(False)
    run([domain])


def outer_kernel(visc, fric, driv, mask, obs, _, edge):
    field = field_of(visc, fric, driv, mask, obs)
    lane = lanes()
    for part in range(PARTS):
        for m in range(-(-ARRAYS // PER)):
            strips = []
            for at in range(0, TILE, SUB):
                row = first_row(part, at)
                packed = jnp.zeros((SUB, TILE), F32)
                if row is not None:
                    for k in range(min(PER, ARRAYS - PER * m)):
                        value = field(PER * m + k, slice(row, row + SUB))
                        moved = pltpu.roll(value, (SLOT * k + INNER) % TILE, 1)
                        packed = jnp.where(lax.div(lane, SLOT) == k, moved, packed)
                strips.append(packed)
            base = TILE * (2 * part + m)
            edge[base : base + TILE, :] = jnp.concatenate(strips, axis=0).T


def columns_kernel(row_a, row_b, edge, to_a, to_b, turned):
    even = is_even(ROW_AXES)
    above = jnp.where(even, row_b[...], row_a[...])
    below = jnp.where(even, row_a[...], row_b[...])
    halo = jnp.concatenate([above, below, jnp.zeros((TILE - 2 * EDGE, TILE), F32)], axis=0).T
    turned[:INNER, :] = halo[TILE - INNER :]
    turned[INNER:, :] = halo[:INNER]
    even, at_end = position(COL_AXES)
    row = lax.broadcasted_iota(jnp.int32, (SUB, TILE), 0)

    def put(out, right, left):
        to_a[out : out + HALO, :] = jnp.where(even, right, left)
        to_b[out : out + HALO, :] = jnp.where(at_end, 0.0, jnp.where(even, left, right))

    for part in range(2):
        right, left = [], []
        for a in range(ARRAYS):
            at = slot(part, a) + INNER
            right.append(edge[at - HALO : at, :])
            left.append(edge[at : at + HALO, :])
        for k in range(2):
            seen_r, seen_l = right[OBS + k], left[OBS + k]
            g = 1 + 2 * k
            right[g] = jnp.where(row < 2, pltpu.roll(seen_r, 2, 0), right[g])
            right[g + 1] = jnp.where(row < 2, pltpu.roll(seen_r, 4, 0), right[g + 1])
            left[g] = jnp.where(row >= 6, pltpu.roll(seen_l, 6, 0), left[g])
            left[g + 1] = jnp.where(row >= 6, pltpu.roll(seen_l, 4, 0), left[g + 1])
        for g in range(GROUPS):
            put(HALO * (GROUPS * part + g), right[g], left[g])
    put(2 * GROUPS * HALO, halo[TILE - HALO :], halo[:HALO])


def strided(stack, base):
    span = STRIP // SUB
    return lambda a, j: stack[pl.ds(base + STRIP * a + j, SUB, stride=span), :]


def velocity(domain, plain, base):
    for j in range(domain.span):
        at = domain.at(j)
        for k in range(2):
            plain[pl.ds(base + STRIP * k + j, SUB, stride=domain.span), :] = domain.refs[6 + k][at, :]


def density(domain, plain, base, out, place):
    w0, w1 = domain.refs[6:8]
    for j in range(domain.span):
        at = domain.at(j)
        v0, v1 = (plain[pl.ds(base + STRIP * k + j, SUB, stride=domain.span), :] for k in range(2))
        value = -domain.source(FRIC, j) * (w0[at, :] * v0 + w1[at, :] * v1)
        out[pl.ds(place + j, SUB, stride=domain.span), :] = value


def beside():
    lane = lanes()
    return (lane < HALO) | (lane >= TILE - HALO)


OUTER = (HALO, SLOT)


def top_bottom_kernel(row_a, row_b, visc, fric, driv, mask, obs, _, stack, plain, n2, n4, c, i, vel, *refs):
    rows = visc.shape[0]
    even = is_even(ROW_AXES)
    field = field_of(visc, fric, driv, mask, obs)
    for a in range(ARRAYS):
        at = slice(HALO * a, HALO * (a + 1))
        got_a, got_b = row_a[at, :], row_b[at, :]
        base = STRIP * a
        stack[base : base + HALO, :] = jnp.where(even, got_b, got_a)
        stack[base + HALO : base + HALO + INNER, :] = field(a, slice(0, INNER))
        stack[base + HALO + INNER : base + HALO + SLOT, :] = field(a, slice(rows - INNER, rows))
        stack[base + HALO + SLOT : base + STRIP, :] = jnp.where(even, got_a, got_b)
    strips = Domain((n2, n4, c, i, *refs), 0, STRIP // SUB, strided(stack, 0))
    strips.prepare(False)
    run([strips])
    velocity(strips, plain, 0)
    for k in range(2):
        for e in range(2):
            out = HALO * (2 * k + e)
            vel[out : out + HALO, :] = plain[STRIP * k + OUTER[e] : STRIP * k + OUTER[e] + HALO, :]


def adjoint_kernel(
    visc, fric, driv, mask, obs, n2, n4, c, i, v0, v1, stack, plain, s_n2, s_n4, s_c, s_i, basis_p, basis_q, _,
    wide,
    dens, total, *refs,
):
    rows = visc.shape[0]
    span = rows // SUB
    field = field_of(visc, fric, driv, mask, obs)
    work = FIELDS - 4
    strips = Domain((s_n2, s_n4, s_c, s_i, *refs[:work]), 0, STRIP // SUB, strided(stack, 0))
    interior = Domain(
        (n2, n4, c, i, *refs[work:]), 0, span, lambda a, j: field(a, pl.ds(j, SUB, stride=span))
    )
    strips.retarget(False, lambda k, j: plain[pl.ds(STRIP * k + j, SUB, stride=strips.span), :])
    interior.retarget(False, lambda k, j: (v0, v1)[k][interior.at(j), :])
    run([interior, strips])
    w0, w1 = interior.refs[6:8]
    for j in range(span):
        at = interior.at(j)
        value = -interior.source(FRIC, j) * (w0[at, :] * v0[at, :] + w1[at, :] * v1[at, :])
        dens[pl.ds(j, SUB, stride=span), :] = value
    density(strips, plain, 0, dens, rows)

    side = beside()
    for s in range(0, TILE, SUB):
        summed = jnp.zeros((SUB, TILE), F32)
        for row in range(s, rows, TILE):
            at = rows + OUTER[0] if row == 0 else rows + OUTER[1] if row == rows - SUB else row
            summed += dens[at : at + SUB, :]
        total[s : s + SUB, :] = jnp.where(side, 0.0, summed)
    exact = dict(precision=lax.Precision.HIGHEST, preferred_element_type=F32)
    half = jnp.dot(basis_p[...], total[...], **exact)
    wide[...] = jnp.dot(half, basis_q[...], **exact)


def left_right_kernel(
    edge, turned, col_a, col_b, wide_in, block, basis_rows, basis_cols,
    strips, coef,
    stack, plain, *refs,
):
    even = is_even(COL_AXES)
    lane = lanes()
    row = lax.broadcasted_iota(jnp.int32, (SUB, TILE), 0)
    upper = (lane >= UPPER + HALO) & (lane < UPPER + SLOT)
    lower = (lane >= LOWER) & (lane < LOWER + INNER + HALO)
    seam_t0 = lane >= TILE - INNER - HALO
    seam_t1 = lane < INNER + HALO
    corner = ((lane >= UPPER) & (lane < UPPER + HALO)) | ((lane >= LOWER + INNER + HALO) & (lane < LOWER + SLOT))

    def place(part, a):
        return STRIP * (ARRAYS * part + a)

    for from_left in (True, False):
        groups = []
        for g in range(2 * GROUPS + 1):
            got_a, got_b = col_a[HALO * g : HALO * (g + 1), :], col_b[HALO * g : HALO * (g + 1), :]
            groups.append(jnp.where(even, got_b, got_a) if from_left else jnp.where(even, got_a, got_b))
        tiles = []
        for part in range(2):
            tile = groups[GROUPS * part : GROUPS * (part + 1)]
            for k in range(2):
                g, h = tile[1 + 2 * k], tile[2 + 2 * k]
                if from_left:
                    tile.append(jnp.where(row >= 6, pltpu.roll(g, 6, 0), pltpu.roll(h, 4, 0)))
                else:
                    tile.append(jnp.where(row < 2, pltpu.roll(g, 2, 0), pltpu.roll(h, 4, 0)))
            tiles.append(tile)
        for a in range(ARRAYS):
            t0, t1 = tiles[0][a], tiles[1][a]
            third = jnp.where(corner, pltpu.roll(groups[-1], (UPPER - HALO * a) % TILE, 1), 0.0)
            third = jnp.where(upper, pltpu.roll(t0, UPPER + HALO, 1), third)
            third = jnp.where(lower, pltpu.roll(t1, LOWER + INNER + HALO, 1), third)
            third = jnp.where(seam_t0, t0, jnp.where(seam_t1, t1, third))
            for part, value in enumerate((t0, t1, third)):
                base = place(part, a) + (0 if from_left else HALO + SLOT)
                stack[base : base + HALO, :] = value
    for a in range(ARRAYS):
        for part in range(PARTS):
            base = place(part, a) + HALO
            for r in range(0, SLOT, SUB):
                value = edge[slot(part, a) + r : slot(part, a) + r + SUB, :]
                if part == 2:
                    moved = pltpu.roll(turned[r : r + SUB, :], (UPPER - HALO * a) % TILE, 1)
                    value = jnp.where(corner, moved, value)
                to = base + (r + INNER) % SLOT
                stack[to : to + SUB, :] = value

    domains = [
        Domain(refs, STRIP * part, STRIP // SUB, strided(stack, place(part, 0))) for part in range(PARTS)
    ]
    for domain in domains:
        domain.prepare(True)
    run(domains)
    for part, domain in enumerate(domains):
        velocity(domain, strips, 2 * STRIP * part)
        domain.retarget(True)
    run(domains)
    for part, domain in enumerate(domains):
        density(domain, strips, 2 * STRIP * part, plain, STRIP * part)

    def side(part):
        base = STRIP * part
        return jnp.concatenate(
            [plain[base + HALO : base + 2 * HALO, :], plain[base + SLOT : base + SLOT + HALO, :]], axis=0
        )

    lane = lax.broadcasted_iota(jnp.int32, (2 * HALO, TILE), 1)
    straight = (lane >= HALO) & (lane < TILE - HALO)
    seam = (lane < HALO) | (lane >= TILE - HALO)
    top = (lane >= UPPER + HALO) & (lane < UPPER + 2 * HALO)
    bottom = (lane >= LOWER + INNER) & (lane < LOWER + INNER + HALO)
    dens = jnp.concatenate(
        [jnp.where(straight, side(0) + side(1), 0.0), jnp.where(seam | top | bottom, side(2), 0.0)], axis=1
    )
    exact = dict(precision=lax.Precision.HIGHEST, preferred_element_type=F32)
    half = jnp.dot(dens, basis_rows[...], **exact)
    wide = wide_in[...] + lax.dot_general(half, basis_cols[...], (((0,), (0,)), ((), ())), **exact)
    lane = lanes()
    which = lax.div(lane, MODES)
    flat = wide[:SUB]
    for j in range(1, MODES // SUB):
        flat = jnp.where(which == j, wide[SUB * j : SUB * (j + 1)], flat)
    mark = jnp.broadcast_to(block[:1, :].astype(F32), (1, TILE))
    pieces = [flat[r : r + 1] for r in range(SUB)] + [mark]
    chunk = min(32, coef.shape[0])

    def spread(d, carry):
        for e in range(chunk):
            for r, piece in enumerate(pieces):
                coef[d * chunk + e, :, TILE * r : TILE * (r + 1)] = piece
        return carry

    lax.fori_loop(0, coef.shape[0] // chunk, spread, 0)


def join_kernel(v0, v1, ends, strips, vel, turned):
    rows = vel.shape[1]
    span = rows // SUB
    middle = jnp.zeros((TILE - 2 * HALO, TILE), F32)
    side = beside()
    for k, v in enumerate((v0, v1)):
        for part in range(PARTS):
            base = STRIP * (2 * part + 1 - k)
            first = strips[base + HALO : base + 2 * HALO, :]
            last = strips[base + SLOT : base + SLOT + HALO, :]
            at = TILE * (2 * part + k)
            turned[at : at + TILE, :] = jnp.concatenate([first, middle, last], axis=0).T
        for row in range(0, rows, SUB):
            if row == 0:
                value = ends[2 * HALO * k : 2 * HALO * k + HALO, :]
            elif row == rows - SUB:
                value = ends[2 * HALO * k + HALO : 2 * HALO * (k + 1), :]
            else:
                value = v[pl.ds(SUB * (row % span) + row // span, SUB, stride=SUB), :]
            part, lane = right_part(row)
            at = TILE * (2 * part + k) + lane
            vel[k, row : row + SUB, :] = jnp.where(side, turned[at : at + SUB, :], value)


def bases():
    places = np.arange(TILE) + 0.5
    basis = np.cos(math.pi * places[:, None] * np.arange(MODES)[None, :] / TILE)
    groups = MODES // SUB
    order = np.arange(MODES).reshape(SUB, groups).T.reshape(-1)
    rows = basis[:, order] / TILE
    cols = np.tile(basis, (1, groups))
    placed = np.zeros((2 * TILE, MODES))
    for row in range(0, 2 * TILE, SUB):
        part, lane = right_part(row)
        at = lane + (TILE if part == 2 else 0)
        placed[at : at + SUB] = rows[row % TILE : row % TILE + SUB]
    outer = np.concatenate([cols[:HALO], cols[TILE - HALO :]])
    return [jnp.asarray(x, F32) for x in (rows.T, cols, placed, outer)]


def pick_kernel(owners, every, out):
    mine = out.shape[1]
    own = lax.axis_index("own")
    wanted = [owners[pl.ds(own, 1), k : k + 1].astype(F32) for k in range(mine)]
    lines = SUB + 1
    devices = every.shape[0] // lines
    chunk = min(4, devices // SUB)

    def body(d, sums):
        sums = list(sums)
        for e in range(chunk):
            base = (d * chunk + e) * SUB * lines
            mark = every[pl.ds(base + SUB, SUB, stride=lines), :]
            hits = [mark == wanted[k] for k in range(mine)]
            for r in range(SUB):
                part = every[pl.ds(base + r, SUB, stride=lines), :]
                for k in range(mine):
                    sums[SUB * k + r] += jnp.where(hits[k], part, 0.0)
        return tuple(sums)

    start = (jnp.zeros((SUB, TILE), F32),) * (mine * SUB)
    sums = lax.fori_loop(0, devices // SUB // chunk, body, start)
    for k in range(mine):
        for r in range(SUB):
            total = jnp.sum(sums[SUB * k + r], axis=0, keepdims=True)
            out[0, k : k + 1, TILE * r : TILE * (r + 1)] = total


def local(viscosity, friction, driving, observed, ice_mask, tile_block, owner_list):
    rows, cols = viscosity.shape
    assert (rows, cols) == (2 * TILE, TILE)
    inputs = (viscosity, friction, driving, ice_mask, observed)
    near = [pltpu.with_memory_space_constraint(x, pltpu.VMEM) for x in inputs]
    basis_p, basis_q, basis_rows, basis_cols = bases()
    to_a, to_b = call(
        ends_kernel,
        "ends",
        (vmem(EDGE, cols), vmem(EDGE, cols)),
        [
            vmem(2, 2, HALO, cols),
            vmem(2, 2, 2, HALO, cols),
            pltpu.VMEM((2, HALO, cols), jnp.int32),
            pltpu.SemaphoreType.DMA((2, 5)),
        ],
        10**6,
        *(pltpu.with_memory_space_constraint(x, pltpu.HBM) for x in inputs),
    )
    row_a = swap(to_a, ROW_AXES, 0)
    forward = call(
        interior_kernel,
        "interior",
        (vmem(rows, cols),) * 6,
        [vmem(rows, cols)] * (FIELDS - 6),
        4 * 10**6,
        *near,
    )
    to_b = hold(to_b, row_a, forward[-1])
    row_b = swap(to_b, ROW_AXES, 1)
    edge = call(outer_kernel, "outer", vmem(2 * PARTS * TILE, TILE), [], 4 * 10**6, *near, to_b)
    to_a, to_b, turned = call(
        columns_kernel,
        "columns",
        (vmem(SENT, TILE), vmem(SENT, TILE), vmem(SLOT, TILE)),
        [],
        10**5,
        row_a,
        row_b,
        edge,
    )
    col_a = swap(to_a, COL_AXES, 0)
    *strips, vel_ends = call(
        top_bottom_kernel,
        "top_bottom",
        (vmem(ARRAYS * STRIP, cols), vmem(2 * STRIP, cols))
        + (vmem(STRIP, cols),) * 4
        + (vmem(4 * HALO, cols),),
        [vmem(STRIP, cols)] * (FIELDS - 4),
        4 * 10**6,
        row_a,
        row_b,
        *near,
        to_a,
    )
    to_b = hold(to_b, col_a, vel_ends)
    col_b = swap(to_b, COL_AXES, 1)
    wide = call(
        adjoint_kernel,
        "adjoint",
        vmem(MODES, TILE),
        [vmem(rows + STRIP, cols), vmem(TILE, cols)]
        + [vmem(STRIP, cols)] * (FIELDS - 4)
        + [vmem(rows, cols)] * (FIELDS - 4),
        4 * 10**6,
        *near,
        *forward,
        *strips,
        basis_p,
        basis_q,
        to_b,
    )
    devices = lax.axis_size(ROW_AXES + COL_AXES)
    sides, coef = call(
        left_right_kernel,
        "left_right",
        (vmem(PARTS * 2 * STRIP, TILE), vmem(devices, 1, SUB * TILE + TILE)),
        [vmem(PARTS * ARRAYS * STRIP, TILE), vmem(PARTS * STRIP, TILE)]
        + [vmem(PARTS * STRIP, TILE)] * FIELDS,
        4 * 10**6,
        edge,
        turned,
        col_a,
        col_b,
        wide,
        tile_block,
        basis_rows,
        basis_cols,
    )
    parts = lax.all_to_all(coef, ROW_AXES + COL_AXES, 0, 0, tiled=True)
    state = call(
        join_kernel,
        "join",
        jax.ShapeDtypeStruct((2, rows, cols), F32),
        [vmem(2 * PARTS * TILE, TILE)],
        4 * 10**6,
        *forward[4:],
        vel_ends,
        sides,
    )
    owners = owner_list.reshape(lax.axis_size("own"), -1)
    picked = call(
        pick_kernel,
        "pick",
        jax.ShapeDtypeStruct((1, owners.shape[1], MODES * MODES), F32),
        [],
        10**5,
        owners,
        parts.reshape(-1, TILE),
    )
    return (state, picked)


def solution(mesh):
    return jax.shard_map(
        local,
        mesh=mesh,
        in_specs=(
            P(("row", "own"), "col"),
            P(("row", "own"), "col"),
            P(None, ("row", "own"), "col"),
            P(None, ("row", "own"), "col"),
            P(("row", "own"), "col"),
            P(("row", "own"), "col"),
            P(),
        ),
        out_specs=(P(None, ("row", "own"), "col"), P("own", None, None)),
        check_vma=False,
    )
```

```python
import math

import jax
import jax.numpy as jnp
import numpy as np
from jax import lax
from jax.experimental import pallas as pl
from jax.experimental.pallas import tpu as pltpu
from jax.sharding import PartitionSpec as P

TILE = 128
MODES = 32
SWEEPS = 3
SUB = 8
HALO = 8
INNER = 2 * HALO
STRIP = 2 * (HALO + INNER)
ARRAYS = 7
VISC, FRIC, DRIV, MASK, OBS = 0, 1, 2, 4, 5
EDGE = ARRAYS * HALO
SLOT = 2 * INNER
PER = TILE // SLOT
GROUPS = 5
SENT = 2 * GROUPS * HALO + HALO
PARTS = 3
UPPER, LOWER = 32, 64
ROW_AXES = ("row", "own")
COL_AXES = ("col",)
F32 = jnp.float32
LIMIT = 40 * 1024 * 1024


def swap(x, axis, first):
    sizes = lax.axis_size(ROW_AXES), lax.axis_size(COL_AXES)
    owners = lax.axis_size("own")

    def device(i, j):
        return (i // owners * sizes[1] + j) * owners + i % owners

    pairs = []
    for i in range(sizes[0]):
        for j in range(sizes[1]):
            place = [i, j]
            if first and place[axis] in (0, sizes[axis] - 1):
                place[1 - axis] ^= 1
            else:
                place[axis] = ((place[axis] + first) ^ 1) - first
            pairs.append((device(i, j), device(*place)))
    return lax.ppermute(x, ("row", "col", "own"), pairs)


def position(axes):
    index, size = 0, 1
    for axis in axes:
        index = index * lax.axis_size(axis) + lax.axis_index(axis)
        size *= lax.axis_size(axis)
    assert size % 2 == 0
    return lax.rem(index, 2) == 0, (index == 0) | (index == size - 1)


def is_even(axes):
    return position(axes)[0]


def lanes():
    return lax.broadcasted_iota(jnp.int32, (SUB, TILE), 1)


def call(kernel, name, outs, scratch, cost, *args):
    return pl.pallas_call(
        kernel,
        out_shape=outs,
        scratch_shapes=scratch,
        compiler_params=pltpu.CompilerParams(vmem_limit_bytes=LIMIT),
        cost_estimate=pl.CostEstimate(flops=cost, bytes_accessed=cost, transcendentals=0),
        name=name,
    )(*args)


def vmem(*shape):
    return pltpu.VMEM(shape, F32)


FIELDS = 14


class Domain:
    def __init__(self, refs, base, span, source):
        self.refs, self.base, self.span, self.source = refs, base, span, source

    def at(self, j):
        return pl.ds(self.base + SUB * j, SUB)

    def prepare(self, flipped):
        n2, n4, c, i, b0, b1 = self.refs[:6]
        visc = [self.source(VISC, j) for j in range(self.span)]
        for j in range(self.span):
            at = self.at(j)
            before = visc[j - 1] if j else pltpu.roll(visc[-1], 1, 0)
            pair = visc[j] + before
            fric = self.source(FRIC, j)
            diag = 1.25 * (pair + pltpu.roll(pair, 1, 1)) + fric
            on = self.source(MASK, j) > 0.0
            inv = jnp.where(on, 0.5 / jnp.where(on, diag, 1.0), 0.0)
            half = 0.5 * visc[j]
            n2[at, :] = half
            n4[at, :] = 0.5 * half
            c[at, :] = 1.0 - fric * inv
            i[at, :] = inv
            for k, b in enumerate((b0, b1)):
                value = inv * self.source(DRIV + (1 - k if flipped else k), j)
                b[at, :] = value
                self.write(k, at, value + value)

    def write(self, k, at, value):
        self.refs[6 + k][at, :] = value
        self.refs[8 + k][at, :] = pltpu.roll(value, TILE - 1, 1)

    def retarget(self, flipped, velocity=None):
        i, b0, b1 = self.refs[3:6]
        w0, w1 = velocity or self.refs[6:8]
        for j in range(self.span):
            at = self.at(j)
            for k, (b, w) in enumerate(((b0, w0), (b1, w1))):
                value = i[at, :] * (w[at, :] - self.source(OBS + (1 - k if flipped else k), j))
                b[at, :] = value
                self.write(k, at, value + value)

    def differences(self):
        n2, n4 = self.refs[:2]
        fields = self.refs[6:10]
        parts = self.refs[10:14]

        def corners(j, here, below):
            w0, w1, r0, r1 = here
            v0, v1, s0, s1 = below
            a1, a2 = s0 - w0, v0 - r0
            e1, e2 = s1 - w1, v1 - r1
            x, y = a1 + a2, e1 - e2
            q = (a1 - a2) + (e1 + e2)
            both = x + y
            at = self.at(j)
            half = n2[at, :]
            return half * (both + x), n4[at, :] * q, half * (both + y)

        def load(j):
            at = self.at(j)
            return [field[at, :] for field in fields]

        top = load(0)
        last = corners(self.span - 1, load(self.span - 1), [pltpu.roll(v, SUB - 1, 0) for v in top])
        up = [pltpu.roll(v, 1, 0) for v in last]
        here = top
        for j in range(self.span):
            at = self.at(j)
            if j < self.span - 1:
                below = load(j + 1)
                p, q, r = corners(j, here, below)
                here = below
            else:
                p, q, r = last
            g, t = up[0] - p, up[1] + q
            gq, tr = up[1] - q, up[2] + r
            parts[0][at, :] = g - t
            parts[1][at, :] = gq - tr
            parts[2][at, :] = pltpu.roll(g + t, 1, 1)
            parts[3][at, :] = pltpu.roll(gq + tr, 1, 1)
            up = (p, q, r)

    def update(self):
        c, i, b0, b1, w0, w1 = self.refs[2:8]
        parts = self.refs[10:14]
        for j in range(self.span):
            at = self.at(j)
            cv, iv = c[at, :], i[at, :]
            for k, (b, w) in enumerate(((b0, w0), (b1, w1))):
                value = (cv * w[at, :] + b[at, :]) - iv * (parts[k][at, :] + parts[k + 2][at, :])
                self.write(k, at, value)


def run(domains):
    def body(_, carry):
        for domain in domains:
            domain.differences()
        for domain in domains:
            domain.update()
        return carry

    lax.fori_loop(0, SWEEPS, body, 0)


def ends_kernel(visc, fric, driv, mask, obs, to_a, to_b, one, two, flags, sems):
    rows = visc.shape[0]
    copies = []
    for e, first in enumerate((0, rows - HALO)):
        at = pl.ds(first, HALO)
        pieces = [
            (visc.at[at], one.at[e, 0]),
            (fric.at[at], one.at[e, 1]),
            (driv.at[:, at], two.at[e, 0]),
            (mask.at[at], flags.at[e]),
            (obs.at[:, at], two.at[e, 1]),
        ]
        for n, (source, place) in enumerate(pieces):
            copies.append(pltpu.make_async_copy(source, place, sems.at[e, n]))
    for copy in copies:
        copy.start()
    for copy in copies:
        copy.wait()
    even, at_end = position(ROW_AXES)

    def edge(e):
        return [one[e, 0], one[e, 1], two[e, 0, 0], two[e, 0, 1], flags[e].astype(F32), two[e, 1, 0], two[e, 1, 1]]

    for a, (head, tail) in enumerate(zip(edge(0), edge(1))):
        at = slice(HALO * a, HALO * (a + 1))
        to_a[at, :] = jnp.where(even, tail, head)
        to_b[at, :] = jnp.where(at_end, 0.0, jnp.where(even, head, tail))


def field_of(visc, fric, driv, mask, obs):
    def field(a, at):
        if a == MASK:
            return mask[at, :].astype(F32)
        if a >= OBS:
            return obs[a - OBS, at, :]
        if a >= DRIV:
            return driv[a - DRIV, at, :]
        return (visc, fric)[a][at, :]

    return field


def first_row(part, lane):
    if part < 2:
        return TILE * part + lane
    if lane < INNER + HALO:
        return TILE + lane
    if lane >= TILE - INNER - HALO:
        return lane
    if UPPER + HALO <= lane < UPPER + SLOT:
        return lane - UPPER - HALO
    if LOWER <= lane < LOWER + INNER + HALO:
        return 2 * TILE - INNER - HALO + lane - LOWER
    return None


def right_part(row):
    seam = TILE - HALO <= row < TILE + HALO
    part = 2 if seam or row == 0 or row == 2 * TILE - HALO else row // TILE
    return part, [lane for lane in range(0, TILE, SUB) if first_row(part, lane) == row][-1]


def slot(part, a):
    return TILE * (2 * part + a // PER) + SLOT * (a % PER)


def interior_kernel(visc, fric, driv, mask, obs, edge, n2, n4, c, i, v0, v1, *refs):
    span = visc.shape[0] // SUB
    field = field_of(visc, fric, driv, mask, obs)
    lane = lanes()
    for part in range(PARTS):
        for m in range(-(-ARRAYS // PER)):
            strips = []
            for at in range(0, TILE, SUB):
                row = first_row(part, at)
                packed = jnp.zeros((SUB, TILE), F32)
                if row is not None:
                    for k in range(min(PER, ARRAYS - PER * m)):
                        value = field(PER * m + k, slice(row, row + SUB))
                        moved = pltpu.roll(value, (SLOT * k + INNER) % TILE, 1)
                        packed = jnp.where(lax.div(lane, SLOT) == k, moved, packed)
                strips.append(packed)
            base = TILE * (2 * part + m)
            edge[base : base + TILE, :] = jnp.concatenate(strips, axis=0).T
    refs = (n2, n4, c, i, *refs[:2], v0, v1, *refs[2:])
    domain = Domain(refs, 0, span, lambda a, j: field(a, pl.ds(j, SUB, stride=span)))
    domain.prepare(False)
    run([domain])


def columns_kernel(row_a, row_b, edge, to_a, to_b, turned):
    even = is_even(ROW_AXES)
    above = jnp.where(even, row_b[...], row_a[...])
    below = jnp.where(even, row_a[...], row_b[...])
    halo = jnp.concatenate([above, below, jnp.zeros((TILE - 2 * EDGE, TILE), F32)], axis=0).T
    turned[:INNER, :] = halo[TILE - INNER :]
    turned[INNER:, :] = halo[:INNER]
    even, at_end = position(COL_AXES)
    row = lax.broadcasted_iota(jnp.int32, (SUB, TILE), 0)

    def put(out, right, left):
        to_a[out : out + HALO, :] = jnp.where(even, right, left)
        to_b[out : out + HALO, :] = jnp.where(at_end, 0.0, jnp.where(even, left, right))

    for part in range(2):
        right, left = [], []
        for a in range(ARRAYS):
            at = slot(part, a) + INNER
            right.append(edge[at - HALO : at, :])
            left.append(edge[at : at + HALO, :])
        for k in range(2):
            seen_r, seen_l = right[OBS + k], left[OBS + k]
            g = 1 + 2 * k
            right[g] = jnp.where(row < 2, pltpu.roll(seen_r, 2, 0), right[g])
            right[g + 1] = jnp.where(row < 2, pltpu.roll(seen_r, 4, 0), right[g + 1])
            left[g] = jnp.where(row >= 6, pltpu.roll(seen_l, 6, 0), left[g])
            left[g + 1] = jnp.where(row >= 6, pltpu.roll(seen_l, 4, 0), left[g + 1])
        for g in range(GROUPS):
            put(HALO * (GROUPS * part + g), right[g], left[g])
    put(2 * GROUPS * HALO, halo[TILE - HALO :], halo[:HALO])


def strided(stack, base):
    span = STRIP // SUB
    return lambda a, j: stack[pl.ds(base + STRIP * a + j, SUB, stride=span), :]


def velocity(domain, plain, base):
    for j in range(domain.span):
        at = domain.at(j)
        for k in range(2):
            plain[pl.ds(base + STRIP * k + j, SUB, stride=domain.span), :] = domain.refs[6 + k][at, :]


def density(domain, plain, base, out, place):
    w0, w1 = domain.refs[6:8]
    for j in range(domain.span):
        at = domain.at(j)
        v0, v1 = (plain[pl.ds(base + STRIP * k + j, SUB, stride=domain.span), :] for k in range(2))
        value = -domain.source(FRIC, j) * (w0[at, :] * v0 + w1[at, :] * v1)
        out[pl.ds(place + j, SUB, stride=domain.span), :] = value


def beside():
    lane = lanes()
    return (lane < HALO) | (lane >= TILE - HALO)


def adjoint_kernel(
    row_a, row_b, visc, fric, driv, mask, obs, n2, n4, c, i, v0, v1, basis_p, basis_q,
    vel, wide,
    stack, plain, dens, total, *refs,
):
    rows = visc.shape[0]
    span = rows // SUB
    even = is_even(ROW_AXES)
    field = field_of(visc, fric, driv, mask, obs)
    for a in range(ARRAYS):
        at = slice(HALO * a, HALO * (a + 1))
        got_a, got_b = row_a[at, :], row_b[at, :]
        base = STRIP * a
        stack[base : base + HALO, :] = jnp.where(even, got_b, got_a)
        stack[base + HALO : base + HALO + INNER, :] = field(a, slice(0, INNER))
        stack[base + HALO + INNER : base + HALO + SLOT, :] = field(a, slice(rows - INNER, rows))
        stack[base + HALO + SLOT : base + STRIP, :] = jnp.where(even, got_a, got_b)
    strips = Domain(refs[:FIELDS], 0, STRIP // SUB, strided(stack, 0))
    strips.prepare(False)
    run([strips])
    velocity(strips, plain, 0)
    outer = (HALO, SLOT)
    for k in range(2):
        for e in range(2):
            out = HALO * (2 * k + e)
            vel[out : out + HALO, :] = plain[STRIP * k + outer[e] : STRIP * k + outer[e] + HALO, :]
    interior = Domain(
        (n2, n4, c, i, *refs[FIELDS:]), 0, span, lambda a, j: field(a, pl.ds(j, SUB, stride=span))
    )
    strips.retarget(False)
    interior.retarget(False, (v0, v1))
    run([interior, strips])
    w0, w1 = interior.refs[6:8]
    for j in range(span):
        at = interior.at(j)
        value = -interior.source(FRIC, j) * (w0[at, :] * v0[at, :] + w1[at, :] * v1[at, :])
        dens[pl.ds(j, SUB, stride=span), :] = value
    density(strips, plain, 0, dens, rows)

    side = beside()
    for s in range(0, TILE, SUB):
        summed = jnp.zeros((SUB, TILE), F32)
        for row in range(s, rows, TILE):
            at = rows + outer[0] if row == 0 else rows + outer[1] if row == rows - SUB else row
            summed += dens[at : at + SUB, :]
        total[s : s + SUB, :] = jnp.where(side, 0.0, summed)
    exact = dict(precision=lax.Precision.HIGHEST, preferred_element_type=F32)
    half = jnp.dot(basis_p[...], total[...], **exact)
    wide[...] = jnp.dot(half, basis_q[...], **exact)


def left_right_kernel(
    edge, turned, col_a, col_b, wide_in, block, basis_rows, basis_cols,
    strips, coef,
    stack, plain, *refs,
):
    even = is_even(COL_AXES)
    lane = lanes()
    row = lax.broadcasted_iota(jnp.int32, (SUB, TILE), 0)
    upper = (lane >= UPPER + HALO) & (lane < UPPER + SLOT)
    lower = (lane >= LOWER) & (lane < LOWER + INNER + HALO)
    seam_t0 = lane >= TILE - INNER - HALO
    seam_t1 = lane < INNER + HALO
    corner = ((lane >= UPPER) & (lane < UPPER + HALO)) | ((lane >= LOWER + INNER + HALO) & (lane < LOWER + SLOT))

    def place(part, a):
        return STRIP * (ARRAYS * part + a)

    for from_left in (True, False):
        groups = []
        for g in range(2 * GROUPS + 1):
            got_a, got_b = col_a[HALO * g : HALO * (g + 1), :], col_b[HALO * g : HALO * (g + 1), :]
            groups.append(jnp.where(even, got_b, got_a) if from_left else jnp.where(even, got_a, got_b))
        tiles = []
        for part in range(2):
            tile = groups[GROUPS * part : GROUPS * (part + 1)]
            for k in range(2):
                g, h = tile[1 + 2 * k], tile[2 + 2 * k]
                if from_left:
                    tile.append(jnp.where(row >= 6, pltpu.roll(g, 6, 0), pltpu.roll(h, 4, 0)))
                else:
                    tile.append(jnp.where(row < 2, pltpu.roll(g, 2, 0), pltpu.roll(h, 4, 0)))
            tiles.append(tile)
        for a in range(ARRAYS):
            t0, t1 = tiles[0][a], tiles[1][a]
            third = jnp.where(corner, pltpu.roll(groups[-1], (UPPER - HALO * a) % TILE, 1), 0.0)
            third = jnp.where(upper, pltpu.roll(t0, UPPER + HALO, 1), third)
            third = jnp.where(lower, pltpu.roll(t1, LOWER + INNER + HALO, 1), third)
            third = jnp.where(seam_t0, t0, jnp.where(seam_t1, t1, third))
            for part, value in enumerate((t0, t1, third)):
                base = place(part, a) + (0 if from_left else HALO + SLOT)
                stack[base : base + HALO, :] = value
    for a in range(ARRAYS):
        for part in range(PARTS):
            base = place(part, a) + HALO
            for r in range(0, SLOT, SUB):
                value = edge[slot(part, a) + r : slot(part, a) + r + SUB, :]
                if part == 2:
                    moved = pltpu.roll(turned[r : r + SUB, :], (UPPER - HALO * a) % TILE, 1)
                    value = jnp.where(corner, moved, value)
                to = base + (r + INNER) % SLOT
                stack[to : to + SUB, :] = value

    domains = [
        Domain(refs, STRIP * part, STRIP // SUB, strided(stack, place(part, 0))) for part in range(PARTS)
    ]
    for domain in domains:
        domain.prepare(True)
    run(domains)
    for part, domain in enumerate(domains):
        velocity(domain, strips, 2 * STRIP * part)
        domain.retarget(True)
    run(domains)
    for part, domain in enumerate(domains):
        density(domain, strips, 2 * STRIP * part, plain, STRIP * part)

    def side(part):
        base = STRIP * part
        return jnp.concatenate(
            [plain[base + HALO : base + 2 * HALO, :], plain[base + SLOT : base + SLOT + HALO, :]], axis=0
        )

    lane = lax.broadcasted_iota(jnp.int32, (2 * HALO, TILE), 1)
    straight = (lane >= HALO) & (lane < TILE - HALO)
    seam = (lane < HALO) | (lane >= TILE - HALO)
    top = (lane >= UPPER + HALO) & (lane < UPPER + 2 * HALO)
    bottom = (lane >= LOWER + INNER) & (lane < LOWER + INNER + HALO)
    dens = jnp.concatenate(
        [jnp.where(straight, side(0) + side(1), 0.0), jnp.where(seam | top | bottom, side(2), 0.0)], axis=1
    )
    exact = dict(precision=lax.Precision.HIGHEST, preferred_element_type=F32)
    half = jnp.dot(dens, basis_rows[...], **exact)
    wide = wide_in[...] + lax.dot_general(half, basis_cols[...], (((0,), (0,)), ((), ())), **exact)
    lane = lanes()
    which = lax.div(lane, MODES)
    flat = wide[:SUB]
    for j in range(1, MODES // SUB):
        flat = jnp.where(which == j, wide[SUB * j : SUB * (j + 1)], flat)
    mark = jnp.broadcast_to(block[:1, :].astype(F32), (1, TILE))
    pieces = [flat[r : r + 1] for r in range(SUB)] + [mark]
    chunk = min(32, coef.shape[0])

    def spread(d, carry):
        for e in range(chunk):
            for r, piece in enumerate(pieces):
                coef[d * chunk + e, :, TILE * r : TILE * (r + 1)] = piece
        return carry

    lax.fori_loop(0, coef.shape[0] // chunk, spread, 0)


def join_kernel(v0, v1, ends, strips, vel, turned):
    rows = vel.shape[1]
    span = rows // SUB
    middle = jnp.zeros((TILE - 2 * HALO, TILE), F32)
    side = beside()
    for k, v in enumerate((v0, v1)):
        for part in range(PARTS):
            base = STRIP * (2 * part + 1 - k)
            first = strips[base + HALO : base + 2 * HALO, :]
            last = strips[base + SLOT : base + SLOT + HALO, :]
            at = TILE * (2 * part + k)
            turned[at : at + TILE, :] = jnp.concatenate([first, middle, last], axis=0).T
        for row in range(0, rows, SUB):
            if row == 0:
                value = ends[2 * HALO * k : 2 * HALO * k + HALO, :]
            elif row == rows - SUB:
                value = ends[2 * HALO * k + HALO : 2 * HALO * (k + 1), :]
            else:
                value = v[pl.ds(SUB * (row % span) + row // span, SUB, stride=SUB), :]
            part, lane = right_part(row)
            at = TILE * (2 * part + k) + lane
            vel[k, row : row + SUB, :] = jnp.where(side, turned[at : at + SUB, :], value)


def bases():
    places = np.arange(TILE) + 0.5
    basis = np.cos(math.pi * places[:, None] * np.arange(MODES)[None, :] / TILE)
    groups = MODES // SUB
    order = np.arange(MODES).reshape(SUB, groups).T.reshape(-1)
    rows = basis[:, order] / TILE
    cols = np.tile(basis, (1, groups))
    placed = np.zeros((2 * TILE, MODES))
    for row in range(0, 2 * TILE, SUB):
        part, lane = right_part(row)
        at = lane + (TILE if part == 2 else 0)
        placed[at : at + SUB] = rows[row % TILE : row % TILE + SUB]
    outer = np.concatenate([cols[:HALO], cols[TILE - HALO :]])
    return [jnp.asarray(x, F32) for x in (rows.T, cols, placed, outer)]


def pick_kernel(owners, every, out):
    mine = out.shape[1]
    own = lax.axis_index("own")
    wanted = [owners[pl.ds(own, 1), k : k + 1].astype(F32) for k in range(mine)]
    lines = SUB + 1
    devices = every.shape[0] // lines
    chunk = min(4, devices // SUB)

    def body(d, sums):
        sums = list(sums)
        for e in range(chunk):
            base = (d * chunk + e) * SUB * lines
            mark = every[pl.ds(base + SUB, SUB, stride=lines), :]
            hits = [mark == wanted[k] for k in range(mine)]
            for r in range(SUB):
                part = every[pl.ds(base + r, SUB, stride=lines), :]
                for k in range(mine):
                    sums[SUB * k + r] += jnp.where(hits[k], part, 0.0)
        return tuple(sums)

    start = (jnp.zeros((SUB, TILE), F32),) * (mine * SUB)
    sums = lax.fori_loop(0, devices // SUB // chunk, body, start)
    for k in range(mine):
        for r in range(SUB):
            total = jnp.sum(sums[SUB * k + r], axis=0, keepdims=True)
            out[0, k : k + 1, TILE * r : TILE * (r + 1)] = total


def local(viscosity, friction, driving, observed, ice_mask, tile_block, owner_list):
    rows, cols = viscosity.shape
    assert (rows, cols) == (2 * TILE, TILE)
    inputs = (viscosity, friction, driving, ice_mask, observed)
    near = [pltpu.with_memory_space_constraint(x, pltpu.VMEM) for x in inputs]
    basis_p, basis_q, basis_rows, basis_cols = bases()
    to_a, to_b = call(
        ends_kernel,
        "ends",
        (vmem(EDGE, cols), vmem(EDGE, cols)),
        [
            vmem(2, 2, HALO, cols),
            vmem(2, 2, 2, HALO, cols),
            pltpu.VMEM((2, HALO, cols), jnp.int32),
            pltpu.SemaphoreType.DMA((2, 5)),
        ],
        10**6,
        *(pltpu.with_memory_space_constraint(x, pltpu.HBM) for x in inputs),
    )
    row_b = swap(to_b, 0, 1)
    row_a = swap(to_a, 0, 0)
    edge, *forward = call(
        interior_kernel,
        "interior",
        (vmem(2 * PARTS * TILE, TILE),) + (vmem(rows, cols),) * 6,
        [vmem(rows, cols)] * (FIELDS - 6),
        8 * 10**6,
        *near,
    )
    to_a, to_b, turned = call(
        columns_kernel,
        "columns",
        (vmem(SENT, TILE), vmem(SENT, TILE), vmem(SLOT, TILE)),
        [],
        10**5,
        row_a,
        row_b,
        edge,
    )
    col_a = swap(to_a, 1, 0)
    col_b = swap(to_b, 1, 1)
    vel_ends, wide = call(
        adjoint_kernel,
        "adjoint",
        (vmem(4 * HALO, cols), vmem(MODES, TILE)),
        [vmem(ARRAYS * STRIP, cols), vmem(2 * STRIP, cols), vmem(rows + STRIP, cols), vmem(TILE, cols)]
        + [vmem(STRIP, cols)] * FIELDS
        + [vmem(rows, cols)] * (FIELDS - 4),
        8 * 10**6,
        row_a,
        row_b,
        *near,
        *forward,
        basis_p,
        basis_q,
    )
    devices = lax.axis_size(ROW_AXES + COL_AXES)
    strips, coef = call(
        left_right_kernel,
        "left_right",
        (vmem(PARTS * 2 * STRIP, TILE), vmem(devices, 1, SUB * TILE + TILE)),
        [vmem(PARTS * ARRAYS * STRIP, TILE), vmem(PARTS * STRIP, TILE)]
        + [vmem(PARTS * STRIP, TILE)] * FIELDS,
        4 * 10**6,
        edge,
        turned,
        col_a,
        col_b,
        wide,
        tile_block,
        basis_rows,
        basis_cols,
    )
    parts = lax.all_to_all(coef, ROW_AXES + COL_AXES, 0, 0, tiled=True)
    state = call(
        join_kernel,
        "join",
        jax.ShapeDtypeStruct((2, rows, cols), F32),
        [vmem(2 * PARTS * TILE, TILE)],
        4 * 10**6,
        *forward[4:],
        vel_ends,
        strips,
    )
    owners = owner_list.reshape(lax.axis_size("own"), -1)
    picked = call(
        pick_kernel,
        "pick",
        jax.ShapeDtypeStruct((1, owners.shape[1], MODES * MODES), F32),
        [],
        10**5,
        owners,
        parts.reshape(-1, TILE),
    )
    return (state, picked)


def solution(mesh):
    return jax.shard_map(
        local,
        mesh=mesh,
        in_specs=(
            P(("row", "own"), "col"),
            P(("row", "own"), "col"),
            P(None, ("row", "own"), "col"),
            P(None, ("row", "own"), "col"),
            P(("row", "own"), "col"),
            P(("row", "own"), "col"),
            P(),
        ),
        out_specs=(P(None, ("row", "own"), "col"), P("own", None, None)),
        check_vma=False,
    )
```

```python
import math

import jax
import jax.numpy as jnp
import numpy as np
from jax import lax
from jax.experimental import pallas as pl
from jax.experimental.pallas import tpu as pltpu
from jax.sharding import PartitionSpec as P

TILE = 128
MODES = 32
SWEEPS = 3
SUB = 8
HALO = 8
INNER = 2 * HALO
STRIP = 40
LEAD = HALO - 1
KEPT = 12
OUTER = (LEAD, STRIP - 2 * HALO)
NEAR, FAR = 7, 6
ARRAYS = 7
VISC, FRIC, DRIV, MASK, OBS = 0, 1, 2, 4, 5
EDGE = ARRAYS * HALO
SLOT = 2 * INNER
PER = TILE // SLOT
GROUPS = 5
SENT = 2 * GROUPS * HALO + HALO
PARTS = 3
UPPER, LOWER = 32, 64
ROW_AXES = ("row", "own")
COL_AXES = ("col",)
F32 = jnp.float32
LIMIT = 40 * 1024 * 1024


def swap(x, axis, first):
    sizes = lax.axis_size(ROW_AXES), lax.axis_size(COL_AXES)
    owners = lax.axis_size("own")

    def device(i, j):
        return (i // owners * sizes[1] + j) * owners + i % owners

    pairs = []
    for i in range(sizes[0]):
        for j in range(sizes[1]):
            place = [i, j]
            if first and place[axis] in (0, sizes[axis] - 1):
                place[1 - axis] ^= 1
            else:
                place[axis] = ((place[axis] + first) ^ 1) - first
            pairs.append((device(i, j), device(*place)))
    return lax.ppermute(x, ("row", "col", "own"), pairs)


def position(axes):
    index, size = 0, 1
    for axis in axes:
        index = index * lax.axis_size(axis) + lax.axis_index(axis)
        size *= lax.axis_size(axis)
    assert size % 2 == 0
    return lax.rem(index, 2) == 0, (index == 0) | (index == size - 1)


def is_even(axes):
    return position(axes)[0]


def lanes():
    return lax.broadcasted_iota(jnp.int32, (SUB, TILE), 1)


def call(kernel, name, outs, scratch, cost, *args, aliases={}):
    return pl.pallas_call(
        kernel,
        out_shape=outs,
        scratch_shapes=scratch,
        input_output_aliases=aliases,
        compiler_params=pltpu.CompilerParams(vmem_limit_bytes=LIMIT),
        cost_estimate=pl.CostEstimate(flops=cost, bytes_accessed=cost, transcendentals=0),
        name=name,
    )(*args)


def vmem(*shape):
    return pltpu.VMEM(shape, F32)


FIELDS = 14


class Domain:
    def __init__(self, refs, base, span, source, seam=None):
        self.refs, self.base, self.span, self.source, self.seam = refs, base, span, source, seam

    def at(self, j):
        return pl.ds(self.base + SUB * j, SUB)

    def prepare(self, flipped):
        n2, n4, c, i, b0, b1 = self.refs[:6]
        visc = [self.source(VISC, j) for j in range(self.span)]
        for j in range(self.span):
            at = self.at(j)
            before = visc[j - 1] if j else pltpu.roll(visc[-1], 1, 0)
            if self.seam and not j:
                row = lax.broadcasted_iota(jnp.int32, (SUB, TILE), 0)
                before = jnp.where(row == SUB // 2, self.seam(), before)
            pair = visc[j] + before
            fric = self.source(FRIC, j)
            diag = 1.25 * (pair + pltpu.roll(pair, 1, 1)) + fric
            on = self.source(MASK, j) > 0.0
            inv = jnp.where(on, 0.5 / jnp.where(on, diag, 1.0), 0.0)
            half = 0.5 * visc[j]
            n2[at, :] = half
            n4[at, :] = 0.5 * half
            c[at, :] = 1.0 - fric * inv
            i[at, :] = inv
            for k, b in enumerate((b0, b1)):
                value = inv * self.source(DRIV + (1 - k if flipped else k), j)
                b[at, :] = value
                self.write(k, at, value + value)

    def write(self, k, at, value):
        self.refs[6 + k][at, :] = value
        self.refs[8 + k][at, :] = pltpu.roll(value, TILE - 1, 1)

    def retarget(self, flipped, velocity=None):
        i, b0, b1 = self.refs[3:6]
        w0, w1 = velocity or self.refs[6:8]
        for j in range(self.span):
            at = self.at(j)
            for k, (b, w) in enumerate(((b0, w0), (b1, w1))):
                value = i[at, :] * (w[at, :] - self.source(OBS + (1 - k if flipped else k), j))
                b[at, :] = value
                self.write(k, at, value + value)

    def differences(self):
        n2, n4 = self.refs[:2]
        fields = self.refs[6:10]
        parts = self.refs[10:14]

        def corners(j, here, below):
            w0, w1, r0, r1 = here
            v0, v1, s0, s1 = below
            a1, a2 = s0 - w0, v0 - r0
            e1, e2 = s1 - w1, v1 - r1
            x, y = a1 + a2, e1 - e2
            q = (a1 - a2) + (e1 + e2)
            both = x + y
            at = self.at(j)
            half = n2[at, :]
            return half * (both + x), n4[at, :] * q, half * (both + y)

        def load(j):
            at = self.at(j)
            return [field[at, :] for field in fields]

        top = load(0)
        last = corners(self.span - 1, load(self.span - 1), [pltpu.roll(v, SUB - 1, 0) for v in top])
        up = [pltpu.roll(v, 1, 0) for v in last]
        here = top
        for j in range(self.span):
            at = self.at(j)
            if j < self.span - 1:
                below = load(j + 1)
                p, q, r = corners(j, here, below)
                here = below
            else:
                p, q, r = last
            g, t = up[0] - p, up[1] + q
            gq, tr = up[1] - q, up[2] + r
            parts[0][at, :] = g - t
            parts[1][at, :] = gq - tr
            parts[2][at, :] = pltpu.roll(g + t, 1, 1)
            parts[3][at, :] = pltpu.roll(gq + tr, 1, 1)
            up = (p, q, r)

    def update(self):
        c, i, b0, b1, w0, w1 = self.refs[2:8]
        parts = self.refs[10:14]
        for j in range(self.span):
            at = self.at(j)
            cv, iv = c[at, :], i[at, :]
            for k, (b, w) in enumerate(((b0, w0), (b1, w1))):
                value = (cv * w[at, :] + b[at, :]) - iv * (parts[k][at, :] + parts[k + 2][at, :])
                self.write(k, at, value)


def run(domains):
    def body(_, carry):
        for domain in domains:
            domain.differences()
        for domain in domains:
            domain.update()
        return carry

    lax.fori_loop(0, SWEEPS, body, 0)


def ends_kernel(visc, fric, driv, mask, obs, to_b, to_a, one, two, flags, sems):
    rows = visc.shape[0]
    copies = []
    for e, first in enumerate((0, rows - HALO)):
        at = pl.ds(first, HALO)
        pieces = [
            (visc.at[at], one.at[e, 0]),
            (fric.at[at], one.at[e, 1]),
            (driv.at[:, at], two.at[e, 0]),
            (mask.at[at], flags.at[e]),
            (obs.at[:, at], two.at[e, 1]),
        ]
        for n, (source, place) in enumerate(pieces):
            copies.append(pltpu.make_async_copy(source, place, sems.at[e, n]))
    for copy in copies:
        copy.start()
    for copy in copies:
        copy.wait()
    even, at_end = position(ROW_AXES)

    def edge(e):
        return [one[e, 0], one[e, 1], two[e, 0, 0], two[e, 0, 1], flags[e].astype(F32), two[e, 1, 0], two[e, 1, 1]]

    for a, (head, tail) in enumerate(zip(edge(0), edge(1))):
        at = slice(HALO * a, HALO * (a + 1))
        to_a[at, :] = jnp.where(even, tail, head)
        to_b[at, :] = jnp.where(at_end, 0.0, jnp.where(even, head, tail))


def field_of(visc, fric, driv, mask, obs):
    def field(a, at):
        if a == MASK:
            return mask[at, :].astype(F32)
        if a >= OBS:
            return obs[a - OBS, at, :]
        if a >= DRIV:
            return driv[a - DRIV, at, :]
        return (visc, fric)[a][at, :]

    return field


def first_row(part, lane):
    if part < 2:
        return TILE * part + lane
    if lane < INNER + HALO:
        return TILE + lane
    if lane >= TILE - INNER - HALO:
        return lane
    if UPPER + HALO <= lane < UPPER + SLOT:
        return lane - UPPER - HALO
    if LOWER <= lane < LOWER + INNER + HALO:
        return 2 * TILE - INNER - HALO + lane - LOWER
    return None


def right_part(row):
    seam = TILE - HALO <= row < TILE + HALO
    part = 2 if seam or row == 0 or row == 2 * TILE - HALO else row // TILE
    return part, [lane for lane in range(0, TILE, SUB) if first_row(part, lane) == row][-1]


def slot(part, a):
    return TILE * (2 * part + a // PER) + SLOT * (a % PER)


def interior_kernel(visc, fric, driv, mask, obs, edge, n2, n4, c, i, v0, v1, *refs):
    span = visc.shape[0] // SUB
    field = field_of(visc, fric, driv, mask, obs)
    lane = lanes()
    for part in range(PARTS):
        for m in range(-(-ARRAYS // PER)):
            strips = []
            for at in range(0, TILE, SUB):
                row = first_row(part, at)
                packed = jnp.zeros((SUB, TILE), F32)
                if row is not None:
                    for k in range(min(PER, ARRAYS - PER * m)):
                        value = field(PER * m + k, slice(row, row + SUB))
                        moved = pltpu.roll(value, (SLOT * k + INNER) % TILE, 1)
                        packed = jnp.where(lax.div(lane, SLOT) == k, moved, packed)
                strips.append(packed)
            base = TILE * (2 * part + m)
            edge[base : base + TILE, :] = jnp.concatenate(strips, axis=0).T
    refs = (n2, n4, c, i, *refs[:2], v0, v1, *refs[2:])
    domain = Domain(refs, 0, span, lambda a, j: field(a, pl.ds(j, SUB, stride=span)))
    domain.prepare(False)
    run([domain])


def columns_kernel(row_b, row_a, edge, to_b, to_a, turned):
    even = is_even(ROW_AXES)
    above = jnp.where(even, row_b[...], row_a[...])
    below = jnp.where(even, row_a[...], row_b[...])
    halo = jnp.concatenate([above, below, jnp.zeros((TILE - 2 * EDGE, TILE), F32)], axis=0).T
    turned[:INNER, :] = halo[TILE - INNER :]
    turned[INNER:, :] = halo[:INNER]
    even, at_end = position(COL_AXES)
    row = lax.broadcasted_iota(jnp.int32, (SUB, TILE), 0)

    def put(out, right, left):
        right = pltpu.roll(right, LEAD, 0)
        to_a[out : out + HALO, :] = jnp.where(even, right, left)
        to_b[out : out + HALO, :] = jnp.where(at_end, 0.0, jnp.where(even, left, right))

    for part in range(2):
        right, left = [], []
        for a in range(ARRAYS):
            at = slot(part, a) + INNER
            right.append(edge[at - HALO : at, :])
            left.append(edge[at : at + HALO, :])
        for k in range(2):
            seen_r, seen_l = right[OBS + k], left[OBS + k]
            g = 1 + 2 * k
            right[g] = jnp.where(row < 2, pltpu.roll(seen_r, 2, 0), right[g])
            right[g + 1] = jnp.where(row < 2, pltpu.roll(seen_r, 4, 0), right[g + 1])
            left[g] = jnp.where(row >= 6, pltpu.roll(seen_l, 6, 0), left[g])
            left[g + 1] = jnp.where(row >= 6, pltpu.roll(seen_l, 4, 0), left[g + 1])
        for g in range(GROUPS):
            put(HALO * (GROUPS * part + g), right[g], left[g])
    put(2 * GROUPS * HALO, halo[TILE - HALO :], halo[:HALO])


def strided(stack, base):
    span = STRIP // SUB
    return lambda a, j: stack[pl.ds(base + STRIP * a + j, SUB, stride=span), :]


def fill(stack, base, first, last):
    row = lax.broadcasted_iota(jnp.int32, (SUB, TILE), 0)
    one, two = (pltpu.roll(value, LEAD, 0) for value in first)
    mixed = [jnp.where(row == LEAD, two, one), jnp.where(row < SUB // 2, two, last[0])]
    for k, value in enumerate((one, *mixed, last[1])):
        stack[base + SUB * k : base + SUB * (k + 1), :] = value


def velocity(domain, plain, base):
    for j in range(domain.span):
        at = domain.at(j)
        for k in range(2):
            plain[pl.ds(base + STRIP * k + j, SUB, stride=domain.span), :] = domain.refs[6 + k][at, :]


def density(domain, plain, base, out, place):
    w0, w1 = domain.refs[6:8]
    for j in range(domain.span):
        at = domain.at(j)
        v0, v1 = (plain[pl.ds(base + STRIP * k + j, SUB, stride=domain.span), :] for k in range(2))
        value = -domain.source(FRIC, j) * (w0[at, :] * v0 + w1[at, :] * v1)
        out[pl.ds(place + j, SUB, stride=domain.span), :] = value


def beside():
    lane = lanes()
    return (lane < NEAR) | (lane >= TILE - FAR)


def ends(second):
    row = lax.broadcasted_iota(jnp.int32, (SUB, TILE), 0)
    return row >= SUB - FAR if second else row < NEAR


def adjoint_kernel(
    row_b, row_a, visc, fric, driv, mask, obs, n2, n4, c, i, v0, v1, basis_p, basis_q, edge, turned,
    vel, wide, sides, seams,
    stack, plain, dens, total, *refs,
):
    rows = visc.shape[0]
    span = rows // SUB
    even = is_even(ROW_AXES)
    field = field_of(visc, fric, driv, mask, obs)
    for a in range(ARRAYS):
        at = slice(HALO * a, HALO * (a + 1))
        got_a, got_b = row_a[at, :], row_b[at, :]
        base = STRIP * a
        first = [field(a, slice(at, at + SUB)) for at in (0, SUB)]
        last = [field(a, slice(at, at + SUB)) for at in (rows - 2 * SUB, rows - SUB)]
        fill(stack, base, first, last)
        stack[base : base + LEAD, :] = jnp.where(even, got_b, got_a)[HALO - LEAD :]
        stack[base + STRIP - HALO : base + STRIP, :] = jnp.where(even, got_a, got_b)
    strips = Domain(refs[:FIELDS], 0, STRIP // SUB, strided(stack, 0), lambda: visc[rows - KEPT - 1 : rows - KEPT, :])
    strips.prepare(False)
    run([strips])
    velocity(strips, plain, 0)
    for k in range(2):
        for e in range(2):
            out = HALO * (2 * k + e)
            vel[out : out + HALO, :] = plain[STRIP * k + OUTER[e] : STRIP * k + OUTER[e] + HALO, :]
    interior = Domain(
        (n2, n4, c, i, *refs[FIELDS:]), 0, span, lambda a, j: field(a, pl.ds(j, SUB, stride=span))
    )
    strips.retarget(False)
    interior.retarget(False, (v0, v1))
    run([interior, strips])
    w0, w1 = interior.refs[6:8]
    for j in range(span):
        at = interior.at(j)
        value = -interior.source(FRIC, j) * (w0[at, :] * v0[at, :] + w1[at, :] * v1[at, :])
        dens[pl.ds(j, SUB, stride=span), :] = value
    density(strips, plain, 0, dens, rows)

    side = beside()
    for s in range(0, TILE, SUB):
        summed = jnp.zeros((SUB, TILE), F32)
        for row in range(s, rows, TILE):
            value = dens[row : row + SUB, :]
            if row in (0, rows - SUB):
                at = rows + OUTER[row > 0]
                value = jnp.where(ends(row > 0), dens[at : at + SUB, :], value)
            summed += value
        total[s : s + SUB, :] = jnp.where(side, 0.0, summed)
    exact = dict(precision=lax.Precision.HIGHEST, preferred_element_type=F32)
    half = jnp.dot(basis_p[...], total[...], **exact)
    wide[...] = jnp.dot(half, basis_q[...], **exact)

    corner = corners()
    for part in range(PARTS):
        for a in range(ARRAYS):
            columns = []
            for r in range(0, SLOT, SUB):
                value = edge[slot(part, a) + r : slot(part, a) + r + SUB, :]
                if part == 2:
                    moved = pltpu.roll(turned[r : r + SUB, :], (UPPER - HALO * a) % TILE, 1)
                    value = jnp.where(corner, moved, value)
                columns.append(value)
            fill(sides, strip(part, a), columns[2:], columns[:2])
            if a == VISC:
                seams[SUB * part : SUB * (part + 1), :] = columns[0]


def strip(part, a):
    return STRIP * (ARRAYS * part + a)


def corners():
    lane = lanes()
    above = (lane >= UPPER) & (lane < UPPER + HALO)
    return above | ((lane >= LOWER + INNER + HALO) & (lane < LOWER + SLOT))


def left_right_kernel(
    _, seams, col_b, col_a, wide_in, block, basis_rows, basis_cols,
    stack, strips, coef,
    plain, *refs,
):
    even = is_even(COL_AXES)
    lane = lanes()
    row = lax.broadcasted_iota(jnp.int32, (SUB, TILE), 0)
    upper = (lane >= UPPER + HALO) & (lane < UPPER + SLOT)
    lower = (lane >= LOWER) & (lane < LOWER + INNER + HALO)
    seam_t0 = lane >= TILE - INNER - HALO
    seam_t1 = lane < INNER + HALO
    corner = corners()
    for from_left in (True, False):
        groups = []
        for g in range(2 * GROUPS + 1):
            got_a, got_b = col_a[HALO * g : HALO * (g + 1), :], col_b[HALO * g : HALO * (g + 1), :]
            groups.append(jnp.where(even, got_b, got_a) if from_left else jnp.where(even, got_a, got_b))
        tiles = []
        for part in range(2):
            tile = groups[GROUPS * part : GROUPS * (part + 1)]
            for k in range(2):
                g, h = tile[1 + 2 * k], tile[2 + 2 * k]
                if from_left:
                    tile.append(jnp.where(row >= 5, pltpu.roll(g, 6, 0), pltpu.roll(h, 4, 0)))
                else:
                    tile.append(jnp.where(row < 2, pltpu.roll(g, 2, 0), pltpu.roll(h, 4, 0)))
            tiles.append(tile)
        for a in range(ARRAYS):
            t0, t1 = tiles[0][a], tiles[1][a]
            third = jnp.where(corner, pltpu.roll(groups[-1], (UPPER - HALO * a) % TILE, 1), 0.0)
            third = jnp.where(upper, pltpu.roll(t0, UPPER + HALO, 1), third)
            third = jnp.where(lower, pltpu.roll(t1, LOWER + INNER + HALO, 1), third)
            third = jnp.where(seam_t0, t0, jnp.where(seam_t1, t1, third))
            for part, value in enumerate((t0, t1, third)):
                base = strip(part, a)
                if from_left:
                    stack[base : base + LEAD, :] = value[:LEAD]
                else:
                    stack[base + STRIP - HALO : base + STRIP, :] = value
    last = INNER - KEPT - 1
    before = [lambda at=SUB * part + last: seams[at : at + 1, :] for part in range(PARTS)]
    domains = [
        Domain(refs, STRIP * part, STRIP // SUB, strided(stack, strip(part, 0)), seam)
        for part, seam in enumerate(before)
    ]
    for domain in domains:
        domain.prepare(True)
    run(domains)
    for part, domain in enumerate(domains):
        velocity(domain, strips, 2 * STRIP * part)
        domain.retarget(True)
    run(domains)
    for part, domain in enumerate(domains):
        density(domain, strips, 2 * STRIP * part, plain, STRIP * part)

    def side(part):
        base = STRIP * part
        return jnp.concatenate(
            [plain[base + at : base + at + HALO, :] for at in OUTER], axis=0
        )

    lane = lax.broadcasted_iota(jnp.int32, (2 * HALO, TILE), 1)
    row = lax.broadcasted_iota(jnp.int32, (2 * HALO, TILE), 0)
    right = (row < NEAR) | (row >= 2 * HALO - FAR)
    straight = (lane >= HALO) & (lane < TILE - HALO)
    seam = (lane < HALO) | (lane >= TILE - HALO)
    top = (lane >= UPPER + HALO) & (lane < UPPER + 2 * HALO)
    bottom = (lane >= LOWER + INNER) & (lane < LOWER + INNER + HALO)
    dens = jnp.concatenate(
        [
            jnp.where(right & straight, side(0) + side(1), 0.0),
            jnp.where(right & (seam | top | bottom), side(2), 0.0),
        ],
        axis=1,
    )
    exact = dict(precision=lax.Precision.HIGHEST, preferred_element_type=F32)
    half = jnp.dot(dens, basis_rows[...], **exact)
    wide = wide_in[...] + lax.dot_general(half, basis_cols[...], (((0,), (0,)), ((), ())), **exact)
    lane = lanes()
    which = lax.div(lane, MODES)
    flat = wide[:SUB]
    for j in range(1, MODES // SUB):
        flat = jnp.where(which == j, wide[SUB * j : SUB * (j + 1)], flat)
    mark = jnp.broadcast_to(block[:1, :].astype(F32), (SUB, TILE))
    row = lax.broadcasted_iota(jnp.int32, (SUB, TILE), 0)
    moved = [flat] + [pltpu.roll(flat, r, 0) for r in range(1, SUB)] + [flat]
    lines = [flat] + [
        jnp.where(row < r - 1, moved[r - 1], jnp.where(row == r - 1, mark, moved[r])) for r in range(1, SUB + 1)
    ]
    cycle = SUB * (SUB + 1)
    chunk = min(4, coef.shape[0] // cycle)

    def spread(d, carry):
        for e in range(chunk):
            for r, line in enumerate(lines):
                coef[pl.ds(pl.multiple_of((d * chunk + e) * cycle + SUB * r, SUB), SUB), :] = line
        return carry

    lax.fori_loop(0, coef.shape[0] // cycle // chunk, spread, 0)


def join_kernel(v0, v1, vel_ends, strips, vel, turned):
    rows = vel.shape[1]
    span = rows // SUB
    middle = jnp.zeros((TILE - 2 * HALO, TILE), F32)
    side = beside()
    for k, v in enumerate((v0, v1)):
        for part in range(PARTS):
            base = STRIP * (2 * part + 1 - k)
            first, last = (strips[base + at : base + at + HALO, :] for at in OUTER)
            at = TILE * (2 * part + k)
            turned[at : at + TILE, :] = jnp.concatenate([first, middle, last], axis=0).T
        for row in range(0, rows, SUB):
            value = v[pl.ds(SUB * (row % span) + row // span, SUB, stride=SUB), :]
            if row in (0, rows - SUB):
                at = HALO * (2 * k + (row > 0))
                value = jnp.where(ends(row > 0), vel_ends[at : at + HALO, :], value)
            part, lane = right_part(row)
            at = TILE * (2 * part + k) + lane
            vel[k, row : row + SUB, :] = jnp.where(side, turned[at : at + SUB, :], value)


def bases():
    places = np.arange(TILE) + 0.5
    basis = np.cos(math.pi * places[:, None] * np.arange(MODES)[None, :] / TILE)
    groups = MODES // SUB
    order = np.arange(MODES).reshape(SUB, groups).T.reshape(-1)
    rows = basis[:, order] / TILE
    cols = np.tile(basis, (1, groups))
    placed = np.zeros((2 * TILE, MODES))
    for row in range(0, 2 * TILE, SUB):
        part, lane = right_part(row)
        at = lane + (TILE if part == 2 else 0)
        placed[at : at + SUB] = rows[row % TILE : row % TILE + SUB]
    outer = np.concatenate([cols[:HALO], cols[TILE - HALO :]])
    return [jnp.asarray(x, F32) for x in (rows.T, cols, placed, outer)]


def pick_kernel(owners, every, out):
    mine = out.shape[1]
    own = lax.axis_index("own")
    wanted = [owners[pl.ds(own, 1), k : k + 1].astype(F32) for k in range(mine)]
    lines = SUB + 1
    devices = every.shape[0] // lines
    chunk = min(4, devices // SUB)

    def body(d, sums):
        sums = list(sums)
        for e in range(chunk):
            base = (d * chunk + e) * SUB * lines
            mark = every[pl.ds(base + SUB, SUB, stride=lines), :]
            hits = [mark == wanted[k] for k in range(mine)]
            for r in range(SUB):
                part = every[pl.ds(base + r, SUB, stride=lines), :]
                for k in range(mine):
                    sums[SUB * k + r] += jnp.where(hits[k], part, 0.0)
        return tuple(sums)

    start = (jnp.zeros((SUB, TILE), F32),) * (mine * SUB)
    sums = lax.fori_loop(0, devices // SUB // chunk, body, start)
    for k in range(mine):
        for r in range(SUB):
            total = jnp.sum(sums[SUB * k + r], axis=0, keepdims=True)
            out[0, k : k + 1, TILE * r : TILE * (r + 1)] = total


def local(viscosity, friction, driving, observed, ice_mask, tile_block, owner_list):
    rows, cols = viscosity.shape
    assert (rows, cols) == (2 * TILE, TILE)
    inputs = (viscosity, friction, driving, ice_mask, observed)
    near = [pltpu.with_memory_space_constraint(x, pltpu.VMEM) for x in inputs]
    basis_p, basis_q, basis_rows, basis_cols = bases()
    to_b, to_a = call(
        ends_kernel,
        "ends",
        (vmem(EDGE, cols), vmem(EDGE, cols)),
        [
            vmem(2, 2, HALO, cols),
            vmem(2, 2, 2, HALO, cols),
            pltpu.VMEM((2, HALO, cols), jnp.int32),
            pltpu.SemaphoreType.DMA((2, 5)),
        ],
        10**6,
        *(pltpu.with_memory_space_constraint(x, pltpu.HBM) for x in inputs),
    )
    row_b = swap(to_b, 0, 1)
    row_a = swap(to_a, 0, 0)
    edge, *forward = call(
        interior_kernel,
        "interior",
        (vmem(2 * PARTS * TILE, TILE),) + (vmem(rows, cols),) * 6,
        [vmem(rows, cols)] * (FIELDS - 6),
        8 * 10**6,
        *near,
    )
    to_b, to_a, turned = call(
        columns_kernel,
        "columns",
        (vmem(SENT, TILE), vmem(SENT, TILE), vmem(SLOT, TILE)),
        [],
        10**5,
        row_b,
        row_a,
        edge,
    )
    col_b = swap(to_b, 1, 1)
    col_a = swap(to_a, 1, 0)
    vel_ends, wide, sides, seams = call(
        adjoint_kernel,
        "adjoint",
        (
            vmem(4 * HALO, cols),
            vmem(MODES, TILE),
            vmem(PARTS * ARRAYS * STRIP, TILE),
            vmem(PARTS * SUB, TILE),
        ),
        [vmem(ARRAYS * STRIP, cols), vmem(2 * STRIP, cols), vmem(rows + STRIP, cols), vmem(TILE, cols)]
        + [vmem(STRIP, cols)] * FIELDS
        + [vmem(rows, cols)] * (FIELDS - 4),
        8 * 10**6,
        row_b,
        row_a,
        *near,
        *forward,
        basis_p,
        basis_q,
        edge,
        turned,
    )
    devices = lax.axis_size(ROW_AXES + COL_AXES)
    _, strips, coef = call(
        left_right_kernel,
        "left_right",
        (
            vmem(PARTS * ARRAYS * STRIP, TILE),
            vmem(PARTS * 2 * STRIP, TILE),
            vmem(devices * (SUB + 1), TILE),
        ),
        [vmem(PARTS * STRIP, TILE)] * (FIELDS + 1),
        4 * 10**6,
        sides,
        seams,
        col_b,
        col_a,
        wide,
        tile_block,
        basis_rows,
        basis_cols,
        aliases={0: 0},
    )
    coef = coef.reshape(devices, 1, (SUB + 1) * TILE)
    parts = lax.all_to_all(coef, ROW_AXES + COL_AXES, 0, 0, tiled=True)
    state = call(
        join_kernel,
        "join",
        jax.ShapeDtypeStruct((2, rows, cols), F32),
        [vmem(2 * PARTS * TILE, TILE)],
        4 * 10**6,
        *forward[4:],
        vel_ends,
        strips,
    )
    owners = owner_list.reshape(lax.axis_size("own"), -1)
    picked = call(
        pick_kernel,
        "pick",
        jax.ShapeDtypeStruct((1, owners.shape[1], MODES * MODES), F32),
        [],
        10**5,
        owners,
        parts.reshape(-1, TILE),
    )
    return (state, picked)


def solution(mesh):
    return jax.shard_map(
        local,
        mesh=mesh,
        in_specs=(
            P(("row", "own"), "col"),
            P(("row", "own"), "col"),
            P(None, ("row", "own"), "col"),
            P(None, ("row", "own"), "col"),
            P(("row", "own"), "col"),
            P(("row", "own"), "col"),
            P(),
        ),
        out_specs=(P(None, ("row", "own"), "col"), P("own", None, None)),
        check_vma=False,
    )
```

```python
import math

import jax
import jax.numpy as jnp
import numpy as np
from jax import lax
from jax.experimental import pallas as pl
from jax.experimental.pallas import tpu as pltpu
from jax.sharding import PartitionSpec as P

TILE = 128
MODES = 32
SWEEPS = 3
SUB = 8
HALO = 8
INNER = 2 * HALO
STRIP = 40
LEAD = HALO - 1
KEPT = 12
OUTER = (LEAD, STRIP - 2 * HALO)
NEAR, FAR = 7, 6
ARRAYS = 7
VISC, FRIC, DRIV, MASK, OBS = 0, 1, 2, 4, 5
EDGE = ARRAYS * HALO
SLOT = 2 * INNER
PER = TILE // SLOT
GROUPS = 5
SENT = 2 * GROUPS * HALO + HALO
PARTS = 3
UPPER, LOWER = 32, 64
ROW_AXES = ("row", "own")
COL_AXES = ("col",)
F32 = jnp.float32
LIMIT = 40 * 1024 * 1024


def swap(x, axis, first):
    sizes = lax.axis_size(ROW_AXES), lax.axis_size(COL_AXES)
    owners = lax.axis_size("own")

    def device(i, j):
        return (i // owners * sizes[1] + j) * owners + i % owners

    pairs = []
    for i in range(sizes[0]):
        for j in range(sizes[1]):
            place = [i, j]
            if first and place[axis] in (0, sizes[axis] - 1):
                place[1 - axis] ^= 1
            else:
                place[axis] = ((place[axis] + first) ^ 1) - first
            pairs.append((device(i, j), device(*place)))
    return lax.ppermute(x, ("row", "col", "own"), pairs)


def position(axes):
    index, size = 0, 1
    for axis in axes:
        index = index * lax.axis_size(axis) + lax.axis_index(axis)
        size *= lax.axis_size(axis)
    assert size % 2 == 0
    return lax.rem(index, 2) == 0, (index == 0) | (index == size - 1)


def is_even(axes):
    return position(axes)[0]


def lanes():
    return lax.broadcasted_iota(jnp.int32, (SUB, TILE), 1)


def call(kernel, name, outs, scratch, cost, *args, aliases={}):
    return pl.pallas_call(
        kernel,
        out_shape=outs,
        scratch_shapes=scratch,
        input_output_aliases=aliases,
        compiler_params=pltpu.CompilerParams(vmem_limit_bytes=LIMIT),
        cost_estimate=pl.CostEstimate(flops=cost, bytes_accessed=cost, transcendentals=0),
        name=name,
    )(*args)


def vmem(*shape):
    return pltpu.VMEM(shape, F32)


FIELDS = 14
STRIP_FIELDS = 24


class Domain:
    def __init__(self, refs, base, span, source, seam=None):
        self.refs, self.base, self.span, self.source, self.seam = refs, base, span, source, seam

    def at(self, j):
        return pl.ds(self.base + SUB * j, SUB)

    def prepare(self, flipped):
        n2, n4, c, i, b0, b1 = self.refs[:6]
        visc = [self.source(VISC, j) for j in range(self.span)]
        for j in range(self.span):
            at = self.at(j)
            before = visc[j - 1] if j else pltpu.roll(visc[-1], 1, 0)
            if self.seam and not j:
                row = lax.broadcasted_iota(jnp.int32, (SUB, TILE), 0)
                before = jnp.where(row == SUB // 2, self.seam(), before)
            pair = visc[j] + before
            fric = self.source(FRIC, j)
            diag = 1.25 * (pair + pltpu.roll(pair, 1, 1)) + fric
            on = self.source(MASK, j) > 0.0
            inv = jnp.where(on, 0.5 / jnp.where(on, diag, 1.0), 0.0)
            half = 0.5 * visc[j]
            n2[at, :] = half
            n4[at, :] = 0.5 * half
            c[at, :] = 1.0 - fric * inv
            i[at, :] = inv
            for k, b in enumerate((b0, b1)):
                value = inv * self.source(DRIV + (1 - k if flipped else k), j)
                b[at, :] = value
                self.write(k, at, value + value)

    def write(self, k, at, value):
        self.refs[6 + k][at, :] = value
        self.refs[8 + k][at, :] = pltpu.roll(value, TILE - 1, 1)

    def retarget(self, flipped, velocity=None):
        i, b0, b1 = self.refs[3:6]
        w0, w1 = velocity or self.refs[6:8]
        for j in range(self.span):
            at = self.at(j)
            for k, (b, w) in enumerate(((b0, w0), (b1, w1))):
                value = i[at, :] * (w[at, :] - self.source(OBS + (1 - k if flipped else k), j))
                b[at, :] = value
                self.write(k, at, value + value)

    def differences(self):
        n2, n4 = self.refs[:2]
        fields = self.refs[6:10]
        parts = self.refs[10:14]

        def corners(j, here, below):
            w0, w1, r0, r1 = here
            v0, v1, s0, s1 = below
            a1, a2 = s0 - w0, v0 - r0
            e1, e2 = s1 - w1, v1 - r1
            x, y = a1 + a2, e1 - e2
            q = (a1 - a2) + (e1 + e2)
            both = x + y
            at = self.at(j)
            half = n2[at, :]
            return half * (both + x), n4[at, :] * q, half * (both + y)

        def load(j):
            at = self.at(j)
            return [field[at, :] for field in fields]

        top = load(0)
        last = corners(self.span - 1, load(self.span - 1), [pltpu.roll(v, SUB - 1, 0) for v in top])
        up = [pltpu.roll(v, 1, 0) for v in last]
        here = top
        for j in range(self.span):
            at = self.at(j)
            if j < self.span - 1:
                below = load(j + 1)
                p, q, r = corners(j, here, below)
                here = below
            else:
                p, q, r = last
            g, t = up[0] - p, up[1] + q
            gq, tr = up[1] - q, up[2] + r
            parts[0][at, :] = g - t
            parts[1][at, :] = gq - tr
            parts[2][at, :] = pltpu.roll(g + t, 1, 1)
            parts[3][at, :] = pltpu.roll(gq + tr, 1, 1)
            up = (p, q, r)

    def update(self):
        c, i, b0, b1, w0, w1 = self.refs[2:8]
        parts = self.refs[10:14]
        for j in range(self.span):
            at = self.at(j)
            cv, iv = c[at, :], i[at, :]
            for k, (b, w) in enumerate(((b0, w0), (b1, w1))):
                value = (cv * w[at, :] + b[at, :]) - iv * (parts[k][at, :] + parts[k + 2][at, :])
                self.write(k, at, value)


class Strips(Domain):
    def prepare(self, flipped):
        super().prepare(flipped)
        for j in range(self.span):
            at = self.at(j)
            for now, later in zip(self.refs[2:6], self.refs[10:14]):
                later[at, :] = pltpu.roll(now[at, :], TILE - 1, 1)
        for now, before in zip(self.refs[:2], self.refs[14:16]):
            before[self.at(0), :] = pltpu.roll(now[self.at(self.span - 1), :], 1, 0)

    def retarget(self, flipped, velocity=None):
        super().retarget(flipped, velocity)
        for j in range(self.span):
            at = self.at(j)
            for now, later in zip(self.refs[4:6], self.refs[12:14]):
                later[at, :] = pltpu.roll(now[at, :], TILE - 1, 1)

    def differences(self):
        fields = self.refs[6:10]
        kept, turned, kept_next, turned_next = (self.refs[16 + 2 * k : 18 + 2 * k] for k in range(4))

        def corners(halves, quarters, j, here, below):
            w0, w1, r0, r1 = here
            v0, v1, s0, s1 = below
            a1, a2 = s0 - w0, v0 - r0
            e1, e2 = s1 - w1, v1 - r1
            x, y = a1 + a2, e1 - e2
            q = (a1 - a2) + (e1 + e2)
            both = x + y
            at = self.at(j)
            half = halves[at, :]
            return half * (both + x), quarters[at, :] * q, half * (both + y)

        def load(j):
            at = self.at(j)
            return [field[at, :] for field in fields]

        top, end = load(0), load(self.span - 1)
        up = corners(*self.refs[14:16], 0, [pltpu.roll(v, 1, 0) for v in end], top)
        here = top
        for j in range(self.span):
            at = self.at(j)
            below = load(j + 1) if j < self.span - 1 else [pltpu.roll(v, SUB - 1, 0) for v in top]
            p, q, r = corners(*self.refs[:2], j, here, below)
            g, t = up[0] - p, up[1] + q
            gq, tr = up[1] - q, up[2] + r
            for k, (stay, move) in enumerate(((g - t, g + t), (gq - tr, gq + tr))):
                kept[k][at, :] = stay
                turned_next[k][at, :] = move
                turned[k][at, :] = pltpu.roll(move, 1, 1)
                kept_next[k][at, :] = pltpu.roll(stay, TILE - 1, 1)
            up, here = (p, q, r), below

    def update(self):
        for first, offset, parts in ((2, 6, (16, 18)), (10, 8, (20, 22))):
            c, i, *b = self.refs[first : first + 4]
            for j in range(self.span):
                at = self.at(j)
                cv, iv = c[at, :], i[at, :]
                for k in range(2):
                    w = self.refs[offset + k]
                    change = self.refs[parts[0] + k][at, :] + self.refs[parts[1] + k][at, :]
                    w[at, :] = (cv * w[at, :] + b[k][at, :]) - iv * change


def run(domains):
    def body(_, carry):
        for domain in domains:
            domain.differences()
        for domain in domains:
            domain.update()
        return carry

    lax.fori_loop(0, SWEEPS, body, 0)


def ends_kernel(visc, fric, driv, mask, obs, to_b, to_a, one, two, flags, sems):
    rows = visc.shape[0]
    copies = []
    for e, first in enumerate((0, rows - HALO)):
        at = pl.ds(first, HALO)
        pieces = [
            (visc.at[at], one.at[e, 0]),
            (fric.at[at], one.at[e, 1]),
            (driv.at[:, at], two.at[e, 0]),
            (mask.at[at], flags.at[e]),
            (obs.at[:, at], two.at[e, 1]),
        ]
        for n, (source, place) in enumerate(pieces):
            copies.append(pltpu.make_async_copy(source, place, sems.at[e, n]))
    for copy in copies:
        copy.start()
    for copy in copies:
        copy.wait()
    even, at_end = position(ROW_AXES)

    def edge(e):
        return [one[e, 0], one[e, 1], two[e, 0, 0], two[e, 0, 1], flags[e].astype(F32), two[e, 1, 0], two[e, 1, 1]]

    for a, (head, tail) in enumerate(zip(edge(0), edge(1))):
        at = slice(HALO * a, HALO * (a + 1))
        to_a[at, :] = jnp.where(even, tail, head)
        to_b[at, :] = jnp.where(at_end, 0.0, jnp.where(even, head, tail))


def field_of(visc, fric, driv, mask, obs):
    def field(a, at):
        if a == MASK:
            return mask[at, :].astype(F32)
        if a >= OBS:
            return obs[a - OBS, at, :]
        if a >= DRIV:
            return driv[a - DRIV, at, :]
        return (visc, fric)[a][at, :]

    return field


def first_row(part, lane):
    if part < 2:
        return TILE * part + lane
    if lane < INNER + HALO:
        return TILE + lane
    if lane >= TILE - INNER - HALO:
        return lane
    if UPPER + HALO <= lane < UPPER + SLOT:
        return lane - UPPER - HALO
    if LOWER <= lane < LOWER + INNER + HALO:
        return 2 * TILE - INNER - HALO + lane - LOWER
    return None


def right_part(row):
    seam = TILE - HALO <= row < TILE + HALO
    part = 2 if seam or row == 0 or row == 2 * TILE - HALO else row // TILE
    return part, [lane for lane in range(0, TILE, SUB) if first_row(part, lane) == row][-1]


def slot(part, a):
    return TILE * (2 * part + a // PER) + SLOT * (a % PER)


def interior_kernel(visc, fric, driv, mask, obs, edge, n2, n4, c, i, v0, v1, *refs):
    span = visc.shape[0] // SUB
    field = field_of(visc, fric, driv, mask, obs)
    lane = lanes()
    for part in range(PARTS):
        for m in range(-(-ARRAYS // PER)):
            strips = []
            for at in range(0, TILE, SUB):
                row = first_row(part, at)
                packed = jnp.zeros((SUB, TILE), F32)
                if row is not None:
                    for k in range(min(PER, ARRAYS - PER * m)):
                        value = field(PER * m + k, slice(row, row + SUB))
                        moved = pltpu.roll(value, (SLOT * k + INNER) % TILE, 1)
                        packed = jnp.where(lax.div(lane, SLOT) == k, moved, packed)
                strips.append(packed)
            base = TILE * (2 * part + m)
            edge[base : base + TILE, :] = jnp.concatenate(strips, axis=0).T
    refs = (n2, n4, c, i, *refs[:2], v0, v1, *refs[2:])
    domain = Domain(refs, 0, span, lambda a, j: field(a, pl.ds(j, SUB, stride=span)))
    domain.prepare(False)
    run([domain])


def columns_kernel(row_b, row_a, edge, to_b, to_a, turned):
    even = is_even(ROW_AXES)
    above = jnp.where(even, row_b[...], row_a[...])
    below = jnp.where(even, row_a[...], row_b[...])
    halo = jnp.concatenate([above, below, jnp.zeros((TILE - 2 * EDGE, TILE), F32)], axis=0).T
    turned[:INNER, :] = halo[TILE - INNER :]
    turned[INNER:, :] = halo[:INNER]
    even, at_end = position(COL_AXES)
    row = lax.broadcasted_iota(jnp.int32, (SUB, TILE), 0)

    def put(out, right, left):
        right = pltpu.roll(right, LEAD, 0)
        to_a[out : out + HALO, :] = jnp.where(even, right, left)
        to_b[out : out + HALO, :] = jnp.where(at_end, 0.0, jnp.where(even, left, right))

    for part in range(2):
        right, left = [], []
        for a in range(ARRAYS):
            at = slot(part, a) + INNER
            right.append(edge[at - HALO : at, :])
            left.append(edge[at : at + HALO, :])
        for k in range(2):
            seen_r, seen_l = right[OBS + k], left[OBS + k]
            g = 1 + 2 * k
            right[g] = jnp.where(row < 2, pltpu.roll(seen_r, 2, 0), right[g])
            right[g + 1] = jnp.where(row < 2, pltpu.roll(seen_r, 4, 0), right[g + 1])
            left[g] = jnp.where(row >= 6, pltpu.roll(seen_l, 6, 0), left[g])
            left[g + 1] = jnp.where(row >= 6, pltpu.roll(seen_l, 4, 0), left[g + 1])
        for g in range(GROUPS):
            put(HALO * (GROUPS * part + g), right[g], left[g])
    put(2 * GROUPS * HALO, halo[TILE - HALO :], halo[:HALO])


def strided(stack, base):
    span = STRIP // SUB
    return lambda a, j: stack[pl.ds(base + STRIP * a + j, SUB, stride=span), :]


def fill(stack, base, first, last):
    row = lax.broadcasted_iota(jnp.int32, (SUB, TILE), 0)
    one, two = (pltpu.roll(value, LEAD, 0) for value in first)
    mixed = [jnp.where(row == LEAD, two, one), jnp.where(row < SUB // 2, two, last[0])]
    for k, value in enumerate((one, *mixed, last[1])):
        stack[base + SUB * k : base + SUB * (k + 1), :] = value


def velocity(domain, plain, base):
    for j in range(domain.span):
        at = domain.at(j)
        for k in range(2):
            plain[pl.ds(base + STRIP * k + j, SUB, stride=domain.span), :] = domain.refs[6 + k][at, :]


def density(domain, plain, base, out, place):
    w0, w1 = domain.refs[6:8]
    for j in range(domain.span):
        at = domain.at(j)
        v0, v1 = (plain[pl.ds(base + STRIP * k + j, SUB, stride=domain.span), :] for k in range(2))
        value = -domain.source(FRIC, j) * (w0[at, :] * v0 + w1[at, :] * v1)
        out[pl.ds(place + j, SUB, stride=domain.span), :] = value


def beside():
    lane = lanes()
    return (lane < NEAR) | (lane >= TILE - FAR)


def ends(second):
    row = lax.broadcasted_iota(jnp.int32, (SUB, TILE), 0)
    return row >= SUB - FAR if second else row < NEAR


def adjoint_kernel(
    row_b, row_a, visc, fric, driv, mask, obs, n2, n4, c, i, v0, v1, basis_p, basis_q, edge, turned,
    vel, wide, sides, seams,
    stack, plain, dens, total, *refs,
):
    rows = visc.shape[0]
    span = rows // SUB
    even = is_even(ROW_AXES)
    field = field_of(visc, fric, driv, mask, obs)
    for a in range(ARRAYS):
        at = slice(HALO * a, HALO * (a + 1))
        got_a, got_b = row_a[at, :], row_b[at, :]
        base = STRIP * a
        first = [field(a, slice(at, at + SUB)) for at in (0, SUB)]
        last = [field(a, slice(at, at + SUB)) for at in (rows - 2 * SUB, rows - SUB)]
        fill(stack, base, first, last)
        stack[base : base + LEAD, :] = jnp.where(even, got_b, got_a)[HALO - LEAD :]
        stack[base + STRIP - HALO : base + STRIP, :] = jnp.where(even, got_a, got_b)
    strips = Strips(refs[:STRIP_FIELDS], 0, STRIP // SUB, strided(stack, 0), lambda: visc[rows - KEPT - 1 : rows - KEPT, :])
    strips.prepare(False)
    run([strips])
    velocity(strips, plain, 0)
    for k in range(2):
        for e in range(2):
            out = HALO * (2 * k + e)
            vel[out : out + HALO, :] = plain[STRIP * k + OUTER[e] : STRIP * k + OUTER[e] + HALO, :]
    interior = Domain(
        (n2, n4, c, i, *refs[STRIP_FIELDS:]), 0, span, lambda a, j: field(a, pl.ds(j, SUB, stride=span))
    )
    strips.retarget(False)
    interior.retarget(False, (v0, v1))
    run([interior, strips])
    w0, w1 = interior.refs[6:8]
    for j in range(span):
        at = interior.at(j)
        value = -interior.source(FRIC, j) * (w0[at, :] * v0[at, :] + w1[at, :] * v1[at, :])
        dens[pl.ds(j, SUB, stride=span), :] = value
    density(strips, plain, 0, dens, rows)

    side = beside()
    for s in range(0, TILE, SUB):
        summed = jnp.zeros((SUB, TILE), F32)
        for row in range(s, rows, TILE):
            value = dens[row : row + SUB, :]
            if row in (0, rows - SUB):
                at = rows + OUTER[row > 0]
                value = jnp.where(ends(row > 0), dens[at : at + SUB, :], value)
            summed += value
        total[s : s + SUB, :] = jnp.where(side, 0.0, summed)
    exact = dict(precision=lax.Precision.HIGHEST, preferred_element_type=F32)
    half = jnp.dot(basis_p[...], total[...], **exact)
    wide[...] = jnp.dot(half, basis_q[...], **exact)

    corner = corners()
    for part in range(PARTS):
        for a in range(ARRAYS):
            columns = []
            for r in range(0, SLOT, SUB):
                value = edge[slot(part, a) + r : slot(part, a) + r + SUB, :]
                if part == 2:
                    moved = pltpu.roll(turned[r : r + SUB, :], (UPPER - HALO * a) % TILE, 1)
                    value = jnp.where(corner, moved, value)
                columns.append(value)
            fill(sides, strip(part, a), columns[2:], columns[:2])
            if a == VISC:
                seams[SUB * part : SUB * (part + 1), :] = columns[0]


def strip(part, a):
    return STRIP * (ARRAYS * part + a)


def corners():
    lane = lanes()
    above = (lane >= UPPER) & (lane < UPPER + HALO)
    return above | ((lane >= LOWER + INNER + HALO) & (lane < LOWER + SLOT))


def left_right_kernel(
    _, seams, col_b, col_a, wide_in, block, basis_rows, basis_cols,
    stack, strips, coef,
    plain, *refs,
):
    even = is_even(COL_AXES)
    lane = lanes()
    row = lax.broadcasted_iota(jnp.int32, (SUB, TILE), 0)
    upper = (lane >= UPPER + HALO) & (lane < UPPER + SLOT)
    lower = (lane >= LOWER) & (lane < LOWER + INNER + HALO)
    seam_t0 = lane >= TILE - INNER - HALO
    seam_t1 = lane < INNER + HALO
    corner = corners()
    for from_left in (True, False):
        groups = []
        for g in range(2 * GROUPS + 1):
            got_a, got_b = col_a[HALO * g : HALO * (g + 1), :], col_b[HALO * g : HALO * (g + 1), :]
            groups.append(jnp.where(even, got_b, got_a) if from_left else jnp.where(even, got_a, got_b))
        tiles = []
        for part in range(2):
            tile = groups[GROUPS * part : GROUPS * (part + 1)]
            for k in range(2):
                g, h = tile[1 + 2 * k], tile[2 + 2 * k]
                if from_left:
                    tile.append(jnp.where(row >= 5, pltpu.roll(g, 6, 0), pltpu.roll(h, 4, 0)))
                else:
                    tile.append(jnp.where(row < 2, pltpu.roll(g, 2, 0), pltpu.roll(h, 4, 0)))
            tiles.append(tile)
        for a in range(ARRAYS):
            t0, t1 = tiles[0][a], tiles[1][a]
            third = jnp.where(corner, pltpu.roll(groups[-1], (UPPER - HALO * a) % TILE, 1), 0.0)
            third = jnp.where(upper, pltpu.roll(t0, UPPER + HALO, 1), third)
            third = jnp.where(lower, pltpu.roll(t1, LOWER + INNER + HALO, 1), third)
            third = jnp.where(seam_t0, t0, jnp.where(seam_t1, t1, third))
            for part, value in enumerate((t0, t1, third)):
                base = strip(part, a)
                if from_left:
                    stack[base : base + LEAD, :] = value[:LEAD]
                else:
                    stack[base + STRIP - HALO : base + STRIP, :] = value
    last = INNER - KEPT - 1
    before = [lambda at=SUB * part + last: seams[at : at + 1, :] for part in range(PARTS)]
    domains = [
        Strips(refs, STRIP * part, STRIP // SUB, strided(stack, strip(part, 0)), seam)
        for part, seam in enumerate(before)
    ]
    for domain in domains:
        domain.prepare(True)
    run(domains)
    for part, domain in enumerate(domains):
        velocity(domain, strips, 2 * STRIP * part)
        domain.retarget(True)
    run(domains)
    for part, domain in enumerate(domains):
        density(domain, strips, 2 * STRIP * part, plain, STRIP * part)

    def side(part):
        base = STRIP * part
        return jnp.concatenate(
            [plain[base + at : base + at + HALO, :] for at in OUTER], axis=0
        )

    lane = lax.broadcasted_iota(jnp.int32, (2 * HALO, TILE), 1)
    row = lax.broadcasted_iota(jnp.int32, (2 * HALO, TILE), 0)
    right = (row < NEAR) | (row >= 2 * HALO - FAR)
    straight = (lane >= HALO) & (lane < TILE - HALO)
    seam = (lane < HALO) | (lane >= TILE - HALO)
    top = (lane >= UPPER + HALO) & (lane < UPPER + 2 * HALO)
    bottom = (lane >= LOWER + INNER) & (lane < LOWER + INNER + HALO)
    dens = jnp.concatenate(
        [
            jnp.where(right & straight, side(0) + side(1), 0.0),
            jnp.where(right & (seam | top | bottom), side(2), 0.0),
        ],
        axis=1,
    )
    exact = dict(precision=lax.Precision.HIGHEST, preferred_element_type=F32)
    half = jnp.dot(dens, basis_rows[...], **exact)
    wide = wide_in[...] + lax.dot_general(half, basis_cols[...], (((0,), (0,)), ((), ())), **exact)
    lane = lanes()
    which = lax.div(lane, MODES)
    flat = wide[:SUB]
    for j in range(1, MODES // SUB):
        flat = jnp.where(which == j, wide[SUB * j : SUB * (j + 1)], flat)
    mark = jnp.broadcast_to(block[:1, :].astype(F32), (SUB, TILE))
    row = lax.broadcasted_iota(jnp.int32, (SUB, TILE), 0)
    moved = [flat] + [pltpu.roll(flat, r, 0) for r in range(1, SUB)] + [flat]
    lines = [flat] + [
        jnp.where(row < r - 1, moved[r - 1], jnp.where(row == r - 1, mark, moved[r])) for r in range(1, SUB + 1)
    ]
    cycle = SUB * (SUB + 1)
    chunk = min(4, coef.shape[0] // cycle)

    def spread(d, carry):
        for e in range(chunk):
            for r, line in enumerate(lines):
                coef[pl.ds(pl.multiple_of((d * chunk + e) * cycle + SUB * r, SUB), SUB), :] = line
        return carry

    lax.fori_loop(0, coef.shape[0] // cycle // chunk, spread, 0)


def join_kernel(v0, v1, vel_ends, strips, vel, turned):
    rows = vel.shape[1]
    span = rows // SUB
    middle = jnp.zeros((TILE - 2 * HALO, TILE), F32)
    side = beside()
    for k, v in enumerate((v0, v1)):
        for part in range(PARTS):
            base = STRIP * (2 * part + 1 - k)
            first, last = (strips[base + at : base + at + HALO, :] for at in OUTER)
            at = TILE * (2 * part + k)
            turned[at : at + TILE, :] = jnp.concatenate([first, middle, last], axis=0).T
        for row in range(0, rows, SUB):
            value = v[pl.ds(SUB * (row % span) + row // span, SUB, stride=SUB), :]
            if row in (0, rows - SUB):
                at = HALO * (2 * k + (row > 0))
                value = jnp.where(ends(row > 0), vel_ends[at : at + HALO, :], value)
            part, lane = right_part(row)
            at = TILE * (2 * part + k) + lane
            vel[k, row : row + SUB, :] = jnp.where(side, turned[at : at + SUB, :], value)


def bases():
    places = np.arange(TILE) + 0.5
    basis = np.cos(math.pi * places[:, None] * np.arange(MODES)[None, :] / TILE)
    groups = MODES // SUB
    order = np.arange(MODES).reshape(SUB, groups).T.reshape(-1)
    rows = basis[:, order] / TILE
    cols = np.tile(basis, (1, groups))
    placed = np.zeros((2 * TILE, MODES))
    for row in range(0, 2 * TILE, SUB):
        part, lane = right_part(row)
        at = lane + (TILE if part == 2 else 0)
        placed[at : at + SUB] = rows[row % TILE : row % TILE + SUB]
    outer = np.concatenate([cols[:HALO], cols[TILE - HALO :]])
    return [jnp.asarray(x, F32) for x in (rows.T, cols, placed, outer)]


def pick_kernel(owners, every, out):
    mine = out.shape[1]
    own = lax.axis_index("own")
    wanted = [owners[pl.ds(own, 1), k : k + 1].astype(F32) for k in range(mine)]
    lines = SUB + 1
    devices = every.shape[0] // lines
    chunk = min(4, devices // SUB)

    def body(d, sums):
        sums = list(sums)
        for e in range(chunk):
            base = (d * chunk + e) * SUB * lines
            mark = every[pl.ds(base + SUB, SUB, stride=lines), :]
            hits = [mark == wanted[k] for k in range(mine)]
            for r in range(SUB):
                part = every[pl.ds(base + r, SUB, stride=lines), :]
                for k in range(mine):
                    sums[SUB * k + r] += jnp.where(hits[k], part, 0.0)
        return tuple(sums)

    start = (jnp.zeros((SUB, TILE), F32),) * (mine * SUB)
    sums = lax.fori_loop(0, devices // SUB // chunk, body, start)
    for k in range(mine):
        for r in range(SUB):
            total = jnp.sum(sums[SUB * k + r], axis=0, keepdims=True)
            out[0, k : k + 1, TILE * r : TILE * (r + 1)] = total


def local(viscosity, friction, driving, observed, ice_mask, tile_block, owner_list):
    rows, cols = viscosity.shape
    assert (rows, cols) == (2 * TILE, TILE)
    inputs = (viscosity, friction, driving, ice_mask, observed)
    near = [pltpu.with_memory_space_constraint(x, pltpu.VMEM) for x in inputs]
    basis_p, basis_q, basis_rows, basis_cols = bases()
    to_b, to_a = call(
        ends_kernel,
        "ends",
        (vmem(EDGE, cols), vmem(EDGE, cols)),
        [
            vmem(2, 2, HALO, cols),
            vmem(2, 2, 2, HALO, cols),
            pltpu.VMEM((2, HALO, cols), jnp.int32),
            pltpu.SemaphoreType.DMA((2, 5)),
        ],
        10**6,
        *(pltpu.with_memory_space_constraint(x, pltpu.HBM) for x in inputs),
    )
    row_b = swap(to_b, 0, 1)
    row_a = swap(to_a, 0, 0)
    edge, *forward = call(
        interior_kernel,
        "interior",
        (vmem(2 * PARTS * TILE, TILE),) + (vmem(rows, cols),) * 6,
        [vmem(rows, cols)] * (FIELDS - 6),
        8 * 10**6,
        *near,
    )
    to_b, to_a, turned = call(
        columns_kernel,
        "columns",
        (vmem(SENT, TILE), vmem(SENT, TILE), vmem(SLOT, TILE)),
        [],
        10**5,
        row_b,
        row_a,
        edge,
    )
    col_b = swap(to_b, 1, 1)
    col_a = swap(to_a, 1, 0)
    vel_ends, wide, sides, seams = call(
        adjoint_kernel,
        "adjoint",
        (
            vmem(4 * HALO, cols),
            vmem(MODES, TILE),
            vmem(PARTS * ARRAYS * STRIP, TILE),
            vmem(PARTS * SUB, TILE),
        ),
        [vmem(ARRAYS * STRIP, cols), vmem(2 * STRIP, cols), vmem(rows + STRIP, cols), vmem(TILE, cols)]
        + [vmem(STRIP, cols)] * STRIP_FIELDS
        + [vmem(rows, cols)] * (FIELDS - 4),
        8 * 10**6,
        row_b,
        row_a,
        *near,
        *forward,
        basis_p,
        basis_q,
        edge,
        turned,
    )
    devices = lax.axis_size(ROW_AXES + COL_AXES)
    _, strips, coef = call(
        left_right_kernel,
        "left_right",
        (
            vmem(PARTS * ARRAYS * STRIP, TILE),
            vmem(PARTS * 2 * STRIP, TILE),
            vmem(devices * (SUB + 1), TILE),
        ),
        [vmem(PARTS * STRIP, TILE)] * (STRIP_FIELDS + 1),
        4 * 10**6,
        sides,
        seams,
        col_b,
        col_a,
        wide,
        tile_block,
        basis_rows,
        basis_cols,
        aliases={0: 0},
    )
    coef = coef.reshape(devices, 1, (SUB + 1) * TILE)
    parts = lax.all_to_all(coef, ROW_AXES + COL_AXES, 0, 0, tiled=True)
    state = call(
        join_kernel,
        "join",
        jax.ShapeDtypeStruct((2, rows, cols), F32),
        [vmem(2 * PARTS * TILE, TILE)],
        4 * 10**6,
        *forward[4:],
        vel_ends,
        strips,
    )
    owners = owner_list.reshape(lax.axis_size("own"), -1)
    picked = call(
        pick_kernel,
        "pick",
        jax.ShapeDtypeStruct((1, owners.shape[1], MODES * MODES), F32),
        [],
        10**5,
        owners,
        parts.reshape(-1, TILE),
    )
    return (state, picked)


def solution(mesh):
    return jax.shard_map(
        local,
        mesh=mesh,
        in_specs=(
            P(("row", "own"), "col"),
            P(("row", "own"), "col"),
            P(None, ("row", "own"), "col"),
            P(None, ("row", "own"), "col"),
            P(("row", "own"), "col"),
            P(("row", "own"), "col"),
            P(),
        ),
        out_specs=(P(None, ("row", "own"), "col"), P("own", None, None)),
        check_vma=False,
    )
```

```python
import math

import jax
import jax.numpy as jnp
import numpy as np
from jax import lax
from jax.experimental import pallas as pl
from jax.experimental.pallas import tpu as pltpu
from jax.sharding import PartitionSpec as P

TILE = 128
MODES = 32
SWEEPS = 3
SUB = 8
HALO = 8
INNER = 2 * HALO
STRIP = 40
LEAD = HALO - 1
KEPT = 12
OUTER = (LEAD, STRIP - 2 * HALO)
NEAR, FAR = 7, 6
ARRAYS = 7
VISC, FRIC, DRIV, MASK, OBS = 0, 1, 2, 4, 5
EDGE = ARRAYS * HALO
SLOT = 2 * INNER
PER = TILE // SLOT
GROUPS = 5
SENT = 2 * GROUPS * HALO + HALO
PARTS = 3
UPPER, LOWER = 32, 64
ROW_AXES = ("row", "own")
COL_AXES = ("col",)
F32 = jnp.float32
LIMIT = 40 * 1024 * 1024


def swap(x, axis, first):
    sizes = lax.axis_size(ROW_AXES), lax.axis_size(COL_AXES)
    owners = lax.axis_size("own")

    def device(i, j):
        return (i // owners * sizes[1] + j) * owners + i % owners

    pairs = []
    for i in range(sizes[0]):
        for j in range(sizes[1]):
            place = [i, j]
            if first and place[axis] in (0, sizes[axis] - 1):
                place[1 - axis] ^= 1
            else:
                place[axis] = ((place[axis] + first) ^ 1) - first
            pairs.append((device(i, j), device(*place)))
    return lax.ppermute(x, ("row", "col", "own"), pairs)


def position(axes):
    index, size = 0, 1
    for axis in axes:
        index = index * lax.axis_size(axis) + lax.axis_index(axis)
        size *= lax.axis_size(axis)
    assert size % 2 == 0
    return lax.rem(index, 2) == 0, (index == 0) | (index == size - 1)


def is_even(axes):
    return position(axes)[0]


def lanes():
    return lax.broadcasted_iota(jnp.int32, (SUB, TILE), 1)


def call(kernel, name, outs, scratch, cost, *args, aliases={}):
    return pl.pallas_call(
        kernel,
        out_shape=outs,
        scratch_shapes=scratch,
        input_output_aliases=aliases,
        compiler_params=pltpu.CompilerParams(vmem_limit_bytes=LIMIT),
        cost_estimate=pl.CostEstimate(flops=cost, bytes_accessed=cost, transcendentals=0),
        name=name,
    )(*args)


def vmem(*shape):
    return pltpu.VMEM(shape, F32)


FIELDS = 14
STRIP_FIELDS = 24


class Domain:
    def __init__(self, refs, base, span, source, seam=None):
        self.refs, self.base, self.span, self.source, self.seam = refs, base, span, source, seam

    def at(self, j):
        return pl.ds(self.base + SUB * j, SUB)

    def prepare(self, flipped):
        n2, n4, c, i, b0, b1 = self.refs[:6]
        visc = [self.source(VISC, j) for j in range(self.span)]
        for j in range(self.span):
            at = self.at(j)
            before = visc[j - 1] if j else pltpu.roll(visc[-1], 1, 0)
            if self.seam and not j:
                row = lax.broadcasted_iota(jnp.int32, (SUB, TILE), 0)
                before = jnp.where(row == SUB // 2, self.seam(), before)
            pair = visc[j] + before
            fric = self.source(FRIC, j)
            diag = 1.25 * (pair + pltpu.roll(pair, 1, 1)) + fric
            on = self.source(MASK, j) > 0.0
            inv = jnp.where(on, 0.5 / jnp.where(on, diag, 1.0), 0.0)
            half = 0.5 * visc[j]
            n2[at, :] = half
            n4[at, :] = 0.5 * half
            c[at, :] = 1.0 - fric * inv
            i[at, :] = inv
            for k, b in enumerate((b0, b1)):
                value = inv * self.source(DRIV + (1 - k if flipped else k), j)
                b[at, :] = value
                self.write(k, at, value + value)

    def write(self, k, at, value):
        self.refs[6 + k][at, :] = value
        self.refs[8 + k][at, :] = pltpu.roll(value, TILE - 1, 1)

    def retarget(self, flipped, velocity=None):
        i, b0, b1 = self.refs[3:6]
        w0, w1 = velocity or self.refs[6:8]
        for j in range(self.span):
            at = self.at(j)
            for k, (b, w) in enumerate(((b0, w0), (b1, w1))):
                value = i[at, :] * (w[at, :] - self.source(OBS + (1 - k if flipped else k), j))
                b[at, :] = value
                self.write(k, at, value + value)

    def differences(self):
        n2, n4 = self.refs[:2]
        fields = self.refs[6:10]
        parts = self.refs[10:14]

        def corners(j, here, below):
            w0, w1, r0, r1 = here
            v0, v1, s0, s1 = below
            a1, a2 = s0 - w0, v0 - r0
            e1, e2 = s1 - w1, v1 - r1
            x, y = a1 + a2, e1 - e2
            q = (a1 - a2) + (e1 + e2)
            both = x + y
            at = self.at(j)
            half = n2[at, :]
            return half * (both + x), n4[at, :] * q, half * (both + y)

        def load(j):
            at = self.at(j)
            return [field[at, :] for field in fields]

        top = load(0)
        last = corners(self.span - 1, load(self.span - 1), [pltpu.roll(v, SUB - 1, 0) for v in top])
        up = [pltpu.roll(v, 1, 0) for v in last]
        here = top
        for j in range(self.span):
            at = self.at(j)
            if j < self.span - 1:
                below = load(j + 1)
                p, q, r = corners(j, here, below)
                here = below
            else:
                p, q, r = last
            g, t = up[0] - p, up[1] + q
            gq, tr = up[1] - q, up[2] + r
            parts[0][at, :] = g - t
            parts[1][at, :] = gq - tr
            parts[2][at, :] = pltpu.roll(g + t, 1, 1)
            parts[3][at, :] = pltpu.roll(gq + tr, 1, 1)
            up = (p, q, r)

    def update(self):
        c, i, b0, b1, w0, w1 = self.refs[2:8]
        parts = self.refs[10:14]
        for j in range(self.span):
            at = self.at(j)
            cv, iv = c[at, :], i[at, :]
            for k, (b, w) in enumerate(((b0, w0), (b1, w1))):
                value = (cv * w[at, :] + b[at, :]) - iv * (parts[k][at, :] + parts[k + 2][at, :])
                self.write(k, at, value)


class Strips(Domain):
    def prepare(self, flipped):
        super().prepare(flipped)
        for j in range(self.span):
            at = self.at(j)
            for now, later in zip(self.refs[2:6], self.refs[10:14]):
                later[at, :] = pltpu.roll(now[at, :], TILE - 1, 1)
        for now, before in zip(self.refs[:2], self.refs[14:16]):
            before[self.at(0), :] = pltpu.roll(now[self.at(self.span - 1), :], 1, 0)

    def retarget(self, flipped, velocity=None):
        super().retarget(flipped, velocity)
        for j in range(self.span):
            at = self.at(j)
            for now, later in zip(self.refs[4:6], self.refs[12:14]):
                later[at, :] = pltpu.roll(now[at, :], TILE - 1, 1)

    def differences(self):
        fields = self.refs[6:10]
        kept, turned, kept_next, turned_next = (self.refs[16 + 2 * k : 18 + 2 * k] for k in range(4))

        def corners(halves, quarters, j, here, below):
            w0, w1, r0, r1 = here
            v0, v1, s0, s1 = below
            a1, a2 = s0 - w0, v0 - r0
            e1, e2 = s1 - w1, v1 - r1
            x, y = a1 + a2, e1 - e2
            q = (a1 - a2) + (e1 + e2)
            both = x + y
            at = self.at(j)
            half = halves[at, :]
            return half * (both + x), quarters[at, :] * q, half * (both + y)

        def load(j):
            at = self.at(j)
            return [field[at, :] for field in fields]

        top, end = load(0), load(self.span - 1)
        up = corners(*self.refs[14:16], 0, [pltpu.roll(v, 1, 0) for v in end], top)
        here = top
        for j in range(self.span):
            at = self.at(j)
            below = load(j + 1) if j < self.span - 1 else [pltpu.roll(v, SUB - 1, 0) for v in top]
            p, q, r = corners(*self.refs[:2], j, here, below)
            g, t = up[0] - p, up[1] + q
            gq, tr = up[1] - q, up[2] + r
            for k, (stay, move) in enumerate(((g - t, g + t), (gq - tr, gq + tr))):
                kept[k][at, :] = stay
                turned_next[k][at, :] = move
                turned[k][at, :] = pltpu.roll(move, 1, 1)
                kept_next[k][at, :] = pltpu.roll(stay, TILE - 1, 1)
            up, here = (p, q, r), below

    def update(self):
        for first, offset, parts in ((2, 6, (16, 18)), (10, 8, (20, 22))):
            c, i, *b = self.refs[first : first + 4]
            for j in range(self.span):
                at = self.at(j)
                cv, iv = c[at, :], i[at, :]
                for k in range(2):
                    w = self.refs[offset + k]
                    change = self.refs[parts[0] + k][at, :] + self.refs[parts[1] + k][at, :]
                    w[at, :] = (cv * w[at, :] + b[k][at, :]) - iv * change


def run(domains, written_out=False):
    def body(_, carry):
        for domain in domains:
            domain.differences()
        for domain in domains:
            domain.update()
        return carry

    if written_out:
        for k in range(SWEEPS):
            body(k, 0)
    else:
        lax.fori_loop(0, SWEEPS, body, 0)


def ends_kernel(visc, fric, driv, mask, obs, to_b, to_a, one, two, flags, sems):
    rows = visc.shape[0]
    copies = []
    for e, first in enumerate((0, rows - HALO)):
        at = pl.ds(first, HALO)
        pieces = [
            (visc.at[at], one.at[e, 0]),
            (fric.at[at], one.at[e, 1]),
            (driv.at[:, at], two.at[e, 0]),
            (mask.at[at], flags.at[e]),
            (obs.at[:, at], two.at[e, 1]),
        ]
        for n, (source, place) in enumerate(pieces):
            copies.append(pltpu.make_async_copy(source, place, sems.at[e, n]))
    for copy in copies:
        copy.start()
    for copy in copies:
        copy.wait()
    even, at_end = position(ROW_AXES)

    def edge(e):
        return [one[e, 0], one[e, 1], two[e, 0, 0], two[e, 0, 1], flags[e].astype(F32), two[e, 1, 0], two[e, 1, 1]]

    for a, (head, tail) in enumerate(zip(edge(0), edge(1))):
        at = slice(HALO * a, HALO * (a + 1))
        to_a[at, :] = jnp.where(even, tail, head)
        to_b[at, :] = jnp.where(at_end, 0.0, jnp.where(even, head, tail))


def field_of(visc, fric, driv, mask, obs):
    def field(a, at):
        if a == MASK:
            return mask[at, :].astype(F32)
        if a >= OBS:
            return obs[a - OBS, at, :]
        if a >= DRIV:
            return driv[a - DRIV, at, :]
        return (visc, fric)[a][at, :]

    return field


def first_row(part, lane):
    if part < 2:
        return TILE * part + lane
    if lane < INNER + HALO:
        return TILE + lane
    if lane >= TILE - INNER - HALO:
        return lane
    if UPPER + HALO <= lane < UPPER + SLOT:
        return lane - UPPER - HALO
    if LOWER <= lane < LOWER + INNER + HALO:
        return 2 * TILE - INNER - HALO + lane - LOWER
    return None


def right_part(row):
    seam = TILE - HALO <= row < TILE + HALO
    part = 2 if seam or row == 0 or row == 2 * TILE - HALO else row // TILE
    return part, [lane for lane in range(0, TILE, SUB) if first_row(part, lane) == row][-1]


def slot(part, a):
    return TILE * (2 * part + a // PER) + SLOT * (a % PER)


def interior_kernel(visc, fric, driv, mask, obs, edge, n2, n4, c, i, v0, v1, *refs):
    span = visc.shape[0] // SUB
    field = field_of(visc, fric, driv, mask, obs)
    lane = lanes()
    for part in range(PARTS):
        for m in range(-(-ARRAYS // PER)):
            strips = []
            for at in range(0, TILE, SUB):
                row = first_row(part, at)
                packed = jnp.zeros((SUB, TILE), F32)
                if row is not None:
                    for k in range(min(PER, ARRAYS - PER * m)):
                        value = field(PER * m + k, slice(row, row + SUB))
                        moved = pltpu.roll(value, (SLOT * k + INNER) % TILE, 1)
                        packed = jnp.where(lax.div(lane, SLOT) == k, moved, packed)
                strips.append(packed)
            base = TILE * (2 * part + m)
            edge[base : base + TILE, :] = jnp.concatenate(strips, axis=0).T
    refs = (n2, n4, c, i, *refs[:2], v0, v1, *refs[2:])
    domain = Domain(refs, 0, span, lambda a, j: field(a, pl.ds(j, SUB, stride=span)))
    domain.prepare(False)
    run([domain])


def columns_kernel(row_b, row_a, edge, to_b, to_a, turned):
    even = is_even(ROW_AXES)
    above = jnp.where(even, row_b[...], row_a[...])
    below = jnp.where(even, row_a[...], row_b[...])
    halo = jnp.concatenate([above, below, jnp.zeros((TILE - 2 * EDGE, TILE), F32)], axis=0).T
    turned[:INNER, :] = halo[TILE - INNER :]
    turned[INNER:, :] = halo[:INNER]
    even, at_end = position(COL_AXES)
    row = lax.broadcasted_iota(jnp.int32, (SUB, TILE), 0)

    def put(out, right, left):
        right = pltpu.roll(right, LEAD, 0)
        to_a[out : out + HALO, :] = jnp.where(even, right, left)
        to_b[out : out + HALO, :] = jnp.where(at_end, 0.0, jnp.where(even, left, right))

    for part in range(2):
        right, left = [], []
        for a in range(ARRAYS):
            at = slot(part, a) + INNER
            right.append(edge[at - HALO : at, :])
            left.append(edge[at : at + HALO, :])
        for k in range(2):
            seen_r, seen_l = right[OBS + k], left[OBS + k]
            g = 1 + 2 * k
            right[g] = jnp.where(row < 2, pltpu.roll(seen_r, 2, 0), right[g])
            right[g + 1] = jnp.where(row < 2, pltpu.roll(seen_r, 4, 0), right[g + 1])
            left[g] = jnp.where(row >= 6, pltpu.roll(seen_l, 6, 0), left[g])
            left[g + 1] = jnp.where(row >= 6, pltpu.roll(seen_l, 4, 0), left[g + 1])
        for g in range(GROUPS):
            put(HALO * (GROUPS * part + g), right[g], left[g])
    put(2 * GROUPS * HALO, halo[TILE - HALO :], halo[:HALO])


def strided(stack, base):
    span = STRIP // SUB
    return lambda a, j: stack[pl.ds(base + STRIP * a + j, SUB, stride=span), :]


def fill(stack, base, first, last):
    row = lax.broadcasted_iota(jnp.int32, (SUB, TILE), 0)
    one, two = (pltpu.roll(value, LEAD, 0) for value in first)
    mixed = [jnp.where(row == LEAD, two, one), jnp.where(row < SUB // 2, two, last[0])]
    for k, value in enumerate((one, *mixed, last[1])):
        stack[base + SUB * k : base + SUB * (k + 1), :] = value


def velocity(domain, plain, base):
    for j in range(domain.span):
        at = domain.at(j)
        for k in range(2):
            plain[pl.ds(base + STRIP * k + j, SUB, stride=domain.span), :] = domain.refs[6 + k][at, :]


def density(domain, plain, base, out, place):
    w0, w1 = domain.refs[6:8]
    for j in range(domain.span):
        at = domain.at(j)
        v0, v1 = (plain[pl.ds(base + STRIP * k + j, SUB, stride=domain.span), :] for k in range(2))
        value = -domain.source(FRIC, j) * (w0[at, :] * v0 + w1[at, :] * v1)
        out[pl.ds(place + j, SUB, stride=domain.span), :] = value


def beside():
    lane = lanes()
    return (lane < NEAR) | (lane >= TILE - FAR)


def ends(second):
    row = lax.broadcasted_iota(jnp.int32, (SUB, TILE), 0)
    return row >= SUB - FAR if second else row < NEAR


def adjoint_kernel(
    row_b, row_a, visc, fric, driv, mask, obs, n2, n4, c, i, v0, v1, basis_p, basis_q, edge, turned,
    vel, wide, sides, seams,
    stack, plain, dens, total, *refs,
):
    rows = visc.shape[0]
    span = rows // SUB
    even = is_even(ROW_AXES)
    field = field_of(visc, fric, driv, mask, obs)
    for a in range(ARRAYS):
        at = slice(HALO * a, HALO * (a + 1))
        got_a, got_b = row_a[at, :], row_b[at, :]
        base = STRIP * a
        first = [field(a, slice(at, at + SUB)) for at in (0, SUB)]
        last = [field(a, slice(at, at + SUB)) for at in (rows - 2 * SUB, rows - SUB)]
        fill(stack, base, first, last)
        stack[base : base + LEAD, :] = jnp.where(even, got_b, got_a)[HALO - LEAD :]
        stack[base + STRIP - HALO : base + STRIP, :] = jnp.where(even, got_a, got_b)
    strips = Strips(refs[:STRIP_FIELDS], 0, STRIP // SUB, strided(stack, 0), lambda: visc[rows - KEPT - 1 : rows - KEPT, :])
    strips.prepare(False)
    run([strips])
    velocity(strips, plain, 0)
    for k in range(2):
        for e in range(2):
            out = HALO * (2 * k + e)
            vel[out : out + HALO, :] = plain[STRIP * k + OUTER[e] : STRIP * k + OUTER[e] + HALO, :]
    interior = Domain(
        (n2, n4, c, i, *refs[STRIP_FIELDS:]), 0, span, lambda a, j: field(a, pl.ds(j, SUB, stride=span))
    )
    strips.retarget(False)
    interior.retarget(False, (v0, v1))
    run([interior, strips])
    w0, w1 = interior.refs[6:8]
    for j in range(span):
        at = interior.at(j)
        value = -interior.source(FRIC, j) * (w0[at, :] * v0[at, :] + w1[at, :] * v1[at, :])
        dens[pl.ds(j, SUB, stride=span), :] = value
    density(strips, plain, 0, dens, rows)

    side = beside()
    for s in range(0, TILE, SUB):
        summed = jnp.zeros((SUB, TILE), F32)
        for row in range(s, rows, TILE):
            value = dens[row : row + SUB, :]
            if row in (0, rows - SUB):
                at = rows + OUTER[row > 0]
                value = jnp.where(ends(row > 0), dens[at : at + SUB, :], value)
            summed += value
        total[s : s + SUB, :] = jnp.where(side, 0.0, summed)
    exact = dict(precision=lax.Precision.HIGHEST, preferred_element_type=F32)
    half = jnp.dot(basis_p[...], total[...], **exact)
    wide[...] = jnp.dot(half, basis_q[...], **exact)

    corner = corners()
    for part in range(PARTS):
        for a in range(ARRAYS):
            columns = []
            for r in range(0, SLOT, SUB):
                value = edge[slot(part, a) + r : slot(part, a) + r + SUB, :]
                if part == 2:
                    moved = pltpu.roll(turned[r : r + SUB, :], (UPPER - HALO * a) % TILE, 1)
                    value = jnp.where(corner, moved, value)
                columns.append(value)
            fill(sides, strip(part, a), columns[2:], columns[:2])
            if a == VISC:
                seams[SUB * part : SUB * (part + 1), :] = columns[0]


def strip(part, a):
    return STRIP * (ARRAYS * part + a)


def corners():
    lane = lanes()
    above = (lane >= UPPER) & (lane < UPPER + HALO)
    return above | ((lane >= LOWER + INNER + HALO) & (lane < LOWER + SLOT))


def split(x, axis):
    high = x.astype(jnp.bfloat16)
    low = (x - high.astype(F32)).astype(jnp.bfloat16)
    return jnp.concatenate([high, high, low], axis=axis)


def split_constant(x, axis):
    x = np.asarray(x, np.float32)
    high = np.asarray(x, jnp.bfloat16)
    low = np.asarray(x - np.asarray(high, np.float32), jnp.bfloat16)
    return jnp.asarray(np.concatenate([high, low, high], axis=axis))


def left_right_kernel(
    _, seams, col_b, col_a, wide_in, block, basis_rows, basis_cols,
    stack, strips, coef,
    plain, *refs,
):
    even = is_even(COL_AXES)
    lane = lanes()
    row = lax.broadcasted_iota(jnp.int32, (SUB, TILE), 0)
    upper = (lane >= UPPER + HALO) & (lane < UPPER + SLOT)
    lower = (lane >= LOWER) & (lane < LOWER + INNER + HALO)
    seam_t0 = lane >= TILE - INNER - HALO
    seam_t1 = lane < INNER + HALO
    corner = corners()
    for from_left in (True, False):
        groups = []
        for g in range(2 * GROUPS + 1):
            got_a, got_b = col_a[HALO * g : HALO * (g + 1), :], col_b[HALO * g : HALO * (g + 1), :]
            groups.append(jnp.where(even, got_b, got_a) if from_left else jnp.where(even, got_a, got_b))
        tiles = []
        for part in range(2):
            tile = groups[GROUPS * part : GROUPS * (part + 1)]
            for k in range(2):
                g, h = tile[1 + 2 * k], tile[2 + 2 * k]
                if from_left:
                    tile.append(jnp.where(row >= 5, pltpu.roll(g, 6, 0), pltpu.roll(h, 4, 0)))
                else:
                    tile.append(jnp.where(row < 2, pltpu.roll(g, 2, 0), pltpu.roll(h, 4, 0)))
            tiles.append(tile)
        for a in range(ARRAYS):
            t0, t1 = tiles[0][a], tiles[1][a]
            third = jnp.where(corner, pltpu.roll(groups[-1], (UPPER - HALO * a) % TILE, 1), 0.0)
            third = jnp.where(upper, pltpu.roll(t0, UPPER + HALO, 1), third)
            third = jnp.where(lower, pltpu.roll(t1, LOWER + INNER + HALO, 1), third)
            third = jnp.where(seam_t0, t0, jnp.where(seam_t1, t1, third))
            for part, value in enumerate((t0, t1, third)):
                base = strip(part, a)
                if from_left:
                    stack[base : base + LEAD, :] = value[:LEAD]
                else:
                    stack[base + STRIP - HALO : base + STRIP, :] = value
    last = INNER - KEPT - 1
    before = [lambda at=SUB * part + last: seams[at : at + 1, :] for part in range(PARTS)]
    domains = [
        Strips(refs, STRIP * part, STRIP // SUB, strided(stack, strip(part, 0)), seam)
        for part, seam in enumerate(before)
    ]
    for domain in domains:
        domain.prepare(True)
    run(domains, True)
    for part, domain in enumerate(domains):
        velocity(domain, strips, 2 * STRIP * part)
        domain.retarget(True)
    run(domains, True)
    for part, domain in enumerate(domains):
        density(domain, strips, 2 * STRIP * part, plain, STRIP * part)

    def side(part):
        base = STRIP * part
        return jnp.concatenate(
            [plain[base + at : base + at + HALO, :] for at in OUTER], axis=0
        )

    lane = lax.broadcasted_iota(jnp.int32, (2 * HALO, TILE), 1)
    row = lax.broadcasted_iota(jnp.int32, (2 * HALO, TILE), 0)
    right = (row < NEAR) | (row >= 2 * HALO - FAR)
    straight = (lane >= HALO) & (lane < TILE - HALO)
    seam = (lane < HALO) | (lane >= TILE - HALO)
    top = (lane >= UPPER + HALO) & (lane < UPPER + 2 * HALO)
    bottom = (lane >= LOWER + INNER) & (lane < LOWER + INNER + HALO)
    dens = jnp.concatenate(
        [
            jnp.where(right & straight, side(0) + side(1), 0.0),
            jnp.where(right & (seam | top | bottom), side(2), 0.0),
        ],
        axis=1,
    )
    half = lax.dot_general(
        basis_rows[...], split(dens, 1), (((1,), (1,)), ((), ())), preferred_element_type=F32
    )
    wide = wide_in[...] + jnp.dot(split(half, 1), basis_cols[...], preferred_element_type=F32)
    lane = lanes()
    which = lax.div(lane, MODES)
    flat = wide[:SUB]
    for j in range(1, MODES // SUB):
        flat = jnp.where(which == j, wide[SUB * j : SUB * (j + 1)], flat)
    mark = jnp.broadcast_to(block[:1, :].astype(F32), (SUB, TILE))
    row = lax.broadcasted_iota(jnp.int32, (SUB, TILE), 0)
    moved = [flat] + [pltpu.roll(flat, r, 0) for r in range(1, SUB)] + [flat]
    lines = [flat] + [
        jnp.where(row < r - 1, moved[r - 1], jnp.where(row == r - 1, mark, moved[r])) for r in range(1, SUB + 1)
    ]
    cycle = SUB * (SUB + 1)
    chunk = min(4, coef.shape[0] // cycle)

    def spread(d, carry):
        for e in range(chunk):
            for r, line in enumerate(lines):
                coef[pl.ds(pl.multiple_of((d * chunk + e) * cycle + SUB * r, SUB), SUB), :] = line
        return carry

    lax.fori_loop(0, coef.shape[0] // cycle // chunk, spread, 0)


def join_kernel(v0, v1, vel_ends, strips, vel, turned):
    rows = vel.shape[1]
    span = rows // SUB
    middle = jnp.zeros((TILE - 2 * HALO, TILE), F32)
    side = beside()
    for k, v in enumerate((v0, v1)):
        for part in range(PARTS):
            base = STRIP * (2 * part + 1 - k)
            first, last = (strips[base + at : base + at + HALO, :] for at in OUTER)
            at = TILE * (2 * part + k)
            turned[at : at + TILE, :] = jnp.concatenate([first, middle, last], axis=0).T
        for row in range(0, rows, SUB):
            value = v[pl.ds(SUB * (row % span) + row // span, SUB, stride=SUB), :]
            if row in (0, rows - SUB):
                at = HALO * (2 * k + (row > 0))
                value = jnp.where(ends(row > 0), vel_ends[at : at + HALO, :], value)
            part, lane = right_part(row)
            at = TILE * (2 * part + k) + lane
            vel[k, row : row + SUB, :] = jnp.where(side, turned[at : at + SUB, :], value)


def bases():
    places = np.arange(TILE) + 0.5
    basis = np.cos(math.pi * places[:, None] * np.arange(MODES)[None, :] / TILE)
    groups = MODES // SUB
    order = np.arange(MODES).reshape(SUB, groups).T.reshape(-1)
    rows = basis[:, order] / TILE
    cols = np.tile(basis, (1, groups))
    placed = np.zeros((2 * TILE, MODES))
    for row in range(0, 2 * TILE, SUB):
        part, lane = right_part(row)
        at = lane + (TILE if part == 2 else 0)
        placed[at : at + SUB] = rows[row % TILE : row % TILE + SUB]
    outer = np.concatenate([cols[:HALO], cols[TILE - HALO :]])
    return jnp.asarray(rows.T, F32), jnp.asarray(cols, F32), split_constant(placed.T, 1), split_constant(outer, 0)


def pick_kernel(owners, every, out):
    mine = out.shape[1]
    own = lax.axis_index("own")
    wanted = [owners[pl.ds(own, 1), k : k + 1].astype(F32) for k in range(mine)]
    lines = SUB + 1
    devices = every.shape[0] // lines
    chunk = min(4, devices // SUB)

    def body(d, sums):
        sums = list(sums)
        for e in range(chunk):
            base = (d * chunk + e) * SUB * lines
            mark = every[pl.ds(base + SUB, SUB, stride=lines), :]
            hits = [mark == wanted[k] for k in range(mine)]
            for r in range(SUB):
                part = every[pl.ds(base + r, SUB, stride=lines), :]
                for k in range(mine):
                    sums[SUB * k + r] += jnp.where(hits[k], part, 0.0)
        return tuple(sums)

    start = (jnp.zeros((SUB, TILE), F32),) * (mine * SUB)
    sums = lax.fori_loop(0, devices // SUB // chunk, body, start)
    for k in range(mine):
        for r in range(SUB):
            total = jnp.sum(sums[SUB * k + r], axis=0, keepdims=True)
            out[0, k : k + 1, TILE * r : TILE * (r + 1)] = total


def local(viscosity, friction, driving, observed, ice_mask, tile_block, owner_list):
    rows, cols = viscosity.shape
    assert (rows, cols) == (2 * TILE, TILE)
    inputs = (viscosity, friction, driving, ice_mask, observed)
    near = [pltpu.with_memory_space_constraint(x, pltpu.VMEM) for x in inputs]
    basis_p, basis_q, basis_rows, basis_cols = bases()
    to_b, to_a = call(
        ends_kernel,
        "ends",
        (vmem(EDGE, cols), vmem(EDGE, cols)),
        [
            vmem(2, 2, HALO, cols),
            vmem(2, 2, 2, HALO, cols),
            pltpu.VMEM((2, HALO, cols), jnp.int32),
            pltpu.SemaphoreType.DMA((2, 5)),
        ],
        10**6,
        *(pltpu.with_memory_space_constraint(x, pltpu.HBM) for x in inputs),
    )
    row_b = swap(to_b, 0, 1)
    row_a = swap(to_a, 0, 0)
    edge, *forward = call(
        interior_kernel,
        "interior",
        (vmem(2 * PARTS * TILE, TILE),) + (vmem(rows, cols),) * 6,
        [vmem(rows, cols)] * (FIELDS - 6),
        8 * 10**6,
        *near,
    )
    to_b, to_a, turned = call(
        columns_kernel,
        "columns",
        (vmem(SENT, TILE), vmem(SENT, TILE), vmem(SLOT, TILE)),
        [],
        10**5,
        row_b,
        row_a,
        edge,
    )
    col_b = swap(to_b, 1, 1)
    col_a = swap(to_a, 1, 0)
    vel_ends, wide, sides, seams = call(
        adjoint_kernel,
        "adjoint",
        (
            vmem(4 * HALO, cols),
            vmem(MODES, TILE),
            vmem(PARTS * ARRAYS * STRIP, TILE),
            vmem(PARTS * SUB, TILE),
        ),
        [vmem(ARRAYS * STRIP, cols), vmem(2 * STRIP, cols), vmem(rows + STRIP, cols), vmem(TILE, cols)]
        + [vmem(STRIP, cols)] * STRIP_FIELDS
        + [vmem(rows, cols)] * (FIELDS - 4),
        8 * 10**6,
        row_b,
        row_a,
        *near,
        *forward,
        basis_p,
        basis_q,
        edge,
        turned,
    )
    devices = lax.axis_size(ROW_AXES + COL_AXES)
    _, strips, coef = call(
        left_right_kernel,
        "left_right",
        (
            vmem(PARTS * ARRAYS * STRIP, TILE),
            vmem(PARTS * 2 * STRIP, TILE),
            vmem(devices * (SUB + 1), TILE),
        ),
        [vmem(PARTS * STRIP, TILE)] * (STRIP_FIELDS + 1),
        4 * 10**6,
        sides,
        seams,
        col_b,
        col_a,
        wide,
        tile_block,
        basis_rows,
        basis_cols,
        aliases={0: 0},
    )
    coef = coef.reshape(devices, 1, (SUB + 1) * TILE)
    parts = lax.all_to_all(coef, ROW_AXES + COL_AXES, 0, 0, tiled=True)
    state = call(
        join_kernel,
        "join",
        jax.ShapeDtypeStruct((2, rows, cols), F32),
        [vmem(2 * PARTS * TILE, TILE)],
        4 * 10**6,
        *forward[4:],
        vel_ends,
        strips,
    )
    owners = owner_list.reshape(lax.axis_size("own"), -1)
    picked = call(
        pick_kernel,
        "pick",
        jax.ShapeDtypeStruct((1, owners.shape[1], MODES * MODES), F32),
        [],
        10**5,
        owners,
        parts.reshape(-1, TILE),
    )
    return (state, picked)


def solution(mesh):
    return jax.shard_map(
        local,
        mesh=mesh,
        in_specs=(
            P(("row", "own"), "col"),
            P(("row", "own"), "col"),
            P(None, ("row", "own"), "col"),
            P(None, ("row", "own"), "col"),
            P(("row", "own"), "col"),
            P(("row", "own"), "col"),
            P(),
        ),
        out_specs=(P(None, ("row", "own"), "col"), P("own", None, None)),
        check_vma=False,
    )
```

```python
import math

import jax
import jax.numpy as jnp
import numpy as np
from jax import lax
from jax.experimental import pallas as pl
from jax.experimental.pallas import tpu as pltpu
from jax.sharding import PartitionSpec as P

TILE = 128
MODES = 32
SWEEPS = 3
SUB = 8
HALO = 8
INNER = 2 * HALO
STRIP = 40
LEAD = HALO - 1
KEPT = 12
OUTER = (LEAD, STRIP - 2 * HALO)
NEAR, FAR = 7, 6
ARRAYS = 7
VISC, FRIC, DRIV, MASK, OBS = 0, 1, 2, 4, 5
EDGE = ARRAYS * HALO
SLOT = 2 * INNER
PER = TILE // SLOT
GROUPS = 5
SENT = 2 * GROUPS * HALO + HALO
PARTS = 3
UPPER, LOWER = 32, 64
ROW_AXES = ("row", "own")
COL_AXES = ("col",)
F32 = jnp.float32
LIMIT = 40 * 1024 * 1024


def swap(x, axis, first):
    sizes = lax.axis_size(ROW_AXES), lax.axis_size(COL_AXES)
    owners = lax.axis_size("own")

    def device(i, j):
        return (i // owners * sizes[1] + j) * owners + i % owners

    pairs = []
    for i in range(sizes[0]):
        for j in range(sizes[1]):
            place = [i, j]
            if first and place[axis] in (0, sizes[axis] - 1):
                place[1 - axis] ^= 1
            else:
                place[axis] = ((place[axis] + first) ^ 1) - first
            pairs.append((device(i, j), device(*place)))
    return lax.ppermute(x, ("row", "col", "own"), pairs)


def position(axes):
    index, size = 0, 1
    for axis in axes:
        index = index * lax.axis_size(axis) + lax.axis_index(axis)
        size *= lax.axis_size(axis)
    assert size % 2 == 0
    return lax.rem(index, 2) == 0, (index == 0) | (index == size - 1)


def is_even(axes):
    return position(axes)[0]


def lanes():
    return lax.broadcasted_iota(jnp.int32, (SUB, TILE), 1)


def call(kernel, name, outs, scratch, cost, *args, aliases={}):
    return pl.pallas_call(
        kernel,
        out_shape=outs,
        scratch_shapes=scratch,
        input_output_aliases=aliases,
        compiler_params=pltpu.CompilerParams(vmem_limit_bytes=LIMIT),
        cost_estimate=pl.CostEstimate(flops=cost, bytes_accessed=cost, transcendentals=0),
        name=name,
    )(*args)


def vmem(*shape):
    return pltpu.VMEM(shape, F32)


FIELDS = 14
STRIP_FIELDS = 24


class Domain:
    def __init__(self, refs, base, span, source, seam=None):
        self.refs, self.base, self.span, self.source, self.seam = refs, base, span, source, seam

    def at(self, j):
        return pl.ds(self.base + SUB * j, SUB)

    def prepare(self, flipped):
        n2, n4, c, i, b0, b1 = self.refs[:6]
        visc = [self.source(VISC, j) for j in range(self.span)]
        for j in range(self.span):
            at = self.at(j)
            before = visc[j - 1] if j else pltpu.roll(visc[-1], 1, 0)
            if self.seam and not j:
                row = lax.broadcasted_iota(jnp.int32, (SUB, TILE), 0)
                before = jnp.where(row == SUB // 2, self.seam(), before)
            pair = visc[j] + before
            fric = self.source(FRIC, j)
            diag = 1.25 * (pair + pltpu.roll(pair, 1, 1)) + fric
            on = self.source(MASK, j) > 0.0
            inv = jnp.where(on, 0.5 / jnp.where(on, diag, 1.0), 0.0)
            half = 0.5 * visc[j]
            n2[at, :] = half
            n4[at, :] = 0.5 * half
            c[at, :] = 1.0 - fric * inv
            i[at, :] = inv
            for k, b in enumerate((b0, b1)):
                value = inv * self.source(DRIV + (1 - k if flipped else k), j)
                b[at, :] = value
                self.write(k, at, value + value)

    def write(self, k, at, value):
        self.refs[6 + k][at, :] = value
        self.refs[8 + k][at, :] = pltpu.roll(value, TILE - 1, 1)

    def retarget(self, flipped, velocity=None):
        i, b0, b1 = self.refs[3:6]
        w0, w1 = velocity or self.refs[6:8]
        for j in range(self.span):
            at = self.at(j)
            for k, (b, w) in enumerate(((b0, w0), (b1, w1))):
                value = i[at, :] * (w[at, :] - self.source(OBS + (1 - k if flipped else k), j))
                b[at, :] = value
                self.write(k, at, value + value)

    def differences(self):
        n2, n4 = self.refs[:2]
        fields = self.refs[6:10]
        parts = self.refs[10:14]

        def corners(j, here, below):
            w0, w1, r0, r1 = here
            v0, v1, s0, s1 = below
            a1, a2 = s0 - w0, v0 - r0
            e1, e2 = s1 - w1, v1 - r1
            x, y = a1 + a2, e1 - e2
            q = (a1 - a2) + (e1 + e2)
            both = x + y
            at = self.at(j)
            half = n2[at, :]
            return half * (both + x), n4[at, :] * q, half * (both + y)

        def load(j):
            at = self.at(j)
            return [field[at, :] for field in fields]

        top = load(0)
        last = corners(self.span - 1, load(self.span - 1), [pltpu.roll(v, SUB - 1, 0) for v in top])
        up = [pltpu.roll(v, 1, 0) for v in last]
        here = top
        for j in range(self.span):
            at = self.at(j)
            if j < self.span - 1:
                below = load(j + 1)
                p, q, r = corners(j, here, below)
                here = below
            else:
                p, q, r = last
            g, t = up[0] - p, up[1] + q
            gq, tr = up[1] - q, up[2] + r
            parts[0][at, :] = g - t
            parts[1][at, :] = gq - tr
            parts[2][at, :] = pltpu.roll(g + t, 1, 1)
            parts[3][at, :] = pltpu.roll(gq + tr, 1, 1)
            up = (p, q, r)

    def update(self):
        c, i, b0, b1, w0, w1 = self.refs[2:8]
        parts = self.refs[10:14]
        for j in range(self.span):
            at = self.at(j)
            cv, iv = c[at, :], i[at, :]
            for k, (b, w) in enumerate(((b0, w0), (b1, w1))):
                value = (cv * w[at, :] + b[at, :]) - iv * (parts[k][at, :] + parts[k + 2][at, :])
                self.write(k, at, value)


class Strips(Domain):
    def prepare(self, flipped):
        super().prepare(flipped)
        for j in range(self.span):
            at = self.at(j)
            for now, later in zip(self.refs[2:6], self.refs[10:14]):
                later[at, :] = pltpu.roll(now[at, :], TILE - 1, 1)
        for now, before in zip(self.refs[:2], self.refs[14:16]):
            before[self.at(0), :] = pltpu.roll(now[self.at(self.span - 1), :], 1, 0)

    def retarget(self, flipped, velocity=None):
        super().retarget(flipped, velocity)
        for j in range(self.span):
            at = self.at(j)
            for now, later in zip(self.refs[4:6], self.refs[12:14]):
                later[at, :] = pltpu.roll(now[at, :], TILE - 1, 1)

    def differences(self):
        fields = self.refs[6:10]
        kept, turned, kept_next, turned_next = (self.refs[16 + 2 * k : 18 + 2 * k] for k in range(4))

        def corners(halves, quarters, j, here, below):
            w0, w1, r0, r1 = here
            v0, v1, s0, s1 = below
            a1, a2 = s0 - w0, v0 - r0
            e1, e2 = s1 - w1, v1 - r1
            x, y = a1 + a2, e1 - e2
            q = (a1 - a2) + (e1 + e2)
            both = x + y
            at = self.at(j)
            half = halves[at, :]
            return half * (both + x), quarters[at, :] * q, half * (both + y)

        def load(j):
            at = self.at(j)
            return [field[at, :] for field in fields]

        top, end = load(0), load(self.span - 1)
        up = corners(*self.refs[14:16], 0, [pltpu.roll(v, 1, 0) for v in end], top)
        here = top
        for j in range(self.span):
            at = self.at(j)
            below = load(j + 1) if j < self.span - 1 else [pltpu.roll(v, SUB - 1, 0) for v in top]
            p, q, r = corners(*self.refs[:2], j, here, below)
            g, t = up[0] - p, up[1] + q
            gq, tr = up[1] - q, up[2] + r
            for k, (stay, move) in enumerate(((g - t, g + t), (gq - tr, gq + tr))):
                kept[k][at, :] = stay
                turned_next[k][at, :] = move
                turned[k][at, :] = pltpu.roll(move, 1, 1)
                kept_next[k][at, :] = pltpu.roll(stay, TILE - 1, 1)
            up, here = (p, q, r), below

    def update(self):
        for first, offset, parts in ((2, 6, (16, 18)), (10, 8, (20, 22))):
            c, i, *b = self.refs[first : first + 4]
            for j in range(self.span):
                at = self.at(j)
                cv, iv = c[at, :], i[at, :]
                for k in range(2):
                    w = self.refs[offset + k]
                    change = self.refs[parts[0] + k][at, :] + self.refs[parts[1] + k][at, :]
                    w[at, :] = (cv * w[at, :] + b[k][at, :]) - iv * change


def run(domains, written_out=False):
    def body(_, carry):
        for domain in domains:
            domain.differences()
        for domain in domains:
            domain.update()
        return carry

    if written_out:
        for k in range(SWEEPS):
            body(k, 0)
    else:
        lax.fori_loop(0, SWEEPS, body, 0)


def ends_kernel(visc, fric, driv, mask, obs, to_b, to_a, one, two, flags, sems):
    rows = visc.shape[0]
    copies = []
    for e, first in enumerate((0, rows - HALO)):
        at = pl.ds(first, HALO)
        pieces = [
            (visc.at[at], one.at[e, 0]),
            (fric.at[at], one.at[e, 1]),
            (driv.at[:, at], two.at[e, 0]),
            (mask.at[at], flags.at[e]),
            (obs.at[:, at], two.at[e, 1]),
        ]
        for n, (source, place) in enumerate(pieces):
            copies.append(pltpu.make_async_copy(source, place, sems.at[e, n]))
    for copy in copies:
        copy.start()
    for copy in copies:
        copy.wait()
    even, at_end = position(ROW_AXES)

    def edge(e):
        return [one[e, 0], one[e, 1], two[e, 0, 0], two[e, 0, 1], flags[e].astype(F32), two[e, 1, 0], two[e, 1, 1]]

    for a, (head, tail) in enumerate(zip(edge(0), edge(1))):
        at = slice(HALO * a, HALO * (a + 1))
        to_a[at, :] = jnp.where(even, tail, head)
        to_b[at, :] = jnp.where(at_end, 0.0, jnp.where(even, head, tail))


def field_of(visc, fric, driv, mask, obs):
    def field(a, at):
        if a == MASK:
            return mask[at, :].astype(F32)
        if a >= OBS:
            return obs[a - OBS, at, :]
        if a >= DRIV:
            return driv[a - DRIV, at, :]
        return (visc, fric)[a][at, :]

    return field


def first_row(part, lane):
    if part < 2:
        return TILE * part + lane
    if lane < INNER + HALO:
        return TILE + lane
    if lane >= TILE - INNER - HALO:
        return lane
    if UPPER + HALO <= lane < UPPER + SLOT:
        return lane - UPPER - HALO
    if LOWER <= lane < LOWER + INNER + HALO:
        return 2 * TILE - INNER - HALO + lane - LOWER
    return None


def right_part(row):
    seam = TILE - HALO <= row < TILE + HALO
    part = 2 if seam or row == 0 or row == 2 * TILE - HALO else row // TILE
    return part, [lane for lane in range(0, TILE, SUB) if first_row(part, lane) == row][-1]


def slot(part, a):
    return TILE * (2 * part + a // PER) + SLOT * (a % PER)


def interior_kernel(visc, fric, driv, mask, obs, edge, n2, n4, c, i, v0, v1, *refs):
    span = visc.shape[0] // SUB
    field = field_of(visc, fric, driv, mask, obs)
    lane = lanes()
    for part in range(PARTS):
        for m in range(-(-ARRAYS // PER)):
            strips = []
            for at in range(0, TILE, SUB):
                row = first_row(part, at)
                packed = jnp.zeros((SUB, TILE), F32)
                if row is not None:
                    for k in range(min(PER, ARRAYS - PER * m)):
                        value = field(PER * m + k, slice(row, row + SUB))
                        moved = pltpu.roll(value, (SLOT * k + INNER) % TILE, 1)
                        packed = jnp.where(lax.div(lane, SLOT) == k, moved, packed)
                strips.append(packed)
            base = TILE * (2 * part + m)
            edge[base : base + TILE, :] = jnp.concatenate(strips, axis=0).T
    refs = (n2, n4, c, i, *refs[:2], v0, v1, *refs[2:])
    domain = Domain(refs, 0, span, lambda a, j: field(a, pl.ds(j, SUB, stride=span)))
    domain.prepare(False)
    run([domain])


def columns_kernel(row_b, row_a, edge, to_b, to_a, turned):
    even = is_even(ROW_AXES)
    above = jnp.where(even, row_b[...], row_a[...])
    below = jnp.where(even, row_a[...], row_b[...])
    halo = jnp.concatenate([above, below, jnp.zeros((TILE - 2 * EDGE, TILE), F32)], axis=0).T
    turned[:INNER, :] = halo[TILE - INNER :]
    turned[INNER:, :] = halo[:INNER]
    even, at_end = position(COL_AXES)
    row = lax.broadcasted_iota(jnp.int32, (SUB, TILE), 0)

    def put(out, right, left):
        right = pltpu.roll(right, LEAD, 0)
        to_a[out : out + HALO, :] = jnp.where(even, right, left)
        to_b[out : out + HALO, :] = jnp.where(at_end, 0.0, jnp.where(even, left, right))

    for part in range(2):
        right, left = [], []
        for a in range(ARRAYS):
            at = slot(part, a) + INNER
            right.append(edge[at - HALO : at, :])
            left.append(edge[at : at + HALO, :])
        for k in range(2):
            seen_r, seen_l = right[OBS + k], left[OBS + k]
            g = 1 + 2 * k
            right[g] = jnp.where(row < 2, pltpu.roll(seen_r, 2, 0), right[g])
            right[g + 1] = jnp.where(row < 2, pltpu.roll(seen_r, 4, 0), right[g + 1])
            left[g] = jnp.where(row >= 6, pltpu.roll(seen_l, 6, 0), left[g])
            left[g + 1] = jnp.where(row >= 6, pltpu.roll(seen_l, 4, 0), left[g + 1])
        for g in range(GROUPS):
            put(HALO * (GROUPS * part + g), right[g], left[g])
    put(2 * GROUPS * HALO, halo[TILE - HALO :], halo[:HALO])


def strided(stack, base):
    span = STRIP // SUB
    return lambda a, j: stack[pl.ds(base + STRIP * a + j, SUB, stride=span), :]


def fill(stack, base, first, last):
    row = lax.broadcasted_iota(jnp.int32, (SUB, TILE), 0)
    one, two = (pltpu.roll(value, LEAD, 0) for value in first)
    mixed = [jnp.where(row == LEAD, two, one), jnp.where(row < SUB // 2, two, last[0])]
    for k, value in enumerate((one, *mixed, last[1])):
        stack[base + SUB * k : base + SUB * (k + 1), :] = value


def velocity(domain, plain, base):
    for j in range(domain.span):
        at = domain.at(j)
        for k in range(2):
            plain[pl.ds(base + STRIP * k + j, SUB, stride=domain.span), :] = domain.refs[6 + k][at, :]


def density(domain, plain, base, out, place):
    w0, w1 = domain.refs[6:8]
    for j in range(domain.span):
        at = domain.at(j)
        v0, v1 = (plain[pl.ds(base + STRIP * k + j, SUB, stride=domain.span), :] for k in range(2))
        value = -domain.source(FRIC, j) * (w0[at, :] * v0 + w1[at, :] * v1)
        out[pl.ds(place + j, SUB, stride=domain.span), :] = value


def beside():
    lane = lanes()
    return (lane < NEAR) | (lane >= TILE - FAR)


def ends(second):
    row = lax.broadcasted_iota(jnp.int32, (SUB, TILE), 0)
    return row >= SUB - FAR if second else row < NEAR


def adjoint_kernel(
    row_b, row_a, visc, fric, driv, mask, obs, n2, n4, c, i, v0, v1, basis_p, basis_q, edge, turned,
    vel, wide, sides, seams,
    stack, plain, dens, total, *refs,
):
    rows = visc.shape[0]
    span = rows // SUB
    even = is_even(ROW_AXES)
    field = field_of(visc, fric, driv, mask, obs)
    for a in range(ARRAYS):
        at = slice(HALO * a, HALO * (a + 1))
        got_a, got_b = row_a[at, :], row_b[at, :]
        base = STRIP * a
        first = [field(a, slice(at, at + SUB)) for at in (0, SUB)]
        last = [field(a, slice(at, at + SUB)) for at in (rows - 2 * SUB, rows - SUB)]
        fill(stack, base, first, last)
        stack[base : base + LEAD, :] = jnp.where(even, got_b, got_a)[HALO - LEAD :]
        stack[base + STRIP - HALO : base + STRIP, :] = jnp.where(even, got_a, got_b)
    strips = Strips(refs[:STRIP_FIELDS], 0, STRIP // SUB, strided(stack, 0), lambda: visc[rows - KEPT - 1 : rows - KEPT, :])
    strips.prepare(False)
    run([strips])
    velocity(strips, plain, 0)
    for k in range(2):
        for e in range(2):
            out = HALO * (2 * k + e)
            vel[out : out + HALO, :] = plain[STRIP * k + OUTER[e] : STRIP * k + OUTER[e] + HALO, :]
    interior = Domain(
        (n2, n4, c, i, *refs[STRIP_FIELDS:]), 0, span, lambda a, j: field(a, pl.ds(j, SUB, stride=span))
    )
    strips.retarget(False)
    interior.retarget(False, (v0, v1))
    run([interior, strips])
    w0, w1 = interior.refs[6:8]
    for j in range(span):
        at = interior.at(j)
        value = -interior.source(FRIC, j) * (w0[at, :] * v0[at, :] + w1[at, :] * v1[at, :])
        dens[pl.ds(j, SUB, stride=span), :] = value
    density(strips, plain, 0, dens, rows)

    side = beside()
    for s in range(0, TILE, SUB):
        summed = jnp.zeros((SUB, TILE), F32)
        for row in range(s, rows, TILE):
            value = dens[row : row + SUB, :]
            if row in (0, rows - SUB):
                at = rows + OUTER[row > 0]
                value = jnp.where(ends(row > 0), dens[at : at + SUB, :], value)
            summed += value
        total[s : s + SUB, :] = jnp.where(side, 0.0, summed)
    exact = dict(precision=lax.Precision.HIGHEST, preferred_element_type=F32)
    half = jnp.dot(basis_p[...], total[...], **exact)
    wide[...] = jnp.dot(half, basis_q[...], **exact)

    corner = corners()
    for part in range(PARTS):
        for a in range(ARRAYS):
            columns = []
            for r in range(0, SLOT, SUB):
                value = edge[slot(part, a) + r : slot(part, a) + r + SUB, :]
                if part == 2:
                    moved = pltpu.roll(turned[r : r + SUB, :], (UPPER - HALO * a) % TILE, 1)
                    value = jnp.where(corner, moved, value)
                columns.append(value)
            fill(sides, strip(part, a), columns[2:], columns[:2])
            if a == VISC:
                seams[SUB * part : SUB * (part + 1), :] = columns[0]


def strip(part, a):
    return STRIP * (ARRAYS * part + a)


def corners():
    lane = lanes()
    above = (lane >= UPPER) & (lane < UPPER + HALO)
    return above | ((lane >= LOWER + INNER + HALO) & (lane < LOWER + SLOT))


def split(x, axis):
    high = x.astype(jnp.bfloat16)
    low = (x - high.astype(F32)).astype(jnp.bfloat16)
    return jnp.concatenate([high, high, low], axis=axis)


def split_constant(x, axis):
    x = np.asarray(x, np.float32)
    high = np.asarray(x, jnp.bfloat16)
    low = np.asarray(x - np.asarray(high, np.float32), jnp.bfloat16)
    return jnp.asarray(np.concatenate([high, low, high], axis=axis))


def left_right_kernel(
    _, seams, col_b, col_a, wide_in, block, basis_rows, basis_cols,
    stack, strips, coef,
    plain, *refs,
):
    even = is_even(COL_AXES)
    lane = lanes()
    row = lax.broadcasted_iota(jnp.int32, (SUB, TILE), 0)
    upper = (lane >= UPPER + HALO) & (lane < UPPER + SLOT)
    lower = (lane >= LOWER) & (lane < LOWER + INNER + HALO)
    seam_t0 = lane >= TILE - INNER - HALO
    seam_t1 = lane < INNER + HALO
    corner = corners()
    for from_left in (True, False):
        groups = []
        for g in range(2 * GROUPS + 1):
            got_a, got_b = col_a[HALO * g : HALO * (g + 1), :], col_b[HALO * g : HALO * (g + 1), :]
            groups.append(jnp.where(even, got_b, got_a) if from_left else jnp.where(even, got_a, got_b))
        tiles = []
        for part in range(2):
            tile = groups[GROUPS * part : GROUPS * (part + 1)]
            for k in range(2):
                g, h = tile[1 + 2 * k], tile[2 + 2 * k]
                if from_left:
                    tile.append(jnp.where(row >= 5, pltpu.roll(g, 6, 0), pltpu.roll(h, 4, 0)))
                else:
                    tile.append(jnp.where(row < 2, pltpu.roll(g, 2, 0), pltpu.roll(h, 4, 0)))
            tiles.append(tile)
        for a in range(ARRAYS):
            t0, t1 = tiles[0][a], tiles[1][a]
            third = jnp.where(corner, pltpu.roll(groups[-1], (UPPER - HALO * a) % TILE, 1), 0.0)
            third = jnp.where(upper, pltpu.roll(t0, UPPER + HALO, 1), third)
            third = jnp.where(lower, pltpu.roll(t1, LOWER + INNER + HALO, 1), third)
            third = jnp.where(seam_t0, t0, jnp.where(seam_t1, t1, third))
            for part, value in enumerate((t0, t1, third)):
                base = strip(part, a)
                if from_left:
                    stack[base : base + LEAD, :] = value[:LEAD]
                else:
                    stack[base + STRIP - HALO : base + STRIP, :] = value
    last = INNER - KEPT - 1
    before = [lambda at=SUB * part + last: seams[at : at + 1, :] for part in range(PARTS)]
    domains = [
        Strips(refs, STRIP * part, STRIP // SUB, strided(stack, strip(part, 0)), seam)
        for part, seam in enumerate(before)
    ]
    for domain in domains:
        domain.prepare(True)
    run(domains, True)
    for part, domain in enumerate(domains):
        velocity(domain, strips, 2 * STRIP * part)
        domain.retarget(True)
    run(domains, True)
    for part, domain in enumerate(domains):
        density(domain, strips, 2 * STRIP * part, plain, STRIP * part)

    def side(part):
        base = STRIP * part
        return jnp.concatenate(
            [plain[base + at : base + at + HALO, :] for at in OUTER], axis=0
        )

    lane = lax.broadcasted_iota(jnp.int32, (2 * HALO, TILE), 1)
    row = lax.broadcasted_iota(jnp.int32, (2 * HALO, TILE), 0)
    right = (row < NEAR) | (row >= 2 * HALO - FAR)
    straight = (lane >= HALO) & (lane < TILE - HALO)
    seam = (lane < HALO) | (lane >= TILE - HALO)
    top = (lane >= UPPER + HALO) & (lane < UPPER + 2 * HALO)
    bottom = (lane >= LOWER + INNER) & (lane < LOWER + INNER + HALO)
    dens = jnp.concatenate(
        [
            jnp.where(right & straight, side(0) + side(1), 0.0),
            jnp.where(right & (seam | top | bottom), side(2), 0.0),
        ],
        axis=1,
    )
    half = lax.dot_general(
        basis_rows[...], split(dens, 1), (((1,), (1,)), ((), ())), preferred_element_type=F32
    )
    wide = wide_in[...] + jnp.dot(split(half, 1), basis_cols[...], preferred_element_type=F32)
    lane = lanes()
    which = lax.div(lane, MODES)
    flat = wide[:SUB]
    for j in range(1, MODES // SUB):
        flat = jnp.where(which == j, wide[SUB * j : SUB * (j + 1)], flat)
    mark = jnp.broadcast_to(block[:1, :].astype(F32), (SUB, TILE))
    row = lax.broadcasted_iota(jnp.int32, (SUB, TILE), 0)
    moved = [flat] + [pltpu.roll(flat, r, 0) for r in range(1, SUB)] + [flat]
    lines = [flat] + [
        jnp.where(row < r - 1, moved[r - 1], jnp.where(row == r - 1, mark, moved[r])) for r in range(1, SUB + 1)
    ]
    cycle = SUB * (SUB + 1)
    chunk = min(4, coef.shape[0] // cycle)

    def spread(d, carry):
        for e in range(chunk):
            for r, line in enumerate(lines):
                coef[pl.ds(pl.multiple_of((d * chunk + e) * cycle + SUB * r, SUB), SUB), :] = line
        return carry

    lax.fori_loop(0, coef.shape[0] // cycle // chunk, spread, 0)


def join_kernel(v0, v1, vel_ends, strips, vel, turned):
    rows = vel.shape[1]
    span = rows // SUB
    middle = jnp.zeros((TILE - 2 * HALO, TILE), F32)
    side = beside()
    for k, v in enumerate((v0, v1)):
        for part in range(PARTS):
            base = STRIP * (2 * part + 1 - k)
            first, last = (strips[base + at : base + at + HALO, :] for at in OUTER)
            at = TILE * (2 * part + k)
            turned[at : at + TILE, :] = jnp.concatenate([first, middle, last], axis=0).T
        for row in range(0, rows, SUB):
            value = v[pl.ds(SUB * (row % span) + row // span, SUB, stride=SUB), :]
            if row in (0, rows - SUB):
                at = HALO * (2 * k + (row > 0))
                value = jnp.where(ends(row > 0), vel_ends[at : at + HALO, :], value)
            part, lane = right_part(row)
            at = TILE * (2 * part + k) + lane
            vel[k, row : row + SUB, :] = jnp.where(side, turned[at : at + SUB, :], value)


def bases():
    places = np.arange(TILE) + 0.5
    basis = np.cos(math.pi * places[:, None] * np.arange(MODES)[None, :] / TILE)
    groups = MODES // SUB
    order = np.arange(MODES).reshape(SUB, groups).T.reshape(-1)
    rows = basis[:, order] / TILE
    cols = np.tile(basis, (1, groups))
    placed = np.zeros((2 * TILE, MODES))
    for row in range(0, 2 * TILE, SUB):
        part, lane = right_part(row)
        at = lane + (TILE if part == 2 else 0)
        placed[at : at + SUB] = rows[row % TILE : row % TILE + SUB]
    outer = np.concatenate([cols[:HALO], cols[TILE - HALO :]])
    return jnp.asarray(rows.T, F32), jnp.asarray(cols, F32), split_constant(placed.T, 1), split_constant(outer, 0)


def pick_kernel(owners, every, out):
    mine = out.shape[1]
    own = lax.axis_index("own")
    wanted = [owners[pl.ds(own, 1), k : k + 1].astype(F32) for k in range(mine)]
    lines = SUB + 1
    devices = every.shape[0] // lines
    chunk = min(4, devices // SUB)

    def body(d, sums):
        sums = list(sums)
        for e in range(chunk):
            base = (d * chunk + e) * SUB * lines
            mark = every[pl.ds(base + SUB, SUB, stride=lines), :]
            hits = [mark == wanted[k] for k in range(mine)]
            for r in range(SUB):
                part = every[pl.ds(base + r, SUB, stride=lines), :]
                for k in range(mine):
                    sums[SUB * k + r] += jnp.where(hits[k], part, 0.0)
        return tuple(sums)

    start = (jnp.zeros((SUB, TILE), F32),) * (mine * SUB)
    sums = lax.fori_loop(0, devices // SUB // chunk, body, start)
    for k in range(mine):
        for r in range(SUB):
            total = jnp.sum(sums[SUB * k + r], axis=0, keepdims=True)
            out[0, k : k + 1, TILE * r : TILE * (r + 1)] = total


def local(viscosity, friction, driving, observed, ice_mask, tile_block, owner_list):
    rows, cols = viscosity.shape
    assert (rows, cols) == (2 * TILE, TILE)
    inputs = (viscosity, friction, driving, ice_mask, observed)
    near = [pltpu.with_memory_space_constraint(x, pltpu.VMEM) for x in inputs]
    basis_p, basis_q, basis_rows, basis_cols = bases()
    to_b, to_a = call(
        ends_kernel,
        "ends",
        (vmem(EDGE, cols), vmem(EDGE, cols)),
        [
            vmem(2, 2, HALO, cols),
            vmem(2, 2, 2, HALO, cols),
            pltpu.VMEM((2, HALO, cols), jnp.int32),
            pltpu.SemaphoreType.DMA((2, 5)),
        ],
        10**6,
        *(pltpu.with_memory_space_constraint(x, pltpu.HBM) for x in inputs),
    )
    row_b = swap(to_b, 0, 1)
    row_a = swap(to_a, 0, 0)
    edge, *forward = call(
        interior_kernel,
        "interior",
        (vmem(2 * PARTS * TILE, TILE),) + (vmem(rows, cols),) * 6,
        [vmem(rows, cols)] * (FIELDS - 6),
        8 * 10**6,
        *near,
    )
    to_b, to_a, turned = call(
        columns_kernel,
        "columns",
        (vmem(SENT, TILE), vmem(SENT, TILE), vmem(SLOT, TILE)),
        [],
        10**5,
        row_b,
        row_a,
        edge,
    )
    col_b = swap(to_b, 1, 1)
    col_a = swap(to_a, 1, 0)
    vel_ends, wide, sides, seams = call(
        adjoint_kernel,
        "adjoint",
        (
            vmem(4 * HALO, cols),
            vmem(MODES, TILE),
            vmem(PARTS * ARRAYS * STRIP, TILE),
            vmem(PARTS * SUB, TILE),
        ),
        [vmem(ARRAYS * STRIP, cols), vmem(2 * STRIP, cols), vmem(rows + STRIP, cols), vmem(TILE, cols)]
        + [vmem(STRIP, cols)] * STRIP_FIELDS
        + [vmem(rows, cols)] * (FIELDS - 4),
        8 * 10**6,
        row_b,
        row_a,
        *near,
        *forward,
        basis_p,
        basis_q,
        edge,
        turned,
    )
    devices = lax.axis_size(ROW_AXES + COL_AXES)
    _, strips, coef = call(
        left_right_kernel,
        "left_right",
        (
            vmem(PARTS * ARRAYS * STRIP, TILE),
            vmem(PARTS * 2 * STRIP, TILE),
            vmem(devices * (SUB + 1), TILE),
        ),
        [vmem(PARTS * STRIP, TILE)] * (STRIP_FIELDS + 1),
        4 * 10**6,
        sides,
        seams,
        col_b,
        col_a,
        wide,
        tile_block,
        basis_rows,
        basis_cols,
        aliases={0: 0},
    )
    coef = coef.reshape(devices, 1, (SUB + 1) * TILE)
    first = (lax.axis_size(COL_AXES) - 1) // 2 * lax.axis_size("own") + 1
    members = [(first + k) % devices for k in range(devices)]
    parts = lax.all_to_all(coef, ("row", "col", "own"), 0, 0, axis_index_groups=[members], tiled=True)
    state = call(
        join_kernel,
        "join",
        jax.ShapeDtypeStruct((2, rows, cols), F32),
        [vmem(2 * PARTS * TILE, TILE)],
        4 * 10**6,
        *forward[4:],
        vel_ends,
        strips,
    )
    owners = owner_list.reshape(lax.axis_size("own"), -1)
    picked = call(
        pick_kernel,
        "pick",
        jax.ShapeDtypeStruct((1, owners.shape[1], MODES * MODES), F32),
        [],
        10**5,
        owners,
        parts.reshape(-1, TILE),
    )
    return (state, picked)


def solution(mesh):
    return jax.shard_map(
        local,
        mesh=mesh,
        in_specs=(
            P(("row", "own"), "col"),
            P(("row", "own"), "col"),
            P(None, ("row", "own"), "col"),
            P(None, ("row", "own"), "col"),
            P(("row", "own"), "col"),
            P(("row", "own"), "col"),
            P(),
        ),
        out_specs=(P(None, ("row", "own"), "col"), P("own", None, None)),
        check_vma=False,
    )
```

```python
import math

import jax
import jax.numpy as jnp
import numpy as np
from jax import lax
from jax.experimental import pallas as pl
from jax.experimental.pallas import tpu as pltpu
from jax.sharding import PartitionSpec as P

TILE = 128
MODES = 32
SWEEPS = 3
SUB = 8
HALO = 8
INNER = 2 * HALO
STRIP = 40
LEAD = HALO - 1
KEPT = 12
OUTER = (LEAD, STRIP - 2 * HALO)
NEAR, FAR = 7, 6
PADDED = 48
ARRAYS = 7
VISC, FRIC, DRIV, MASK, OBS = 0, 1, 2, 4, 5
EDGE = ARRAYS * HALO
SLOT = 2 * INNER
PER = TILE // SLOT
GROUPS = 5
SENT = 2 * GROUPS * HALO + HALO
PARTS = 3
UPPER, LOWER = 32, 64
ROW_AXES = ("row", "own")
COL_AXES = ("col",)
F32 = jnp.float32
LIMIT = 40 * 1024 * 1024


def swap_rows(x, first):
    def partner(i, j, rows, cols):
        if first and i in (0, rows - 1):
            return i, j ^ 1
        return ((i + first) ^ 1) - first, j

    return exchange(x, partner)


def swap_cols(x, first):
    def partner(i, j, rows, cols):
        offset = first ^ (i % 2 == 0)
        if offset and j in (0, cols - 1):
            return i ^ 2, j
        return i, ((j + offset) ^ 1) - offset

    return exchange(x, partner)


def exchange(x, partner):
    rows, cols, owners = lax.axis_size(ROW_AXES), lax.axis_size(COL_AXES), lax.axis_size("own")

    def device(i, j):
        return (i // owners * cols + j) * owners + i % owners

    pairs = [
        (device(i, j), device(*partner(i, j, rows, cols))) for i in range(rows) for j in range(cols)
    ]
    return lax.ppermute(x, ("row", "col", "own"), pairs)


def position(axes):
    index, size = 0, 1
    for axis in axes:
        index = index * lax.axis_size(axis) + lax.axis_index(axis)
        size *= lax.axis_size(axis)
    assert size % 2 == 0
    return lax.rem(index, 2) == 0, (index == 0) | (index == size - 1)


def is_even(axes):
    return position(axes)[0]


def lanes():
    return lax.broadcasted_iota(jnp.int32, (SUB, TILE), 1)


def call(kernel, name, outs, scratch, cost, *args, aliases={}):
    return pl.pallas_call(
        kernel,
        out_shape=outs,
        scratch_shapes=scratch,
        input_output_aliases=aliases,
        compiler_params=pltpu.CompilerParams(vmem_limit_bytes=LIMIT),
        cost_estimate=pl.CostEstimate(flops=cost, bytes_accessed=cost, transcendentals=0),
        name=name,
    )(*args)


def vmem(*shape):
    return pltpu.VMEM(shape, F32)


FIELDS = 14
STRIP_FIELDS = 24


class Domain:
    def __init__(self, refs, base, span, source, seam=None):
        self.refs, self.base, self.span, self.source, self.seam = refs, base, span, source, seam

    def at(self, j):
        return pl.ds(self.base + SUB * j, SUB)

    def prepare(self, flipped):
        n2, n4, c, i, b0, b1 = self.refs[:6]
        visc = [self.source(VISC, j) for j in range(self.span)]
        for j in range(self.span):
            at = self.at(j)
            before = visc[j - 1] if j else pltpu.roll(visc[-1], 1, 0)
            if self.seam and not j:
                row = lax.broadcasted_iota(jnp.int32, (SUB, TILE), 0)
                before = jnp.where(row == SUB // 2, self.seam(), before)
            pair = visc[j] + before
            fric = self.source(FRIC, j)
            diag = 1.25 * (pair + pltpu.roll(pair, 1, 1)) + fric
            on = self.source(MASK, j) > 0.0
            inv = jnp.where(on, 0.5 / jnp.where(on, diag, 1.0), 0.0)
            half = 0.5 * visc[j]
            n2[at, :] = half
            n4[at, :] = 0.5 * half
            c[at, :] = 1.0 - fric * inv
            i[at, :] = inv
            for k, b in enumerate((b0, b1)):
                value = inv * self.source(DRIV + (1 - k if flipped else k), j)
                b[at, :] = value
                self.write(k, at, value + value)

    def write(self, k, at, value):
        self.refs[6 + k][at, :] = value
        self.refs[8 + k][at, :] = pltpu.roll(value, TILE - 1, 1)

    def retarget(self, flipped, velocity=None):
        i, b0, b1 = self.refs[3:6]
        w0, w1 = velocity or self.refs[6:8]
        for j in range(self.span):
            at = self.at(j)
            for k, (b, w) in enumerate(((b0, w0), (b1, w1))):
                value = i[at, :] * (w[at, :] - self.source(OBS + (1 - k if flipped else k), j))
                b[at, :] = value
                self.write(k, at, value + value)

    def differences(self):
        n2, n4 = self.refs[:2]
        fields = self.refs[6:10]
        parts = self.refs[10:14]

        def corners(j, here, below):
            w0, w1, r0, r1 = here
            v0, v1, s0, s1 = below
            a1, a2 = s0 - w0, v0 - r0
            e1, e2 = s1 - w1, v1 - r1
            x, y = a1 + a2, e1 - e2
            q = (a1 - a2) + (e1 + e2)
            both = x + y
            at = self.at(j)
            half = n2[at, :]
            return half * (both + x), n4[at, :] * q, half * (both + y)

        def load(j):
            at = self.at(j)
            return [field[at, :] for field in fields]

        top = load(0)
        last = corners(self.span - 1, load(self.span - 1), [pltpu.roll(v, SUB - 1, 0) for v in top])
        up = [pltpu.roll(v, 1, 0) for v in last]
        here = top
        for j in range(self.span):
            at = self.at(j)
            if j < self.span - 1:
                below = load(j + 1)
                p, q, r = corners(j, here, below)
                here = below
            else:
                p, q, r = last
            g, t = up[0] - p, up[1] + q
            gq, tr = up[1] - q, up[2] + r
            parts[0][at, :] = g - t
            parts[1][at, :] = gq - tr
            parts[2][at, :] = pltpu.roll(g + t, 1, 1)
            parts[3][at, :] = pltpu.roll(gq + tr, 1, 1)
            up = (p, q, r)

    def update(self):
        c, i, b0, b1, w0, w1 = self.refs[2:8]
        parts = self.refs[10:14]
        for j in range(self.span):
            at = self.at(j)
            cv, iv = c[at, :], i[at, :]
            for k, (b, w) in enumerate(((b0, w0), (b1, w1))):
                value = (cv * w[at, :] + b[at, :]) - iv * (parts[k][at, :] + parts[k + 2][at, :])
                self.write(k, at, value)


class Strips(Domain):
    def prepare(self, flipped):
        super().prepare(flipped)
        for j in range(self.span):
            at = self.at(j)
            for now, later in zip(self.refs[2:6], self.refs[10:14]):
                later[at, :] = pltpu.roll(now[at, :], TILE - 1, 1)
        for now, before in zip(self.refs[:2], self.refs[14:16]):
            before[self.at(0), :] = pltpu.roll(now[self.at(self.span - 1), :], 1, 0)

    def retarget(self, flipped, velocity=None):
        super().retarget(flipped, velocity)
        for j in range(self.span):
            at = self.at(j)
            for now, later in zip(self.refs[4:6], self.refs[12:14]):
                later[at, :] = pltpu.roll(now[at, :], TILE - 1, 1)

    def differences(self):
        fields = self.refs[6:10]
        kept, turned, kept_next, turned_next = (self.refs[16 + 2 * k : 18 + 2 * k] for k in range(4))

        def corners(halves, quarters, j, here, below):
            w0, w1, r0, r1 = here
            v0, v1, s0, s1 = below
            a1, a2 = s0 - w0, v0 - r0
            e1, e2 = s1 - w1, v1 - r1
            x, y = a1 + a2, e1 - e2
            q = (a1 - a2) + (e1 + e2)
            both = x + y
            at = self.at(j)
            half = halves[at, :]
            return half * (both + x), quarters[at, :] * q, half * (both + y)

        def load(j):
            at = self.at(j)
            return [field[at, :] for field in fields]

        top, end = load(0), load(self.span - 1)
        up = corners(*self.refs[14:16], 0, [pltpu.roll(v, 1, 0) for v in end], top)
        here = top
        for j in range(self.span):
            at = self.at(j)
            below = load(j + 1) if j < self.span - 1 else [pltpu.roll(v, SUB - 1, 0) for v in top]
            p, q, r = corners(*self.refs[:2], j, here, below)
            g, t = up[0] - p, up[1] + q
            gq, tr = up[1] - q, up[2] + r
            for k, (stay, move) in enumerate(((g - t, g + t), (gq - tr, gq + tr))):
                kept[k][at, :] = stay
                turned_next[k][at, :] = move
                turned[k][at, :] = pltpu.roll(move, 1, 1)
                kept_next[k][at, :] = pltpu.roll(stay, TILE - 1, 1)
            up, here = (p, q, r), below

    def update(self):
        for first, offset, parts in ((2, 6, (16, 18)), (10, 8, (20, 22))):
            c, i, *b = self.refs[first : first + 4]
            for j in range(self.span):
                at = self.at(j)
                cv, iv = c[at, :], i[at, :]
                for k in range(2):
                    w = self.refs[offset + k]
                    change = self.refs[parts[0] + k][at, :] + self.refs[parts[1] + k][at, :]
                    w[at, :] = (cv * w[at, :] + b[k][at, :]) - iv * change


def run(domains, written_out=False):
    def body(_, carry):
        for domain in domains:
            domain.differences()
        for domain in domains:
            domain.update()
        return carry

    if written_out:
        for k in range(SWEEPS):
            body(k, 0)
    else:
        lax.fori_loop(0, SWEEPS, body, 0)


def ends_kernel(visc, fric, driv, mask, obs, to_b, to_a, one, two, flags, sems):
    rows = visc.shape[0]
    copies = []
    for e, first in enumerate((0, rows - HALO)):
        at = pl.ds(first, HALO)
        pieces = [
            (visc.at[at], one.at[e, 0]),
            (fric.at[at], one.at[e, 1]),
            (driv.at[:, at], two.at[e, 0]),
            (mask.at[at], flags.at[e]),
            (obs.at[:, at], two.at[e, 1]),
        ]
        for n, (source, place) in enumerate(pieces):
            copies.append(pltpu.make_async_copy(source, place, sems.at[e, n]))
    for copy in copies:
        copy.start()
    for copy in copies:
        copy.wait()
    even, at_end = position(ROW_AXES)

    def edge(e):
        return [one[e, 0], one[e, 1], two[e, 0, 0], two[e, 0, 1], flags[e].astype(F32), two[e, 1, 0], two[e, 1, 1]]

    for a, (head, tail) in enumerate(zip(edge(0), edge(1))):
        at = slice(HALO * a, HALO * (a + 1))
        to_a[at, :] = jnp.where(even, tail, head)
        to_b[at, :] = jnp.where(at_end, 0.0, jnp.where(even, head, tail))


def field_of(visc, fric, driv, mask, obs):
    def field(a, at):
        if a == MASK:
            return mask[at, :].astype(F32)
        if a >= OBS:
            return obs[a - OBS, at, :]
        if a >= DRIV:
            return driv[a - DRIV, at, :]
        return (visc, fric)[a][at, :]

    return field


def first_row(part, lane):
    if part < 2:
        return TILE * part + lane
    if lane < INNER + HALO:
        return TILE + lane
    if lane >= TILE - INNER - HALO:
        return lane
    if UPPER + HALO <= lane < UPPER + SLOT:
        return lane - UPPER - HALO
    if LOWER <= lane < LOWER + INNER + HALO:
        return 2 * TILE - INNER - HALO + lane - LOWER
    return None


def right_part(row):
    seam = TILE - HALO <= row < TILE + HALO
    part = 2 if seam or row == 0 or row == 2 * TILE - HALO else row // TILE
    return part, [lane for lane in range(0, TILE, SUB) if first_row(part, lane) == row][-1]


def slot(part, a):
    return TILE * (2 * part + a // PER) + SLOT * (a % PER)


def interior_kernel(visc, fric, driv, mask, obs, edge, n2, n4, c, i, v0, v1, *refs):
    span = visc.shape[0] // SUB
    field = field_of(visc, fric, driv, mask, obs)
    lane = lanes()
    for part in range(PARTS):
        for m in range(-(-ARRAYS // PER)):
            strips = []
            for at in range(0, TILE, SUB):
                row = first_row(part, at)
                packed = jnp.zeros((SUB, TILE), F32)
                if row is not None:
                    for k in range(min(PER, ARRAYS - PER * m)):
                        value = field(PER * m + k, slice(row, row + SUB))
                        moved = pltpu.roll(value, (SLOT * k + INNER) % TILE, 1)
                        packed = jnp.where(lax.div(lane, SLOT) == k, moved, packed)
                strips.append(packed)
            base = TILE * (2 * part + m)
            edge[base : base + TILE, :] = jnp.concatenate(strips, axis=0).T
    refs = (n2, n4, c, i, *refs[:2], v0, v1, *refs[2:])
    domain = Domain(refs, 0, span, lambda a, j: field(a, pl.ds(j, SUB, stride=span)))
    domain.prepare(False)
    run([domain])


def columns_kernel(row_b, row_a, edge, to_b, to_a, turned):
    even = is_even(ROW_AXES)
    above = jnp.where(even, row_b[...], row_a[...])
    below = jnp.where(even, row_a[...], row_b[...])
    halo = jnp.concatenate([above, below, jnp.zeros((TILE - 2 * EDGE, TILE), F32)], axis=0).T
    turned[:INNER, :] = halo[TILE - INNER :]
    turned[INNER:, :] = halo[:INNER]
    row_even, (col_even, at_end) = even, position(COL_AXES)
    even = row_even != col_even
    row = lax.broadcasted_iota(jnp.int32, (SUB, TILE), 0)

    def put(out, right, left):
        right = pltpu.roll(right, LEAD, 0)
        to_a[out : out + HALO, :] = jnp.where(at_end & row_even, 0.0, jnp.where(even, right, left))
        to_b[out : out + HALO, :] = jnp.where(at_end & ~row_even, 0.0, jnp.where(even, left, right))

    for part in range(2):
        right, left = [], []
        for a in range(ARRAYS):
            at = slot(part, a) + INNER
            right.append(edge[at - HALO : at, :])
            left.append(edge[at : at + HALO, :])
        for k in range(2):
            seen_r, seen_l = right[OBS + k], left[OBS + k]
            g = 1 + 2 * k
            right[g] = jnp.where(row < 2, pltpu.roll(seen_r, 2, 0), right[g])
            right[g + 1] = jnp.where(row < 2, pltpu.roll(seen_r, 4, 0), right[g + 1])
            left[g] = jnp.where(row >= 6, pltpu.roll(seen_l, 6, 0), left[g])
            left[g + 1] = jnp.where(row >= 6, pltpu.roll(seen_l, 4, 0), left[g + 1])
        for g in range(GROUPS):
            put(HALO * (GROUPS * part + g), right[g], left[g])
    put(2 * GROUPS * HALO, halo[TILE - HALO :], halo[:HALO])


def strided(stack, base):
    span = STRIP // SUB
    return lambda a, j: stack[pl.ds(base + STRIP * a + j, SUB, stride=span), :]


def fill(stack, base, first, last):
    row = lax.broadcasted_iota(jnp.int32, (SUB, TILE), 0)
    one, two = (pltpu.roll(value, LEAD, 0) for value in first)
    mixed = [jnp.where(row == LEAD, two, one), jnp.where(row < SUB // 2, two, last[0])]
    for k, value in enumerate((one, *mixed, last[1])):
        stack[base + SUB * k : base + SUB * (k + 1), :] = value


def velocity(domain, plain, base):
    for j in range(domain.span):
        at = domain.at(j)
        for k in range(2):
            plain[pl.ds(base + STRIP * k + j, SUB, stride=domain.span), :] = domain.refs[6 + k][at, :]


def density(domain, plain, base, j):
    at = domain.at(j)
    w0, w1 = (w[at, :] for w in domain.refs[6:8])
    v0, v1 = (plain[pl.ds(base + STRIP * k + j, SUB, stride=domain.span), :] for k in range(2))
    return -domain.source(FRIC, j) * (w0 * v0 + w1 * v1)


def beside():
    lane = lanes()
    return (lane < NEAR) | (lane >= TILE - FAR)


def ends(second):
    row = lax.broadcasted_iota(jnp.int32, (SUB, TILE), 0)
    return row >= SUB - FAR if second else row < NEAR


def adjoint_kernel(
    row_b, row_a, visc, fric, driv, mask, obs, n2, n4, c, i, v0, v1, basis_p, basis_q, edge, turned,
    vel, wide, sides, seams,
    stack, plain, dens, total, *refs,
):
    rows = visc.shape[0]
    span = rows // SUB
    even = is_even(ROW_AXES)
    field = field_of(visc, fric, driv, mask, obs)
    for a in range(ARRAYS):
        at = slice(HALO * a, HALO * (a + 1))
        got_a, got_b = row_a[at, :], row_b[at, :]
        base = STRIP * a
        first = [field(a, slice(at, at + SUB)) for at in (0, SUB)]
        last = [field(a, slice(at, at + SUB)) for at in (rows - 2 * SUB, rows - SUB)]
        fill(stack, base, first, last)
        stack[base : base + LEAD, :] = jnp.where(even, got_b, got_a)[HALO - LEAD :]
        stack[base + STRIP - HALO : base + STRIP, :] = jnp.where(even, got_a, got_b)
    strips = Strips(refs[:STRIP_FIELDS], 0, STRIP // SUB, strided(stack, 0), lambda: visc[rows - KEPT - 1 : rows - KEPT, :])
    strips.prepare(False)
    run([strips])
    velocity(strips, plain, 0)
    for k in range(2):
        for e in range(2):
            out = HALO * (2 * k + e)
            vel[out : out + HALO, :] = plain[STRIP * k + OUTER[e] : STRIP * k + OUTER[e] + HALO, :]
    interior = Domain(
        (n2, n4, c, i, *refs[STRIP_FIELDS:]), 0, span, lambda a, j: field(a, pl.ds(j, SUB, stride=span))
    )
    strips.retarget(False)
    interior.retarget(False, (v0, v1))
    run([interior, strips])
    w0, w1 = interior.refs[6:8]
    for j in range(span):
        at = interior.at(j)
        value = -interior.source(FRIC, j) * (w0[at, :] * v0[at, :] + w1[at, :] * v1[at, :])
        dens[pl.ds(j, SUB, stride=span), :] = value
    for j in range(strips.span):
        dens[pl.ds(rows + j, SUB, stride=strips.span), :] = density(strips, plain, 0, j)

    side = beside()
    for s in range(0, TILE, SUB):
        summed = jnp.zeros((SUB, TILE), F32)
        for row in range(s, rows, TILE):
            value = dens[row : row + SUB, :]
            if row in (0, rows - SUB):
                at = rows + OUTER[row > 0]
                value = jnp.where(ends(row > 0), dens[at : at + SUB, :], value)
            summed += value
        total[s : s + SUB, :] = jnp.where(side, 0.0, summed)
    exact = dict(precision=lax.Precision.HIGHEST, preferred_element_type=F32)
    half = jnp.dot(basis_p[...], total[...], **exact)
    wide[...] = jnp.dot(half, basis_q[...], **exact)

    corner = corners()
    for part in range(PARTS):
        for a in range(ARRAYS):
            columns = []
            for r in range(0, SLOT, SUB):
                value = edge[slot(part, a) + r : slot(part, a) + r + SUB, :]
                if part == 2:
                    moved = pltpu.roll(turned[r : r + SUB, :], (UPPER - HALO * a) % TILE, 1)
                    value = jnp.where(corner, moved, value)
                columns.append(value)
            fill(sides, strip(part, a), columns[2:], columns[:2])
            if a == VISC:
                seams[SUB * part : SUB * (part + 1), :] = columns[0]


def strip(part, a):
    return STRIP * (ARRAYS * part + a)


def corners():
    lane = lanes()
    above = (lane >= UPPER) & (lane < UPPER + HALO)
    return above | ((lane >= LOWER + INNER + HALO) & (lane < LOWER + SLOT))


def split(x, axis):
    high = x.astype(jnp.bfloat16)
    low = (x - high.astype(F32)).astype(jnp.bfloat16)
    return jnp.concatenate([high, high, low], axis=axis)


def split_constant(x, axis):
    x = np.asarray(x, np.float32)
    high = np.asarray(x, jnp.bfloat16)
    low = np.asarray(x - np.asarray(high, np.float32), jnp.bfloat16)
    return jnp.asarray(np.concatenate([high, low, high], axis=axis))


def left_right_kernel(
    _, seams, col_b, col_a, wide_in, block, basis_rows, basis_cols,
    stack, strips, coef,
    *refs,
):
    even = is_even(COL_AXES) != is_even(ROW_AXES)
    lane = lanes()
    row = lax.broadcasted_iota(jnp.int32, (SUB, TILE), 0)
    upper = (lane >= UPPER + HALO) & (lane < UPPER + SLOT)
    lower = (lane >= LOWER) & (lane < LOWER + INNER + HALO)
    seam_t0 = lane >= TILE - INNER - HALO
    seam_t1 = lane < INNER + HALO
    corner = corners()
    for from_left in (True, False):
        groups = []
        for g in range(2 * GROUPS + 1):
            got_a, got_b = col_a[HALO * g : HALO * (g + 1), :], col_b[HALO * g : HALO * (g + 1), :]
            groups.append(jnp.where(even, got_b, got_a) if from_left else jnp.where(even, got_a, got_b))
        tiles = []
        for part in range(2):
            tile = groups[GROUPS * part : GROUPS * (part + 1)]
            for k in range(2):
                g, h = tile[1 + 2 * k], tile[2 + 2 * k]
                if from_left:
                    tile.append(jnp.where(row >= 5, pltpu.roll(g, 6, 0), pltpu.roll(h, 4, 0)))
                else:
                    tile.append(jnp.where(row < 2, pltpu.roll(g, 2, 0), pltpu.roll(h, 4, 0)))
            tiles.append(tile)
        for a in range(ARRAYS):
            t0, t1 = tiles[0][a], tiles[1][a]
            third = jnp.where(corner, pltpu.roll(groups[-1], (UPPER - HALO * a) % TILE, 1), 0.0)
            third = jnp.where(upper, pltpu.roll(t0, UPPER + HALO, 1), third)
            third = jnp.where(lower, pltpu.roll(t1, LOWER + INNER + HALO, 1), third)
            third = jnp.where(seam_t0, t0, jnp.where(seam_t1, t1, third))
            for part, value in enumerate((t0, t1, third)):
                base = strip(part, a)
                if from_left:
                    stack[base : base + LEAD, :] = value[:LEAD]
                else:
                    stack[base + STRIP - HALO : base + STRIP, :] = value
    last = INNER - KEPT - 1
    before = [lambda at=SUB * part + last: seams[at : at + 1, :] for part in range(PARTS)]
    domains = [
        Strips(refs, STRIP * part, STRIP // SUB, strided(stack, strip(part, 0)), seam)
        for part, seam in enumerate(before)
    ]
    for domain in domains:
        domain.prepare(True)
    run(domains, True)
    for part, domain in enumerate(domains):
        velocity(domain, strips, 2 * STRIP * part)
        domain.retarget(True)
    run(domains, True)
    straight = (lane >= HALO) & (lane < TILE - HALO)
    seam = (lane < HALO) | (lane >= TILE - HALO)
    top = (lane >= UPPER + HALO) & (lane < UPPER + 2 * HALO)
    bottom = (lane >= LOWER + INNER) & (lane < LOWER + INNER + HALO)
    span = STRIP // SUB
    dens = []
    for j in range(span):
        at = span * row + j
        right = ((at >= OUTER[0]) & (at < OUTER[0] + NEAR)) | (
            (at >= OUTER[1] + HALO - FAR) & (at < OUTER[1] + HALO)
        )
        value = [density(domain, strips, 2 * STRIP * part, j) for part, domain in enumerate(domains)]
        both = jnp.where(right & straight, value[0] + value[1], 0.0)
        dens.append(jnp.concatenate([both, jnp.where(right & (seam | top | bottom), value[2], 0.0)], axis=1))
    dens = jnp.concatenate(dens + [jnp.zeros((PADDED - STRIP, 2 * TILE), F32)], axis=0)
    half = lax.dot_general(
        basis_rows[...], split(dens, 1), (((1,), (1,)), ((), ())), preferred_element_type=F32
    )
    wide = wide_in[...] + jnp.dot(split(half, 1), basis_cols[...], preferred_element_type=F32)
    which = lax.div(lane, MODES)
    flat = wide[:SUB]
    for j in range(1, MODES // SUB):
        flat = jnp.where(which == j, wide[SUB * j : SUB * (j + 1)], flat)
    mark = jnp.broadcast_to(block[:1, :].astype(F32), (SUB, TILE))
    moved = [flat] + [pltpu.roll(flat, r, 0) for r in range(1, SUB)] + [flat]
    lines = [flat] + [
        jnp.where(row < r - 1, moved[r - 1], jnp.where(row == r - 1, mark, moved[r])) for r in range(1, SUB + 1)
    ]
    cycle = SUB * (SUB + 1)
    chunk = min(4, coef.shape[0] // cycle)

    def spread(d, carry):
        for e in range(chunk):
            for r, line in enumerate(lines):
                coef[pl.ds(pl.multiple_of((d * chunk + e) * cycle + SUB * r, SUB), SUB), :] = line
        return carry

    lax.fori_loop(0, coef.shape[0] // cycle // chunk, spread, 0)


def join_kernel(v0, v1, vel_ends, strips, vel, turned):
    rows = vel.shape[1]
    span = rows // SUB
    middle = jnp.zeros((TILE - 2 * HALO, TILE), F32)
    side = beside()
    for k, v in enumerate((v0, v1)):
        for part in range(PARTS):
            base = STRIP * (2 * part + 1 - k)
            first, last = (strips[base + at : base + at + HALO, :] for at in OUTER)
            at = TILE * (2 * part + k)
            turned[at : at + TILE, :] = jnp.concatenate([first, middle, last], axis=0).T
        for row in range(0, rows, SUB):
            value = v[pl.ds(SUB * (row % span) + row // span, SUB, stride=SUB), :]
            if row in (0, rows - SUB):
                at = HALO * (2 * k + (row > 0))
                value = jnp.where(ends(row > 0), vel_ends[at : at + HALO, :], value)
            part, lane = right_part(row)
            at = TILE * (2 * part + k) + lane
            vel[k, row : row + SUB, :] = jnp.where(side, turned[at : at + SUB, :], value)


def bases():
    places = np.arange(TILE) + 0.5
    basis = np.cos(math.pi * places[:, None] * np.arange(MODES)[None, :] / TILE)
    groups = MODES // SUB
    order = np.arange(MODES).reshape(SUB, groups).T.reshape(-1)
    rows = basis[:, order] / TILE
    cols = np.tile(basis, (1, groups))
    placed = np.zeros((2 * TILE, MODES))
    for row in range(0, 2 * TILE, SUB):
        part, lane = right_part(row)
        at = lane + (TILE if part == 2 else 0)
        placed[at : at + SUB] = rows[row % TILE : row % TILE + SUB]
    outer = np.zeros((PADDED, TILE))
    for j in range(STRIP // SUB):
        for k in range(SUB):
            at = STRIP // SUB * k + j
            if OUTER[0] <= at < OUTER[0] + NEAR:
                outer[SUB * j + k] = cols[at - OUTER[0]]
            if OUTER[1] + HALO - FAR <= at < OUTER[1] + HALO:
                outer[SUB * j + k] = cols[TILE - HALO + at - OUTER[1]]
    return jnp.asarray(rows.T, F32), jnp.asarray(cols, F32), split_constant(placed.T, 1), split_constant(outer, 0)


def pick_kernel(owners, every, out):
    mine = out.shape[1]
    own = lax.axis_index("own")
    wanted = [owners[pl.ds(own, 1), k : k + 1].astype(F32) for k in range(mine)]
    lines = SUB + 1
    devices = every.shape[0] // lines
    chunk = min(4, devices // SUB)

    def body(d, sums):
        sums = list(sums)
        for e in range(chunk):
            base = (d * chunk + e) * SUB * lines
            mark = every[pl.ds(base + SUB, SUB, stride=lines), :]
            hits = [mark == wanted[k] for k in range(mine)]
            for r in range(SUB):
                part = every[pl.ds(base + r, SUB, stride=lines), :]
                for k in range(mine):
                    sums[SUB * k + r] += jnp.where(hits[k], part, 0.0)
        return tuple(sums)

    start = (jnp.zeros((SUB, TILE), F32),) * (mine * SUB)
    sums = lax.fori_loop(0, devices // SUB // chunk, body, start)
    for k in range(mine):
        for r in range(SUB):
            total = jnp.sum(sums[SUB * k + r], axis=0, keepdims=True)
            out[0, k : k + 1, TILE * r : TILE * (r + 1)] = total


def local(viscosity, friction, driving, observed, ice_mask, tile_block, owner_list):
    rows, cols = viscosity.shape
    assert (rows, cols) == (2 * TILE, TILE)
    inputs = (viscosity, friction, driving, ice_mask, observed)
    near = [pltpu.with_memory_space_constraint(x, pltpu.VMEM) for x in inputs]
    basis_p, basis_q, basis_rows, basis_cols = bases()
    to_b, to_a = call(
        ends_kernel,
        "ends",
        (vmem(EDGE, cols), vmem(EDGE, cols)),
        [
            vmem(2, 2, HALO, cols),
            vmem(2, 2, 2, HALO, cols),
            pltpu.VMEM((2, HALO, cols), jnp.int32),
            pltpu.SemaphoreType.DMA((2, 5)),
        ],
        10**6,
        *(pltpu.with_memory_space_constraint(x, pltpu.HBM) for x in inputs),
    )
    row_b = swap_rows(to_b, 1)
    row_a = swap_rows(to_a, 0)
    edge, *forward = call(
        interior_kernel,
        "interior",
        (vmem(2 * PARTS * TILE, TILE),) + (vmem(rows, cols),) * 6,
        [vmem(rows, cols)] * (FIELDS - 6),
        8 * 10**6,
        *near,
    )
    to_b, to_a, turned = call(
        columns_kernel,
        "columns",
        (vmem(SENT, TILE), vmem(SENT, TILE), vmem(SLOT, TILE)),
        [],
        10**5,
        row_b,
        row_a,
        edge,
    )
    col_a = swap_cols(to_a, 0)
    col_b = swap_cols(to_b, 1)
    vel_ends, wide, sides, seams = call(
        adjoint_kernel,
        "adjoint",
        (
            vmem(4 * HALO, cols),
            vmem(MODES, TILE),
            vmem(PARTS * ARRAYS * STRIP, TILE),
            vmem(PARTS * SUB, TILE),
        ),
        [vmem(ARRAYS * STRIP, cols), vmem(2 * STRIP, cols), vmem(rows + STRIP, cols), vmem(TILE, cols)]
        + [vmem(STRIP, cols)] * STRIP_FIELDS
        + [vmem(rows, cols)] * (FIELDS - 4),
        8 * 10**6,
        row_b,
        row_a,
        *near,
        *forward,
        basis_p,
        basis_q,
        edge,
        turned,
    )
    devices = lax.axis_size(ROW_AXES + COL_AXES)
    _, strips, coef = call(
        left_right_kernel,
        "left_right",
        (
            vmem(PARTS * ARRAYS * STRIP, TILE),
            vmem(PARTS * 2 * STRIP, TILE),
            vmem(devices * (SUB + 1), TILE),
        ),
        [vmem(PARTS * STRIP, TILE)] * STRIP_FIELDS,
        4 * 10**6,
        sides,
        seams,
        col_b,
        col_a,
        wide,
        tile_block,
        basis_rows,
        basis_cols,
        aliases={0: 0},
    )
    coef = coef.reshape(devices, 1, (SUB + 1) * TILE)
    parts = lax.all_to_all(coef, ROW_AXES + COL_AXES, 0, 0, tiled=True)
    state = call(
        join_kernel,
        "join",
        jax.ShapeDtypeStruct((2, rows, cols), F32),
        [vmem(2 * PARTS * TILE, TILE)],
        4 * 10**6,
        *forward[4:],
        vel_ends,
        strips,
    )
    owners = owner_list.reshape(lax.axis_size("own"), -1)
    picked = call(
        pick_kernel,
        "pick",
        jax.ShapeDtypeStruct((1, owners.shape[1], MODES * MODES), F32),
        [],
        10**5,
        owners,
        parts.reshape(-1, TILE),
    )
    return (state, picked)


def solution(mesh):
    return jax.shard_map(
        local,
        mesh=mesh,
        in_specs=(
            P(("row", "own"), "col"),
            P(("row", "own"), "col"),
            P(None, ("row", "own"), "col"),
            P(None, ("row", "own"), "col"),
            P(("row", "own"), "col"),
            P(("row", "own"), "col"),
            P(),
        ),
        out_specs=(P(None, ("row", "own"), "col"), P("own", None, None)),
        check_vma=False,
    )
```

```python
import math

import jax
import jax.numpy as jnp
import numpy as np
from jax import lax
from jax.experimental import pallas as pl
from jax.experimental.pallas import tpu as pltpu
from jax.sharding import PartitionSpec as P

TILE = 128
MODES = 32
SWEEPS = 3
SUB = 8
HALO = 8
INNER = 2 * HALO
STRIP = 40
LEAD = HALO - 1
KEPT = 12
OUTER = (LEAD, STRIP - 2 * HALO)
NEAR, FAR = 7, 6
ARRAYS = 7
VISC, FRIC, DRIV, MASK, OBS = 0, 1, 2, 4, 5
EDGE = ARRAYS * HALO
SLOT = 2 * INNER
PER = TILE // SLOT
GROUPS = 5
SENT = 2 * GROUPS * HALO + HALO
PARTS = 3
UPPER, LOWER = 32, 64
ROW_AXES = ("row", "own")
COL_AXES = ("col",)
F32 = jnp.float32
LIMIT = 40 * 1024 * 1024


def swap(x, axis, first):
    sizes = lax.axis_size(ROW_AXES), lax.axis_size(COL_AXES)
    owners = lax.axis_size("own")

    def device(i, j):
        return (i // owners * sizes[1] + j) * owners + i % owners

    pairs = []
    for i in range(sizes[0]):
        for j in range(sizes[1]):
            place = [i, j]
            if first and place[axis] in (0, sizes[axis] - 1):
                place[1 - axis] ^= 1
            else:
                place[axis] = ((place[axis] + first) ^ 1) - first
            pairs.append((device(i, j), device(*place)))
    return lax.ppermute(x, ("row", "col", "own"), pairs)


def position(axes):
    index, size = 0, 1
    for axis in axes:
        index = index * lax.axis_size(axis) + lax.axis_index(axis)
        size *= lax.axis_size(axis)
    assert size % 2 == 0
    return lax.rem(index, 2) == 0, (index == 0) | (index == size - 1)


def is_even(axes):
    return position(axes)[0]


def lanes():
    return lax.broadcasted_iota(jnp.int32, (SUB, TILE), 1)


def call(kernel, name, outs, scratch, cost, *args, aliases={}):
    return pl.pallas_call(
        kernel,
        out_shape=outs,
        scratch_shapes=scratch,
        input_output_aliases=aliases,
        compiler_params=pltpu.CompilerParams(vmem_limit_bytes=LIMIT),
        cost_estimate=pl.CostEstimate(flops=cost, bytes_accessed=cost, transcendentals=0),
        name=name,
    )(*args)


def vmem(*shape):
    return pltpu.VMEM(shape, F32)


FIELDS = 14
STRIP_FIELDS = 16


class Domain:
    def __init__(self, refs, base, span, source, seam=None):
        self.refs, self.base, self.span, self.source, self.seam = refs, base, span, source, seam

    def at(self, j):
        return pl.ds(self.base + SUB * j, SUB)

    def prepare(self, flipped):
        n2, n4, c, i, b0, b1 = self.refs[:6]
        visc = [self.source(VISC, j) for j in range(self.span)]
        for j in range(self.span):
            at = self.at(j)
            before = visc[j - 1] if j else pltpu.roll(visc[-1], 1, 0)
            if self.seam and not j:
                row = lax.broadcasted_iota(jnp.int32, (SUB, TILE), 0)
                before = jnp.where(row == SUB // 2, self.seam(), before)
            pair = visc[j] + before
            fric = self.source(FRIC, j)
            diag = 1.25 * (pair + pltpu.roll(pair, 1, 1)) + fric
            on = self.source(MASK, j) > 0.0
            inv = jnp.where(on, 0.5 / jnp.where(on, diag, 1.0), 0.0)
            half = 0.5 * visc[j]
            n2[at, :] = half
            n4[at, :] = 0.5 * half
            c[at, :] = 1.0 - fric * inv
            i[at, :] = inv
            for k, b in enumerate((b0, b1)):
                value = inv * self.source(DRIV + (1 - k if flipped else k), j)
                b[at, :] = value
                self.write(k, at, value + value)

    def write(self, k, at, value):
        self.refs[6 + k][at, :] = value
        self.refs[8 + k][at, :] = pltpu.roll(value, TILE - 1, 1)

    def retarget(self, flipped, velocity=None):
        i, b0, b1 = self.refs[3:6]
        w0, w1 = velocity or self.refs[6:8]
        for j in range(self.span):
            at = self.at(j)
            for k, (b, w) in enumerate(((b0, w0), (b1, w1))):
                value = i[at, :] * (w[at, :] - self.source(OBS + (1 - k if flipped else k), j))
                b[at, :] = value
                self.write(k, at, value + value)

    def sweep(self):
        self.differences()
        self.update()

    def differences(self):
        n2, n4 = self.refs[:2]
        fields = self.refs[6:10]
        parts = self.refs[10:14]

        def corners(j, here, below):
            w0, w1, r0, r1 = here
            v0, v1, s0, s1 = below
            a1, a2 = s0 - w0, v0 - r0
            e1, e2 = s1 - w1, v1 - r1
            x, y = a1 + a2, e1 - e2
            q = (a1 - a2) + (e1 + e2)
            both = x + y
            at = self.at(j)
            half = n2[at, :]
            return half * (both + x), n4[at, :] * q, half * (both + y)

        def load(j):
            at = self.at(j)
            return [field[at, :] for field in fields]

        top = load(0)
        last = corners(self.span - 1, load(self.span - 1), [pltpu.roll(v, SUB - 1, 0) for v in top])
        up = [pltpu.roll(v, 1, 0) for v in last]
        here = top
        for j in range(self.span):
            at = self.at(j)
            if j < self.span - 1:
                below = load(j + 1)
                p, q, r = corners(j, here, below)
                here = below
            else:
                p, q, r = last
            g, t = up[0] - p, up[1] + q
            gq, tr = up[1] - q, up[2] + r
            parts[0][at, :] = g - t
            parts[1][at, :] = gq - tr
            parts[2][at, :] = pltpu.roll(g + t, 1, 1)
            parts[3][at, :] = pltpu.roll(gq + tr, 1, 1)
            up = (p, q, r)

    def update(self):
        c, i, b0, b1, w0, w1 = self.refs[2:8]
        parts = self.refs[10:14]
        for j in range(self.span):
            at = self.at(j)
            cv, iv = c[at, :], i[at, :]
            for k, (b, w) in enumerate(((b0, w0), (b1, w1))):
                value = (cv * w[at, :] + b[at, :]) - iv * (parts[k][at, :] + parts[k + 2][at, :])
                self.write(k, at, value)


class Strips(Domain):
    def prepare(self, flipped):
        super().prepare(flipped)
        for j in range(self.span):
            at = self.at(j)
            for now, later in zip(self.refs[2:6], self.refs[10:14]):
                later[at, :] = pltpu.roll(now[at, :], TILE - 1, 1)
        for now, before in zip(self.refs[:2], self.refs[14:16]):
            before[self.at(0), :] = pltpu.roll(now[self.at(self.span - 1), :], 1, 0)

    def retarget(self, flipped, velocity=None):
        super().retarget(flipped, velocity)
        for j in range(self.span):
            at = self.at(j)
            for now, later in zip(self.refs[4:6], self.refs[12:14]):
                later[at, :] = pltpu.roll(now[at, :], TILE - 1, 1)

    def sweep(self):
        fields = self.refs[6:10]

        def corners(halves, quarters, j, here, below):
            w0, w1, r0, r1 = here
            v0, v1, s0, s1 = below
            a1, a2 = s0 - w0, v0 - r0
            e1, e2 = s1 - w1, v1 - r1
            x, y = a1 + a2, e1 - e2
            q = (a1 - a2) + (e1 + e2)
            both = x + y
            at = self.at(j)
            half = halves[at, :]
            return half * (both + x), quarters[at, :] * q, half * (both + y)

        def load(j):
            at = self.at(j)
            return [field[at, :] for field in fields]

        top, end = load(0), load(self.span - 1)
        up = corners(*self.refs[14:16], 0, [pltpu.roll(v, 1, 0) for v in end], top)
        bottom = [pltpu.roll(v, SUB - 1, 0) for v in top]
        here = top
        for j in range(self.span):
            at = self.at(j)
            below = load(j + 1) if j < self.span - 1 else bottom
            p, q, r = corners(*self.refs[:2], j, here, below)
            g, t = up[0] - p, up[1] + q
            gq, tr = up[1] - q, up[2] + r
            for k, (stay, move) in enumerate(((g - t, g + t), (gq - tr, gq + tr))):
                changes = stay + pltpu.roll(move, 1, 1), pltpu.roll(stay, TILE - 1, 1) + move
                for change, first, offset in zip(changes, (2, 10), (0, 2)):
                    c, i = self.refs[first : first + 2]
                    b = self.refs[first + 2 + k]
                    kept = (c[at, :] * here[offset + k] + b[at, :]) - i[at, :] * change
                    self.refs[6 + offset + k][at, :] = kept
            up, here = (p, q, r), below


def run(domains, written_out=False):
    def body(_, carry):
        for domain in domains:
            domain.sweep()
        return carry

    if written_out:
        for k in range(SWEEPS):
            body(k, 0)
    else:
        lax.fori_loop(0, SWEEPS, body, 0)


def ends_kernel(visc, fric, driv, mask, obs, to_b, to_a, one, two, flags, sems):
    rows = visc.shape[0]
    copies = []
    for e, first in enumerate((0, rows - HALO)):
        at = pl.ds(first, HALO)
        pieces = [
            (visc.at[at], one.at[e, 0]),
            (fric.at[at], one.at[e, 1]),
            (driv.at[:, at], two.at[e, 0]),
            (mask.at[at], flags.at[e]),
            (obs.at[:, at], two.at[e, 1]),
        ]
        for n, (source, place) in enumerate(pieces):
            copies.append(pltpu.make_async_copy(source, place, sems.at[e, n]))
    for copy in copies:
        copy.start()
    for copy in copies:
        copy.wait()
    even, at_end = position(ROW_AXES)

    def edge(e):
        return [one[e, 0], one[e, 1], two[e, 0, 0], two[e, 0, 1], flags[e].astype(F32), two[e, 1, 0], two[e, 1, 1]]

    for a, (head, tail) in enumerate(zip(edge(0), edge(1))):
        at = slice(HALO * a, HALO * (a + 1))
        to_a[at, :] = jnp.where(even, tail, head)
        to_b[at, :] = jnp.where(at_end, 0.0, jnp.where(even, head, tail))


def field_of(visc, fric, driv, mask, obs):
    def field(a, at):
        if a == MASK:
            return mask[at, :].astype(F32)
        if a >= OBS:
            return obs[a - OBS, at, :]
        if a >= DRIV:
            return driv[a - DRIV, at, :]
        return (visc, fric)[a][at, :]

    return field


def first_row(part, lane):
    if part < 2:
        return TILE * part + lane
    if lane < INNER + HALO:
        return TILE + lane
    if lane >= TILE - INNER - HALO:
        return lane
    if UPPER + HALO <= lane < UPPER + SLOT:
        return lane - UPPER - HALO
    if LOWER <= lane < LOWER + INNER + HALO:
        return 2 * TILE - INNER - HALO + lane - LOWER
    return None


def right_part(row):
    seam = TILE - HALO <= row < TILE + HALO
    part = 2 if seam or row == 0 or row == 2 * TILE - HALO else row // TILE
    return part, [lane for lane in range(0, TILE, SUB) if first_row(part, lane) == row][-1]


def slot(part, a):
    return TILE * (2 * part + a // PER) + SLOT * (a % PER)


def interior_kernel(visc, fric, driv, mask, obs, edge, n2, n4, c, i, v0, v1, *refs):
    span = visc.shape[0] // SUB
    field = field_of(visc, fric, driv, mask, obs)
    lane = lanes()
    for part in range(PARTS):
        for m in range(-(-ARRAYS // PER)):
            strips = []
            for at in range(0, TILE, SUB):
                row = first_row(part, at)
                packed = jnp.zeros((SUB, TILE), F32)
                if row is not None:
                    for k in range(min(PER, ARRAYS - PER * m)):
                        value = field(PER * m + k, slice(row, row + SUB))
                        moved = pltpu.roll(value, (SLOT * k + INNER) % TILE, 1)
                        packed = jnp.where(lax.div(lane, SLOT) == k, moved, packed)
                strips.append(packed)
            base = TILE * (2 * part + m)
            edge[base : base + TILE, :] = jnp.concatenate(strips, axis=0).T
    refs = (n2, n4, c, i, *refs[:2], v0, v1, *refs[2:])
    domain = Domain(refs, 0, span, lambda a, j: field(a, pl.ds(j, SUB, stride=span)))
    domain.prepare(False)
    run([domain])


def columns_kernel(row_b, row_a, edge, to_b, to_a, turned):
    even = is_even(ROW_AXES)
    above = jnp.where(even, row_b[...], row_a[...])
    below = jnp.where(even, row_a[...], row_b[...])
    halo = jnp.concatenate([above, below, jnp.zeros((TILE - 2 * EDGE, TILE), F32)], axis=0).T
    turned[:INNER, :] = halo[TILE - INNER :]
    turned[INNER:, :] = halo[:INNER]
    even, at_end = position(COL_AXES)
    row = lax.broadcasted_iota(jnp.int32, (SUB, TILE), 0)

    def put(out, right, left):
        right = pltpu.roll(right, LEAD, 0)
        to_a[out : out + HALO, :] = jnp.where(even, right, left)
        to_b[out : out + HALO, :] = jnp.where(at_end, 0.0, jnp.where(even, left, right))

    for part in range(2):
        right, left = [], []
        for a in range(ARRAYS):
            at = slot(part, a) + INNER
            right.append(edge[at - HALO : at, :])
            left.append(edge[at : at + HALO, :])
        for k in range(2):
            seen_r, seen_l = right[OBS + k], left[OBS + k]
            g = 1 + 2 * k
            right[g] = jnp.where(row < 2, pltpu.roll(seen_r, 2, 0), right[g])
            right[g + 1] = jnp.where(row < 2, pltpu.roll(seen_r, 4, 0), right[g + 1])
            left[g] = jnp.where(row >= 6, pltpu.roll(seen_l, 6, 0), left[g])
            left[g + 1] = jnp.where(row >= 6, pltpu.roll(seen_l, 4, 0), left[g + 1])
        for g in range(GROUPS):
            put(HALO * (GROUPS * part + g), right[g], left[g])
    put(2 * GROUPS * HALO, halo[TILE - HALO :], halo[:HALO])


def strided(stack, base):
    span = STRIP // SUB
    return lambda a, j: stack[pl.ds(base + STRIP * a + j, SUB, stride=span), :]


def fill(stack, base, first, last):
    row = lax.broadcasted_iota(jnp.int32, (SUB, TILE), 0)
    one, two = (pltpu.roll(value, LEAD, 0) for value in first)
    mixed = [jnp.where(row == LEAD, two, one), jnp.where(row < SUB // 2, two, last[0])]
    for k, value in enumerate((one, *mixed, last[1])):
        stack[base + SUB * k : base + SUB * (k + 1), :] = value


def velocity(domain, plain, base):
    for j in range(domain.span):
        at = domain.at(j)
        for k in range(2):
            plain[pl.ds(base + STRIP * k + j, SUB, stride=domain.span), :] = domain.refs[6 + k][at, :]


def density(domain, plain, base, out, place):
    w0, w1 = domain.refs[6:8]
    for j in range(domain.span):
        at = domain.at(j)
        v0, v1 = (plain[pl.ds(base + STRIP * k + j, SUB, stride=domain.span), :] for k in range(2))
        value = -domain.source(FRIC, j) * (w0[at, :] * v0 + w1[at, :] * v1)
        out[pl.ds(place + j, SUB, stride=domain.span), :] = value


def beside():
    lane = lanes()
    return (lane < NEAR) | (lane >= TILE - FAR)


def ends(second):
    row = lax.broadcasted_iota(jnp.int32, (SUB, TILE), 0)
    return row >= SUB - FAR if second else row < NEAR


def adjoint_kernel(
    row_b, row_a, visc, fric, driv, mask, obs, n2, n4, c, i, v0, v1, basis_p, basis_q, edge, turned,
    vel, wide, sides, seams,
    stack, plain, dens, total, *refs,
):
    rows = visc.shape[0]
    span = rows // SUB
    even = is_even(ROW_AXES)
    field = field_of(visc, fric, driv, mask, obs)
    for a in range(ARRAYS):
        at = slice(HALO * a, HALO * (a + 1))
        got_a, got_b = row_a[at, :], row_b[at, :]
        base = STRIP * a
        first = [field(a, slice(at, at + SUB)) for at in (0, SUB)]
        last = [field(a, slice(at, at + SUB)) for at in (rows - 2 * SUB, rows - SUB)]
        fill(stack, base, first, last)
        stack[base : base + LEAD, :] = jnp.where(even, got_b, got_a)[HALO - LEAD :]
        stack[base + STRIP - HALO : base + STRIP, :] = jnp.where(even, got_a, got_b)
    strips = Strips(refs[:STRIP_FIELDS], 0, STRIP // SUB, strided(stack, 0), lambda: visc[rows - KEPT - 1 : rows - KEPT, :])
    strips.prepare(False)
    run([strips])
    velocity(strips, plain, 0)
    for k in range(2):
        for e in range(2):
            out = HALO * (2 * k + e)
            vel[out : out + HALO, :] = plain[STRIP * k + OUTER[e] : STRIP * k + OUTER[e] + HALO, :]
    interior = Domain(
        (n2, n4, c, i, *refs[STRIP_FIELDS:]), 0, span, lambda a, j: field(a, pl.ds(j, SUB, stride=span))
    )
    strips.retarget(False)
    interior.retarget(False, (v0, v1))
    run([interior, strips])
    w0, w1 = interior.refs[6:8]
    for j in range(span):
        at = interior.at(j)
        value = -interior.source(FRIC, j) * (w0[at, :] * v0[at, :] + w1[at, :] * v1[at, :])
        dens[pl.ds(j, SUB, stride=span), :] = value
    density(strips, plain, 0, dens, rows)

    side = beside()
    for s in range(0, TILE, SUB):
        summed = jnp.zeros((SUB, TILE), F32)
        for row in range(s, rows, TILE):
            value = dens[row : row + SUB, :]
            if row in (0, rows - SUB):
                at = rows + OUTER[row > 0]
                value = jnp.where(ends(row > 0), dens[at : at + SUB, :], value)
            summed += value
        total[s : s + SUB, :] = jnp.where(side, 0.0, summed)
    exact = dict(precision=lax.Precision.HIGHEST, preferred_element_type=F32)
    half = jnp.dot(basis_p[...], total[...], **exact)
    wide[...] = jnp.dot(half, basis_q[...], **exact)

    corner = corners()
    for part in range(PARTS):
        for a in range(ARRAYS):
            columns = []
            for r in range(0, SLOT, SUB):
                value = edge[slot(part, a) + r : slot(part, a) + r + SUB, :]
                if part == 2:
                    moved = pltpu.roll(turned[r : r + SUB, :], (UPPER - HALO * a) % TILE, 1)
                    value = jnp.where(corner, moved, value)
                columns.append(value)
            fill(sides, strip(part, a), columns[2:], columns[:2])
            if a == VISC:
                seams[SUB * part : SUB * (part + 1), :] = columns[0]


def strip(part, a):
    return STRIP * (ARRAYS * part + a)


def corners():
    lane = lanes()
    above = (lane >= UPPER) & (lane < UPPER + HALO)
    return above | ((lane >= LOWER + INNER + HALO) & (lane < LOWER + SLOT))


def split(x, axis):
    high = x.astype(jnp.bfloat16)
    low = (x - high.astype(F32)).astype(jnp.bfloat16)
    return jnp.concatenate([high, high, low], axis=axis)


def split_constant(x, axis):
    x = np.asarray(x, np.float32)
    high = np.asarray(x, jnp.bfloat16)
    low = np.asarray(x - np.asarray(high, np.float32), jnp.bfloat16)
    return jnp.asarray(np.concatenate([high, low, high], axis=axis))


def left_right_kernel(
    _, seams, col_b, col_a, wide_in, block, basis_rows, basis_cols,
    stack, strips, coef,
    plain, *refs,
):
    even = is_even(COL_AXES)
    lane = lanes()
    row = lax.broadcasted_iota(jnp.int32, (SUB, TILE), 0)
    upper = (lane >= UPPER + HALO) & (lane < UPPER + SLOT)
    lower = (lane >= LOWER) & (lane < LOWER + INNER + HALO)
    seam_t0 = lane >= TILE - INNER - HALO
    seam_t1 = lane < INNER + HALO
    corner = corners()
    for from_left in (True, False):
        groups = []
        for g in range(2 * GROUPS + 1):
            got_a, got_b = col_a[HALO * g : HALO * (g + 1), :], col_b[HALO * g : HALO * (g + 1), :]
            groups.append(jnp.where(even, got_b, got_a) if from_left else jnp.where(even, got_a, got_b))
        tiles = []
        for part in range(2):
            tile = groups[GROUPS * part : GROUPS * (part + 1)]
            for k in range(2):
                g, h = tile[1 + 2 * k], tile[2 + 2 * k]
                if from_left:
                    tile.append(jnp.where(row >= 5, pltpu.roll(g, 6, 0), pltpu.roll(h, 4, 0)))
                else:
                    tile.append(jnp.where(row < 2, pltpu.roll(g, 2, 0), pltpu.roll(h, 4, 0)))
            tiles.append(tile)
        for a in range(ARRAYS):
            t0, t1 = tiles[0][a], tiles[1][a]
            third = jnp.where(corner, pltpu.roll(groups[-1], (UPPER - HALO * a) % TILE, 1), 0.0)
            third = jnp.where(upper, pltpu.roll(t0, UPPER + HALO, 1), third)
            third = jnp.where(lower, pltpu.roll(t1, LOWER + INNER + HALO, 1), third)
            third = jnp.where(seam_t0, t0, jnp.where(seam_t1, t1, third))
            for part, value in enumerate((t0, t1, third)):
                base = strip(part, a)
                if from_left:
                    stack[base : base + LEAD, :] = value[:LEAD]
                else:
                    stack[base + STRIP - HALO : base + STRIP, :] = value
    last = INNER - KEPT - 1
    before = [lambda at=SUB * part + last: seams[at : at + 1, :] for part in range(PARTS)]
    domains = [
        Strips(refs, STRIP * part, STRIP // SUB, strided(stack, strip(part, 0)), seam)
        for part, seam in enumerate(before)
    ]
    for domain in domains:
        domain.prepare(True)
    run(domains, True)
    for part, domain in enumerate(domains):
        velocity(domain, strips, 2 * STRIP * part)
        domain.retarget(True)
    run(domains, True)
    for part, domain in enumerate(domains):
        density(domain, strips, 2 * STRIP * part, plain, STRIP * part)

    def side(part):
        base = STRIP * part
        return jnp.concatenate(
            [plain[base + at : base + at + HALO, :] for at in OUTER], axis=0
        )

    lane = lax.broadcasted_iota(jnp.int32, (2 * HALO, TILE), 1)
    row = lax.broadcasted_iota(jnp.int32, (2 * HALO, TILE), 0)
    right = (row < NEAR) | (row >= 2 * HALO - FAR)
    straight = (lane >= HALO) & (lane < TILE - HALO)
    seam = (lane < HALO) | (lane >= TILE - HALO)
    top = (lane >= UPPER + HALO) & (lane < UPPER + 2 * HALO)
    bottom = (lane >= LOWER + INNER) & (lane < LOWER + INNER + HALO)
    dens = jnp.concatenate(
        [
            jnp.where(right & straight, side(0) + side(1), 0.0),
            jnp.where(right & (seam | top | bottom), side(2), 0.0),
        ],
        axis=1,
    )
    half = jnp.dot(split(dens, 1), basis_rows[...], preferred_element_type=F32)
    wide = wide_in[...] + jnp.dot(split(half.T, 1), basis_cols[...], preferred_element_type=F32)
    lane = lanes()
    which = lax.div(lane, MODES)
    flat = wide[:SUB]
    for j in range(1, MODES // SUB):
        flat = jnp.where(which == j, wide[SUB * j : SUB * (j + 1)], flat)
    mark = jnp.broadcast_to(block[:1, :].astype(F32), (SUB, TILE))
    row = lax.broadcasted_iota(jnp.int32, (SUB, TILE), 0)
    moved = [flat] + [pltpu.roll(flat, r, 0) for r in range(1, SUB)] + [flat]
    lines = [flat] + [
        jnp.where(row < r - 1, moved[r - 1], jnp.where(row == r - 1, mark, moved[r])) for r in range(1, SUB + 1)
    ]
    cycle = SUB * (SUB + 1)
    chunk = min(4, coef.shape[0] // cycle)

    def spread(d, carry):
        for e in range(chunk):
            for r, line in enumerate(lines):
                coef[pl.ds(pl.multiple_of((d * chunk + e) * cycle + SUB * r, SUB), SUB), :] = line
        return carry

    lax.fori_loop(0, coef.shape[0] // cycle // chunk, spread, 0)


def join_kernel(v0, v1, vel_ends, strips, vel, turned):
    rows = vel.shape[1]
    span = rows // SUB
    middle = jnp.zeros((TILE - 2 * HALO, TILE), F32)
    side = beside()
    for k, v in enumerate((v0, v1)):
        for part in range(PARTS):
            base = STRIP * (2 * part + 1 - k)
            first, last = (strips[base + at : base + at + HALO, :] for at in OUTER)
            at = TILE * (2 * part + k)
            turned[at : at + TILE, :] = jnp.concatenate([first, middle, last], axis=0).T
        for row in range(0, rows, SUB):
            value = v[pl.ds(SUB * (row % span) + row // span, SUB, stride=SUB), :]
            if row in (0, rows - SUB):
                at = HALO * (2 * k + (row > 0))
                value = jnp.where(ends(row > 0), vel_ends[at : at + HALO, :], value)
            part, lane = right_part(row)
            at = TILE * (2 * part + k) + lane
            vel[k, row : row + SUB, :] = jnp.where(side, turned[at : at + SUB, :], value)


def bases():
    places = np.arange(TILE) + 0.5
    basis = np.cos(math.pi * places[:, None] * np.arange(MODES)[None, :] / TILE)
    groups = MODES // SUB
    order = np.arange(MODES).reshape(SUB, groups).T.reshape(-1)
    rows = basis[:, order] / TILE
    cols = np.tile(basis, (1, groups))
    placed = np.zeros((2 * TILE, MODES))
    for row in range(0, 2 * TILE, SUB):
        part, lane = right_part(row)
        at = lane + (TILE if part == 2 else 0)
        placed[at : at + SUB] = rows[row % TILE : row % TILE + SUB]
    outer = np.concatenate([cols[:HALO], cols[TILE - HALO :]])
    return jnp.asarray(rows.T, F32), jnp.asarray(cols, F32), split_constant(placed, 0), split_constant(outer, 0)


def pick_kernel(owners, every, out):
    mine = out.shape[1]
    own = lax.axis_index("own")
    wanted = [owners[pl.ds(own, 1), k : k + 1].astype(F32) for k in range(mine)]
    lines = SUB + 1
    devices = every.shape[0] // lines
    chunk = min(4, devices // SUB)

    def body(d, sums):
        sums = list(sums)
        for e in range(chunk):
            base = (d * chunk + e) * SUB * lines
            mark = every[pl.ds(base + SUB, SUB, stride=lines), :]
            hits = [mark == wanted[k] for k in range(mine)]
            for r in range(SUB):
                part = every[pl.ds(base + r, SUB, stride=lines), :]
                for k in range(mine):
                    sums[SUB * k + r] += jnp.where(hits[k], part, 0.0)
        return tuple(sums)

    start = (jnp.zeros((SUB, TILE), F32),) * (mine * SUB)
    sums = lax.fori_loop(0, devices // SUB // chunk, body, start)
    for k in range(mine):
        for r in range(SUB):
            total = jnp.sum(sums[SUB * k + r], axis=0, keepdims=True)
            out[0, k : k + 1, TILE * r : TILE * (r + 1)] = total


def local(viscosity, friction, driving, observed, ice_mask, tile_block, owner_list):
    rows, cols = viscosity.shape
    assert (rows, cols) == (2 * TILE, TILE)
    inputs = (viscosity, friction, driving, ice_mask, observed)
    near = [pltpu.with_memory_space_constraint(x, pltpu.VMEM) for x in inputs]
    basis_p, basis_q, basis_rows, basis_cols = bases()
    to_b, to_a = call(
        ends_kernel,
        "ends",
        (vmem(EDGE, cols), vmem(EDGE, cols)),
        [
            vmem(2, 2, HALO, cols),
            vmem(2, 2, 2, HALO, cols),
            pltpu.VMEM((2, HALO, cols), jnp.int32),
            pltpu.SemaphoreType.DMA((2, 5)),
        ],
        10**6,
        *(pltpu.with_memory_space_constraint(x, pltpu.HBM) for x in inputs),
    )
    row_b = swap(to_b, 0, 1)
    row_a = swap(to_a, 0, 0)
    edge, *forward = call(
        interior_kernel,
        "interior",
        (vmem(2 * PARTS * TILE, TILE),) + (vmem(rows, cols),) * 6,
        [vmem(rows, cols)] * (FIELDS - 6),
        8 * 10**6,
        *near,
    )
    to_b, to_a, turned = call(
        columns_kernel,
        "columns",
        (vmem(SENT, TILE), vmem(SENT, TILE), vmem(SLOT, TILE)),
        [],
        10**5,
        row_b,
        row_a,
        edge,
    )
    col_b = swap(to_b, 1, 1)
    col_a = swap(to_a, 1, 0)
    vel_ends, wide, sides, seams = call(
        adjoint_kernel,
        "adjoint",
        (
            vmem(4 * HALO, cols),
            vmem(MODES, TILE),
            vmem(PARTS * ARRAYS * STRIP, TILE),
            vmem(PARTS * SUB, TILE),
        ),
        [vmem(ARRAYS * STRIP, cols), vmem(2 * STRIP, cols), vmem(rows + STRIP, cols), vmem(TILE, cols)]
        + [vmem(STRIP, cols)] * STRIP_FIELDS
        + [vmem(rows, cols)] * (FIELDS - 4),
        8 * 10**6,
        row_b,
        row_a,
        *near,
        *forward,
        basis_p,
        basis_q,
        edge,
        turned,
    )
    devices = lax.axis_size(ROW_AXES + COL_AXES)
    _, strips, coef = call(
        left_right_kernel,
        "left_right",
        (
            vmem(PARTS * ARRAYS * STRIP, TILE),
            vmem(PARTS * 2 * STRIP, TILE),
            vmem(devices * (SUB + 1), TILE),
        ),
        [vmem(PARTS * STRIP, TILE)] * (STRIP_FIELDS + 1),
        4 * 10**6,
        sides,
        seams,
        col_b,
        col_a,
        wide,
        tile_block,
        basis_rows,
        basis_cols,
        aliases={0: 0},
    )
    coef = coef.reshape(devices, 1, (SUB + 1) * TILE)
    parts = lax.all_to_all(coef, ROW_AXES + COL_AXES, 0, 0, tiled=True)
    state = call(
        join_kernel,
        "join",
        jax.ShapeDtypeStruct((2, rows, cols), F32),
        [vmem(2 * PARTS * TILE, TILE)],
        4 * 10**6,
        *forward[4:],
        vel_ends,
        strips,
    )
    owners = owner_list.reshape(lax.axis_size("own"), -1)
    picked = call(
        pick_kernel,
        "pick",
        jax.ShapeDtypeStruct((1, owners.shape[1], MODES * MODES), F32),
        [],
        10**5,
        owners,
        parts.reshape(-1, TILE),
    )
    return (state, picked)


def solution(mesh):
    return jax.shard_map(
        local,
        mesh=mesh,
        in_specs=(
            P(("row", "own"), "col"),
            P(("row", "own"), "col"),
            P(None, ("row", "own"), "col"),
            P(None, ("row", "own"), "col"),
            P(("row", "own"), "col"),
            P(("row", "own"), "col"),
            P(),
        ),
        out_specs=(P(None, ("row", "own"), "col"), P("own", None, None)),
        check_vma=False,
    )
```

```python
import math

import jax
import jax.numpy as jnp
import numpy as np
from jax import lax
from jax.experimental import pallas as pl
from jax.experimental.pallas import tpu as pltpu
from jax.sharding import PartitionSpec as P

TILE = 128
MODES = 32
SWEEPS = 3
SUB = 8
HALO = 8
INNER = 2 * HALO
STRIP = 40
LEAD = HALO - 1
KEPT = 12
OUTER = (LEAD, STRIP - 2 * HALO)
NEAR, FAR = 7, 6
LENGTH = STRIP // 2
ARRAYS = 7
VISC, FRIC, DRIV, MASK, OBS = 0, 1, 2, 4, 5
EDGE = ARRAYS * HALO
SLOT = 2 * INNER
PER = TILE // SLOT
GROUPS = 5
SENT = 2 * GROUPS * HALO + HALO
PARTS = 3
UPPER, LOWER = 32, 64
ROW_AXES = ("row", "own")
COL_AXES = ("col",)
F32 = jnp.float32
LIMIT = 40 * 1024 * 1024


def swap(x, axis, first):
    sizes = lax.axis_size(ROW_AXES), lax.axis_size(COL_AXES)
    owners = lax.axis_size("own")

    def device(i, j):
        return (i // owners * sizes[1] + j) * owners + i % owners

    pairs = []
    for i in range(sizes[0]):
        for j in range(sizes[1]):
            place = [i, j]
            if first and place[axis] in (0, sizes[axis] - 1):
                place[1 - axis] ^= 1
            else:
                place[axis] = ((place[axis] + first) ^ 1) - first
            pairs.append((device(i, j), device(*place)))
    return lax.ppermute(x, ("row", "col", "own"), pairs)


def position(axes):
    index, size = 0, 1
    for axis in axes:
        index = index * lax.axis_size(axis) + lax.axis_index(axis)
        size *= lax.axis_size(axis)
    assert size % 2 == 0
    return lax.rem(index, 2) == 0, (index == 0) | (index == size - 1)


def is_even(axes):
    return position(axes)[0]


def lanes():
    return lax.broadcasted_iota(jnp.int32, (SUB, TILE), 1)


def call(kernel, name, outs, scratch, cost, *args, aliases={}):
    return pl.pallas_call(
        kernel,
        out_shape=outs,
        scratch_shapes=scratch,
        input_output_aliases=aliases,
        compiler_params=pltpu.CompilerParams(vmem_limit_bytes=LIMIT),
        cost_estimate=pl.CostEstimate(flops=cost, bytes_accessed=cost, transcendentals=0),
        name=name,
    )(*args)


def vmem(*shape):
    return pltpu.VMEM(shape, F32)


FIELDS = 14
STRIP_FIELDS = 24


class Domain:
    def __init__(self, refs, base, span, source, seam=None):
        self.refs, self.base, self.span, self.source, self.seam = refs, base, span, source, seam

    def at(self, j):
        return pl.ds(self.base + SUB * j, SUB)

    def prepare(self, flipped):
        n2, n4, c, i, b0, b1 = self.refs[:6]
        visc = [self.source(VISC, j) for j in range(self.span)]
        for j in range(self.span):
            at = self.at(j)
            pair = visc[j] + (visc[j - 1] if j else self.before(visc[-1]))
            fric = self.source(FRIC, j)
            diag = 1.25 * (pair + pltpu.roll(pair, 1, 1)) + fric
            on = self.source(MASK, j) > 0.0
            inv = jnp.where(on, 0.5 / jnp.where(on, diag, 1.0), 0.0)
            half = 0.5 * visc[j]
            n2[at, :] = half
            n4[at, :] = 0.5 * half
            c[at, :] = 1.0 - fric * inv
            i[at, :] = inv
            for k, b in enumerate((b0, b1)):
                value = inv * self.source(DRIV + (1 - k if flipped else k), j)
                b[at, :] = value
                self.write(k, at, value + value)

    def before(self, last):
        wrapped = pltpu.roll(last, 1, 0)
        if self.seam is None:
            return wrapped
        row = lax.broadcasted_iota(jnp.int32, (SUB, TILE), 0)
        return jnp.where(row == SUB // 2, self.seam(), wrapped)

    def write(self, k, at, value):
        self.refs[6 + k][at, :] = value
        self.refs[8 + k][at, :] = pltpu.roll(value, TILE - 1, 1)

    def retarget(self, flipped, velocity=None):
        i, b0, b1 = self.refs[3:6]
        w0, w1 = velocity or self.refs[6:8]
        for j in range(self.span):
            at = self.at(j)
            for k, (b, w) in enumerate(((b0, w0), (b1, w1))):
                value = i[at, :] * (w[at, :] - self.source(OBS + (1 - k if flipped else k), j))
                b[at, :] = value
                self.write(k, at, value + value)

    def differences(self):
        n2, n4 = self.refs[:2]
        fields = self.refs[6:10]
        parts = self.refs[10:14]

        def corners(j, here, below):
            w0, w1, r0, r1 = here
            v0, v1, s0, s1 = below
            a1, a2 = s0 - w0, v0 - r0
            e1, e2 = s1 - w1, v1 - r1
            x, y = a1 + a2, e1 - e2
            q = (a1 - a2) + (e1 + e2)
            both = x + y
            at = self.at(j)
            half = n2[at, :]
            return half * (both + x), n4[at, :] * q, half * (both + y)

        def load(j):
            at = self.at(j)
            return [field[at, :] for field in fields]

        top = load(0)
        last = corners(self.span - 1, load(self.span - 1), [pltpu.roll(v, SUB - 1, 0) for v in top])
        up = [pltpu.roll(v, 1, 0) for v in last]
        here = top
        for j in range(self.span):
            at = self.at(j)
            if j < self.span - 1:
                below = load(j + 1)
                p, q, r = corners(j, here, below)
                here = below
            else:
                p, q, r = last
            g, t = up[0] - p, up[1] + q
            gq, tr = up[1] - q, up[2] + r
            parts[0][at, :] = g - t
            parts[1][at, :] = gq - tr
            parts[2][at, :] = pltpu.roll(g + t, 1, 1)
            parts[3][at, :] = pltpu.roll(gq + tr, 1, 1)
            up = (p, q, r)

    def update(self):
        c, i, b0, b1, w0, w1 = self.refs[2:8]
        parts = self.refs[10:14]
        for j in range(self.span):
            at = self.at(j)
            cv, iv = c[at, :], i[at, :]
            for k, (b, w) in enumerate(((b0, w0), (b1, w1))):
                value = (cv * w[at, :] + b[at, :]) - iv * (parts[k][at, :] + parts[k + 2][at, :])
                self.write(k, at, value)


class Strips(Domain):
    wraps = True

    def prepare(self, flipped):
        super().prepare(flipped)
        for j in range(self.span):
            at = self.at(j)
            for now, later in zip(self.refs[2:6], self.refs[10:14]):
                later[at, :] = pltpu.roll(now[at, :], TILE - 1, 1)
        if self.wraps:
            for now, before in zip(self.refs[:2], self.refs[14:16]):
                before[self.at(0), :] = pltpu.roll(now[self.at(self.span - 1), :], 1, 0)

    def retarget(self, flipped, velocity=None):
        super().retarget(flipped, velocity)
        for j in range(self.span):
            at = self.at(j)
            for now, later in zip(self.refs[4:6], self.refs[12:14]):
                later[at, :] = pltpu.roll(now[at, :], TILE - 1, 1)

    def differences(self):
        fields = self.refs[6:10]
        kept, turned, kept_next, turned_next = (self.refs[16 + 2 * k : 18 + 2 * k] for k in range(4))

        def corners(halves, quarters, j, here, below):
            w0, w1, r0, r1 = here
            v0, v1, s0, s1 = below
            a1, a2 = s0 - w0, v0 - r0
            e1, e2 = s1 - w1, v1 - r1
            x, y = a1 + a2, e1 - e2
            q = (a1 - a2) + (e1 + e2)
            both = x + y
            at = self.at(j)
            half = halves[at, :]
            return half * (both + x), quarters[at, :] * q, half * (both + y)

        def load(j):
            at = self.at(j)
            return [field[at, :] for field in fields]

        top, end = load(0), load(self.span - 1)
        if self.wraps:
            up = corners(*self.refs[14:16], 0, [pltpu.roll(v, 1, 0) for v in end], top)
            bottom = [pltpu.roll(v, SUB - 1, 0) for v in top]
        else:
            up, bottom = [jnp.zeros((SUB, TILE), F32)] * 3, [jnp.zeros((SUB, TILE), F32)] * 4
        here = top
        for j in range(self.span):
            at = self.at(j)
            below = load(j + 1) if j < self.span - 1 else bottom
            p, q, r = corners(*self.refs[:2], j, here, below)
            g, t = up[0] - p, up[1] + q
            gq, tr = up[1] - q, up[2] + r
            for k, (stay, move) in enumerate(((g - t, g + t), (gq - tr, gq + tr))):
                kept[k][at, :] = stay
                turned_next[k][at, :] = move
                turned[k][at, :] = pltpu.roll(move, 1, 1)
                kept_next[k][at, :] = pltpu.roll(stay, TILE - 1, 1)
            up, here = (p, q, r), below

    def update(self):
        for first, offset, parts in ((2, 6, (16, 18)), (10, 8, (20, 22))):
            c, i, *b = self.refs[first : first + 4]
            for j in range(self.span):
                at = self.at(j)
                cv, iv = c[at, :], i[at, :]
                for k in range(2):
                    w = self.refs[offset + k]
                    change = self.refs[parts[0] + k][at, :] + self.refs[parts[1] + k][at, :]
                    w[at, :] = (cv * w[at, :] + b[k][at, :]) - iv * change


class Bands(Strips):
    wraps = False

    def before(self, last):
        return self.source(VISC, -1)


def run(domains, written_out=False):
    def body(_, carry):
        for domain in domains:
            domain.differences()
        for domain in domains:
            domain.update()
        return carry

    if written_out:
        for k in range(SWEEPS):
            body(k, 0)
    else:
        lax.fori_loop(0, SWEEPS, body, 0)


def ends_kernel(visc, fric, driv, mask, obs, to_b, to_a, one, two, flags, sems):
    rows = visc.shape[0]
    copies = []
    for e, first in enumerate((0, rows - HALO)):
        at = pl.ds(first, HALO)
        pieces = [
            (visc.at[at], one.at[e, 0]),
            (fric.at[at], one.at[e, 1]),
            (driv.at[:, at], two.at[e, 0]),
            (mask.at[at], flags.at[e]),
            (obs.at[:, at], two.at[e, 1]),
        ]
        for n, (source, place) in enumerate(pieces):
            copies.append(pltpu.make_async_copy(source, place, sems.at[e, n]))
    for copy in copies:
        copy.start()
    for copy in copies:
        copy.wait()
    even, at_end = position(ROW_AXES)

    def edge(e):
        return [one[e, 0], one[e, 1], two[e, 0, 0], two[e, 0, 1], flags[e].astype(F32), two[e, 1, 0], two[e, 1, 1]]

    for a, (head, tail) in enumerate(zip(edge(0), edge(1))):
        at = slice(HALO * a, HALO * (a + 1))
        to_a[at, :] = jnp.where(even, tail, head)
        to_b[at, :] = jnp.where(at_end, 0.0, jnp.where(even, head, tail))


def field_of(visc, fric, driv, mask, obs):
    def field(a, at):
        if a == MASK:
            return mask[at, :].astype(F32)
        if a >= OBS:
            return obs[a - OBS, at, :]
        if a >= DRIV:
            return driv[a - DRIV, at, :]
        return (visc, fric)[a][at, :]

    return field


def first_row(part, lane):
    if part < 2:
        return TILE * part + lane
    if lane < INNER + HALO:
        return TILE + lane
    if lane >= TILE - INNER - HALO:
        return lane
    if UPPER + HALO <= lane < UPPER + SLOT:
        return lane - UPPER - HALO
    if LOWER <= lane < LOWER + INNER + HALO:
        return 2 * TILE - INNER - HALO + lane - LOWER
    return None


def right_part(row):
    seam = TILE - HALO <= row < TILE + HALO
    part = 2 if seam or row == 0 or row == 2 * TILE - HALO else row // TILE
    return part, [lane for lane in range(0, TILE, SUB) if first_row(part, lane) == row][-1]


def slot(part, a):
    return TILE * (2 * part + a // PER) + SLOT * (a % PER)


def interior_kernel(visc, fric, driv, mask, obs, edge, n2, n4, c, i, v0, v1, *refs):
    span = visc.shape[0] // SUB
    field = field_of(visc, fric, driv, mask, obs)
    lane = lanes()
    for part in range(PARTS):
        for m in range(-(-ARRAYS // PER)):
            strips = []
            for at in range(0, TILE, SUB):
                row = first_row(part, at)
                packed = jnp.zeros((SUB, TILE), F32)
                if row is not None:
                    for k in range(min(PER, ARRAYS - PER * m)):
                        value = field(PER * m + k, slice(row, row + SUB))
                        moved = pltpu.roll(value, (SLOT * k + INNER) % TILE, 1)
                        packed = jnp.where(lax.div(lane, SLOT) == k, moved, packed)
                strips.append(packed)
            base = TILE * (2 * part + m)
            edge[base : base + TILE, :] = jnp.concatenate(strips, axis=0).T
    refs = (n2, n4, c, i, *refs[:2], v0, v1, *refs[2:])
    domain = Domain(refs, 0, span, lambda a, j: field(a, pl.ds(j, SUB, stride=span)))
    domain.prepare(False)
    run([domain])


def columns_kernel(row_b, row_a, edge, to_b, to_a, turned):
    even = is_even(ROW_AXES)
    above = jnp.where(even, row_b[...], row_a[...])
    below = jnp.where(even, row_a[...], row_b[...])
    halo = jnp.concatenate([above, below, jnp.zeros((TILE - 2 * EDGE, TILE), F32)], axis=0).T
    turned[:INNER, :] = halo[TILE - INNER :]
    turned[INNER:, :] = halo[:INNER]
    even, at_end = position(COL_AXES)
    row = lax.broadcasted_iota(jnp.int32, (SUB, TILE), 0)

    def put(out, right, left):
        right = pltpu.roll(right, LEAD, 0)
        to_a[out : out + HALO, :] = jnp.where(even, right, left)
        to_b[out : out + HALO, :] = jnp.where(at_end, 0.0, jnp.where(even, left, right))

    for part in range(2):
        right, left = [], []
        for a in range(ARRAYS):
            at = slot(part, a) + INNER
            right.append(edge[at - HALO : at, :])
            left.append(edge[at : at + HALO, :])
        for k in range(2):
            seen_r, seen_l = right[OBS + k], left[OBS + k]
            g = 1 + 2 * k
            right[g] = jnp.where(row < 2, pltpu.roll(seen_r, 2, 0), right[g])
            right[g + 1] = jnp.where(row < 2, pltpu.roll(seen_r, 4, 0), right[g + 1])
            left[g] = jnp.where(row >= 6, pltpu.roll(seen_l, 6, 0), left[g])
            left[g + 1] = jnp.where(row >= 6, pltpu.roll(seen_l, 4, 0), left[g + 1])
        for g in range(GROUPS):
            put(HALO * (GROUPS * part + g), right[g], left[g])
    put(2 * GROUPS * HALO, halo[TILE - HALO :], halo[:HALO])


def strided(stack, base):
    span = STRIP // SUB
    return lambda a, j: stack[pl.ds(base + STRIP * a + j, SUB, stride=span), :]


def fill(stack, base, first, last):
    row = lax.broadcasted_iota(jnp.int32, (SUB, TILE), 0)
    one, two = (pltpu.roll(value, LEAD, 0) for value in first)
    mixed = [jnp.where(row == LEAD, two, one), jnp.where(row < SUB // 2, two, last[0])]
    for k, value in enumerate((one, *mixed, last[1])):
        stack[base + SUB * k : base + SUB * (k + 1), :] = value


def velocity(domain, plain, base):
    for j in range(domain.span):
        at = domain.at(j)
        for k in range(2):
            plain[pl.ds(base + STRIP * k + j, SUB, stride=domain.span), :] = domain.refs[6 + k][at, :]


def density(domain, plain, base, out, place):
    w0, w1 = domain.refs[6:8]
    for j in range(domain.span):
        at = domain.at(j)
        v0, v1 = (plain[pl.ds(base + STRIP * k + j, SUB, stride=domain.span), :] for k in range(2))
        value = -domain.source(FRIC, j) * (w0[at, :] * v0 + w1[at, :] * v1)
        out[pl.ds(place + j, SUB, stride=domain.span), :] = value


def beside():
    lane = lanes()
    return (lane < NEAR) | (lane >= TILE - FAR)


def ends(second):
    row = lax.broadcasted_iota(jnp.int32, (SUB, TILE), 0)
    return row >= SUB - FAR if second else row < NEAR


def adjoint_kernel(
    row_b, row_a, visc, fric, driv, mask, obs, n2, n4, c, i, v0, v1, basis_p, basis_q, edge, turned,
    vel, wide, sides,
    stack, plain, dens, total, *refs,
):
    rows = visc.shape[0]
    span = rows // SUB
    even = is_even(ROW_AXES)
    field = field_of(visc, fric, driv, mask, obs)
    for a in range(ARRAYS):
        at = slice(HALO * a, HALO * (a + 1))
        got_a, got_b = row_a[at, :], row_b[at, :]
        base = STRIP * a
        first = [field(a, slice(at, at + SUB)) for at in (0, SUB)]
        last = [field(a, slice(at, at + SUB)) for at in (rows - 2 * SUB, rows - SUB)]
        fill(stack, base, first, last)
        stack[base : base + LEAD, :] = jnp.where(even, got_b, got_a)[HALO - LEAD :]
        stack[base + STRIP - HALO : base + STRIP, :] = jnp.where(even, got_a, got_b)
    strips = Strips(refs[:STRIP_FIELDS], 0, STRIP // SUB, strided(stack, 0), lambda: visc[rows - KEPT - 1 : rows - KEPT, :])
    strips.prepare(False)
    run([strips])
    velocity(strips, plain, 0)
    for k in range(2):
        for e in range(2):
            out = HALO * (2 * k + e)
            vel[out : out + HALO, :] = plain[STRIP * k + OUTER[e] : STRIP * k + OUTER[e] + HALO, :]
    interior = Domain(
        (n2, n4, c, i, *refs[STRIP_FIELDS:]), 0, span, lambda a, j: field(a, pl.ds(j, SUB, stride=span))
    )
    strips.retarget(False)
    interior.retarget(False, (v0, v1))
    run([interior, strips])
    w0, w1 = interior.refs[6:8]
    for j in range(span):
        at = interior.at(j)
        value = -interior.source(FRIC, j) * (w0[at, :] * v0[at, :] + w1[at, :] * v1[at, :])
        dens[pl.ds(j, SUB, stride=span), :] = value
    density(strips, plain, 0, dens, rows)

    side = beside()
    for s in range(0, TILE, SUB):
        summed = jnp.zeros((SUB, TILE), F32)
        for row in range(s, rows, TILE):
            value = dens[row : row + SUB, :]
            if row in (0, rows - SUB):
                at = rows + OUTER[row > 0]
                value = jnp.where(ends(row > 0), dens[at : at + SUB, :], value)
            summed += value
        total[s : s + SUB, :] = jnp.where(side, 0.0, summed)
    exact = dict(precision=lax.Precision.HIGHEST, preferred_element_type=F32)
    half = jnp.dot(basis_p[...], total[...], **exact)
    wide[...] = jnp.dot(half, basis_q[...], **exact)

    corner = corners()
    for part in range(PARTS):
        for a in range(ARRAYS):
            columns = []
            for r in range(0, SLOT, SUB):
                value = edge[slot(part, a) + r : slot(part, a) + r + SUB, :]
                if part == 2:
                    moved = pltpu.roll(turned[r : r + SUB, :], (UPPER - HALO * a) % TILE, 1)
                    value = jnp.where(corner, moved, value)
                columns.append(value)
            first, second = columns[2:]
            sides[band(a, 0, part, LEAD, SUB), :] = first
            sides[band(a, 0, part, LEAD + SUB, LENGTH - LEAD - SUB), :] = second[: LENGTH - LEAD - SUB]
            sides[band(a, 1, part, 0, SUB // 2), :] = pltpu.roll(columns[0], SUB // 2, 0)[: SUB // 2]
            sides[band(a, 1, part, SUB // 2, SUB), :] = columns[1]
            if a == VISC:
                sides[band(a, 0, part, -1, 1), :] = first[:1]
                sides[band(a, 1, part, -1, 1), :] = columns[0][SUB // 2 - 1 : SUB // 2]


def band(a, side, part, first, count):
    return pl.ds(SUB * ((LENGTH + 1) * a + 1 + first) + PARTS * side + part, count, stride=SUB)


def corners():
    lane = lanes()
    above = (lane >= UPPER) & (lane < UPPER + HALO)
    return above | ((lane >= LOWER + INNER + HALO) & (lane < LOWER + SLOT))


def split(x, axis):
    high = x.astype(jnp.bfloat16)
    low = (x - high.astype(F32)).astype(jnp.bfloat16)
    return jnp.concatenate([high, high, low], axis=axis)


def split_constant(x, axis):
    x = np.asarray(x, np.float32)
    high = np.asarray(x, jnp.bfloat16)
    low = np.asarray(x - np.asarray(high, np.float32), jnp.bfloat16)
    return jnp.asarray(np.concatenate([high, low, high], axis=axis))


def outermost(side, part):
    first = LENGTH - 2 * HALO if side else LEAD
    return pl.ds(SUB * first + PARTS * side + part, HALO, stride=SUB)


def left_right_kernel(
    _, col_b, col_a, wide_in, block, basis_rows, basis_cols,
    stack, vel0, vel1, coef,
    plain, *refs,
):
    even = is_even(COL_AXES)
    lane = lanes()
    row = lax.broadcasted_iota(jnp.int32, (SUB, TILE), 0)
    upper = (lane >= UPPER + HALO) & (lane < UPPER + SLOT)
    lower = (lane >= LOWER) & (lane < LOWER + INNER + HALO)
    seam_t0 = lane >= TILE - INNER - HALO
    seam_t1 = lane < INNER + HALO
    corner = corners()
    for from_left in (True, False):
        groups = []
        for g in range(2 * GROUPS + 1):
            got_a, got_b = col_a[HALO * g : HALO * (g + 1), :], col_b[HALO * g : HALO * (g + 1), :]
            groups.append(jnp.where(even, got_b, got_a) if from_left else jnp.where(even, got_a, got_b))
        tiles = []
        for part in range(2):
            tile = groups[GROUPS * part : GROUPS * (part + 1)]
            for k in range(2):
                g, h = tile[1 + 2 * k], tile[2 + 2 * k]
                if from_left:
                    tile.append(jnp.where(row >= 5, pltpu.roll(g, 6, 0), pltpu.roll(h, 4, 0)))
                else:
                    tile.append(jnp.where(row < 2, pltpu.roll(g, 2, 0), pltpu.roll(h, 4, 0)))
            tiles.append(tile)
        for a in range(ARRAYS):
            t0, t1 = tiles[0][a], tiles[1][a]
            third = jnp.where(corner, pltpu.roll(groups[-1], (UPPER - HALO * a) % TILE, 1), 0.0)
            third = jnp.where(upper, pltpu.roll(t0, UPPER + HALO, 1), third)
            third = jnp.where(lower, pltpu.roll(t1, LOWER + INNER + HALO, 1), third)
            third = jnp.where(seam_t0, t0, jnp.where(seam_t1, t1, third))
            for part, value in enumerate((t0, t1, third)):
                if from_left:
                    stack[band(a, 0, part, 0, LEAD), :] = value[:LEAD]
                else:
                    stack[band(a, 1, part, LENGTH - HALO, HALO), :] = value
    def source(a, j):
        at = SUB * ((LENGTH + 1) * a + 1 + j)
        return stack[at : at + SUB, :]

    bands = Bands(refs, 0, LENGTH, source)
    bands.prepare(True)
    run([bands], True)
    vel0[...] = refs[6][...]
    vel1[...] = refs[7][...]
    bands.retarget(True)
    run([bands], True)
    for j in range(LENGTH):
        at = bands.at(j)
        value = refs[6][at, :] * vel0[at, :] + refs[7][at, :] * vel1[at, :]
        plain[at, :] = -source(FRIC, j) * value

    def side(part):
        return jnp.concatenate([plain[outermost(k, part), :] for k in range(2)], axis=0)

    lane = lax.broadcasted_iota(jnp.int32, (2 * HALO, TILE), 1)
    row = lax.broadcasted_iota(jnp.int32, (2 * HALO, TILE), 0)
    right = (row < NEAR) | (row >= 2 * HALO - FAR)
    straight = (lane >= HALO) & (lane < TILE - HALO)
    seam = (lane < HALO) | (lane >= TILE - HALO)
    top = (lane >= UPPER + HALO) & (lane < UPPER + 2 * HALO)
    bottom = (lane >= LOWER + INNER) & (lane < LOWER + INNER + HALO)
    dens = jnp.concatenate(
        [
            jnp.where(right & straight, side(0) + side(1), 0.0),
            jnp.where(right & (seam | top | bottom), side(2), 0.0),
        ],
        axis=1,
    )
    half = lax.dot_general(
        basis_rows[...], split(dens, 1), (((1,), (1,)), ((), ())), preferred_element_type=F32
    )
    wide = wide_in[...] + jnp.dot(split(half, 1), basis_cols[...], preferred_element_type=F32)
    lane = lanes()
    which = lax.div(lane, MODES)
    flat = wide[:SUB]
    for j in range(1, MODES // SUB):
        flat = jnp.where(which == j, wide[SUB * j : SUB * (j + 1)], flat)
    mark = jnp.broadcast_to(block[:1, :].astype(F32), (SUB, TILE))
    row = lax.broadcasted_iota(jnp.int32, (SUB, TILE), 0)
    moved = [flat] + [pltpu.roll(flat, r, 0) for r in range(1, SUB)] + [flat]
    lines = [flat] + [
        jnp.where(row < r - 1, moved[r - 1], jnp.where(row == r - 1, mark, moved[r])) for r in range(1, SUB + 1)
    ]
    cycle = SUB * (SUB + 1)
    chunk = min(4, coef.shape[0] // cycle)

    def spread(d, carry):
        for e in range(chunk):
            for r, line in enumerate(lines):
                coef[pl.ds(pl.multiple_of((d * chunk + e) * cycle + SUB * r, SUB), SUB), :] = line
        return carry

    lax.fori_loop(0, coef.shape[0] // cycle // chunk, spread, 0)


def join_kernel(v0, v1, vel_ends, side0, side1, vel, turned):
    rows = vel.shape[1]
    span = rows // SUB
    middle = jnp.zeros((TILE - 2 * HALO, TILE), F32)
    side = beside()
    for k, (v, strips) in enumerate(((v0, side1), (v1, side0))):
        for part in range(PARTS):
            first, last = (strips[outermost(e, part), :] for e in range(2))
            at = TILE * (2 * part + k)
            turned[at : at + TILE, :] = jnp.concatenate([first, middle, last], axis=0).T
        for row in range(0, rows, SUB):
            value = v[pl.ds(SUB * (row % span) + row // span, SUB, stride=SUB), :]
            if row in (0, rows - SUB):
                at = HALO * (2 * k + (row > 0))
                value = jnp.where(ends(row > 0), vel_ends[at : at + HALO, :], value)
            part, lane = right_part(row)
            at = TILE * (2 * part + k) + lane
            vel[k, row : row + SUB, :] = jnp.where(side, turned[at : at + SUB, :], value)


def bases():
    places = np.arange(TILE) + 0.5
    basis = np.cos(math.pi * places[:, None] * np.arange(MODES)[None, :] / TILE)
    groups = MODES // SUB
    order = np.arange(MODES).reshape(SUB, groups).T.reshape(-1)
    rows = basis[:, order] / TILE
    cols = np.tile(basis, (1, groups))
    placed = np.zeros((2 * TILE, MODES))
    for row in range(0, 2 * TILE, SUB):
        part, lane = right_part(row)
        at = lane + (TILE if part == 2 else 0)
        placed[at : at + SUB] = rows[row % TILE : row % TILE + SUB]
    outer = np.concatenate([cols[:HALO], cols[TILE - HALO :]])
    return jnp.asarray(rows.T, F32), jnp.asarray(cols, F32), split_constant(placed.T, 1), split_constant(outer, 0)


def pick_kernel(owners, every, out):
    mine = out.shape[1]
    own = lax.axis_index("own")
    wanted = [owners[pl.ds(own, 1), k : k + 1].astype(F32) for k in range(mine)]
    lines = SUB + 1
    devices = every.shape[0] // lines
    chunk = min(4, devices // SUB)

    def body(d, sums):
        sums = list(sums)
        for e in range(chunk):
            base = (d * chunk + e) * SUB * lines
            mark = every[pl.ds(base + SUB, SUB, stride=lines), :]
            hits = [mark == wanted[k] for k in range(mine)]
            for r in range(SUB):
                part = every[pl.ds(base + r, SUB, stride=lines), :]
                for k in range(mine):
                    sums[SUB * k + r] += jnp.where(hits[k], part, 0.0)
        return tuple(sums)

    start = (jnp.zeros((SUB, TILE), F32),) * (mine * SUB)
    sums = lax.fori_loop(0, devices // SUB // chunk, body, start)
    for k in range(mine):
        for r in range(SUB):
            total = jnp.sum(sums[SUB * k + r], axis=0, keepdims=True)
            out[0, k : k + 1, TILE * r : TILE * (r + 1)] = total


def local(viscosity, friction, driving, observed, ice_mask, tile_block, owner_list):
    rows, cols = viscosity.shape
    assert (rows, cols) == (2 * TILE, TILE)
    inputs = (viscosity, friction, driving, ice_mask, observed)
    near = [pltpu.with_memory_space_constraint(x, pltpu.VMEM) for x in inputs]
    basis_p, basis_q, basis_rows, basis_cols = bases()
    to_b, to_a = call(
        ends_kernel,
        "ends",
        (vmem(EDGE, cols), vmem(EDGE, cols)),
        [
            vmem(2, 2, HALO, cols),
            vmem(2, 2, 2, HALO, cols),
            pltpu.VMEM((2, HALO, cols), jnp.int32),
            pltpu.SemaphoreType.DMA((2, 5)),
        ],
        10**6,
        *(pltpu.with_memory_space_constraint(x, pltpu.HBM) for x in inputs),
    )
    row_b = swap(to_b, 0, 1)
    row_a = swap(to_a, 0, 0)
    edge, *forward = call(
        interior_kernel,
        "interior",
        (vmem(2 * PARTS * TILE, TILE),) + (vmem(rows, cols),) * 6,
        [vmem(rows, cols)] * (FIELDS - 6),
        8 * 10**6,
        *near,
    )
    to_b, to_a, turned = call(
        columns_kernel,
        "columns",
        (vmem(SENT, TILE), vmem(SENT, TILE), vmem(SLOT, TILE)),
        [],
        10**5,
        row_b,
        row_a,
        edge,
    )
    col_b = swap(to_b, 1, 1)
    col_a = swap(to_a, 1, 0)
    vel_ends, wide, sides = call(
        adjoint_kernel,
        "adjoint",
        (
            vmem(4 * HALO, cols),
            vmem(MODES, TILE),
            vmem(ARRAYS * (LENGTH + 1) * SUB, TILE),
        ),
        [vmem(ARRAYS * STRIP, cols), vmem(2 * STRIP, cols), vmem(rows + STRIP, cols), vmem(TILE, cols)]
        + [vmem(STRIP, cols)] * STRIP_FIELDS
        + [vmem(rows, cols)] * (FIELDS - 4),
        8 * 10**6,
        row_b,
        row_a,
        *near,
        *forward,
        basis_p,
        basis_q,
        edge,
        turned,
    )
    devices = lax.axis_size(ROW_AXES + COL_AXES)
    _, *strips, coef = call(
        left_right_kernel,
        "left_right",
        (
            vmem(ARRAYS * (LENGTH + 1) * SUB, TILE),
            vmem(LENGTH * SUB, TILE),
            vmem(LENGTH * SUB, TILE),
            vmem(devices * (SUB + 1), TILE),
        ),
        [vmem(LENGTH * SUB, TILE)] * (STRIP_FIELDS + 1),
        4 * 10**6,
        sides,
        col_b,
        col_a,
        wide,
        tile_block,
        basis_rows,
        basis_cols,
        aliases={0: 0},
    )
    coef = coef.reshape(devices, 1, (SUB + 1) * TILE)
    parts = lax.all_to_all(coef, ROW_AXES + COL_AXES, 0, 0, tiled=True)
    state = call(
        join_kernel,
        "join",
        jax.ShapeDtypeStruct((2, rows, cols), F32),
        [vmem(2 * PARTS * TILE, TILE)],
        4 * 10**6,
        *forward[4:],
        vel_ends,
        *strips,
    )
    owners = owner_list.reshape(lax.axis_size("own"), -1)
    picked = call(
        pick_kernel,
        "pick",
        jax.ShapeDtypeStruct((1, owners.shape[1], MODES * MODES), F32),
        [],
        10**5,
        owners,
        parts.reshape(-1, TILE),
    )
    return (state, picked)


def solution(mesh):
    return jax.shard_map(
        local,
        mesh=mesh,
        in_specs=(
            P(("row", "own"), "col"),
            P(("row", "own"), "col"),
            P(None, ("row", "own"), "col"),
            P(None, ("row", "own"), "col"),
            P(("row", "own"), "col"),
            P(("row", "own"), "col"),
            P(),
        ),
        out_specs=(P(None, ("row", "own"), "col"), P("own", None, None)),
        check_vma=False,
    )
```

```python
import math

import jax
import jax.numpy as jnp
import numpy as np
from jax import lax
from jax.experimental import pallas as pl
from jax.experimental.pallas import tpu as pltpu
from jax.sharding import PartitionSpec as P

TILE = 128
MODES = 32
SWEEPS = 3
SUB = 8
HALO = 8
INNER = 2 * HALO
STRIP = 40
LEAD = HALO - 1
KEPT = 12
OUTER = (LEAD, STRIP - 2 * HALO)
NEAR, FAR = 7, 6
LENGTH = STRIP // 2
ARRAYS = 7
VISC, FRIC, DRIV, MASK, OBS = 0, 1, 2, 4, 5
EDGE = ARRAYS * HALO
SLOT = 2 * INNER
PER = TILE // SLOT
GROUPS = 5
SENT = 2 * GROUPS * HALO + HALO
PARTS = 3
UPPER, LOWER = 32, 64
ROW_AXES = ("row", "own")
COL_AXES = ("col",)
F32 = jnp.float32
LIMIT = 40 * 1024 * 1024


def swap(x, axis, first):
    sizes = lax.axis_size(ROW_AXES), lax.axis_size(COL_AXES)
    owners = lax.axis_size("own")

    def device(i, j):
        return (i // owners * sizes[1] + j) * owners + i % owners

    pairs = []
    for i in range(sizes[0]):
        for j in range(sizes[1]):
            place = [i, j]
            if first and place[axis] in (0, sizes[axis] - 1):
                place[1 - axis] ^= 1
            else:
                place[axis] = ((place[axis] + first) ^ 1) - first
            pairs.append((device(i, j), device(*place)))
    return lax.ppermute(x, ("row", "col", "own"), pairs)


def position(axes):
    index, size = 0, 1
    for axis in axes:
        index = index * lax.axis_size(axis) + lax.axis_index(axis)
        size *= lax.axis_size(axis)
    assert size % 2 == 0
    return lax.rem(index, 2) == 0, (index == 0) | (index == size - 1)


def is_even(axes):
    return position(axes)[0]


def lanes():
    return lax.broadcasted_iota(jnp.int32, (SUB, TILE), 1)


def call(kernel, name, outs, scratch, cost, *args, aliases={}):
    return pl.pallas_call(
        kernel,
        out_shape=outs,
        scratch_shapes=scratch,
        input_output_aliases=aliases,
        compiler_params=pltpu.CompilerParams(vmem_limit_bytes=LIMIT),
        cost_estimate=pl.CostEstimate(flops=cost, bytes_accessed=cost, transcendentals=0),
        name=name,
    )(*args)


def vmem(*shape):
    return pltpu.VMEM(shape, F32)


FIELDS = 14
STRIP_FIELDS = 24
LAG = 4


class Domain:
    def __init__(self, refs, base, span, source, seam=None):
        self.refs, self.base, self.span, self.source, self.seam = refs, base, span, source, seam

    def at(self, j):
        return pl.ds(self.base + SUB * j, SUB)

    def prepare(self, flipped):
        n2, n4, c, i, b0, b1 = self.refs[:6]
        visc = [self.source(VISC, j) for j in range(self.span)]
        for j in range(self.span):
            at = self.at(j)
            pair = visc[j] + (visc[j - 1] if j else self.before(visc[-1]))
            fric = self.source(FRIC, j)
            diag = 1.25 * (pair + pltpu.roll(pair, 1, 1)) + fric
            on = self.source(MASK, j) > 0.0
            inv = jnp.where(on, 0.5 / jnp.where(on, diag, 1.0), 0.0)
            half = 0.5 * visc[j]
            n2[at, :] = half
            n4[at, :] = 0.5 * half
            c[at, :] = 1.0 - fric * inv
            i[at, :] = inv
            for k, b in enumerate((b0, b1)):
                value = inv * self.source(DRIV + (1 - k if flipped else k), j)
                b[at, :] = value
                self.write(k, at, value + value)

    def before(self, last):
        wrapped = pltpu.roll(last, 1, 0)
        if self.seam is None:
            return wrapped
        row = lax.broadcasted_iota(jnp.int32, (SUB, TILE), 0)
        return jnp.where(row == SUB // 2, self.seam(), wrapped)

    def write(self, k, at, value):
        self.refs[6 + k][at, :] = value
        self.refs[8 + k][at, :] = pltpu.roll(value, TILE - 1, 1)

    def retarget(self, flipped, velocity=None):
        i, b0, b1 = self.refs[3:6]
        w0, w1 = velocity or self.refs[6:8]
        for j in range(self.span):
            at = self.at(j)
            for k, (b, w) in enumerate(((b0, w0), (b1, w1))):
                value = i[at, :] * (w[at, :] - self.source(OBS + (1 - k if flipped else k), j))
                b[at, :] = value
                self.write(k, at, value + value)

    def sweep(self):
        self.differences()
        self.update()

    def differences(self):
        n2, n4 = self.refs[:2]
        fields = self.refs[6:10]
        parts = self.refs[10:14]

        def corners(j, here, below):
            w0, w1, r0, r1 = here
            v0, v1, s0, s1 = below
            a1, a2 = s0 - w0, v0 - r0
            e1, e2 = s1 - w1, v1 - r1
            x, y = a1 + a2, e1 - e2
            q = (a1 - a2) + (e1 + e2)
            both = x + y
            at = self.at(j)
            half = n2[at, :]
            return half * (both + x), n4[at, :] * q, half * (both + y)

        def load(j):
            at = self.at(j)
            return [field[at, :] for field in fields]

        top = load(0)
        last = corners(self.span - 1, load(self.span - 1), [pltpu.roll(v, SUB - 1, 0) for v in top])
        up = [pltpu.roll(v, 1, 0) for v in last]
        here = top
        for j in range(self.span):
            at = self.at(j)
            if j < self.span - 1:
                below = load(j + 1)
                p, q, r = corners(j, here, below)
                here = below
            else:
                p, q, r = last
            g, t = up[0] - p, up[1] + q
            gq, tr = up[1] - q, up[2] + r
            parts[0][at, :] = g - t
            parts[1][at, :] = gq - tr
            parts[2][at, :] = pltpu.roll(g + t, 1, 1)
            parts[3][at, :] = pltpu.roll(gq + tr, 1, 1)
            up = (p, q, r)

    def update(self):
        c, i, b0, b1, w0, w1 = self.refs[2:8]
        parts = self.refs[10:14]
        for j in range(self.span):
            at = self.at(j)
            cv, iv = c[at, :], i[at, :]
            for k, (b, w) in enumerate(((b0, w0), (b1, w1))):
                value = (cv * w[at, :] + b[at, :]) - iv * (parts[k][at, :] + parts[k + 2][at, :])
                self.write(k, at, value)


class Strips(Domain):
    wraps = True

    def prepare(self, flipped):
        super().prepare(flipped)
        for j in range(self.span):
            at = self.at(j)
            for now, later in zip(self.refs[2:6], self.refs[10:14]):
                later[at, :] = pltpu.roll(now[at, :], TILE - 1, 1)
        if self.wraps:
            for now, before in zip(self.refs[:2], self.refs[14:16]):
                before[self.at(0), :] = pltpu.roll(now[self.at(self.span - 1), :], 1, 0)

    def retarget(self, flipped, velocity=None):
        super().retarget(flipped, velocity)
        for j in range(self.span):
            at = self.at(j)
            for now, later in zip(self.refs[4:6], self.refs[12:14]):
                later[at, :] = pltpu.roll(now[at, :], TILE - 1, 1)

    def corners(self, halves, quarters, j, here, below):
        w0, w1, r0, r1 = here
        v0, v1, s0, s1 = below
        a1, a2 = s0 - w0, v0 - r0
        e1, e2 = s1 - w1, v1 - r1
        x, y = a1 + a2, e1 - e2
        q = (a1 - a2) + (e1 + e2)
        both = x + y
        at = self.at(j)
        half = halves[at, :]
        return half * (both + x), quarters[at, :] * q, half * (both + y)

    def load(self, j):
        at = self.at(j)
        return [field[at, :] for field in self.refs[6:10]]

    def differences(self):
        kept, turned, kept_next, turned_next = (self.refs[16 + 2 * k : 18 + 2 * k] for k in range(4))
        corners, load = self.corners, self.load
        top, end = load(0), load(self.span - 1)
        up = corners(*self.refs[14:16], 0, [pltpu.roll(v, 1, 0) for v in end], top)
        bottom = [pltpu.roll(v, SUB - 1, 0) for v in top]
        here = top
        for j in range(self.span):
            at = self.at(j)
            below = load(j + 1) if j < self.span - 1 else bottom
            p, q, r = corners(*self.refs[:2], j, here, below)
            g, t = up[0] - p, up[1] + q
            gq, tr = up[1] - q, up[2] + r
            for k, (stay, move) in enumerate(((g - t, g + t), (gq - tr, gq + tr))):
                kept[k][at, :] = stay
                turned_next[k][at, :] = move
                turned[k][at, :] = pltpu.roll(move, 1, 1)
                kept_next[k][at, :] = pltpu.roll(stay, TILE - 1, 1)
            up, here = (p, q, r), below

    def update(self):
        for first, offset, parts in ((2, 6, (16, 18)), (10, 8, (20, 22))):
            c, i, *b = self.refs[first : first + 4]
            for j in range(self.span):
                at = self.at(j)
                cv, iv = c[at, :], i[at, :]
                for k in range(2):
                    w = self.refs[offset + k]
                    change = self.refs[parts[0] + k][at, :] + self.refs[parts[1] + k][at, :]
                    w[at, :] = (cv * w[at, :] + b[k][at, :]) - iv * change


class Bands(Strips):
    wraps = False

    def before(self, last):
        return self.source(VISC, -1)

    def sweep(self):
        pending = []
        none = jnp.zeros((SUB, TILE), F32)
        up, here = [none] * 3, self.load(0)
        for j in range(self.span):
            below = self.load(j + 1) if j < self.span - 1 else [none] * 4
            p, q, r = self.corners(*self.refs[:2], j, here, below)
            g, t = up[0] - p, up[1] + q
            gq, tr = up[1] - q, up[2] + r
            pending.append(
                [
                    (stay, pltpu.roll(move, 1, 1), pltpu.roll(stay, TILE - 1, 1), move)
                    for stay, move in ((g - t, g + t), (gq - tr, gq + tr))
                ]
            )
            up, here = (p, q, r), below
            if j >= LAG:
                self.change(j - LAG, pending[j - LAG])
        for j in range(self.span - LAG, self.span):
            self.change(j, pending[j])

    def change(self, j, parts):
        at = self.at(j)
        for offset, first in ((0, 2), (2, 10)):
            c, i, *b = (ref[at, :] for ref in self.refs[first : first + 4])
            for k in range(2):
                w = self.refs[6 + offset + k]
                w[at, :] = (c * w[at, :] + b[k]) - i * (parts[k][offset] + parts[k][offset + 1])


def run(domains, written_out=False):
    def body(_, carry):
        for domain in domains:
            domain.sweep()
        return carry

    if written_out:
        for k in range(SWEEPS):
            body(k, 0)
    else:
        lax.fori_loop(0, SWEEPS, body, 0)


def ends_kernel(visc, fric, driv, mask, obs, to_b, to_a, one, two, flags, sems):
    rows = visc.shape[0]
    copies = []
    for e, first in enumerate((0, rows - HALO)):
        at = pl.ds(first, HALO)
        pieces = [
            (visc.at[at], one.at[e, 0]),
            (fric.at[at], one.at[e, 1]),
            (driv.at[:, at], two.at[e, 0]),
            (mask.at[at], flags.at[e]),
            (obs.at[:, at], two.at[e, 1]),
        ]
        for n, (source, place) in enumerate(pieces):
            copies.append(pltpu.make_async_copy(source, place, sems.at[e, n]))
    for copy in copies:
        copy.start()
    for copy in copies:
        copy.wait()
    even, at_end = position(ROW_AXES)

    def edge(e):
        return [one[e, 0], one[e, 1], two[e, 0, 0], two[e, 0, 1], flags[e].astype(F32), two[e, 1, 0], two[e, 1, 1]]

    for a, (head, tail) in enumerate(zip(edge(0), edge(1))):
        at = slice(HALO * a, HALO * (a + 1))
        to_a[at, :] = jnp.where(even, tail, head)
        to_b[at, :] = jnp.where(at_end, 0.0, jnp.where(even, head, tail))


def field_of(visc, fric, driv, mask, obs):
    def field(a, at):
        if a == MASK:
            return mask[at, :].astype(F32)
        if a >= OBS:
            return obs[a - OBS, at, :]
        if a >= DRIV:
            return driv[a - DRIV, at, :]
        return (visc, fric)[a][at, :]

    return field


def first_row(part, lane):
    if part < 2:
        return TILE * part + lane
    if lane < INNER + HALO:
        return TILE + lane
    if lane >= TILE - INNER - HALO:
        return lane
    if UPPER + HALO <= lane < UPPER + SLOT:
        return lane - UPPER - HALO
    if LOWER <= lane < LOWER + INNER + HALO:
        return 2 * TILE - INNER - HALO + lane - LOWER
    return None


def right_part(row):
    seam = TILE - HALO <= row < TILE + HALO
    part = 2 if seam or row == 0 or row == 2 * TILE - HALO else row // TILE
    return part, [lane for lane in range(0, TILE, SUB) if first_row(part, lane) == row][-1]


def slot(part, a):
    return TILE * (2 * part + a // PER) + SLOT * (a % PER)


def interior_kernel(visc, fric, driv, mask, obs, edge, n2, n4, c, i, v0, v1, *refs):
    span = visc.shape[0] // SUB
    field = field_of(visc, fric, driv, mask, obs)
    lane = lanes()
    for part in range(PARTS):
        for m in range(-(-ARRAYS // PER)):
            strips = []
            for at in range(0, TILE, SUB):
                row = first_row(part, at)
                packed = jnp.zeros((SUB, TILE), F32)
                if row is not None:
                    for k in range(min(PER, ARRAYS - PER * m)):
                        value = field(PER * m + k, slice(row, row + SUB))
                        moved = pltpu.roll(value, (SLOT * k + INNER) % TILE, 1)
                        packed = jnp.where(lax.div(lane, SLOT) == k, moved, packed)
                strips.append(packed)
            base = TILE * (2 * part + m)
            edge[base : base + TILE, :] = jnp.concatenate(strips, axis=0).T
    refs = (n2, n4, c, i, *refs[:2], v0, v1, *refs[2:])
    domain = Domain(refs, 0, span, lambda a, j: field(a, pl.ds(j, SUB, stride=span)))
    domain.prepare(False)
    run([domain])


def columns_kernel(row_b, row_a, edge, to_b, to_a, turned):
    even = is_even(ROW_AXES)
    above = jnp.where(even, row_b[...], row_a[...])
    below = jnp.where(even, row_a[...], row_b[...])
    halo = jnp.concatenate([above, below, jnp.zeros((TILE - 2 * EDGE, TILE), F32)], axis=0).T
    turned[:INNER, :] = halo[TILE - INNER :]
    turned[INNER:, :] = halo[:INNER]
    even, at_end = position(COL_AXES)
    row = lax.broadcasted_iota(jnp.int32, (SUB, TILE), 0)

    def put(out, right, left):
        right = pltpu.roll(right, LEAD, 0)
        to_a[out : out + HALO, :] = jnp.where(even, right, left)
        to_b[out : out + HALO, :] = jnp.where(at_end, 0.0, jnp.where(even, left, right))

    for part in range(2):
        right, left = [], []
        for a in range(ARRAYS):
            at = slot(part, a) + INNER
            right.append(edge[at - HALO : at, :])
            left.append(edge[at : at + HALO, :])
        for k in range(2):
            seen_r, seen_l = right[OBS + k], left[OBS + k]
            g = 1 + 2 * k
            right[g] = jnp.where(row < 2, pltpu.roll(seen_r, 2, 0), right[g])
            right[g + 1] = jnp.where(row < 2, pltpu.roll(seen_r, 4, 0), right[g + 1])
            left[g] = jnp.where(row >= 6, pltpu.roll(seen_l, 6, 0), left[g])
            left[g + 1] = jnp.where(row >= 6, pltpu.roll(seen_l, 4, 0), left[g + 1])
        for g in range(GROUPS):
            put(HALO * (GROUPS * part + g), right[g], left[g])
    put(2 * GROUPS * HALO, halo[TILE - HALO :], halo[:HALO])


def strided(stack, base):
    span = STRIP // SUB
    return lambda a, j: stack[pl.ds(base + STRIP * a + j, SUB, stride=span), :]


def fill(stack, base, first, last):
    row = lax.broadcasted_iota(jnp.int32, (SUB, TILE), 0)
    one, two = (pltpu.roll(value, LEAD, 0) for value in first)
    mixed = [jnp.where(row == LEAD, two, one), jnp.where(row < SUB // 2, two, last[0])]
    for k, value in enumerate((one, *mixed, last[1])):
        stack[base + SUB * k : base + SUB * (k + 1), :] = value


def velocity(domain, plain, base):
    for j in range(domain.span):
        at = domain.at(j)
        for k in range(2):
            plain[pl.ds(base + STRIP * k + j, SUB, stride=domain.span), :] = domain.refs[6 + k][at, :]


def density(domain, plain, base, out, place):
    w0, w1 = domain.refs[6:8]
    for j in range(domain.span):
        at = domain.at(j)
        v0, v1 = (plain[pl.ds(base + STRIP * k + j, SUB, stride=domain.span), :] for k in range(2))
        value = -domain.source(FRIC, j) * (w0[at, :] * v0 + w1[at, :] * v1)
        out[pl.ds(place + j, SUB, stride=domain.span), :] = value


def beside():
    lane = lanes()
    return (lane < NEAR) | (lane >= TILE - FAR)


def ends(second):
    row = lax.broadcasted_iota(jnp.int32, (SUB, TILE), 0)
    return row >= SUB - FAR if second else row < NEAR


def adjoint_kernel(
    row_b, row_a, visc, fric, driv, mask, obs, n2, n4, c, i, v0, v1, basis_p, basis_q, edge, turned,
    vel, wide, sides,
    stack, plain, dens, total, *refs,
):
    rows = visc.shape[0]
    span = rows // SUB
    even = is_even(ROW_AXES)
    field = field_of(visc, fric, driv, mask, obs)
    for a in range(ARRAYS):
        at = slice(HALO * a, HALO * (a + 1))
        got_a, got_b = row_a[at, :], row_b[at, :]
        base = STRIP * a
        first = [field(a, slice(at, at + SUB)) for at in (0, SUB)]
        last = [field(a, slice(at, at + SUB)) for at in (rows - 2 * SUB, rows - SUB)]
        fill(stack, base, first, last)
        stack[base : base + LEAD, :] = jnp.where(even, got_b, got_a)[HALO - LEAD :]
        stack[base + STRIP - HALO : base + STRIP, :] = jnp.where(even, got_a, got_b)
    strips = Strips(refs[:STRIP_FIELDS], 0, STRIP // SUB, strided(stack, 0), lambda: visc[rows - KEPT - 1 : rows - KEPT, :])
    strips.prepare(False)
    run([strips])
    velocity(strips, plain, 0)
    for k in range(2):
        for e in range(2):
            out = HALO * (2 * k + e)
            vel[out : out + HALO, :] = plain[STRIP * k + OUTER[e] : STRIP * k + OUTER[e] + HALO, :]
    interior = Domain(
        (n2, n4, c, i, *refs[STRIP_FIELDS:]), 0, span, lambda a, j: field(a, pl.ds(j, SUB, stride=span))
    )
    strips.retarget(False)
    interior.retarget(False, (v0, v1))
    run([interior, strips])
    w0, w1 = interior.refs[6:8]
    for j in range(span):
        at = interior.at(j)
        value = -interior.source(FRIC, j) * (w0[at, :] * v0[at, :] + w1[at, :] * v1[at, :])
        dens[pl.ds(j, SUB, stride=span), :] = value
    density(strips, plain, 0, dens, rows)

    side = beside()
    for s in range(0, TILE, SUB):
        summed = jnp.zeros((SUB, TILE), F32)
        for row in range(s, rows, TILE):
            value = dens[row : row + SUB, :]
            if row in (0, rows - SUB):
                at = rows + OUTER[row > 0]
                value = jnp.where(ends(row > 0), dens[at : at + SUB, :], value)
            summed += value
        total[s : s + SUB, :] = jnp.where(side, 0.0, summed)
    exact = dict(precision=lax.Precision.HIGHEST, preferred_element_type=F32)
    half = jnp.dot(basis_p[...], total[...], **exact)
    wide[...] = jnp.dot(half, basis_q[...], **exact)

    corner = corners()
    for part in range(PARTS):
        for a in range(ARRAYS):
            columns = []
            for r in range(0, SLOT, SUB):
                value = edge[slot(part, a) + r : slot(part, a) + r + SUB, :]
                if part == 2:
                    moved = pltpu.roll(turned[r : r + SUB, :], (UPPER - HALO * a) % TILE, 1)
                    value = jnp.where(corner, moved, value)
                columns.append(value)
            first, second = columns[2:]
            sides[band(a, 0, part, LEAD, SUB), :] = first
            sides[band(a, 0, part, LEAD + SUB, LENGTH - LEAD - SUB), :] = second[: LENGTH - LEAD - SUB]
            sides[band(a, 1, part, 0, SUB // 2), :] = pltpu.roll(columns[0], SUB // 2, 0)[: SUB // 2]
            sides[band(a, 1, part, SUB // 2, SUB), :] = columns[1]
            if a == VISC:
                sides[band(a, 0, part, -1, 1), :] = first[:1]
                sides[band(a, 1, part, -1, 1), :] = columns[0][SUB // 2 - 1 : SUB // 2]


def band(a, side, part, first, count):
    return pl.ds(SUB * ((LENGTH + 1) * a + 1 + first) + PARTS * side + part, count, stride=SUB)


def corners():
    lane = lanes()
    above = (lane >= UPPER) & (lane < UPPER + HALO)
    return above | ((lane >= LOWER + INNER + HALO) & (lane < LOWER + SLOT))


def split(x, axis):
    high = x.astype(jnp.bfloat16)
    low = (x - high.astype(F32)).astype(jnp.bfloat16)
    return jnp.concatenate([high, high, low], axis=axis)


def split_constant(x, axis):
    x = np.asarray(x, np.float32)
    high = np.asarray(x, jnp.bfloat16)
    low = np.asarray(x - np.asarray(high, np.float32), jnp.bfloat16)
    return jnp.asarray(np.concatenate([high, low, high], axis=axis))


def outermost(side, part):
    first = LENGTH - 2 * HALO if side else LEAD
    return pl.ds(SUB * first + PARTS * side + part, HALO, stride=SUB)


def left_right_kernel(
    _, col_b, col_a, wide_in, block, basis_rows, basis_cols,
    stack, vel0, vel1, coef,
    plain, *refs,
):
    even = is_even(COL_AXES)
    lane = lanes()
    row = lax.broadcasted_iota(jnp.int32, (SUB, TILE), 0)
    upper = (lane >= UPPER + HALO) & (lane < UPPER + SLOT)
    lower = (lane >= LOWER) & (lane < LOWER + INNER + HALO)
    seam_t0 = lane >= TILE - INNER - HALO
    seam_t1 = lane < INNER + HALO
    corner = corners()
    for from_left in (True, False):
        groups = []
        for g in range(2 * GROUPS + 1):
            got_a, got_b = col_a[HALO * g : HALO * (g + 1), :], col_b[HALO * g : HALO * (g + 1), :]
            groups.append(jnp.where(even, got_b, got_a) if from_left else jnp.where(even, got_a, got_b))
        tiles = []
        for part in range(2):
            tile = groups[GROUPS * part : GROUPS * (part + 1)]
            for k in range(2):
                g, h = tile[1 + 2 * k], tile[2 + 2 * k]
                if from_left:
                    tile.append(jnp.where(row >= 5, pltpu.roll(g, 6, 0), pltpu.roll(h, 4, 0)))
                else:
                    tile.append(jnp.where(row < 2, pltpu.roll(g, 2, 0), pltpu.roll(h, 4, 0)))
            tiles.append(tile)
        for a in range(ARRAYS):
            t0, t1 = tiles[0][a], tiles[1][a]
            third = jnp.where(corner, pltpu.roll(groups[-1], (UPPER - HALO * a) % TILE, 1), 0.0)
            third = jnp.where(upper, pltpu.roll(t0, UPPER + HALO, 1), third)
            third = jnp.where(lower, pltpu.roll(t1, LOWER + INNER + HALO, 1), third)
            third = jnp.where(seam_t0, t0, jnp.where(seam_t1, t1, third))
            for part, value in enumerate((t0, t1, third)):
                if from_left:
                    stack[band(a, 0, part, 0, LEAD), :] = value[:LEAD]
                else:
                    stack[band(a, 1, part, LENGTH - HALO, HALO), :] = value
    def source(a, j):
        at = SUB * ((LENGTH + 1) * a + 1 + j)
        return stack[at : at + SUB, :]

    bands = Bands(refs, 0, LENGTH, source)
    bands.prepare(True)
    run([bands], True)
    vel0[...] = refs[6][...]
    vel1[...] = refs[7][...]
    bands.retarget(True)
    run([bands], True)
    for j in range(LENGTH):
        at = bands.at(j)
        value = refs[6][at, :] * vel0[at, :] + refs[7][at, :] * vel1[at, :]
        plain[at, :] = -source(FRIC, j) * value

    def side(part):
        return jnp.concatenate([plain[outermost(k, part), :] for k in range(2)], axis=0)

    lane = lax.broadcasted_iota(jnp.int32, (2 * HALO, TILE), 1)
    row = lax.broadcasted_iota(jnp.int32, (2 * HALO, TILE), 0)
    right = (row < NEAR) | (row >= 2 * HALO - FAR)
    straight = (lane >= HALO) & (lane < TILE - HALO)
    seam = (lane < HALO) | (lane >= TILE - HALO)
    top = (lane >= UPPER + HALO) & (lane < UPPER + 2 * HALO)
    bottom = (lane >= LOWER + INNER) & (lane < LOWER + INNER + HALO)
    dens = jnp.concatenate(
        [
            jnp.where(right & straight, side(0) + side(1), 0.0),
            jnp.where(right & (seam | top | bottom), side(2), 0.0),
        ],
        axis=1,
    )
    half = lax.dot_general(
        basis_rows[...], split(dens, 1), (((1,), (1,)), ((), ())), preferred_element_type=F32
    )
    wide = wide_in[...] + jnp.dot(split(half, 1), basis_cols[...], preferred_element_type=F32)
    lane = lanes()
    which = lax.div(lane, MODES)
    flat = wide[:SUB]
    for j in range(1, MODES // SUB):
        flat = jnp.where(which == j, wide[SUB * j : SUB * (j + 1)], flat)
    mark = jnp.broadcast_to(block[:1, :].astype(F32), (SUB, TILE))
    row = lax.broadcasted_iota(jnp.int32, (SUB, TILE), 0)
    moved = [flat] + [pltpu.roll(flat, r, 0) for r in range(1, SUB)] + [flat]
    lines = [flat] + [
        jnp.where(row < r - 1, moved[r - 1], jnp.where(row == r - 1, mark, moved[r])) for r in range(1, SUB + 1)
    ]
    cycle = SUB * (SUB + 1)
    chunk = min(4, coef.shape[0] // cycle)

    def spread(d, carry):
        for e in range(chunk):
            for r, line in enumerate(lines):
                coef[pl.ds(pl.multiple_of((d * chunk + e) * cycle + SUB * r, SUB), SUB), :] = line
        return carry

    lax.fori_loop(0, coef.shape[0] // cycle // chunk, spread, 0)


def join_kernel(v0, v1, vel_ends, side0, side1, vel, turned):
    rows = vel.shape[1]
    span = rows // SUB
    middle = jnp.zeros((TILE - 2 * HALO, TILE), F32)
    side = beside()
    for k, (v, strips) in enumerate(((v0, side1), (v1, side0))):
        for part in range(PARTS):
            first, last = (strips[outermost(e, part), :] for e in range(2))
            at = TILE * (2 * part + k)
            turned[at : at + TILE, :] = jnp.concatenate([first, middle, last], axis=0).T
        for row in range(0, rows, SUB):
            value = v[pl.ds(SUB * (row % span) + row // span, SUB, stride=SUB), :]
            if row in (0, rows - SUB):
                at = HALO * (2 * k + (row > 0))
                value = jnp.where(ends(row > 0), vel_ends[at : at + HALO, :], value)
            part, lane = right_part(row)
            at = TILE * (2 * part + k) + lane
            vel[k, row : row + SUB, :] = jnp.where(side, turned[at : at + SUB, :], value)


def bases():
    places = np.arange(TILE) + 0.5
    basis = np.cos(math.pi * places[:, None] * np.arange(MODES)[None, :] / TILE)
    groups = MODES // SUB
    order = np.arange(MODES).reshape(SUB, groups).T.reshape(-1)
    rows = basis[:, order] / TILE
    cols = np.tile(basis, (1, groups))
    placed = np.zeros((2 * TILE, MODES))
    for row in range(0, 2 * TILE, SUB):
        part, lane = right_part(row)
        at = lane + (TILE if part == 2 else 0)
        placed[at : at + SUB] = rows[row % TILE : row % TILE + SUB]
    outer = np.concatenate([cols[:HALO], cols[TILE - HALO :]])
    return jnp.asarray(rows.T, F32), jnp.asarray(cols, F32), split_constant(placed.T, 1), split_constant(outer, 0)


def pick_kernel(owners, every, out):
    mine = out.shape[1]
    own = lax.axis_index("own")
    wanted = [owners[pl.ds(own, 1), k : k + 1].astype(F32) for k in range(mine)]
    lines = SUB + 1
    devices = every.shape[0] // lines
    chunk = min(4, devices // SUB)

    def body(d, sums):
        sums = list(sums)
        for e in range(chunk):
            base = (d * chunk + e) * SUB * lines
            mark = every[pl.ds(base + SUB, SUB, stride=lines), :]
            hits = [mark == wanted[k] for k in range(mine)]
            for r in range(SUB):
                part = every[pl.ds(base + r, SUB, stride=lines), :]
                for k in range(mine):
                    sums[SUB * k + r] += jnp.where(hits[k], part, 0.0)
        return tuple(sums)

    start = (jnp.zeros((SUB, TILE), F32),) * (mine * SUB)
    sums = lax.fori_loop(0, devices // SUB // chunk, body, start)
    for k in range(mine):
        for r in range(SUB):
            total = jnp.sum(sums[SUB * k + r], axis=0, keepdims=True)
            out[0, k : k + 1, TILE * r : TILE * (r + 1)] = total


def local(viscosity, friction, driving, observed, ice_mask, tile_block, owner_list):
    rows, cols = viscosity.shape
    assert (rows, cols) == (2 * TILE, TILE)
    inputs = (viscosity, friction, driving, ice_mask, observed)
    near = [pltpu.with_memory_space_constraint(x, pltpu.VMEM) for x in inputs]
    basis_p, basis_q, basis_rows, basis_cols = bases()
    to_b, to_a = call(
        ends_kernel,
        "ends",
        (vmem(EDGE, cols), vmem(EDGE, cols)),
        [
            vmem(2, 2, HALO, cols),
            vmem(2, 2, 2, HALO, cols),
            pltpu.VMEM((2, HALO, cols), jnp.int32),
            pltpu.SemaphoreType.DMA((2, 5)),
        ],
        10**6,
        *(pltpu.with_memory_space_constraint(x, pltpu.HBM) for x in inputs),
    )
    row_b = swap(to_b, 0, 1)
    row_a = swap(to_a, 0, 0)
    edge, *forward = call(
        interior_kernel,
        "interior",
        (vmem(2 * PARTS * TILE, TILE),) + (vmem(rows, cols),) * 6,
        [vmem(rows, cols)] * (FIELDS - 6),
        8 * 10**6,
        *near,
    )
    to_b, to_a, turned = call(
        columns_kernel,
        "columns",
        (vmem(SENT, TILE), vmem(SENT, TILE), vmem(SLOT, TILE)),
        [],
        10**5,
        row_b,
        row_a,
        edge,
    )
    col_b = swap(to_b, 1, 1)
    col_a = swap(to_a, 1, 0)
    vel_ends, wide, sides = call(
        adjoint_kernel,
        "adjoint",
        (
            vmem(4 * HALO, cols),
            vmem(MODES, TILE),
            vmem(ARRAYS * (LENGTH + 1) * SUB, TILE),
        ),
        [vmem(ARRAYS * STRIP, cols), vmem(2 * STRIP, cols), vmem(rows + STRIP, cols), vmem(TILE, cols)]
        + [vmem(STRIP, cols)] * STRIP_FIELDS
        + [vmem(rows, cols)] * (FIELDS - 4),
        8 * 10**6,
        row_b,
        row_a,
        *near,
        *forward,
        basis_p,
        basis_q,
        edge,
        turned,
    )
    devices = lax.axis_size(ROW_AXES + COL_AXES)
    _, *strips, coef = call(
        left_right_kernel,
        "left_right",
        (
            vmem(ARRAYS * (LENGTH + 1) * SUB, TILE),
            vmem(LENGTH * SUB, TILE),
            vmem(LENGTH * SUB, TILE),
            vmem(devices * (SUB + 1), TILE),
        ),
        [vmem(LENGTH * SUB, TILE)] * (STRIP_FIELDS + 1),
        4 * 10**6,
        sides,
        col_b,
        col_a,
        wide,
        tile_block,
        basis_rows,
        basis_cols,
        aliases={0: 0},
    )
    coef = coef.reshape(devices, 1, (SUB + 1) * TILE)
    parts = lax.all_to_all(coef, ROW_AXES + COL_AXES, 0, 0, tiled=True)
    state = call(
        join_kernel,
        "join",
        jax.ShapeDtypeStruct((2, rows, cols), F32),
        [vmem(2 * PARTS * TILE, TILE)],
        4 * 10**6,
        *forward[4:],
        vel_ends,
        *strips,
    )
    owners = owner_list.reshape(lax.axis_size("own"), -1)
    picked = call(
        pick_kernel,
        "pick",
        jax.ShapeDtypeStruct((1, owners.shape[1], MODES * MODES), F32),
        [],
        10**5,
        owners,
        parts.reshape(-1, TILE),
    )
    return (state, picked)


def solution(mesh):
    return jax.shard_map(
        local,
        mesh=mesh,
        in_specs=(
            P(("row", "own"), "col"),
            P(("row", "own"), "col"),
            P(None, ("row", "own"), "col"),
            P(None, ("row", "own"), "col"),
            P(("row", "own"), "col"),
            P(("row", "own"), "col"),
            P(),
        ),
        out_specs=(P(None, ("row", "own"), "col"), P("own", None, None)),
        check_vma=False,
    )
```

```python
import math

import jax
import jax.numpy as jnp
import numpy as np
from jax import lax
from jax.experimental import pallas as pl
from jax.experimental.pallas import tpu as pltpu
from jax.sharding import PartitionSpec as P

TILE = 128
MODES = 32
SWEEPS = 3
SUB = 8
HALO = 8
INNER = 2 * HALO
STRIP = 40
LEAD = HALO - 1
KEPT = 12
OUTER = (LEAD, STRIP - 2 * HALO)
NEAR, FAR = 7, 6
LENGTH = STRIP // 2
ARRAYS = 7
VISC, FRIC, DRIV, MASK, OBS = 0, 1, 2, 4, 5
EDGE = ARRAYS * HALO
SLOT = 2 * INNER
PER = TILE // SLOT
GROUPS = 5
SENT = 2 * GROUPS * HALO + HALO
PARTS = 3
UPPER, LOWER = 32, 64
ROW_AXES = ("row", "own")
COL_AXES = ("col",)
F32 = jnp.float32
LIMIT = 40 * 1024 * 1024


def swap(x, axis, first):
    sizes = lax.axis_size(ROW_AXES), lax.axis_size(COL_AXES)
    owners = lax.axis_size("own")

    def device(i, j):
        return (i // owners * sizes[1] + j) * owners + i % owners

    pairs = []
    for i in range(sizes[0]):
        for j in range(sizes[1]):
            place = [i, j]
            if first and place[axis] in (0, sizes[axis] - 1):
                place[1 - axis] ^= 1
            else:
                place[axis] = ((place[axis] + first) ^ 1) - first
            pairs.append((device(i, j), device(*place)))
    return lax.ppermute(x, ("row", "col", "own"), pairs)


def position(axes):
    index, size = 0, 1
    for axis in axes:
        index = index * lax.axis_size(axis) + lax.axis_index(axis)
        size *= lax.axis_size(axis)
    assert size % 2 == 0
    return lax.rem(index, 2) == 0, (index == 0) | (index == size - 1)


def is_even(axes):
    return position(axes)[0]


def lanes():
    return lax.broadcasted_iota(jnp.int32, (SUB, TILE), 1)


def call(kernel, name, outs, scratch, cost, *args, aliases={}):
    return pl.pallas_call(
        kernel,
        out_shape=outs,
        scratch_shapes=scratch,
        input_output_aliases=aliases,
        compiler_params=pltpu.CompilerParams(vmem_limit_bytes=LIMIT),
        cost_estimate=pl.CostEstimate(flops=cost, bytes_accessed=cost, transcendentals=0),
        name=name,
    )(*args)


def vmem(*shape):
    return pltpu.VMEM(shape, F32)


FIELDS = 14
STRIP_FIELDS = 24
LAG = 4


class Domain:
    def __init__(self, refs, base, span, source, seam=None):
        self.refs, self.base, self.span, self.source, self.seam = refs, base, span, source, seam

    def at(self, j):
        return pl.ds(self.base + SUB * j, SUB)

    def prepare(self, flipped):
        n2, n4, c, i, b0, b1 = self.refs[:6]
        visc = [self.source(VISC, j) for j in range(self.span)]
        for j in range(self.span):
            at = self.at(j)
            pair = visc[j] + (visc[j - 1] if j else self.before(visc[-1]))
            fric = self.source(FRIC, j)
            diag = 1.25 * (pair + pltpu.roll(pair, 1, 1)) + fric
            on = self.source(MASK, j) > 0.0
            inv = jnp.where(on, 0.5 / jnp.where(on, diag, 1.0), 0.0)
            half = 0.5 * visc[j]
            n2[at, :] = half
            n4[at, :] = 0.5 * half
            c[at, :] = 1.0 - fric * inv
            i[at, :] = inv
            for k, b in enumerate((b0, b1)):
                value = inv * self.source(DRIV + (1 - k if flipped else k), j)
                b[at, :] = value
                self.write(k, at, value + value)

    def before(self, last):
        wrapped = pltpu.roll(last, 1, 0)
        if self.seam is None:
            return wrapped
        row = lax.broadcasted_iota(jnp.int32, (SUB, TILE), 0)
        return jnp.where(row == SUB // 2, self.seam(), wrapped)

    def write(self, k, at, value):
        self.refs[6 + k][at, :] = value
        self.refs[8 + k][at, :] = pltpu.roll(value, TILE - 1, 1)

    def retarget(self, flipped, velocity=None):
        i, b0, b1 = self.refs[3:6]
        w0, w1 = velocity or self.refs[6:8]
        for j in range(self.span):
            at = self.at(j)
            for k, (b, w) in enumerate(((b0, w0), (b1, w1))):
                value = i[at, :] * (w[at, :] - self.source(OBS + (1 - k if flipped else k), j))
                b[at, :] = value
                self.write(k, at, value + value)

    def sweep(self):
        self.differences()
        self.update()

    def differences(self):
        n2, n4 = self.refs[:2]
        fields = self.refs[6:10]
        parts = self.refs[10:14]

        def corners(j, here, below):
            w0, w1, r0, r1 = here
            v0, v1, s0, s1 = below
            a1, a2 = s0 - w0, v0 - r0
            e1, e2 = s1 - w1, v1 - r1
            x, y = a1 + a2, e1 - e2
            q = (a1 - a2) + (e1 + e2)
            both = x + y
            at = self.at(j)
            half = n2[at, :]
            return half * (both + x), n4[at, :] * q, half * (both + y)

        def load(j):
            at = self.at(j)
            return [field[at, :] for field in fields]

        top = load(0)
        last = corners(self.span - 1, load(self.span - 1), [pltpu.roll(v, SUB - 1, 0) for v in top])
        up = [pltpu.roll(v, 1, 0) for v in last]
        here = top
        for j in range(self.span):
            at = self.at(j)
            if j < self.span - 1:
                below = load(j + 1)
                p, q, r = corners(j, here, below)
                here = below
            else:
                p, q, r = last
            g, t = up[0] - p, up[1] + q
            gq, tr = up[1] - q, up[2] + r
            parts[0][at, :] = g - t
            parts[1][at, :] = gq - tr
            parts[2][at, :] = pltpu.roll(g + t, 1, 1)
            parts[3][at, :] = pltpu.roll(gq + tr, 1, 1)
            up = (p, q, r)

    def update(self):
        c, i, b0, b1, w0, w1 = self.refs[2:8]
        parts = self.refs[10:14]
        for j in range(self.span):
            at = self.at(j)
            cv, iv = c[at, :], i[at, :]
            for k, (b, w) in enumerate(((b0, w0), (b1, w1))):
                value = (cv * w[at, :] + b[at, :]) - iv * (parts[k][at, :] + parts[k + 2][at, :])
                self.write(k, at, value)


class Strips(Domain):
    wraps = True

    def prepare(self, flipped):
        super().prepare(flipped)
        for j in range(self.span):
            at = self.at(j)
            for now, later in zip(self.refs[2:6], self.refs[10:14]):
                later[at, :] = pltpu.roll(now[at, :], TILE - 1, 1)
        if self.wraps:
            for now, before in zip(self.refs[:2], self.refs[14:16]):
                before[self.at(0), :] = pltpu.roll(now[self.at(self.span - 1), :], 1, 0)

    def retarget(self, flipped, velocity=None):
        super().retarget(flipped, velocity)
        for j in range(self.span):
            at = self.at(j)
            for now, later in zip(self.refs[4:6], self.refs[12:14]):
                later[at, :] = pltpu.roll(now[at, :], TILE - 1, 1)

    def corners(self, halves, quarters, j, here, below):
        w0, w1, r0, r1 = here
        v0, v1, s0, s1 = below
        a1, a2 = s0 - w0, v0 - r0
        e1, e2 = s1 - w1, v1 - r1
        x, y = a1 + a2, e1 - e2
        q = (a1 - a2) + (e1 + e2)
        both = x + y
        at = self.at(j)
        half = halves[at, :]
        return half * (both + x), quarters[at, :] * q, half * (both + y)

    def load(self, j):
        at = self.at(j)
        return [field[at, :] for field in self.refs[6:10]]

    def differences(self):
        kept, turned, kept_next, turned_next = (self.refs[16 + 2 * k : 18 + 2 * k] for k in range(4))
        corners, load = self.corners, self.load
        top, end = load(0), load(self.span - 1)
        up = corners(*self.refs[14:16], 0, [pltpu.roll(v, 1, 0) for v in end], top)
        bottom = [pltpu.roll(v, SUB - 1, 0) for v in top]
        here = top
        for j in range(self.span):
            at = self.at(j)
            below = load(j + 1) if j < self.span - 1 else bottom
            p, q, r = corners(*self.refs[:2], j, here, below)
            g, t = up[0] - p, up[1] + q
            gq, tr = up[1] - q, up[2] + r
            for k, (stay, move) in enumerate(((g - t, g + t), (gq - tr, gq + tr))):
                kept[k][at, :] = stay
                turned_next[k][at, :] = move
                turned[k][at, :] = pltpu.roll(move, 1, 1)
                kept_next[k][at, :] = pltpu.roll(stay, TILE - 1, 1)
            up, here = (p, q, r), below

    def update(self):
        for first, offset, parts in ((2, 6, (16, 18)), (10, 8, (20, 22))):
            c, i, *b = self.refs[first : first + 4]
            for j in range(self.span):
                at = self.at(j)
                cv, iv = c[at, :], i[at, :]
                for k in range(2):
                    w = self.refs[offset + k]
                    change = self.refs[parts[0] + k][at, :] + self.refs[parts[1] + k][at, :]
                    w[at, :] = (cv * w[at, :] + b[k][at, :]) - iv * change


class Bands(Strips):
    wraps = False

    def before(self, last):
        return self.source(VISC, -1)

    def sweep(self):
        pending = []
        none = jnp.zeros((SUB, TILE), F32)
        up, here = [none] * 3, self.load(0)
        for j in range(self.span):
            below = self.load(j + 1) if j < self.span - 1 else [none] * 4
            p, q, r = self.corners(*self.refs[:2], j, here, below)
            g, t = up[0] - p, up[1] + q
            gq, tr = up[1] - q, up[2] + r
            pending.append(
                [
                    (stay, pltpu.roll(move, 1, 1), pltpu.roll(stay, TILE - 1, 1), move)
                    for stay, move in ((g - t, g + t), (gq - tr, gq + tr))
                ]
            )
            up, here = (p, q, r), below
            if j >= LAG:
                self.change(j - LAG, pending[j - LAG])
        for j in range(self.span - LAG, self.span):
            self.change(j, pending[j])

    def change(self, j, parts):
        at = self.at(j)
        for offset, first in ((0, 2), (2, 10)):
            c, i, *b = (ref[at, :] for ref in self.refs[first : first + 4])
            for k in range(2):
                w = self.refs[6 + offset + k]
                w[at, :] = (c * w[at, :] + b[k]) - i * (parts[k][offset] + parts[k][offset + 1])


def run(domains):
    def body(_, carry):
        for domain in domains:
            domain.sweep()
        return carry

    lax.fori_loop(0, SWEEPS, body, 0)


def ends_kernel(visc, fric, driv, mask, obs, to_b, to_a, one, two, flags, sems):
    rows = visc.shape[0]
    copies = []
    for e, first in enumerate((0, rows - HALO)):
        at = pl.ds(first, HALO)
        pieces = [
            (visc.at[at], one.at[e, 0]),
            (fric.at[at], one.at[e, 1]),
            (driv.at[:, at], two.at[e, 0]),
            (mask.at[at], flags.at[e]),
            (obs.at[:, at], two.at[e, 1]),
        ]
        for n, (source, place) in enumerate(pieces):
            copies.append(pltpu.make_async_copy(source, place, sems.at[e, n]))
    for copy in copies:
        copy.start()
    for copy in copies:
        copy.wait()
    even, at_end = position(ROW_AXES)

    def edge(e):
        return [one[e, 0], one[e, 1], two[e, 0, 0], two[e, 0, 1], flags[e].astype(F32), two[e, 1, 0], two[e, 1, 1]]

    for a, (head, tail) in enumerate(zip(edge(0), edge(1))):
        at = slice(HALO * a, HALO * (a + 1))
        to_a[at, :] = jnp.where(even, tail, head)
        to_b[at, :] = jnp.where(at_end, 0.0, jnp.where(even, head, tail))


def field_of(visc, fric, driv, mask, obs):
    def field(a, at):
        if a == MASK:
            return mask[at, :].astype(F32)
        if a >= OBS:
            return obs[a - OBS, at, :]
        if a >= DRIV:
            return driv[a - DRIV, at, :]
        return (visc, fric)[a][at, :]

    return field


def first_row(part, lane):
    if part < 2:
        return TILE * part + lane
    if lane < INNER + HALO:
        return TILE + lane
    if lane >= TILE - INNER - HALO:
        return lane
    if UPPER + HALO <= lane < UPPER + SLOT:
        return lane - UPPER - HALO
    if LOWER <= lane < LOWER + INNER + HALO:
        return 2 * TILE - INNER - HALO + lane - LOWER
    return None


def right_part(row):
    seam = TILE - HALO <= row < TILE + HALO
    part = 2 if seam or row == 0 or row == 2 * TILE - HALO else row // TILE
    return part, [lane for lane in range(0, TILE, SUB) if first_row(part, lane) == row][-1]


def slot(part, a):
    return TILE * (2 * part + a // PER) + SLOT * (a % PER)


def interior_kernel(visc, fric, driv, mask, obs, edge, n2, n4, c, i, v0, v1, *refs):
    span = visc.shape[0] // SUB
    field = field_of(visc, fric, driv, mask, obs)
    lane = lanes()
    for part in range(PARTS):
        for m in range(-(-ARRAYS // PER)):
            strips = []
            for at in range(0, TILE, SUB):
                row = first_row(part, at)
                packed = jnp.zeros((SUB, TILE), F32)
                if row is not None:
                    for k in range(min(PER, ARRAYS - PER * m)):
                        value = field(PER * m + k, slice(row, row + SUB))
                        moved = pltpu.roll(value, (SLOT * k + INNER) % TILE, 1)
                        packed = jnp.where(lax.div(lane, SLOT) == k, moved, packed)
                strips.append(packed)
            base = TILE * (2 * part + m)
            edge[base : base + TILE, :] = jnp.concatenate(strips, axis=0).T
    refs = (n2, n4, c, i, *refs[:2], v0, v1, *refs[2:])
    domain = Domain(refs, 0, span, lambda a, j: field(a, pl.ds(j, SUB, stride=span)))
    domain.prepare(False)
    run([domain])


def columns_kernel(row_b, row_a, edge, to_b, to_a, turned):
    even = is_even(ROW_AXES)
    above = jnp.where(even, row_b[...], row_a[...])
    below = jnp.where(even, row_a[...], row_b[...])
    halo = jnp.concatenate([above, below, jnp.zeros((TILE - 2 * EDGE, TILE), F32)], axis=0).T
    turned[:INNER, :] = halo[TILE - INNER :]
    turned[INNER:, :] = halo[:INNER]
    even, at_end = position(COL_AXES)
    row = lax.broadcasted_iota(jnp.int32, (SUB, TILE), 0)

    def put(out, right, left):
        right = pltpu.roll(right, LEAD, 0)
        to_a[out : out + HALO, :] = jnp.where(even, right, left)
        to_b[out : out + HALO, :] = jnp.where(at_end, 0.0, jnp.where(even, left, right))

    for part in range(2):
        right, left = [], []
        for a in range(ARRAYS):
            at = slot(part, a) + INNER
            right.append(edge[at - HALO : at, :])
            left.append(edge[at : at + HALO, :])
        for k in range(2):
            seen_r, seen_l = right[OBS + k], left[OBS + k]
            g = 1 + 2 * k
            right[g] = jnp.where(row < 2, pltpu.roll(seen_r, 2, 0), right[g])
            right[g + 1] = jnp.where(row < 2, pltpu.roll(seen_r, 4, 0), right[g + 1])
            left[g] = jnp.where(row >= 6, pltpu.roll(seen_l, 6, 0), left[g])
            left[g + 1] = jnp.where(row >= 6, pltpu.roll(seen_l, 4, 0), left[g + 1])
        for g in range(GROUPS):
            put(HALO * (GROUPS * part + g), right[g], left[g])
    put(2 * GROUPS * HALO, halo[TILE - HALO :], halo[:HALO])


def strided(stack, base):
    span = STRIP // SUB
    return lambda a, j: stack[pl.ds(base + STRIP * a + j, SUB, stride=span), :]


def fill(stack, base, first, last):
    row = lax.broadcasted_iota(jnp.int32, (SUB, TILE), 0)
    one, two = (pltpu.roll(value, LEAD, 0) for value in first)
    mixed = [jnp.where(row == LEAD, two, one), jnp.where(row < SUB // 2, two, last[0])]
    for k, value in enumerate((one, *mixed, last[1])):
        stack[base + SUB * k : base + SUB * (k + 1), :] = value


def velocity(domain, plain, base):
    for j in range(domain.span):
        at = domain.at(j)
        for k in range(2):
            plain[pl.ds(base + STRIP * k + j, SUB, stride=domain.span), :] = domain.refs[6 + k][at, :]


def density(domain, plain, base, out, place):
    w0, w1 = domain.refs[6:8]
    for j in range(domain.span):
        at = domain.at(j)
        v0, v1 = (plain[pl.ds(base + STRIP * k + j, SUB, stride=domain.span), :] for k in range(2))
        value = -domain.source(FRIC, j) * (w0[at, :] * v0 + w1[at, :] * v1)
        out[pl.ds(place + j, SUB, stride=domain.span), :] = value


def beside():
    lane = lanes()
    return (lane < NEAR) | (lane >= TILE - FAR)


def ends(second):
    row = lax.broadcasted_iota(jnp.int32, (SUB, TILE), 0)
    return row >= SUB - FAR if second else row < NEAR


def adjoint_kernel(
    row_b, row_a, visc, fric, driv, mask, obs, n2, n4, c, i, v0, v1, basis_p, basis_q, edge, turned,
    vel, wide, sides,
    stack, plain, dens, total, *refs,
):
    rows = visc.shape[0]
    span = rows // SUB
    even = is_even(ROW_AXES)
    field = field_of(visc, fric, driv, mask, obs)
    for a in range(ARRAYS):
        at = slice(HALO * a, HALO * (a + 1))
        got_a, got_b = row_a[at, :], row_b[at, :]
        base = STRIP * a
        first = [field(a, slice(at, at + SUB)) for at in (0, SUB)]
        last = [field(a, slice(at, at + SUB)) for at in (rows - 2 * SUB, rows - SUB)]
        fill(stack, base, first, last)
        stack[base : base + LEAD, :] = jnp.where(even, got_b, got_a)[HALO - LEAD :]
        stack[base + STRIP - HALO : base + STRIP, :] = jnp.where(even, got_a, got_b)
    strips = Strips(refs[:STRIP_FIELDS], 0, STRIP // SUB, strided(stack, 0), lambda: visc[rows - KEPT - 1 : rows - KEPT, :])
    strips.prepare(False)
    run([strips])
    velocity(strips, plain, 0)
    for k in range(2):
        for e in range(2):
            out = HALO * (2 * k + e)
            vel[out : out + HALO, :] = plain[STRIP * k + OUTER[e] : STRIP * k + OUTER[e] + HALO, :]
    interior = Domain(
        (n2, n4, c, i, *refs[STRIP_FIELDS:]), 0, span, lambda a, j: field(a, pl.ds(j, SUB, stride=span))
    )
    strips.retarget(False)
    interior.retarget(False, (v0, v1))
    run([interior, strips])
    w0, w1 = interior.refs[6:8]
    for j in range(span):
        at = interior.at(j)
        value = -interior.source(FRIC, j) * (w0[at, :] * v0[at, :] + w1[at, :] * v1[at, :])
        dens[pl.ds(j, SUB, stride=span), :] = value
    density(strips, plain, 0, dens, rows)

    side = beside()
    for s in range(0, TILE, SUB):
        summed = jnp.zeros((SUB, TILE), F32)
        for row in range(s, rows, TILE):
            value = dens[row : row + SUB, :]
            if row in (0, rows - SUB):
                at = rows + OUTER[row > 0]
                value = jnp.where(ends(row > 0), dens[at : at + SUB, :], value)
            summed += value
        total[s : s + SUB, :] = jnp.where(side, 0.0, summed)
    exact = dict(precision=lax.Precision.HIGHEST, preferred_element_type=F32)
    half = jnp.dot(basis_p[...], total[...], **exact)
    wide[...] = jnp.dot(half, basis_q[...], **exact)

    corner = corners()
    for part in range(PARTS):
        for a in range(ARRAYS):
            columns = []
            for r in range(0, SLOT, SUB):
                value = edge[slot(part, a) + r : slot(part, a) + r + SUB, :]
                if part == 2:
                    moved = pltpu.roll(turned[r : r + SUB, :], (UPPER - HALO * a) % TILE, 1)
                    value = jnp.where(corner, moved, value)
                columns.append(value)
            first, second = columns[2:]
            sides[band(a, 0, part, LEAD, SUB), :] = first
            sides[band(a, 0, part, LEAD + SUB, LENGTH - LEAD - SUB), :] = second[: LENGTH - LEAD - SUB]
            sides[band(a, 1, part, 0, SUB // 2), :] = pltpu.roll(columns[0], SUB // 2, 0)[: SUB // 2]
            sides[band(a, 1, part, SUB // 2, SUB), :] = columns[1]
            if a == VISC:
                sides[band(a, 0, part, -1, 1), :] = first[:1]
                sides[band(a, 1, part, -1, 1), :] = columns[0][SUB // 2 - 1 : SUB // 2]


def band(a, side, part, first, count):
    return pl.ds(SUB * ((LENGTH + 1) * a + 1 + first) + PARTS * side + part, count, stride=SUB)


def corners():
    lane = lanes()
    above = (lane >= UPPER) & (lane < UPPER + HALO)
    return above | ((lane >= LOWER + INNER + HALO) & (lane < LOWER + SLOT))


def split(x, axis):
    high = x.astype(jnp.bfloat16)
    low = (x - high.astype(F32)).astype(jnp.bfloat16)
    return jnp.concatenate([high, high, low], axis=axis)


def split_constant(x, axis):
    x = np.asarray(x, np.float32)
    high = np.asarray(x, jnp.bfloat16)
    low = np.asarray(x - np.asarray(high, np.float32), jnp.bfloat16)
    return jnp.asarray(np.concatenate([high, low, high], axis=axis))


def outermost(side, part):
    first = LENGTH - 2 * HALO if side else LEAD
    return pl.ds(SUB * first + PARTS * side + part, HALO, stride=SUB)


def left_right_kernel(
    _, col_b, col_a, wide_in, block, basis_rows, basis_cols,
    stack, vel0, vel1, coef,
    plain, *refs,
):
    even = is_even(COL_AXES)
    lane = lanes()
    row = lax.broadcasted_iota(jnp.int32, (SUB, TILE), 0)
    upper = (lane >= UPPER + HALO) & (lane < UPPER + SLOT)
    lower = (lane >= LOWER) & (lane < LOWER + INNER + HALO)
    seam_t0 = lane >= TILE - INNER - HALO
    seam_t1 = lane < INNER + HALO
    corner = corners()
    for from_left in (True, False):
        groups = []
        for g in range(2 * GROUPS + 1):
            got_a, got_b = col_a[HALO * g : HALO * (g + 1), :], col_b[HALO * g : HALO * (g + 1), :]
            groups.append(jnp.where(even, got_b, got_a) if from_left else jnp.where(even, got_a, got_b))
        tiles = []
        for part in range(2):
            tile = groups[GROUPS * part : GROUPS * (part + 1)]
            for k in range(2):
                g, h = tile[1 + 2 * k], tile[2 + 2 * k]
                if from_left:
                    tile.append(jnp.where(row >= 5, pltpu.roll(g, 6, 0), pltpu.roll(h, 4, 0)))
                else:
                    tile.append(jnp.where(row < 2, pltpu.roll(g, 2, 0), pltpu.roll(h, 4, 0)))
            tiles.append(tile)
        for a in range(ARRAYS):
            t0, t1 = tiles[0][a], tiles[1][a]
            third = jnp.where(corner, pltpu.roll(groups[-1], (UPPER - HALO * a) % TILE, 1), 0.0)
            third = jnp.where(upper, pltpu.roll(t0, UPPER + HALO, 1), third)
            third = jnp.where(lower, pltpu.roll(t1, LOWER + INNER + HALO, 1), third)
            third = jnp.where(seam_t0, t0, jnp.where(seam_t1, t1, third))
            for part, value in enumerate((t0, t1, third)):
                if from_left:
                    stack[band(a, 0, part, 0, LEAD), :] = value[:LEAD]
                else:
                    stack[band(a, 1, part, LENGTH - HALO, HALO), :] = value
    def source(a, j):
        at = SUB * ((LENGTH + 1) * a + 1 + j)
        return stack[at : at + SUB, :]

    bands = Bands(refs, 0, LENGTH, source)
    bands.prepare(True)
    run([bands])
    vel0[...] = refs[6][...]
    vel1[...] = refs[7][...]
    bands.retarget(True)
    run([bands])
    for j in range(LENGTH):
        at = bands.at(j)
        value = refs[6][at, :] * vel0[at, :] + refs[7][at, :] * vel1[at, :]
        plain[at, :] = -source(FRIC, j) * value

    def side(part):
        return jnp.concatenate([plain[outermost(k, part), :] for k in range(2)], axis=0)

    lane = lax.broadcasted_iota(jnp.int32, (2 * HALO, TILE), 1)
    row = lax.broadcasted_iota(jnp.int32, (2 * HALO, TILE), 0)
    right = (row < NEAR) | (row >= 2 * HALO - FAR)
    straight = (lane >= HALO) & (lane < TILE - HALO)
    seam = (lane < HALO) | (lane >= TILE - HALO)
    top = (lane >= UPPER + HALO) & (lane < UPPER + 2 * HALO)
    bottom = (lane >= LOWER + INNER) & (lane < LOWER + INNER + HALO)
    dens = jnp.concatenate(
        [
            jnp.where(right & straight, side(0) + side(1), 0.0),
            jnp.where(right & (seam | top | bottom), side(2), 0.0),
        ],
        axis=1,
    )
    half = lax.dot_general(
        basis_rows[...], split(dens, 1), (((1,), (1,)), ((), ())), preferred_element_type=F32
    )
    wide = wide_in[...] + jnp.dot(split(half, 1), basis_cols[...], preferred_element_type=F32)
    lane = lanes()
    which = lax.div(lane, MODES)
    flat = wide[:SUB]
    for j in range(1, MODES // SUB):
        flat = jnp.where(which == j, wide[SUB * j : SUB * (j + 1)], flat)
    mark = jnp.broadcast_to(block[:1, :].astype(F32), (SUB, TILE))
    row = lax.broadcasted_iota(jnp.int32, (SUB, TILE), 0)
    moved = [flat] + [pltpu.roll(flat, r, 0) for r in range(1, SUB)] + [flat]
    lines = [flat] + [
        jnp.where(row < r - 1, moved[r - 1], jnp.where(row == r - 1, mark, moved[r])) for r in range(1, SUB + 1)
    ]
    cycle = SUB * (SUB + 1)
    chunk = min(4, coef.shape[0] // cycle)

    def spread(d, carry):
        for e in range(chunk):
            for r, line in enumerate(lines):
                coef[pl.ds(pl.multiple_of((d * chunk + e) * cycle + SUB * r, SUB), SUB), :] = line
        return carry

    lax.fori_loop(0, coef.shape[0] // cycle // chunk, spread, 0)


def join_kernel(v0, v1, vel_ends, side0, side1, vel, turned):
    rows = vel.shape[1]
    span = rows // SUB
    middle = jnp.zeros((TILE - 2 * HALO, TILE), F32)
    side = beside()
    for k, (v, strips) in enumerate(((v0, side1), (v1, side0))):
        for part in range(PARTS):
            first, last = (strips[outermost(e, part), :] for e in range(2))
            at = TILE * (2 * part + k)
            turned[at : at + TILE, :] = jnp.concatenate([first, middle, last], axis=0).T
        for row in range(0, rows, SUB):
            value = v[pl.ds(SUB * (row % span) + row // span, SUB, stride=SUB), :]
            if row in (0, rows - SUB):
                at = HALO * (2 * k + (row > 0))
                value = jnp.where(ends(row > 0), vel_ends[at : at + HALO, :], value)
            part, lane = right_part(row)
            at = TILE * (2 * part + k) + lane
            vel[k, row : row + SUB, :] = jnp.where(side, turned[at : at + SUB, :], value)


def bases():
    places = np.arange(TILE) + 0.5
    basis = np.cos(math.pi * places[:, None] * np.arange(MODES)[None, :] / TILE)
    groups = MODES // SUB
    order = np.arange(MODES).reshape(SUB, groups).T.reshape(-1)
    rows = basis[:, order] / TILE
    cols = np.tile(basis, (1, groups))
    placed = np.zeros((2 * TILE, MODES))
    for row in range(0, 2 * TILE, SUB):
        part, lane = right_part(row)
        at = lane + (TILE if part == 2 else 0)
        placed[at : at + SUB] = rows[row % TILE : row % TILE + SUB]
    outer = np.concatenate([cols[:HALO], cols[TILE - HALO :]])
    return jnp.asarray(rows.T, F32), jnp.asarray(cols, F32), split_constant(placed.T, 1), split_constant(outer, 0)


def pick_kernel(owners, every, out):
    mine = out.shape[1]
    own = lax.axis_index("own")
    wanted = [owners[pl.ds(own, 1), k : k + 1].astype(F32) for k in range(mine)]
    lines = SUB + 1
    devices = every.shape[0] // lines
    chunk = min(4, devices // SUB)

    def body(d, sums):
        sums = list(sums)
        for e in range(chunk):
            base = (d * chunk + e) * SUB * lines
            mark = every[pl.ds(base + SUB, SUB, stride=lines), :]
            hits = [mark == wanted[k] for k in range(mine)]
            for r in range(SUB):
                part = every[pl.ds(base + r, SUB, stride=lines), :]
                for k in range(mine):
                    sums[SUB * k + r] += jnp.where(hits[k], part, 0.0)
        return tuple(sums)

    start = (jnp.zeros((SUB, TILE), F32),) * (mine * SUB)
    sums = lax.fori_loop(0, devices // SUB // chunk, body, start)
    for k in range(mine):
        for r in range(SUB):
            total = jnp.sum(sums[SUB * k + r], axis=0, keepdims=True)
            out[0, k : k + 1, TILE * r : TILE * (r + 1)] = total


def local(viscosity, friction, driving, observed, ice_mask, tile_block, owner_list):
    rows, cols = viscosity.shape
    assert (rows, cols) == (2 * TILE, TILE)
    inputs = (viscosity, friction, driving, ice_mask, observed)
    near = [pltpu.with_memory_space_constraint(x, pltpu.VMEM) for x in inputs]
    basis_p, basis_q, basis_rows, basis_cols = bases()
    to_b, to_a = call(
        ends_kernel,
        "ends",
        (vmem(EDGE, cols), vmem(EDGE, cols)),
        [
            vmem(2, 2, HALO, cols),
            vmem(2, 2, 2, HALO, cols),
            pltpu.VMEM((2, HALO, cols), jnp.int32),
            pltpu.SemaphoreType.DMA((2, 5)),
        ],
        10**6,
        *(pltpu.with_memory_space_constraint(x, pltpu.HBM) for x in inputs),
    )
    row_b = swap(to_b, 0, 1)
    row_a = swap(to_a, 0, 0)
    edge, *forward = call(
        interior_kernel,
        "interior",
        (vmem(2 * PARTS * TILE, TILE),) + (vmem(rows, cols),) * 6,
        [vmem(rows, cols)] * (FIELDS - 6),
        8 * 10**6,
        *near,
    )
    to_b, to_a, turned = call(
        columns_kernel,
        "columns",
        (vmem(SENT, TILE), vmem(SENT, TILE), vmem(SLOT, TILE)),
        [],
        10**5,
        row_b,
        row_a,
        edge,
    )
    col_b = swap(to_b, 1, 1)
    col_a = swap(to_a, 1, 0)
    vel_ends, wide, sides = call(
        adjoint_kernel,
        "adjoint",
        (
            vmem(4 * HALO, cols),
            vmem(MODES, TILE),
            vmem(ARRAYS * (LENGTH + 1) * SUB, TILE),
        ),
        [vmem(ARRAYS * STRIP, cols), vmem(2 * STRIP, cols), vmem(rows + STRIP, cols), vmem(TILE, cols)]
        + [vmem(STRIP, cols)] * STRIP_FIELDS
        + [vmem(rows, cols)] * (FIELDS - 4),
        8 * 10**6,
        row_b,
        row_a,
        *near,
        *forward,
        basis_p,
        basis_q,
        edge,
        turned,
    )
    devices = lax.axis_size(ROW_AXES + COL_AXES)
    _, *strips, coef = call(
        left_right_kernel,
        "left_right",
        (
            vmem(ARRAYS * (LENGTH + 1) * SUB, TILE),
            vmem(LENGTH * SUB, TILE),
            vmem(LENGTH * SUB, TILE),
            vmem(devices * (SUB + 1), TILE),
        ),
        [vmem(LENGTH * SUB, TILE)] * (STRIP_FIELDS + 1),
        4 * 10**6,
        sides,
        col_b,
        col_a,
        wide,
        tile_block,
        basis_rows,
        basis_cols,
        aliases={0: 0},
    )
    coef = coef.reshape(devices, 1, (SUB + 1) * TILE)
    parts = lax.all_to_all(coef, ROW_AXES + COL_AXES, 0, 0, tiled=True)
    state = call(
        join_kernel,
        "join",
        jax.ShapeDtypeStruct((2, rows, cols), F32),
        [vmem(2 * PARTS * TILE, TILE)],
        4 * 10**6,
        *forward[4:],
        vel_ends,
        *strips,
    )
    owners = owner_list.reshape(lax.axis_size("own"), -1)
    picked = call(
        pick_kernel,
        "pick",
        jax.ShapeDtypeStruct((1, owners.shape[1], MODES * MODES), F32),
        [],
        10**5,
        owners,
        parts.reshape(-1, TILE),
    )
    return (state, picked)


def solution(mesh):
    return jax.shard_map(
        local,
        mesh=mesh,
        in_specs=(
            P(("row", "own"), "col"),
            P(("row", "own"), "col"),
            P(None, ("row", "own"), "col"),
            P(None, ("row", "own"), "col"),
            P(("row", "own"), "col"),
            P(("row", "own"), "col"),
            P(),
        ),
        out_specs=(P(None, ("row", "own"), "col"), P("own", None, None)),
        check_vma=False,
    )
```

```python
import math

import jax
import jax.numpy as jnp
import numpy as np
from jax import lax
from jax.experimental import pallas as pl
from jax.experimental.pallas import tpu as pltpu
from jax.sharding import PartitionSpec as P

TILE = 128
MODES = 32
SWEEPS = 3
SUB = 8
HALO = 8
INNER = 2 * HALO
STRIP = 40
LEAD = HALO - 1
KEPT = 12
OUTER = (LEAD, STRIP - 2 * HALO)
NEAR, FAR = 7, 6
LENGTH = STRIP // 2
ARRAYS = 7
VISC, FRIC, DRIV, MASK, OBS = 0, 1, 2, 4, 5
EDGE = ARRAYS * HALO
SLOT = 2 * INNER
PER = TILE // SLOT
GROUPS = 5
SENT = 2 * GROUPS * HALO + HALO
PARTS = 3
UPPER, LOWER = 32, 64
ROW_AXES = ("row", "own")
COL_AXES = ("col",)
F32 = jnp.float32
LIMIT = 40 * 1024 * 1024


def swap(x, axis, first):
    sizes = lax.axis_size(ROW_AXES), lax.axis_size(COL_AXES)
    owners = lax.axis_size("own")

    def device(i, j):
        return (i // owners * sizes[1] + j) * owners + i % owners

    pairs = []
    for i in range(sizes[0]):
        for j in range(sizes[1]):
            place = [i, j]
            if first and place[axis] in (0, sizes[axis] - 1):
                place[1 - axis] ^= 1
            else:
                place[axis] = ((place[axis] + first) ^ 1) - first
            pairs.append((device(i, j), device(*place)))
    return lax.ppermute(x, ("row", "col", "own"), pairs)


def position(axes):
    index, size = 0, 1
    for axis in axes:
        index = index * lax.axis_size(axis) + lax.axis_index(axis)
        size *= lax.axis_size(axis)
    assert size % 2 == 0
    return lax.rem(index, 2) == 0, (index == 0) | (index == size - 1)


def is_even(axes):
    return position(axes)[0]


def lanes():
    return lax.broadcasted_iota(jnp.int32, (SUB, TILE), 1)


def call(kernel, name, outs, scratch, cost, *args, aliases={}):
    return pl.pallas_call(
        kernel,
        out_shape=outs,
        scratch_shapes=scratch,
        input_output_aliases=aliases,
        compiler_params=pltpu.CompilerParams(vmem_limit_bytes=LIMIT),
        cost_estimate=pl.CostEstimate(flops=cost, bytes_accessed=cost, transcendentals=0),
        name=name,
    )(*args)


def vmem(*shape):
    return pltpu.VMEM(shape, F32)


FIELDS = 14
STRIP_FIELDS = 24
LAG = 3


class Domain:
    def __init__(self, refs, base, span, source, seam=None):
        self.refs, self.base, self.span, self.source, self.seam = refs, base, span, source, seam

    def at(self, j):
        return pl.ds(self.base + SUB * j, SUB)

    def prepare(self, flipped):
        n2, n4, c, i, b0, b1 = self.refs[:6]
        visc = [self.source(VISC, j) for j in range(self.span)]
        for j in range(self.span):
            at = self.at(j)
            pair = visc[j] + (visc[j - 1] if j else self.before(visc[-1]))
            fric = self.source(FRIC, j)
            diag = 1.25 * (pair + pltpu.roll(pair, 1, 1)) + fric
            on = self.source(MASK, j) > 0.0
            inv = jnp.where(on, 0.5 / jnp.where(on, diag, 1.0), 0.0)
            half = 0.5 * visc[j]
            n2[at, :] = half
            n4[at, :] = 0.5 * half
            c[at, :] = 1.0 - fric * inv
            i[at, :] = inv
            for k, b in enumerate((b0, b1)):
                value = inv * self.source(DRIV + (1 - k if flipped else k), j)
                b[at, :] = value
                self.write(k, at, value + value)

    def before(self, last):
        wrapped = pltpu.roll(last, 1, 0)
        if self.seam is None:
            return wrapped
        row = lax.broadcasted_iota(jnp.int32, (SUB, TILE), 0)
        return jnp.where(row == SUB // 2, self.seam(), wrapped)

    def write(self, k, at, value):
        self.refs[6 + k][at, :] = value
        self.refs[8 + k][at, :] = pltpu.roll(value, TILE - 1, 1)

    def retarget(self, flipped, velocity=None):
        i, b0, b1 = self.refs[3:6]
        w0, w1 = velocity or self.refs[6:8]
        for j in range(self.span):
            at = self.at(j)
            for k, (b, w) in enumerate(((b0, w0), (b1, w1))):
                value = i[at, :] * (w[at, :] - self.source(OBS + (1 - k if flipped else k), j))
                b[at, :] = value
                self.write(k, at, value + value)

    def sweep(self):
        self.differences()
        self.update()

    def differences(self):
        n2, n4 = self.refs[:2]
        fields = self.refs[6:10]
        parts = self.refs[10:14]

        def corners(j, here, below):
            w0, w1, r0, r1 = here
            v0, v1, s0, s1 = below
            a1, a2 = s0 - w0, v0 - r0
            e1, e2 = s1 - w1, v1 - r1
            x, y = a1 + a2, e1 - e2
            q = (a1 - a2) + (e1 + e2)
            both = x + y
            at = self.at(j)
            half = n2[at, :]
            return half * (both + x), n4[at, :] * q, half * (both + y)

        def load(j):
            at = self.at(j)
            return [field[at, :] for field in fields]

        top = load(0)
        last = corners(self.span - 1, load(self.span - 1), [pltpu.roll(v, SUB - 1, 0) for v in top])
        up = [pltpu.roll(v, 1, 0) for v in last]
        here = top
        for j in range(self.span):
            at = self.at(j)
            if j < self.span - 1:
                below = load(j + 1)
                p, q, r = corners(j, here, below)
                here = below
            else:
                p, q, r = last
            g, t = up[0] - p, up[1] + q
            gq, tr = up[1] - q, up[2] + r
            parts[0][at, :] = g - t
            parts[1][at, :] = gq - tr
            parts[2][at, :] = pltpu.roll(g + t, 1, 1)
            parts[3][at, :] = pltpu.roll(gq + tr, 1, 1)
            up = (p, q, r)

    def update(self):
        c, i, b0, b1, w0, w1 = self.refs[2:8]
        parts = self.refs[10:14]
        for j in range(self.span):
            at = self.at(j)
            cv, iv = c[at, :], i[at, :]
            for k, (b, w) in enumerate(((b0, w0), (b1, w1))):
                value = (cv * w[at, :] + b[at, :]) - iv * (parts[k][at, :] + parts[k + 2][at, :])
                self.write(k, at, value)


class Strips(Domain):
    wraps = True

    def prepare(self, flipped):
        super().prepare(flipped)
        for j in range(self.span):
            at = self.at(j)
            for now, later in zip(self.refs[2:6], self.refs[10:14]):
                later[at, :] = pltpu.roll(now[at, :], TILE - 1, 1)
        if self.wraps:
            for now, before in zip(self.refs[:2], self.refs[14:16]):
                before[self.at(0), :] = pltpu.roll(now[self.at(self.span - 1), :], 1, 0)

    def retarget(self, flipped, velocity=None):
        super().retarget(flipped, velocity)
        for j in range(self.span):
            at = self.at(j)
            for now, later in zip(self.refs[4:6], self.refs[12:14]):
                later[at, :] = pltpu.roll(now[at, :], TILE - 1, 1)

    def corners(self, halves, quarters, j, here, below):
        w0, w1, r0, r1 = here
        v0, v1, s0, s1 = below
        a1, a2 = s0 - w0, v0 - r0
        e1, e2 = s1 - w1, v1 - r1
        x, y = a1 + a2, e1 - e2
        q = (a1 - a2) + (e1 + e2)
        both = x + y
        at = self.at(j)
        half = halves[at, :]
        return half * (both + x), quarters[at, :] * q, half * (both + y)

    def load(self, j):
        at = self.at(j)
        return [field[at, :] for field in self.refs[6:10]]

    def differences(self):
        kept, turned, kept_next, turned_next = (self.refs[16 + 2 * k : 18 + 2 * k] for k in range(4))
        corners, load = self.corners, self.load
        top, end = load(0), load(self.span - 1)
        up = corners(*self.refs[14:16], 0, [pltpu.roll(v, 1, 0) for v in end], top)
        bottom = [pltpu.roll(v, SUB - 1, 0) for v in top]
        here = top
        for j in range(self.span):
            at = self.at(j)
            below = load(j + 1) if j < self.span - 1 else bottom
            p, q, r = corners(*self.refs[:2], j, here, below)
            g, t = up[0] - p, up[1] + q
            gq, tr = up[1] - q, up[2] + r
            for k, (stay, move) in enumerate(((g - t, g + t), (gq - tr, gq + tr))):
                kept[k][at, :] = stay
                turned_next[k][at, :] = move
                turned[k][at, :] = pltpu.roll(move, 1, 1)
                kept_next[k][at, :] = pltpu.roll(stay, TILE - 1, 1)
            up, here = (p, q, r), below

    def update(self):
        for first, offset, parts in ((2, 6, (16, 18)), (10, 8, (20, 22))):
            c, i, *b = self.refs[first : first + 4]
            for j in range(self.span):
                at = self.at(j)
                cv, iv = c[at, :], i[at, :]
                for k in range(2):
                    w = self.refs[offset + k]
                    change = self.refs[parts[0] + k][at, :] + self.refs[parts[1] + k][at, :]
                    w[at, :] = (cv * w[at, :] + b[k][at, :]) - iv * change


class Bands(Strips):
    wraps = False

    def before(self, last):
        return self.source(VISC, -1)

    def pipeline(self, flipped, saved, finish):
        stages, offset = [], 0
        for run in range(2):
            for _ in range(SWEEPS):
                stages.append((offset, self.differences_of()))
                stages.append((offset + LAG, self.change))
                offset += LAG + 1
            if run == 0:
                stages.append((offset - 1, lambda j: self.turn(j, flipped, saved)))
        stages.append((offset - 1, finish))
        for step in range(self.span + offset):
            for start, stage in stages:
                if 0 <= step - start < self.span:
                    stage(step - start)

    def differences_of(self):
        none = jnp.zeros((SUB, TILE), F32)
        state = {}

        def stage(j):
            up, here = state.get("up", [none] * 3), state.get("below") or self.load(j)
            below = self.load(j + 1) if j < self.span - 1 else [none] * 4
            p, q, r = self.corners(*self.refs[:2], j, here, below)
            g, t = up[0] - p, up[1] + q
            gq, tr = up[1] - q, up[2] + r
            at = self.at(j)
            for k, (stay, move) in enumerate(((g - t, g + t), (gq - tr, gq + tr))):
                values = stay, pltpu.roll(move, 1, 1), pltpu.roll(stay, TILE - 1, 1), move
                for n, value in enumerate(values):
                    self.refs[16 + 2 * n + k][at, :] = value
            state["up"], state["below"] = (p, q, r), below

        return stage

    def change(self, j):
        at = self.at(j)
        for offset, first in ((0, 2), (2, 10)):
            c, i, *b = (ref[at, :] for ref in self.refs[first : first + 4])
            for k in range(2):
                w = self.refs[6 + offset + k]
                part = 16 + 2 * offset + k
                w[at, :] = (c * w[at, :] + b[k]) - i * (self.refs[part][at, :] + self.refs[part + 2][at, :])

    def turn(self, j, flipped, saved):
        at = self.at(j)
        for k in range(2):
            now = self.refs[6 + k][at, :]
            saved[k][at, :] = now
            value = self.refs[3][at, :] * (now - self.source(OBS + (1 - k if flipped else k), j))
            later = pltpu.roll(value, TILE - 1, 1)
            for first, new in ((4, value), (12, later)):
                self.refs[first + k][at, :] = new
            for first, new in ((6, value), (8, later)):
                self.refs[first + k][at, :] = new + new


def run(domains):
    def body(_, carry):
        for domain in domains:
            domain.sweep()
        return carry

    lax.fori_loop(0, SWEEPS, body, 0)


def ends_kernel(visc, fric, driv, mask, obs, to_b, to_a, one, two, flags, sems):
    rows = visc.shape[0]
    copies = []
    for e, first in enumerate((0, rows - HALO)):
        at = pl.ds(first, HALO)
        pieces = [
            (visc.at[at], one.at[e, 0]),
            (fric.at[at], one.at[e, 1]),
            (driv.at[:, at], two.at[e, 0]),
            (mask.at[at], flags.at[e]),
            (obs.at[:, at], two.at[e, 1]),
        ]
        for n, (source, place) in enumerate(pieces):
            copies.append(pltpu.make_async_copy(source, place, sems.at[e, n]))
    for copy in copies:
        copy.start()
    for copy in copies:
        copy.wait()
    even, at_end = position(ROW_AXES)

    def edge(e):
        return [one[e, 0], one[e, 1], two[e, 0, 0], two[e, 0, 1], flags[e].astype(F32), two[e, 1, 0], two[e, 1, 1]]

    for a, (head, tail) in enumerate(zip(edge(0), edge(1))):
        at = slice(HALO * a, HALO * (a + 1))
        to_a[at, :] = jnp.where(even, tail, head)
        to_b[at, :] = jnp.where(at_end, 0.0, jnp.where(even, head, tail))


def field_of(visc, fric, driv, mask, obs):
    def field(a, at):
        if a == MASK:
            return mask[at, :].astype(F32)
        if a >= OBS:
            return obs[a - OBS, at, :]
        if a >= DRIV:
            return driv[a - DRIV, at, :]
        return (visc, fric)[a][at, :]

    return field


def first_row(part, lane):
    if part < 2:
        return TILE * part + lane
    if lane < INNER + HALO:
        return TILE + lane
    if lane >= TILE - INNER - HALO:
        return lane
    if UPPER + HALO <= lane < UPPER + SLOT:
        return lane - UPPER - HALO
    if LOWER <= lane < LOWER + INNER + HALO:
        return 2 * TILE - INNER - HALO + lane - LOWER
    return None


def right_part(row):
    seam = TILE - HALO <= row < TILE + HALO
    part = 2 if seam or row == 0 or row == 2 * TILE - HALO else row // TILE
    return part, [lane for lane in range(0, TILE, SUB) if first_row(part, lane) == row][-1]


def slot(part, a):
    return TILE * (2 * part + a // PER) + SLOT * (a % PER)


def interior_kernel(visc, fric, driv, mask, obs, edge, n2, n4, c, i, v0, v1, *refs):
    span = visc.shape[0] // SUB
    field = field_of(visc, fric, driv, mask, obs)
    lane = lanes()
    for part in range(PARTS):
        for m in range(-(-ARRAYS // PER)):
            strips = []
            for at in range(0, TILE, SUB):
                row = first_row(part, at)
                packed = jnp.zeros((SUB, TILE), F32)
                if row is not None:
                    for k in range(min(PER, ARRAYS - PER * m)):
                        value = field(PER * m + k, slice(row, row + SUB))
                        moved = pltpu.roll(value, (SLOT * k + INNER) % TILE, 1)
                        packed = jnp.where(lax.div(lane, SLOT) == k, moved, packed)
                strips.append(packed)
            base = TILE * (2 * part + m)
            edge[base : base + TILE, :] = jnp.concatenate(strips, axis=0).T
    refs = (n2, n4, c, i, *refs[:2], v0, v1, *refs[2:])
    domain = Domain(refs, 0, span, lambda a, j: field(a, pl.ds(j, SUB, stride=span)))
    domain.prepare(False)
    run([domain])


def columns_kernel(row_b, row_a, edge, to_b, to_a, turned):
    even = is_even(ROW_AXES)
    above = jnp.where(even, row_b[...], row_a[...])
    below = jnp.where(even, row_a[...], row_b[...])
    halo = jnp.concatenate([above, below, jnp.zeros((TILE - 2 * EDGE, TILE), F32)], axis=0).T
    turned[:INNER, :] = halo[TILE - INNER :]
    turned[INNER:, :] = halo[:INNER]
    even, at_end = position(COL_AXES)
    row = lax.broadcasted_iota(jnp.int32, (SUB, TILE), 0)

    def put(out, right, left):
        right = pltpu.roll(right, LEAD, 0)
        to_a[out : out + HALO, :] = jnp.where(even, right, left)
        to_b[out : out + HALO, :] = jnp.where(at_end, 0.0, jnp.where(even, left, right))

    for part in range(2):
        right, left = [], []
        for a in range(ARRAYS):
            at = slot(part, a) + INNER
            right.append(edge[at - HALO : at, :])
            left.append(edge[at : at + HALO, :])
        for k in range(2):
            seen_r, seen_l = right[OBS + k], left[OBS + k]
            g = 1 + 2 * k
            right[g] = jnp.where(row < 2, pltpu.roll(seen_r, 2, 0), right[g])
            right[g + 1] = jnp.where(row < 2, pltpu.roll(seen_r, 4, 0), right[g + 1])
            left[g] = jnp.where(row >= 6, pltpu.roll(seen_l, 6, 0), left[g])
            left[g + 1] = jnp.where(row >= 6, pltpu.roll(seen_l, 4, 0), left[g + 1])
        for g in range(GROUPS):
            put(HALO * (GROUPS * part + g), right[g], left[g])
    put(2 * GROUPS * HALO, halo[TILE - HALO :], halo[:HALO])


def strided(stack, base):
    span = STRIP // SUB
    return lambda a, j: stack[pl.ds(base + STRIP * a + j, SUB, stride=span), :]


def fill(stack, base, first, last):
    row = lax.broadcasted_iota(jnp.int32, (SUB, TILE), 0)
    one, two = (pltpu.roll(value, LEAD, 0) for value in first)
    mixed = [jnp.where(row == LEAD, two, one), jnp.where(row < SUB // 2, two, last[0])]
    for k, value in enumerate((one, *mixed, last[1])):
        stack[base + SUB * k : base + SUB * (k + 1), :] = value


def velocity(domain, plain, base):
    for j in range(domain.span):
        at = domain.at(j)
        for k in range(2):
            plain[pl.ds(base + STRIP * k + j, SUB, stride=domain.span), :] = domain.refs[6 + k][at, :]


def density(domain, plain, base, out, place):
    w0, w1 = domain.refs[6:8]
    for j in range(domain.span):
        at = domain.at(j)
        v0, v1 = (plain[pl.ds(base + STRIP * k + j, SUB, stride=domain.span), :] for k in range(2))
        value = -domain.source(FRIC, j) * (w0[at, :] * v0 + w1[at, :] * v1)
        out[pl.ds(place + j, SUB, stride=domain.span), :] = value


def beside():
    lane = lanes()
    return (lane < NEAR) | (lane >= TILE - FAR)


def ends(second):
    row = lax.broadcasted_iota(jnp.int32, (SUB, TILE), 0)
    return row >= SUB - FAR if second else row < NEAR


def adjoint_kernel(
    row_b, row_a, visc, fric, driv, mask, obs, n2, n4, c, i, v0, v1, basis_p, basis_q, edge, turned,
    vel, wide, sides,
    stack, plain, dens, total, *refs,
):
    rows = visc.shape[0]
    span = rows // SUB
    even = is_even(ROW_AXES)
    field = field_of(visc, fric, driv, mask, obs)
    for a in range(ARRAYS):
        at = slice(HALO * a, HALO * (a + 1))
        got_a, got_b = row_a[at, :], row_b[at, :]
        base = STRIP * a
        first = [field(a, slice(at, at + SUB)) for at in (0, SUB)]
        last = [field(a, slice(at, at + SUB)) for at in (rows - 2 * SUB, rows - SUB)]
        fill(stack, base, first, last)
        stack[base : base + LEAD, :] = jnp.where(even, got_b, got_a)[HALO - LEAD :]
        stack[base + STRIP - HALO : base + STRIP, :] = jnp.where(even, got_a, got_b)
    strips = Strips(refs[:STRIP_FIELDS], 0, STRIP // SUB, strided(stack, 0), lambda: visc[rows - KEPT - 1 : rows - KEPT, :])
    strips.prepare(False)
    run([strips])
    velocity(strips, plain, 0)
    for k in range(2):
        for e in range(2):
            out = HALO * (2 * k + e)
            vel[out : out + HALO, :] = plain[STRIP * k + OUTER[e] : STRIP * k + OUTER[e] + HALO, :]
    interior = Domain(
        (n2, n4, c, i, *refs[STRIP_FIELDS:]), 0, span, lambda a, j: field(a, pl.ds(j, SUB, stride=span))
    )
    strips.retarget(False)
    interior.retarget(False, (v0, v1))
    run([interior, strips])
    w0, w1 = interior.refs[6:8]
    for j in range(span):
        at = interior.at(j)
        value = -interior.source(FRIC, j) * (w0[at, :] * v0[at, :] + w1[at, :] * v1[at, :])
        dens[pl.ds(j, SUB, stride=span), :] = value
    density(strips, plain, 0, dens, rows)

    side = beside()
    for s in range(0, TILE, SUB):
        summed = jnp.zeros((SUB, TILE), F32)
        for row in range(s, rows, TILE):
            value = dens[row : row + SUB, :]
            if row in (0, rows - SUB):
                at = rows + OUTER[row > 0]
                value = jnp.where(ends(row > 0), dens[at : at + SUB, :], value)
            summed += value
        total[s : s + SUB, :] = jnp.where(side, 0.0, summed)
    exact = dict(precision=lax.Precision.HIGHEST, preferred_element_type=F32)
    half = jnp.dot(basis_p[...], total[...], **exact)
    wide[...] = jnp.dot(half, basis_q[...], **exact)

    corner = corners()
    for part in range(PARTS):
        for a in range(ARRAYS):
            columns = []
            for r in range(0, SLOT, SUB):
                value = edge[slot(part, a) + r : slot(part, a) + r + SUB, :]
                if part == 2:
                    moved = pltpu.roll(turned[r : r + SUB, :], (UPPER - HALO * a) % TILE, 1)
                    value = jnp.where(corner, moved, value)
                columns.append(value)
            first, second = columns[2:]
            sides[band(a, 0, part, LEAD, SUB), :] = first
            sides[band(a, 0, part, LEAD + SUB, LENGTH - LEAD - SUB), :] = second[: LENGTH - LEAD - SUB]
            sides[band(a, 1, part, 0, SUB // 2), :] = pltpu.roll(columns[0], SUB // 2, 0)[: SUB // 2]
            sides[band(a, 1, part, SUB // 2, SUB), :] = columns[1]
            if a == VISC:
                sides[band(a, 0, part, -1, 1), :] = first[:1]
                sides[band(a, 1, part, -1, 1), :] = columns[0][SUB // 2 - 1 : SUB // 2]


def band(a, side, part, first, count):
    return pl.ds(SUB * ((LENGTH + 1) * a + 1 + first) + PARTS * side + part, count, stride=SUB)


def corners():
    lane = lanes()
    above = (lane >= UPPER) & (lane < UPPER + HALO)
    return above | ((lane >= LOWER + INNER + HALO) & (lane < LOWER + SLOT))


def split(x, axis):
    high = x.astype(jnp.bfloat16)
    low = (x - high.astype(F32)).astype(jnp.bfloat16)
    return jnp.concatenate([high, high, low], axis=axis)


def split_constant(x, axis):
    x = np.asarray(x, np.float32)
    high = np.asarray(x, jnp.bfloat16)
    low = np.asarray(x - np.asarray(high, np.float32), jnp.bfloat16)
    return jnp.asarray(np.concatenate([high, low, high], axis=axis))


def outermost(side, part):
    first = LENGTH - 2 * HALO if side else LEAD
    return pl.ds(SUB * first + PARTS * side + part, HALO, stride=SUB)


def left_right_kernel(
    _, col_b, col_a, wide_in, block, basis_rows, basis_cols,
    stack, vel0, vel1, coef,
    plain, *refs,
):
    even = is_even(COL_AXES)
    lane = lanes()
    row = lax.broadcasted_iota(jnp.int32, (SUB, TILE), 0)
    upper = (lane >= UPPER + HALO) & (lane < UPPER + SLOT)
    lower = (lane >= LOWER) & (lane < LOWER + INNER + HALO)
    seam_t0 = lane >= TILE - INNER - HALO
    seam_t1 = lane < INNER + HALO
    corner = corners()
    for from_left in (True, False):
        groups = []
        for g in range(2 * GROUPS + 1):
            got_a, got_b = col_a[HALO * g : HALO * (g + 1), :], col_b[HALO * g : HALO * (g + 1), :]
            groups.append(jnp.where(even, got_b, got_a) if from_left else jnp.where(even, got_a, got_b))
        tiles = []
        for part in range(2):
            tile = groups[GROUPS * part : GROUPS * (part + 1)]
            for k in range(2):
                g, h = tile[1 + 2 * k], tile[2 + 2 * k]
                if from_left:
                    tile.append(jnp.where(row >= 5, pltpu.roll(g, 6, 0), pltpu.roll(h, 4, 0)))
                else:
                    tile.append(jnp.where(row < 2, pltpu.roll(g, 2, 0), pltpu.roll(h, 4, 0)))
            tiles.append(tile)
        for a in range(ARRAYS):
            t0, t1 = tiles[0][a], tiles[1][a]
            third = jnp.where(corner, pltpu.roll(groups[-1], (UPPER - HALO * a) % TILE, 1), 0.0)
            third = jnp.where(upper, pltpu.roll(t0, UPPER + HALO, 1), third)
            third = jnp.where(lower, pltpu.roll(t1, LOWER + INNER + HALO, 1), third)
            third = jnp.where(seam_t0, t0, jnp.where(seam_t1, t1, third))
            for part, value in enumerate((t0, t1, third)):
                if from_left:
                    stack[band(a, 0, part, 0, LEAD), :] = value[:LEAD]
                else:
                    stack[band(a, 1, part, LENGTH - HALO, HALO), :] = value
    def source(a, j):
        at = SUB * ((LENGTH + 1) * a + 1 + j)
        return stack[at : at + SUB, :]

    bands = Bands(refs, 0, LENGTH, source)
    bands.prepare(True)

    def density_of(j):
        at = bands.at(j)
        value = refs[6][at, :] * vel0[at, :] + refs[7][at, :] * vel1[at, :]
        plain[at, :] = -source(FRIC, j) * value

    bands.pipeline(True, (vel0, vel1), density_of)

    def side(part):
        return jnp.concatenate([plain[outermost(k, part), :] for k in range(2)], axis=0)

    lane = lax.broadcasted_iota(jnp.int32, (2 * HALO, TILE), 1)
    row = lax.broadcasted_iota(jnp.int32, (2 * HALO, TILE), 0)
    right = (row < NEAR) | (row >= 2 * HALO - FAR)
    straight = (lane >= HALO) & (lane < TILE - HALO)
    seam = (lane < HALO) | (lane >= TILE - HALO)
    top = (lane >= UPPER + HALO) & (lane < UPPER + 2 * HALO)
    bottom = (lane >= LOWER + INNER) & (lane < LOWER + INNER + HALO)
    dens = jnp.concatenate(
        [
            jnp.where(right & straight, side(0) + side(1), 0.0),
            jnp.where(right & (seam | top | bottom), side(2), 0.0),
        ],
        axis=1,
    )
    half = lax.dot_general(
        basis_rows[...], split(dens, 1), (((1,), (1,)), ((), ())), preferred_element_type=F32
    )
    wide = wide_in[...] + jnp.dot(split(half, 1), basis_cols[...], preferred_element_type=F32)
    lane = lanes()
    which = lax.div(lane, MODES)
    flat = wide[:SUB]
    for j in range(1, MODES // SUB):
        flat = jnp.where(which == j, wide[SUB * j : SUB * (j + 1)], flat)
    mark = jnp.broadcast_to(block[:1, :].astype(F32), (SUB, TILE))
    row = lax.broadcasted_iota(jnp.int32, (SUB, TILE), 0)
    moved = [flat] + [pltpu.roll(flat, r, 0) for r in range(1, SUB)] + [flat]
    lines = [flat] + [
        jnp.where(row < r - 1, moved[r - 1], jnp.where(row == r - 1, mark, moved[r])) for r in range(1, SUB + 1)
    ]
    cycle = SUB * (SUB + 1)
    chunk = min(4, coef.shape[0] // cycle)

    def spread(d, carry):
        for e in range(chunk):
            for r, line in enumerate(lines):
                coef[pl.ds(pl.multiple_of((d * chunk + e) * cycle + SUB * r, SUB), SUB), :] = line
        return carry

    lax.fori_loop(0, coef.shape[0] // cycle // chunk, spread, 0)


def join_kernel(v0, v1, vel_ends, side0, side1, vel, turned):
    rows = vel.shape[1]
    span = rows // SUB
    middle = jnp.zeros((TILE - 2 * HALO, TILE), F32)
    side = beside()
    for k, (v, strips) in enumerate(((v0, side1), (v1, side0))):
        for part in range(PARTS):
            first, last = (strips[outermost(e, part), :] for e in range(2))
            at = TILE * (2 * part + k)
            turned[at : at + TILE, :] = jnp.concatenate([first, middle, last], axis=0).T
        for row in range(0, rows, SUB):
            value = v[pl.ds(SUB * (row % span) + row // span, SUB, stride=SUB), :]
            if row in (0, rows - SUB):
                at = HALO * (2 * k + (row > 0))
                value = jnp.where(ends(row > 0), vel_ends[at : at + HALO, :], value)
            part, lane = right_part(row)
            at = TILE * (2 * part + k) + lane
            vel[k, row : row + SUB, :] = jnp.where(side, turned[at : at + SUB, :], value)


def bases():
    places = np.arange(TILE) + 0.5
    basis = np.cos(math.pi * places[:, None] * np.arange(MODES)[None, :] / TILE)
    groups = MODES // SUB
    order = np.arange(MODES).reshape(SUB, groups).T.reshape(-1)
    rows = basis[:, order] / TILE
    cols = np.tile(basis, (1, groups))
    placed = np.zeros((2 * TILE, MODES))
    for row in range(0, 2 * TILE, SUB):
        part, lane = right_part(row)
        at = lane + (TILE if part == 2 else 0)
        placed[at : at + SUB] = rows[row % TILE : row % TILE + SUB]
    outer = np.concatenate([cols[:HALO], cols[TILE - HALO :]])
    return jnp.asarray(rows.T, F32), jnp.asarray(cols, F32), split_constant(placed.T, 1), split_constant(outer, 0)


def pick_kernel(owners, every, out):
    mine = out.shape[1]
    own = lax.axis_index("own")
    wanted = [owners[pl.ds(own, 1), k : k + 1].astype(F32) for k in range(mine)]
    lines = SUB + 1
    devices = every.shape[0] // lines
    chunk = min(4, devices // SUB)

    def body(d, sums):
        sums = list(sums)
        for e in range(chunk):
            base = (d * chunk + e) * SUB * lines
            mark = every[pl.ds(base + SUB, SUB, stride=lines), :]
            hits = [mark == wanted[k] for k in range(mine)]
            for r in range(SUB):
                part = every[pl.ds(base + r, SUB, stride=lines), :]
                for k in range(mine):
                    sums[SUB * k + r] += jnp.where(hits[k], part, 0.0)
        return tuple(sums)

    start = (jnp.zeros((SUB, TILE), F32),) * (mine * SUB)
    sums = lax.fori_loop(0, devices // SUB // chunk, body, start)
    for k in range(mine):
        for r in range(SUB):
            total = jnp.sum(sums[SUB * k + r], axis=0, keepdims=True)
            out[0, k : k + 1, TILE * r : TILE * (r + 1)] = total


def local(viscosity, friction, driving, observed, ice_mask, tile_block, owner_list):
    rows, cols = viscosity.shape
    assert (rows, cols) == (2 * TILE, TILE)
    inputs = (viscosity, friction, driving, ice_mask, observed)
    near = [pltpu.with_memory_space_constraint(x, pltpu.VMEM) for x in inputs]
    basis_p, basis_q, basis_rows, basis_cols = bases()
    to_b, to_a = call(
        ends_kernel,
        "ends",
        (vmem(EDGE, cols), vmem(EDGE, cols)),
        [
            vmem(2, 2, HALO, cols),
            vmem(2, 2, 2, HALO, cols),
            pltpu.VMEM((2, HALO, cols), jnp.int32),
            pltpu.SemaphoreType.DMA((2, 5)),
        ],
        10**6,
        *(pltpu.with_memory_space_constraint(x, pltpu.HBM) for x in inputs),
    )
    row_b = swap(to_b, 0, 1)
    row_a = swap(to_a, 0, 0)
    edge, *forward = call(
        interior_kernel,
        "interior",
        (vmem(2 * PARTS * TILE, TILE),) + (vmem(rows, cols),) * 6,
        [vmem(rows, cols)] * (FIELDS - 6),
        8 * 10**6,
        *near,
    )
    to_b, to_a, turned = call(
        columns_kernel,
        "columns",
        (vmem(SENT, TILE), vmem(SENT, TILE), vmem(SLOT, TILE)),
        [],
        10**5,
        row_b,
        row_a,
        edge,
    )
    col_b = swap(to_b, 1, 1)
    col_a = swap(to_a, 1, 0)
    vel_ends, wide, sides = call(
        adjoint_kernel,
        "adjoint",
        (
            vmem(4 * HALO, cols),
            vmem(MODES, TILE),
            vmem(ARRAYS * (LENGTH + 1) * SUB, TILE),
        ),
        [vmem(ARRAYS * STRIP, cols), vmem(2 * STRIP, cols), vmem(rows + STRIP, cols), vmem(TILE, cols)]
        + [vmem(STRIP, cols)] * STRIP_FIELDS
        + [vmem(rows, cols)] * (FIELDS - 4),
        8 * 10**6,
        row_b,
        row_a,
        *near,
        *forward,
        basis_p,
        basis_q,
        edge,
        turned,
    )
    devices = lax.axis_size(ROW_AXES + COL_AXES)
    _, *strips, coef = call(
        left_right_kernel,
        "left_right",
        (
            vmem(ARRAYS * (LENGTH + 1) * SUB, TILE),
            vmem(LENGTH * SUB, TILE),
            vmem(LENGTH * SUB, TILE),
            vmem(devices * (SUB + 1), TILE),
        ),
        [vmem(LENGTH * SUB, TILE)] * (STRIP_FIELDS + 1),
        4 * 10**6,
        sides,
        col_b,
        col_a,
        wide,
        tile_block,
        basis_rows,
        basis_cols,
        aliases={0: 0},
    )
    coef = coef.reshape(devices, 1, (SUB + 1) * TILE)
    parts = lax.all_to_all(coef, ROW_AXES + COL_AXES, 0, 0, tiled=True)
    state = call(
        join_kernel,
        "join",
        jax.ShapeDtypeStruct((2, rows, cols), F32),
        [vmem(2 * PARTS * TILE, TILE)],
        4 * 10**6,
        *forward[4:],
        vel_ends,
        *strips,
    )
    owners = owner_list.reshape(lax.axis_size("own"), -1)
    picked = call(
        pick_kernel,
        "pick",
        jax.ShapeDtypeStruct((1, owners.shape[1], MODES * MODES), F32),
        [],
        10**5,
        owners,
        parts.reshape(-1, TILE),
    )
    return (state, picked)


def solution(mesh):
    return jax.shard_map(
        local,
        mesh=mesh,
        in_specs=(
            P(("row", "own"), "col"),
            P(("row", "own"), "col"),
            P(None, ("row", "own"), "col"),
            P(None, ("row", "own"), "col"),
            P(("row", "own"), "col"),
            P(("row", "own"), "col"),
            P(),
        ),
        out_specs=(P(None, ("row", "own"), "col"), P("own", None, None)),
        check_vma=False,
    )
```

```python
import math

import jax
import jax.numpy as jnp
import numpy as np
from jax import lax
from jax.experimental import pallas as pl
from jax.experimental.pallas import tpu as pltpu
from jax.sharding import PartitionSpec as P

TILE = 128
MODES = 32
SWEEPS = 3
SUB = 8
HALO = 8
INNER = 2 * HALO
STRIP = 40
LEAD = HALO - 1
KEPT = 12
OUTER = (LEAD, STRIP - 2 * HALO)
NEAR, FAR = 7, 6
ARRAYS = 7
VISC, FRIC, DRIV, MASK, OBS = 0, 1, 2, 4, 5
EDGE = ARRAYS * HALO
SLOT = 2 * INNER
PER = TILE // SLOT
GROUPS = 5
SENT = 2 * GROUPS * HALO + HALO
PARTS = 3
UPPER, LOWER = 32, 64
ROW_AXES = ("row", "own")
COL_AXES = ("col",)
F32 = jnp.float32
LIMIT = 40 * 1024 * 1024


def swap(x, axis, first):
    sizes = lax.axis_size(ROW_AXES), lax.axis_size(COL_AXES)
    owners = lax.axis_size("own")

    def device(i, j):
        return (i // owners * sizes[1] + j) * owners + i % owners

    pairs = []
    for i in range(sizes[0]):
        for j in range(sizes[1]):
            place = [i, j]
            if first and place[axis] in (0, sizes[axis] - 1):
                place[1 - axis] ^= 1
            else:
                place[axis] = ((place[axis] + first) ^ 1) - first
            pairs.append((device(i, j), device(*place)))
    return lax.ppermute(x, ("row", "col", "own"), pairs)


def position(axes):
    index, size = 0, 1
    for axis in axes:
        index = index * lax.axis_size(axis) + lax.axis_index(axis)
        size *= lax.axis_size(axis)
    assert size % 2 == 0
    return lax.rem(index, 2) == 0, (index == 0) | (index == size - 1)


def is_even(axes):
    return position(axes)[0]


def lanes():
    return lax.broadcasted_iota(jnp.int32, (SUB, TILE), 1)


def call(kernel, name, outs, scratch, cost, *args, aliases={}):
    return pl.pallas_call(
        kernel,
        out_shape=outs,
        scratch_shapes=scratch,
        input_output_aliases=aliases,
        compiler_params=pltpu.CompilerParams(vmem_limit_bytes=LIMIT),
        cost_estimate=pl.CostEstimate(flops=cost, bytes_accessed=cost, transcendentals=0),
        name=name,
    )(*args)


def vmem(*shape):
    return pltpu.VMEM(shape, F32)


FIELDS = 14
STRIP_FIELDS = 24


class Domain:
    def __init__(self, refs, base, span, source, seam=None):
        self.refs, self.base, self.span, self.source, self.seam = refs, base, span, source, seam

    def at(self, j):
        return pl.ds(self.base + SUB * j, SUB)

    def prepare(self, flipped):
        n2, n4, c, i = self.refs[:4]
        visc = [self.source(VISC, j) for j in range(self.span)]
        for j in range(self.span):
            at = self.at(j)
            before = visc[j - 1] if j else pltpu.roll(visc[-1], 1, 0)
            if self.seam and not j:
                row = lax.broadcasted_iota(jnp.int32, (SUB, TILE), 0)
                before = jnp.where(row == SUB // 2, self.seam(), before)
            pair = visc[j] + before
            fric = self.source(FRIC, j)
            diag = 1.25 * (pair + pltpu.roll(pair, 1, 1)) + fric
            on = self.source(MASK, j) > 0.0
            inv = jnp.where(on, 0.5 / jnp.where(on, diag, 1.0), 0.0)
            half = 0.5 * visc[j]
            n2[at, :] = half
            n4[at, :] = 0.5 * half
            c[at, :] = 1.0 - fric * inv
            i[at, :] = inv
            for k in range(2):
                self.start(k, at, inv * self.source(DRIV + (1 - k if flipped else k), j))

    def start(self, k, at, value):
        self.refs[4 + k][at, :] = value
        self.write(k, at, value + value)

    def write(self, k, at, value):
        self.refs[6 + k][at, :] = value
        self.refs[8 + k][at, :] = pltpu.roll(value, TILE - 1, 1)

    def retarget(self, flipped, velocity=None):
        i = self.refs[3]
        velocity = velocity or self.refs[6:8]
        for j in range(self.span):
            at = self.at(j)
            for k in range(2):
                seen = self.source(OBS + (1 - k if flipped else k), j)
                self.start(k, at, i[at, :] * (velocity[k][at, :] - seen))

    def differences(self):
        n2, n4 = self.refs[:2]
        fields = self.refs[6:10]
        parts = self.refs[10:14]

        def corners(j, here, below):
            w0, w1, r0, r1 = here
            v0, v1, s0, s1 = below
            a1, a2 = s0 - w0, v0 - r0
            e1, e2 = s1 - w1, v1 - r1
            x, y = a1 + a2, e1 - e2
            q = (a1 - a2) + (e1 + e2)
            both = x + y
            at = self.at(j)
            half = n2[at, :]
            return half * (both + x), n4[at, :] * q, half * (both + y)

        def load(j):
            at = self.at(j)
            return [field[at, :] for field in fields]

        top = load(0)
        last = corners(self.span - 1, load(self.span - 1), [pltpu.roll(v, SUB - 1, 0) for v in top])
        up = [pltpu.roll(v, 1, 0) for v in last]
        here = top
        for j in range(self.span):
            at = self.at(j)
            if j < self.span - 1:
                below = load(j + 1)
                p, q, r = corners(j, here, below)
                here = below
            else:
                p, q, r = last
            g, t = up[0] - p, up[1] + q
            gq, tr = up[1] - q, up[2] + r
            parts[0][at, :] = g - t
            parts[1][at, :] = gq - tr
            parts[2][at, :] = pltpu.roll(g + t, 1, 1)
            parts[3][at, :] = pltpu.roll(gq + tr, 1, 1)
            up = (p, q, r)

    def update(self):
        c, i, b0, b1, w0, w1 = self.refs[2:8]
        parts = self.refs[10:14]
        for j in range(self.span):
            at = self.at(j)
            cv, iv = c[at, :], i[at, :]
            for k, (b, w) in enumerate(((b0, w0), (b1, w1))):
                value = (cv * w[at, :] + b[at, :]) - iv * (parts[k][at, :] + parts[k + 2][at, :])
                self.write(k, at, value)


class Strips(Domain):
    def prepare(self, flipped):
        super().prepare(flipped)
        for j in range(self.span):
            at = self.at(j)
            for now, later in zip(self.refs[2:4], self.refs[10:12]):
                later[at, :] = pltpu.roll(now[at, :], TILE - 1, 1)
        for now, before in zip(self.refs[:2], self.refs[14:16]):
            before[self.at(0), :] = pltpu.roll(now[self.at(self.span - 1), :], 1, 0)

    def start(self, k, at, value):
        b, w, r, later = (self.refs[n + k] for n in (4, 6, 8, 12))
        b[at, :] = value
        w[at, :] = value + value
        turned = pltpu.roll(value, TILE - 1, 1)
        later[at, :] = turned
        r[at, :] = turned + turned

    def differences(self):
        fields = self.refs[6:10]
        kept, turned, kept_next, turned_next = (self.refs[16 + 2 * k : 18 + 2 * k] for k in range(4))

        def corners(halves, quarters, j, here, below):
            w0, w1, r0, r1 = here
            v0, v1, s0, s1 = below
            a1, a2 = s0 - w0, v0 - r0
            e1, e2 = s1 - w1, v1 - r1
            x, y = a1 + a2, e1 - e2
            q = (a1 - a2) + (e1 + e2)
            both = x + y
            at = self.at(j)
            half = halves[at, :]
            return half * (both + x), quarters[at, :] * q, half * (both + y)

        def load(j):
            at = self.at(j)
            return [field[at, :] for field in fields]

        top, end = load(0), load(self.span - 1)
        up = corners(*self.refs[14:16], 0, [pltpu.roll(v, 1, 0) for v in end], top)
        here = top
        for j in range(self.span):
            at = self.at(j)
            below = load(j + 1) if j < self.span - 1 else [pltpu.roll(v, SUB - 1, 0) for v in top]
            p, q, r = corners(*self.refs[:2], j, here, below)
            g, t = up[0] - p, up[1] + q
            gq, tr = up[1] - q, up[2] + r
            for k, (stay, move) in enumerate(((g - t, g + t), (gq - tr, gq + tr))):
                kept[k][at, :] = stay
                turned_next[k][at, :] = move
                turned[k][at, :] = pltpu.roll(move, 1, 1)
                kept_next[k][at, :] = pltpu.roll(stay, TILE - 1, 1)
            up, here = (p, q, r), below

    def update(self):
        for first, offset, parts in ((2, 6, (16, 18)), (10, 8, (20, 22))):
            c, i, *b = self.refs[first : first + 4]
            for j in range(self.span):
                at = self.at(j)
                cv, iv = c[at, :], i[at, :]
                for k in range(2):
                    w = self.refs[offset + k]
                    change = self.refs[parts[0] + k][at, :] + self.refs[parts[1] + k][at, :]
                    w[at, :] = (cv * w[at, :] + b[k][at, :]) - iv * change


def run(domains, written_out=False):
    def body(_, carry):
        for domain in domains:
            domain.differences()
        for domain in domains:
            domain.update()
        return carry

    if written_out:
        for k in range(SWEEPS):
            body(k, 0)
    else:
        lax.fori_loop(0, SWEEPS, body, 0)


def ends_kernel(visc, fric, driv, mask, obs, to_b, to_a, one, two, flags, sems):
    rows = visc.shape[0]
    copies = []
    for e, first in enumerate((0, rows - HALO)):
        at = pl.ds(first, HALO)
        pieces = [
            (visc.at[at], one.at[e, 0]),
            (fric.at[at], one.at[e, 1]),
            (driv.at[:, at], two.at[e, 0]),
            (mask.at[at], flags.at[e]),
            (obs.at[:, at], two.at[e, 1]),
        ]
        for n, (source, place) in enumerate(pieces):
            copies.append(pltpu.make_async_copy(source, place, sems.at[e, n]))
    for copy in copies:
        copy.start()
    for copy in copies:
        copy.wait()
    even, at_end = position(ROW_AXES)

    def edge(e):
        return [one[e, 0], one[e, 1], two[e, 0, 0], two[e, 0, 1], flags[e].astype(F32), two[e, 1, 0], two[e, 1, 1]]

    for a, (head, tail) in enumerate(zip(edge(0), edge(1))):
        at = slice(HALO * a, HALO * (a + 1))
        to_a[at, :] = jnp.where(even, tail, head)
        to_b[at, :] = jnp.where(at_end, 0.0, jnp.where(even, head, tail))


def field_of(visc, fric, driv, mask, obs):
    def field(a, at):
        if a == MASK:
            return mask[at, :].astype(F32)
        if a >= OBS:
            return obs[a - OBS, at, :]
        if a >= DRIV:
            return driv[a - DRIV, at, :]
        return (visc, fric)[a][at, :]

    return field


def first_row(part, lane):
    if part < 2:
        return TILE * part + lane
    if lane < INNER + HALO:
        return TILE + lane
    if lane >= TILE - INNER - HALO:
        return lane
    if UPPER + HALO <= lane < UPPER + SLOT:
        return lane - UPPER - HALO
    if LOWER <= lane < LOWER + INNER + HALO:
        return 2 * TILE - INNER - HALO + lane - LOWER
    return None


def right_part(row):
    seam = TILE - HALO <= row < TILE + HALO
    part = 2 if seam or row == 0 or row == 2 * TILE - HALO else row // TILE
    return part, [lane for lane in range(0, TILE, SUB) if first_row(part, lane) == row][-1]


def slot(part, a):
    return TILE * (2 * part + a // PER) + SLOT * (a % PER)


def interior_kernel(visc, fric, driv, mask, obs, edge, n2, n4, c, i, v0, v1, *refs):
    span = visc.shape[0] // SUB
    field = field_of(visc, fric, driv, mask, obs)
    lane = lanes()
    for part in range(PARTS):
        for m in range(-(-ARRAYS // PER)):
            strips = []
            for at in range(0, TILE, SUB):
                row = first_row(part, at)
                packed = jnp.zeros((SUB, TILE), F32)
                if row is not None:
                    for k in range(min(PER, ARRAYS - PER * m)):
                        value = field(PER * m + k, slice(row, row + SUB))
                        moved = pltpu.roll(value, (SLOT * k + INNER) % TILE, 1)
                        packed = jnp.where(lax.div(lane, SLOT) == k, moved, packed)
                strips.append(packed)
            base = TILE * (2 * part + m)
            edge[base : base + TILE, :] = jnp.concatenate(strips, axis=0).T
    refs = (n2, n4, c, i, *refs[:2], v0, v1, *refs[2:])
    domain = Domain(refs, 0, span, lambda a, j: field(a, pl.ds(j, SUB, stride=span)))
    domain.prepare(False)
    run([domain])


def columns_kernel(row_b, row_a, edge, to_b, to_a, turned):
    even = is_even(ROW_AXES)
    above = jnp.where(even, row_b[...], row_a[...])
    below = jnp.where(even, row_a[...], row_b[...])
    halo = jnp.concatenate([above, below, jnp.zeros((TILE - 2 * EDGE, TILE), F32)], axis=0).T
    turned[:INNER, :] = halo[TILE - INNER :]
    turned[INNER:, :] = halo[:INNER]
    even, at_end = position(COL_AXES)
    row = lax.broadcasted_iota(jnp.int32, (SUB, TILE), 0)

    def put(out, right, left):
        right = pltpu.roll(right, LEAD, 0)
        to_a[out : out + HALO, :] = jnp.where(even, right, left)
        to_b[out : out + HALO, :] = jnp.where(at_end, 0.0, jnp.where(even, left, right))

    for part in range(2):
        right, left = [], []
        for a in range(ARRAYS):
            at = slot(part, a) + INNER
            right.append(edge[at - HALO : at, :])
            left.append(edge[at : at + HALO, :])
        for k in range(2):
            seen_r, seen_l = right[OBS + k], left[OBS + k]
            g = 1 + 2 * k
            right[g] = jnp.where(row < 2, pltpu.roll(seen_r, 2, 0), right[g])
            right[g + 1] = jnp.where(row < 2, pltpu.roll(seen_r, 4, 0), right[g + 1])
            left[g] = jnp.where(row >= 6, pltpu.roll(seen_l, 6, 0), left[g])
            left[g + 1] = jnp.where(row >= 6, pltpu.roll(seen_l, 4, 0), left[g + 1])
        for g in range(GROUPS):
            put(HALO * (GROUPS * part + g), right[g], left[g])
    put(2 * GROUPS * HALO, halo[TILE - HALO :], halo[:HALO])


def strided(stack, base):
    span = STRIP // SUB
    return lambda a, j: stack[pl.ds(base + STRIP * a + j, SUB, stride=span), :]


def fill(stack, base, first, last):
    row = lax.broadcasted_iota(jnp.int32, (SUB, TILE), 0)
    one, two = (pltpu.roll(value, LEAD, 0) for value in first)
    mixed = [jnp.where(row == LEAD, two, one), jnp.where(row < SUB // 2, two, last[0])]
    for k, value in enumerate((one, *mixed, last[1])):
        stack[base + SUB * k : base + SUB * (k + 1), :] = value


def velocity(domain, plain, base):
    for j in range(domain.span):
        at = domain.at(j)
        for k in range(2):
            plain[pl.ds(base + STRIP * k + j, SUB, stride=domain.span), :] = domain.refs[6 + k][at, :]


def density(domain, plain, base, out, place):
    w0, w1 = domain.refs[6:8]
    for j in range(domain.span):
        at = domain.at(j)
        v0, v1 = (plain[pl.ds(base + STRIP * k + j, SUB, stride=domain.span), :] for k in range(2))
        value = -domain.source(FRIC, j) * (w0[at, :] * v0 + w1[at, :] * v1)
        out[pl.ds(place + j, SUB, stride=domain.span), :] = value


def beside():
    lane = lanes()
    return (lane < NEAR) | (lane >= TILE - FAR)


def ends(second):
    row = lax.broadcasted_iota(jnp.int32, (SUB, TILE), 0)
    return row >= SUB - FAR if second else row < NEAR


def adjoint_kernel(
    row_b, row_a, visc, fric, driv, mask, obs, n2, n4, c, i, v0, v1, basis_p, basis_q, edge, turned,
    vel, wide, sides, seams,
    stack, plain, dens, total, *refs,
):
    rows = visc.shape[0]
    span = rows // SUB
    even = is_even(ROW_AXES)
    field = field_of(visc, fric, driv, mask, obs)
    for a in range(ARRAYS):
        at = slice(HALO * a, HALO * (a + 1))
        got_a, got_b = row_a[at, :], row_b[at, :]
        base = STRIP * a
        first = [field(a, slice(at, at + SUB)) for at in (0, SUB)]
        last = [field(a, slice(at, at + SUB)) for at in (rows - 2 * SUB, rows - SUB)]
        fill(stack, base, first, last)
        stack[base : base + LEAD, :] = jnp.where(even, got_b, got_a)[HALO - LEAD :]
        stack[base + STRIP - HALO : base + STRIP, :] = jnp.where(even, got_a, got_b)
    strips = Strips(refs[:STRIP_FIELDS], 0, STRIP // SUB, strided(stack, 0), lambda: visc[rows - KEPT - 1 : rows - KEPT, :])
    strips.prepare(False)
    run([strips])
    velocity(strips, plain, 0)
    for k in range(2):
        for e in range(2):
            out = HALO * (2 * k + e)
            vel[out : out + HALO, :] = plain[STRIP * k + OUTER[e] : STRIP * k + OUTER[e] + HALO, :]
    interior = Domain(
        (n2, n4, c, i, *refs[STRIP_FIELDS:]), 0, span, lambda a, j: field(a, pl.ds(j, SUB, stride=span))
    )
    strips.retarget(False)
    interior.retarget(False, (v0, v1))
    run([interior, strips])
    w0, w1 = interior.refs[6:8]
    for j in range(span):
        at = interior.at(j)
        value = -interior.source(FRIC, j) * (w0[at, :] * v0[at, :] + w1[at, :] * v1[at, :])
        dens[pl.ds(j, SUB, stride=span), :] = value
    density(strips, plain, 0, dens, rows)

    side = beside()
    for s in range(0, TILE, SUB):
        summed = jnp.zeros((SUB, TILE), F32)
        for row in range(s, rows, TILE):
            value = dens[row : row + SUB, :]
            if row in (0, rows - SUB):
                at = rows + OUTER[row > 0]
                value = jnp.where(ends(row > 0), dens[at : at + SUB, :], value)
            summed += value
        total[s : s + SUB, :] = jnp.where(side, 0.0, summed)
    exact = dict(precision=lax.Precision.HIGHEST, preferred_element_type=F32)
    half = jnp.dot(basis_p[...], total[...], **exact)
    wide[...] = jnp.dot(half, basis_q[...], **exact)

    corner = corners()
    for part in range(PARTS):
        for a in range(ARRAYS):
            columns = []
            for r in range(0, SLOT, SUB):
                value = edge[slot(part, a) + r : slot(part, a) + r + SUB, :]
                if part == 2:
                    moved = pltpu.roll(turned[r : r + SUB, :], (UPPER - HALO * a) % TILE, 1)
                    value = jnp.where(corner, moved, value)
                columns.append(value)
            fill(sides, strip(part, a), columns[2:], columns[:2])
            if a == VISC:
                seams[SUB * part : SUB * (part + 1), :] = columns[0]


def strip(part, a):
    return STRIP * (ARRAYS * part + a)


def corners():
    lane = lanes()
    above = (lane >= UPPER) & (lane < UPPER + HALO)
    return above | ((lane >= LOWER + INNER + HALO) & (lane < LOWER + SLOT))


def split(x, axis):
    high = x.astype(jnp.bfloat16)
    low = (x - high.astype(F32)).astype(jnp.bfloat16)
    return jnp.concatenate([high, high, low], axis=axis)


def split_constant(x, axis):
    x = np.asarray(x, np.float32)
    high = np.asarray(x, jnp.bfloat16)
    low = np.asarray(x - np.asarray(high, np.float32), jnp.bfloat16)
    return jnp.asarray(np.concatenate([high, low, high], axis=axis))


def left_right_kernel(
    _, seams, col_b, col_a, wide_in, block, basis_rows, basis_cols,
    stack, strips, coef,
    plain, *refs,
):
    even = is_even(COL_AXES)
    lane = lanes()
    row = lax.broadcasted_iota(jnp.int32, (SUB, TILE), 0)
    upper = (lane >= UPPER + HALO) & (lane < UPPER + SLOT)
    lower = (lane >= LOWER) & (lane < LOWER + INNER + HALO)
    seam_t0 = lane >= TILE - INNER - HALO
    seam_t1 = lane < INNER + HALO
    corner = corners()
    for from_left in (True, False):
        groups = []
        for g in range(2 * GROUPS + 1):
            got_a, got_b = col_a[HALO * g : HALO * (g + 1), :], col_b[HALO * g : HALO * (g + 1), :]
            groups.append(jnp.where(even, got_b, got_a) if from_left else jnp.where(even, got_a, got_b))
        tiles = []
        for part in range(2):
            tile = groups[GROUPS * part : GROUPS * (part + 1)]
            for k in range(2):
                g, h = tile[1 + 2 * k], tile[2 + 2 * k]
                if from_left:
                    tile.append(jnp.where(row >= 5, pltpu.roll(g, 6, 0), pltpu.roll(h, 4, 0)))
                else:
                    tile.append(jnp.where(row < 2, pltpu.roll(g, 2, 0), pltpu.roll(h, 4, 0)))
            tiles.append(tile)
        for a in range(ARRAYS):
            t0, t1 = tiles[0][a], tiles[1][a]
            third = jnp.where(corner, pltpu.roll(groups[-1], (UPPER - HALO * a) % TILE, 1), 0.0)
            third = jnp.where(upper, pltpu.roll(t0, UPPER + HALO, 1), third)
            third = jnp.where(lower, pltpu.roll(t1, LOWER + INNER + HALO, 1), third)
            third = jnp.where(seam_t0, t0, jnp.where(seam_t1, t1, third))
            for part, value in enumerate((t0, t1, third)):
                base = strip(part, a)
                if from_left:
                    stack[base : base + LEAD, :] = value[:LEAD]
                else:
                    stack[base + STRIP - HALO : base + STRIP, :] = value
    last = INNER - KEPT - 1
    before = [lambda at=SUB * part + last: seams[at : at + 1, :] for part in range(PARTS)]
    domains = [
        Strips(refs, STRIP * part, STRIP // SUB, strided(stack, strip(part, 0)), seam)
        for part, seam in enumerate(before)
    ]
    for domain in domains:
        domain.prepare(True)
    run(domains, True)
    for part, domain in enumerate(domains):
        velocity(domain, strips, 2 * STRIP * part)
        domain.retarget(True)
    run(domains, True)
    for part, domain in enumerate(domains):
        density(domain, strips, 2 * STRIP * part, plain, STRIP * part)

    def side(part):
        base = STRIP * part
        return jnp.concatenate(
            [plain[base + at : base + at + HALO, :] for at in OUTER], axis=0
        )

    lane = lax.broadcasted_iota(jnp.int32, (2 * HALO, TILE), 1)
    row = lax.broadcasted_iota(jnp.int32, (2 * HALO, TILE), 0)
    right = (row < NEAR) | (row >= 2 * HALO - FAR)
    straight = (lane >= HALO) & (lane < TILE - HALO)
    seam = (lane < HALO) | (lane >= TILE - HALO)
    top = (lane >= UPPER + HALO) & (lane < UPPER + 2 * HALO)
    bottom = (lane >= LOWER + INNER) & (lane < LOWER + INNER + HALO)
    dens = jnp.concatenate(
        [
            jnp.where(right & straight, side(0) + side(1), 0.0),
            jnp.where(right & (seam | top | bottom), side(2), 0.0),
        ],
        axis=1,
    )
    half = lax.dot_general(
        basis_rows[...], split(dens, 1), (((1,), (1,)), ((), ())), preferred_element_type=F32
    )
    high = half.astype(jnp.bfloat16)
    low = (half - high.astype(F32)).astype(jnp.bfloat16)
    both = jnp.dot(jnp.concatenate([high, low], axis=0), basis_cols[:INNER], preferred_element_type=F32)
    rest = jnp.dot(high, basis_cols[INNER:], preferred_element_type=F32)
    wide = wide_in[...] + (both[:MODES] + (both[MODES:] + rest))
    lane = lanes()
    which = lax.div(lane, MODES)
    flat = wide[:SUB]
    for j in range(1, MODES // SUB):
        flat = jnp.where(which == j, wide[SUB * j : SUB * (j + 1)], flat)
    mark = jnp.broadcast_to(block[:1, :].astype(F32), (SUB, TILE))
    row = lax.broadcasted_iota(jnp.int32, (SUB, TILE), 0)
    moved = [flat] + [pltpu.roll(flat, r, 0) for r in range(1, SUB)] + [flat]
    lines = [flat] + [
        jnp.where(row < r - 1, moved[r - 1], jnp.where(row == r - 1, mark, moved[r])) for r in range(1, SUB + 1)
    ]
    cycle = SUB * (SUB + 1)
    chunk = min(4, coef.shape[0] // cycle)

    def spread(d, carry):
        for e in range(chunk):
            for r, line in enumerate(lines):
                coef[pl.ds(pl.multiple_of((d * chunk + e) * cycle + SUB * r, SUB), SUB), :] = line
        return carry

    lax.fori_loop(0, coef.shape[0] // cycle // chunk, spread, 0)


def join_kernel(v0, v1, vel_ends, strips, vel, turned):
    rows = vel.shape[1]
    span = rows // SUB
    middle = jnp.zeros((TILE - 2 * HALO, TILE), F32)
    side = beside()
    for k, v in enumerate((v0, v1)):
        for part in range(PARTS):
            base = STRIP * (2 * part + 1 - k)
            first, last = (strips[base + at : base + at + HALO, :] for at in OUTER)
            at = TILE * (2 * part + k)
            turned[at : at + TILE, :] = jnp.concatenate([first, middle, last], axis=0).T
        for row in range(0, rows, SUB):
            value = v[pl.ds(SUB * (row % span) + row // span, SUB, stride=SUB), :]
            if row in (0, rows - SUB):
                at = HALO * (2 * k + (row > 0))
                value = jnp.where(ends(row > 0), vel_ends[at : at + HALO, :], value)
            part, lane = right_part(row)
            at = TILE * (2 * part + k) + lane
            vel[k, row : row + SUB, :] = jnp.where(side, turned[at : at + SUB, :], value)


def bases():
    places = np.arange(TILE) + 0.5
    basis = np.cos(math.pi * places[:, None] * np.arange(MODES)[None, :] / TILE)
    groups = MODES // SUB
    order = np.arange(MODES).reshape(SUB, groups).T.reshape(-1)
    rows = basis[:, order] / TILE
    cols = np.tile(basis, (1, groups))
    placed = np.zeros((2 * TILE, MODES))
    for row in range(0, 2 * TILE, SUB):
        part, lane = right_part(row)
        at = lane + (TILE if part == 2 else 0)
        placed[at : at + SUB] = rows[row % TILE : row % TILE + SUB]
    outer = np.concatenate([cols[:HALO], cols[TILE - HALO :]])
    return jnp.asarray(rows.T, F32), jnp.asarray(cols, F32), split_constant(placed.T, 1), split_constant(outer, 0)[: 2 * INNER]


def pick_kernel(owners, every, out):
    mine = out.shape[1]
    own = lax.axis_index("own")
    wanted = [owners[pl.ds(own, 1), k : k + 1].astype(F32) for k in range(mine)]
    lines = SUB + 1
    devices = every.shape[0] // lines
    chunk = min(4, devices // SUB)

    def body(d, sums):
        sums = list(sums)
        for e in range(chunk):
            base = (d * chunk + e) * SUB * lines
            mark = every[pl.ds(base + SUB, SUB, stride=lines), :]
            hits = [mark == wanted[k] for k in range(mine)]
            for r in range(SUB):
                part = every[pl.ds(base + r, SUB, stride=lines), :]
                for k in range(mine):
                    sums[SUB * k + r] += jnp.where(hits[k], part, 0.0)
        return tuple(sums)

    start = (jnp.zeros((SUB, TILE), F32),) * (mine * SUB)
    sums = lax.fori_loop(0, devices // SUB // chunk, body, start)
    for k in range(mine):
        for r in range(SUB):
            total = jnp.sum(sums[SUB * k + r], axis=0, keepdims=True)
            out[0, k : k + 1, TILE * r : TILE * (r + 1)] = total


def local(viscosity, friction, driving, observed, ice_mask, tile_block, owner_list):
    rows, cols = viscosity.shape
    assert (rows, cols) == (2 * TILE, TILE)
    inputs = (viscosity, friction, driving, ice_mask, observed)
    near = [pltpu.with_memory_space_constraint(x, pltpu.VMEM) for x in inputs]
    basis_p, basis_q, basis_rows, basis_cols = bases()
    to_b, to_a = call(
        ends_kernel,
        "ends",
        (vmem(EDGE, cols), vmem(EDGE, cols)),
        [
            vmem(2, 2, HALO, cols),
            vmem(2, 2, 2, HALO, cols),
            pltpu.VMEM((2, HALO, cols), jnp.int32),
            pltpu.SemaphoreType.DMA((2, 5)),
        ],
        10**6,
        *(pltpu.with_memory_space_constraint(x, pltpu.HBM) for x in inputs),
    )
    row_b = swap(to_b, 0, 1)
    row_a = swap(to_a, 0, 0)
    edge, *forward = call(
        interior_kernel,
        "interior",
        (vmem(2 * PARTS * TILE, TILE),) + (vmem(rows, cols),) * 6,
        [vmem(rows, cols)] * (FIELDS - 6),
        8 * 10**6,
        *near,
    )
    to_b, to_a, turned = call(
        columns_kernel,
        "columns",
        (vmem(SENT, TILE), vmem(SENT, TILE), vmem(SLOT, TILE)),
        [],
        10**5,
        row_b,
        row_a,
        edge,
    )
    col_b = swap(to_b, 1, 1)
    col_a = swap(to_a, 1, 0)
    vel_ends, wide, sides, seams = call(
        adjoint_kernel,
        "adjoint",
        (
            vmem(4 * HALO, cols),
            vmem(MODES, TILE),
            vmem(PARTS * ARRAYS * STRIP, TILE),
            vmem(PARTS * SUB, TILE),
        ),
        [vmem(ARRAYS * STRIP, cols), vmem(2 * STRIP, cols), vmem(rows + STRIP, cols), vmem(TILE, cols)]
        + [vmem(STRIP, cols)] * STRIP_FIELDS
        + [vmem(rows, cols)] * (FIELDS - 4),
        8 * 10**6,
        row_b,
        row_a,
        *near,
        *forward,
        basis_p,
        basis_q,
        edge,
        turned,
    )
    devices = lax.axis_size(ROW_AXES + COL_AXES)
    _, strips, coef = call(
        left_right_kernel,
        "left_right",
        (
            vmem(PARTS * ARRAYS * STRIP, TILE),
            vmem(PARTS * 2 * STRIP, TILE),
            vmem(devices * (SUB + 1), TILE),
        ),
        [vmem(PARTS * STRIP, TILE)] * (STRIP_FIELDS + 1),
        4 * 10**6,
        sides,
        seams,
        col_b,
        col_a,
        wide,
        tile_block,
        basis_rows,
        basis_cols,
        aliases={0: 0},
    )
    coef = coef.reshape(devices, 1, (SUB + 1) * TILE)
    parts = lax.all_to_all(coef, ROW_AXES + COL_AXES, 0, 0, tiled=True)
    state = call(
        join_kernel,
        "join",
        jax.ShapeDtypeStruct((2, rows, cols), F32),
        [vmem(2 * PARTS * TILE, TILE)],
        4 * 10**6,
        *forward[4:],
        vel_ends,
        strips,
    )
    owners = owner_list.reshape(lax.axis_size("own"), -1)
    picked = call(
        pick_kernel,
        "pick",
        jax.ShapeDtypeStruct((1, owners.shape[1], MODES * MODES), F32),
        [],
        10**5,
        owners,
        parts.reshape(-1, TILE),
    )
    return (state, picked)


def solution(mesh):
    return jax.shard_map(
        local,
        mesh=mesh,
        in_specs=(
            P(("row", "own"), "col"),
            P(("row", "own"), "col"),
            P(None, ("row", "own"), "col"),
            P(None, ("row", "own"), "col"),
            P(("row", "own"), "col"),
            P(("row", "own"), "col"),
            P(),
        ),
        out_specs=(P(None, ("row", "own"), "col"), P("own", None, None)),
        check_vma=False,
    )
```

```python
import math

import jax
import jax.numpy as jnp
import numpy as np
from jax import lax
from jax.experimental import pallas as pl
from jax.experimental.pallas import tpu as pltpu
from jax.sharding import PartitionSpec as P

TILE = 128
MODES = 32
SWEEPS = 3
SUB = 8
HALO = 8
INNER = 2 * HALO
STRIP = 40
LEAD = HALO - 1
KEPT = 12
OUTER = (LEAD, STRIP - 2 * HALO)
NEAR, FAR = 7, 6
ARRAYS = 7
VISC, FRIC, DRIV, MASK, OBS = 0, 1, 2, 4, 5
EDGE = ARRAYS * HALO
SLOT = 2 * INNER
PER = TILE // SLOT
GROUPS = 5
SENT = 2 * GROUPS * HALO + HALO
PARTS = 3
UPPER, LOWER = 32, 64
ROW_AXES = ("row", "own")
COL_AXES = ("col",)
F32 = jnp.float32
LIMIT = 40 * 1024 * 1024


def swap(x, axis, first):
    sizes = lax.axis_size(ROW_AXES), lax.axis_size(COL_AXES)
    owners = lax.axis_size("own")

    def device(i, j):
        return (i // owners * sizes[1] + j) * owners + i % owners

    pairs = []
    for i in range(sizes[0]):
        for j in range(sizes[1]):
            place = [i, j]
            if first and place[axis] in (0, sizes[axis] - 1):
                place[1 - axis] ^= 1
            else:
                place[axis] = ((place[axis] + first) ^ 1) - first
            pairs.append((device(i, j), device(*place)))
    return lax.ppermute(x, ("row", "col", "own"), pairs)


def position(axes):
    index, size = 0, 1
    for axis in axes:
        index = index * lax.axis_size(axis) + lax.axis_index(axis)
        size *= lax.axis_size(axis)
    assert size % 2 == 0
    return lax.rem(index, 2) == 0, (index == 0) | (index == size - 1)


def is_even(axes):
    return position(axes)[0]


def lanes():
    return lax.broadcasted_iota(jnp.int32, (SUB, TILE), 1)


def call(kernel, name, outs, scratch, cost, *args, aliases={}):
    return pl.pallas_call(
        kernel,
        out_shape=outs,
        scratch_shapes=scratch,
        input_output_aliases=aliases,
        compiler_params=pltpu.CompilerParams(vmem_limit_bytes=LIMIT),
        cost_estimate=pl.CostEstimate(flops=cost, bytes_accessed=cost, transcendentals=0),
        name=name,
    )(*args)


def vmem(*shape):
    return pltpu.VMEM(shape, F32)


FIELDS = 14
STRIP_FIELDS = 24


class Domain:
    def __init__(self, refs, base, span, source, seam=None):
        self.refs, self.base, self.span, self.source, self.seam = refs, base, span, source, seam

    def at(self, j):
        return pl.ds(self.base + SUB * j, SUB)

    def prepare(self, flipped):
        n2, n4, c, i = self.refs[:4]
        visc = [self.source(VISC, j) for j in range(self.span)]
        for j in range(self.span):
            at = self.at(j)
            before = visc[j - 1] if j else pltpu.roll(visc[-1], 1, 0)
            if self.seam and not j:
                row = lax.broadcasted_iota(jnp.int32, (SUB, TILE), 0)
                before = jnp.where(row == SUB // 2, self.seam(), before)
            pair = visc[j] + before
            fric = self.source(FRIC, j)
            diag = 1.25 * (pair + pltpu.roll(pair, 1, 1)) + fric
            on = self.source(MASK, j) > 0.0
            inv = jnp.where(on, 0.5 / jnp.where(on, diag, 1.0), 0.0)
            half = 0.5 * visc[j]
            n2[at, :] = half
            n4[at, :] = 0.5 * half
            c[at, :] = 1.0 - fric * inv
            i[at, :] = inv
            for k in range(2):
                self.start(k, at, inv * self.source(DRIV + (1 - k if flipped else k), j))

    def start(self, k, at, value):
        self.refs[4 + k][at, :] = value
        self.write(k, at, value + value)

    def write(self, k, at, value):
        self.refs[6 + k][at, :] = value
        self.refs[8 + k][at, :] = pltpu.roll(value, TILE - 1, 1)

    def retarget(self, flipped):
        i = self.refs[3]
        velocity = self.refs[6:8]
        for j in range(self.span):
            at = self.at(j)
            for k in range(2):
                seen = self.source(OBS + (1 - k if flipped else k), j)
                self.start(k, at, i[at, :] * (velocity[k][at, :] - seen))

    def differences(self):
        n2, n4 = self.refs[:2]
        fields = self.refs[6:10]
        parts = self.refs[10:14]

        def corners(j, here, below):
            w0, w1, r0, r1 = here
            v0, v1, s0, s1 = below
            a1, a2 = s0 - w0, v0 - r0
            e1, e2 = s1 - w1, v1 - r1
            x, y = a1 + a2, e1 - e2
            q = (a1 - a2) + (e1 + e2)
            both = x + y
            at = self.at(j)
            half = n2[at, :]
            return half * (both + x), n4[at, :] * q, half * (both + y)

        def load(j):
            at = self.at(j)
            return [field[at, :] for field in fields]

        top = load(0)
        last = corners(self.span - 1, load(self.span - 1), [pltpu.roll(v, SUB - 1, 0) for v in top])
        up = [pltpu.roll(v, 1, 0) for v in last]
        here = top
        for j in range(self.span):
            at = self.at(j)
            if j < self.span - 1:
                below = load(j + 1)
                p, q, r = corners(j, here, below)
                here = below
            else:
                p, q, r = last
            g, t = up[0] - p, up[1] + q
            gq, tr = up[1] - q, up[2] + r
            parts[0][at, :] = g - t
            parts[1][at, :] = gq - tr
            parts[2][at, :] = pltpu.roll(g + t, 1, 1)
            parts[3][at, :] = pltpu.roll(gq + tr, 1, 1)
            up = (p, q, r)

    def update(self):
        c, i, b0, b1, w0, w1 = self.refs[2:8]
        parts = self.refs[10:14]
        for j in range(self.span):
            at = self.at(j)
            cv, iv = c[at, :], i[at, :]
            for k, (b, w) in enumerate(((b0, w0), (b1, w1))):
                value = (cv * w[at, :] + b[at, :]) - iv * (parts[k][at, :] + parts[k + 2][at, :])
                self.write(k, at, value)


class Strips(Domain):
    def prepare(self, flipped):
        super().prepare(flipped)
        for j in range(self.span):
            at = self.at(j)
            for now, later in zip(self.refs[2:4], self.refs[10:12]):
                later[at, :] = pltpu.roll(now[at, :], TILE - 1, 1)
        for now, before in zip(self.refs[:2], self.refs[14:16]):
            before[self.at(0), :] = pltpu.roll(now[self.at(self.span - 1), :], 1, 0)

    def start(self, k, at, value):
        b, w, r, later = (self.refs[n + k] for n in (4, 6, 8, 12))
        b[at, :] = value
        w[at, :] = value + value
        turned = pltpu.roll(value, TILE - 1, 1)
        later[at, :] = turned
        r[at, :] = turned + turned

    def differences(self):
        fields = self.refs[6:10]
        kept, turned, kept_next, turned_next = (self.refs[16 + 2 * k : 18 + 2 * k] for k in range(4))

        def corners(halves, quarters, j, here, below):
            w0, w1, r0, r1 = here
            v0, v1, s0, s1 = below
            a1, a2 = s0 - w0, v0 - r0
            e1, e2 = s1 - w1, v1 - r1
            x, y = a1 + a2, e1 - e2
            q = (a1 - a2) + (e1 + e2)
            both = x + y
            at = self.at(j)
            half = halves[at, :]
            return half * (both + x), quarters[at, :] * q, half * (both + y)

        def load(j):
            at = self.at(j)
            return [field[at, :] for field in fields]

        top, end = load(0), load(self.span - 1)
        up = corners(*self.refs[14:16], 0, [pltpu.roll(v, 1, 0) for v in end], top)
        here = top
        for j in range(self.span):
            at = self.at(j)
            below = load(j + 1) if j < self.span - 1 else [pltpu.roll(v, SUB - 1, 0) for v in top]
            p, q, r = corners(*self.refs[:2], j, here, below)
            g, t = up[0] - p, up[1] + q
            gq, tr = up[1] - q, up[2] + r
            for k, (stay, move) in enumerate(((g - t, g + t), (gq - tr, gq + tr))):
                kept[k][at, :] = stay
                turned_next[k][at, :] = move
                turned[k][at, :] = pltpu.roll(move, 1, 1)
                kept_next[k][at, :] = pltpu.roll(stay, TILE - 1, 1)
            up, here = (p, q, r), below

    def update(self):
        for first, offset, parts in ((2, 6, (16, 18)), (10, 8, (20, 22))):
            c, i, *b = self.refs[first : first + 4]
            for j in range(self.span):
                at = self.at(j)
                cv, iv = c[at, :], i[at, :]
                for k in range(2):
                    w = self.refs[offset + k]
                    change = self.refs[parts[0] + k][at, :] + self.refs[parts[1] + k][at, :]
                    w[at, :] = (cv * w[at, :] + b[k][at, :]) - iv * change


def run(domains, written_out=False):
    def body(_, carry):
        for domain in domains:
            domain.differences()
        for domain in domains:
            domain.update()
        return carry

    if written_out:
        for k in range(SWEEPS):
            body(k, 0)
    else:
        lax.fori_loop(0, SWEEPS, body, 0)


def ends_kernel(visc, fric, driv, mask, obs, to_b, to_a, one, two, flags, sems):
    rows = visc.shape[0]
    copies = []
    for e, first in enumerate((0, rows - HALO)):
        at = pl.ds(first, HALO)
        pieces = [
            (visc.at[at], one.at[e, 0]),
            (fric.at[at], one.at[e, 1]),
            (driv.at[:, at], two.at[e, 0]),
            (mask.at[at], flags.at[e]),
            (obs.at[:, at], two.at[e, 1]),
        ]
        for n, (source, place) in enumerate(pieces):
            copies.append(pltpu.make_async_copy(source, place, sems.at[e, n]))
    for copy in copies:
        copy.start()
    for copy in copies:
        copy.wait()
    even, at_end = position(ROW_AXES)

    def edge(e):
        return [one[e, 0], one[e, 1], two[e, 0, 0], two[e, 0, 1], flags[e].astype(F32), two[e, 1, 0], two[e, 1, 1]]

    for a, (head, tail) in enumerate(zip(edge(0), edge(1))):
        at = slice(HALO * a, HALO * (a + 1))
        to_a[at, :] = jnp.where(even, tail, head)
        to_b[at, :] = jnp.where(at_end, 0.0, jnp.where(even, head, tail))


def first_row(part, lane):
    if part < 2:
        return TILE * part + lane
    if lane < INNER + HALO:
        return TILE + lane
    if lane >= TILE - INNER - HALO:
        return lane
    if UPPER + HALO <= lane < UPPER + SLOT:
        return lane - UPPER - HALO
    if LOWER <= lane < LOWER + INNER + HALO:
        return 2 * TILE - INNER - HALO + lane - LOWER
    return None


def right_part(row):
    seam = TILE - HALO <= row < TILE + HALO
    part = 2 if seam or row == 0 or row == 2 * TILE - HALO else row // TILE
    return part, [lane for lane in range(0, TILE, SUB) if first_row(part, lane) == row][-1]


def slot(part, a):
    return TILE * (2 * part + a // PER) + SLOT * (a % PER)


def field_in(every):
    rows = every.shape[0] // ARRAYS

    def field(a, at):
        return every[rows * a + at.start : rows * a + at.stop, :]

    return field


def load_kernel(visc, fric, driv, mask, obs, _, every, edge, flags, sems):
    rows = visc.shape[0]

    def place(a):
        return every.at[pl.ds(rows * a, rows)]

    pieces = [
        (visc, place(VISC)),
        (fric, place(FRIC)),
        (mask, flags),
        (driv.at[0], place(DRIV)),
        (driv.at[1], place(DRIV + 1)),
        (obs.at[0], place(OBS)),
        (obs.at[1], place(OBS + 1)),
    ]
    copies = [pltpu.make_async_copy(*piece, sems.at[n]) for n, piece in enumerate(pieces)]
    for copy in copies:
        copy.start()
    for copy in copies:
        copy.wait()
    every[MASK * rows : (MASK + 1) * rows, :] = flags[...].astype(F32)
    field = field_in(every)
    lane = lanes()
    for part in range(PARTS):
        for m in range(-(-ARRAYS // PER)):
            strips = []
            for at in range(0, TILE, SUB):
                row = first_row(part, at)
                packed = jnp.zeros((SUB, TILE), F32)
                if row is not None:
                    for k in range(min(PER, ARRAYS - PER * m)):
                        value = field(PER * m + k, slice(row, row + SUB))
                        moved = pltpu.roll(value, (SLOT * k + INNER) % TILE, 1)
                        packed = jnp.where(lax.div(lane, SLOT) == k, moved, packed)
                strips.append(packed)
            base = TILE * (2 * part + m)
            edge[base : base + TILE, :] = jnp.concatenate(strips, axis=0).T

def columns_kernel(row_b, row_a, edge, to_b, to_a, turned):
    even = is_even(ROW_AXES)
    above = jnp.where(even, row_b[...], row_a[...])
    below = jnp.where(even, row_a[...], row_b[...])
    halo = jnp.concatenate([above, below, jnp.zeros((TILE - 2 * EDGE, TILE), F32)], axis=0).T
    turned[:INNER, :] = halo[TILE - INNER :]
    turned[INNER:, :] = halo[:INNER]
    even, at_end = position(COL_AXES)
    row = lax.broadcasted_iota(jnp.int32, (SUB, TILE), 0)

    def put(out, right, left):
        right = pltpu.roll(right, LEAD, 0)
        to_a[out : out + HALO, :] = jnp.where(even, right, left)
        to_b[out : out + HALO, :] = jnp.where(at_end, 0.0, jnp.where(even, left, right))

    for part in range(2):
        right, left = [], []
        for a in range(ARRAYS):
            at = slot(part, a) + INNER
            right.append(edge[at - HALO : at, :])
            left.append(edge[at : at + HALO, :])
        for k in range(2):
            seen_r, seen_l = right[OBS + k], left[OBS + k]
            g = 1 + 2 * k
            right[g] = jnp.where(row < 2, pltpu.roll(seen_r, 2, 0), right[g])
            right[g + 1] = jnp.where(row < 2, pltpu.roll(seen_r, 4, 0), right[g + 1])
            left[g] = jnp.where(row >= 6, pltpu.roll(seen_l, 6, 0), left[g])
            left[g + 1] = jnp.where(row >= 6, pltpu.roll(seen_l, 4, 0), left[g + 1])
        for g in range(GROUPS):
            put(HALO * (GROUPS * part + g), right[g], left[g])
    put(2 * GROUPS * HALO, halo[TILE - HALO :], halo[:HALO])


def strided(stack, base):
    span = STRIP // SUB
    return lambda a, j: stack[pl.ds(base + STRIP * a + j, SUB, stride=span), :]


def fill(stack, base, first, last):
    row = lax.broadcasted_iota(jnp.int32, (SUB, TILE), 0)
    one, two = (pltpu.roll(value, LEAD, 0) for value in first)
    mixed = [jnp.where(row == LEAD, two, one), jnp.where(row < SUB // 2, two, last[0])]
    for k, value in enumerate((one, *mixed, last[1])):
        stack[base + SUB * k : base + SUB * (k + 1), :] = value


def velocity(domain, plain, base):
    for j in range(domain.span):
        at = domain.at(j)
        for k in range(2):
            plain[pl.ds(base + STRIP * k + j, SUB, stride=domain.span), :] = domain.refs[6 + k][at, :]


def density(domain, plain, base, out, place):
    w0, w1 = domain.refs[6:8]
    for j in range(domain.span):
        at = domain.at(j)
        v0, v1 = (plain[pl.ds(base + STRIP * k + j, SUB, stride=domain.span), :] for k in range(2))
        value = -domain.source(FRIC, j) * (w0[at, :] * v0 + w1[at, :] * v1)
        out[pl.ds(place + j, SUB, stride=domain.span), :] = value


def beside():
    lane = lanes()
    return (lane < NEAR) | (lane >= TILE - FAR)


def ends(second):
    row = lax.broadcasted_iota(jnp.int32, (SUB, TILE), 0)
    return row >= SUB - FAR if second else row < NEAR


def adjoint_kernel(
    row_b, row_a, every, basis_p, basis_q, edge, turned,
    vel, wide, sides, seams, v0, v1,
    stack, plain, dens, total, *refs,
):
    rows = every.shape[0] // ARRAYS
    span = rows // SUB
    even = is_even(ROW_AXES)
    field = field_in(every)
    for a in range(ARRAYS):
        at = slice(HALO * a, HALO * (a + 1))
        got_a, got_b = row_a[at, :], row_b[at, :]
        base = STRIP * a
        first = [field(a, slice(at, at + SUB)) for at in (0, SUB)]
        last = [field(a, slice(at, at + SUB)) for at in (rows - 2 * SUB, rows - SUB)]
        fill(stack, base, first, last)
        stack[base : base + LEAD, :] = jnp.where(even, got_b, got_a)[HALO - LEAD :]
        stack[base + STRIP - HALO : base + STRIP, :] = jnp.where(even, got_a, got_b)
    strips = Strips(refs[:STRIP_FIELDS], 0, STRIP // SUB, strided(stack, 0), lambda: every[rows - KEPT - 1 : rows - KEPT, :])
    interior = Domain(
        refs[STRIP_FIELDS:], 0, span, lambda a, j: every[pl.ds(rows * a + j, SUB, stride=span), :]
    )
    strips.prepare(False)
    interior.prepare(False)
    run([interior, strips])
    v0[...] = interior.refs[6][...]
    v1[...] = interior.refs[7][...]
    velocity(strips, plain, 0)
    for k in range(2):
        for e in range(2):
            out = HALO * (2 * k + e)
            vel[out : out + HALO, :] = plain[STRIP * k + OUTER[e] : STRIP * k + OUTER[e] + HALO, :]
    strips.retarget(False)
    interior.retarget(False)
    run([interior, strips])
    w0, w1 = interior.refs[6:8]
    for j in range(span):
        at = interior.at(j)
        value = -interior.source(FRIC, j) * (w0[at, :] * v0[at, :] + w1[at, :] * v1[at, :])
        dens[pl.ds(j, SUB, stride=span), :] = value
    density(strips, plain, 0, dens, rows)

    side = beside()
    for s in range(0, TILE, SUB):
        summed = jnp.zeros((SUB, TILE), F32)
        for row in range(s, rows, TILE):
            value = dens[row : row + SUB, :]
            if row in (0, rows - SUB):
                at = rows + OUTER[row > 0]
                value = jnp.where(ends(row > 0), dens[at : at + SUB, :], value)
            summed += value
        total[s : s + SUB, :] = jnp.where(side, 0.0, summed)
    exact = dict(precision=lax.Precision.HIGHEST, preferred_element_type=F32)
    half = jnp.dot(basis_p[...], total[...], **exact)
    wide[...] = jnp.dot(half, basis_q[...], **exact)

    corner = corners()
    for part in range(PARTS):
        for a in range(ARRAYS):
            columns = []
            for r in range(0, SLOT, SUB):
                value = edge[slot(part, a) + r : slot(part, a) + r + SUB, :]
                if part == 2:
                    moved = pltpu.roll(turned[r : r + SUB, :], (UPPER - HALO * a) % TILE, 1)
                    value = jnp.where(corner, moved, value)
                columns.append(value)
            fill(sides, strip(part, a), columns[2:], columns[:2])
            if a == VISC:
                seams[SUB * part : SUB * (part + 1), :] = columns[0]


def strip(part, a):
    return STRIP * (ARRAYS * part + a)


def corners():
    lane = lanes()
    above = (lane >= UPPER) & (lane < UPPER + HALO)
    return above | ((lane >= LOWER + INNER + HALO) & (lane < LOWER + SLOT))


def split(x, axis):
    high = x.astype(jnp.bfloat16)
    low = (x - high.astype(F32)).astype(jnp.bfloat16)
    return jnp.concatenate([high, high, low], axis=axis)


def split_constant(x, axis):
    x = np.asarray(x, np.float32)
    high = np.asarray(x, jnp.bfloat16)
    low = np.asarray(x - np.asarray(high, np.float32), jnp.bfloat16)
    return jnp.asarray(np.concatenate([high, low, high], axis=axis))


def left_right_kernel(
    _, seams, col_b, col_a, wide_in, block, basis_rows, basis_cols,
    stack, strips, coef,
    plain, *refs,
):
    even = is_even(COL_AXES)
    lane = lanes()
    row = lax.broadcasted_iota(jnp.int32, (SUB, TILE), 0)
    upper = (lane >= UPPER + HALO) & (lane < UPPER + SLOT)
    lower = (lane >= LOWER) & (lane < LOWER + INNER + HALO)
    seam_t0 = lane >= TILE - INNER - HALO
    seam_t1 = lane < INNER + HALO
    corner = corners()
    for from_left in (True, False):
        groups = []
        for g in range(2 * GROUPS + 1):
            got_a, got_b = col_a[HALO * g : HALO * (g + 1), :], col_b[HALO * g : HALO * (g + 1), :]
            groups.append(jnp.where(even, got_b, got_a) if from_left else jnp.where(even, got_a, got_b))
        tiles = []
        for part in range(2):
            tile = groups[GROUPS * part : GROUPS * (part + 1)]
            for k in range(2):
                g, h = tile[1 + 2 * k], tile[2 + 2 * k]
                if from_left:
                    tile.append(jnp.where(row >= 5, pltpu.roll(g, 6, 0), pltpu.roll(h, 4, 0)))
                else:
                    tile.append(jnp.where(row < 2, pltpu.roll(g, 2, 0), pltpu.roll(h, 4, 0)))
            tiles.append(tile)
        for a in range(ARRAYS):
            t0, t1 = tiles[0][a], tiles[1][a]
            third = jnp.where(corner, pltpu.roll(groups[-1], (UPPER - HALO * a) % TILE, 1), 0.0)
            third = jnp.where(upper, pltpu.roll(t0, UPPER + HALO, 1), third)
            third = jnp.where(lower, pltpu.roll(t1, LOWER + INNER + HALO, 1), third)
            third = jnp.where(seam_t0, t0, jnp.where(seam_t1, t1, third))
            for part, value in enumerate((t0, t1, third)):
                base = strip(part, a)
                if from_left:
                    stack[base : base + LEAD, :] = value[:LEAD]
                else:
                    stack[base + STRIP - HALO : base + STRIP, :] = value
    last = INNER - KEPT - 1
    before = [lambda at=SUB * part + last: seams[at : at + 1, :] for part in range(PARTS)]
    domains = [
        Strips(refs, STRIP * part, STRIP // SUB, strided(stack, strip(part, 0)), seam)
        for part, seam in enumerate(before)
    ]
    for domain in domains:
        domain.prepare(True)
    run(domains, True)
    for part, domain in enumerate(domains):
        velocity(domain, strips, 2 * STRIP * part)
        domain.retarget(True)
    run(domains, True)
    for part, domain in enumerate(domains):
        density(domain, strips, 2 * STRIP * part, plain, STRIP * part)

    def side(part):
        base = STRIP * part
        return jnp.concatenate(
            [plain[base + at : base + at + HALO, :] for at in OUTER], axis=0
        )

    lane = lax.broadcasted_iota(jnp.int32, (2 * HALO, TILE), 1)
    row = lax.broadcasted_iota(jnp.int32, (2 * HALO, TILE), 0)
    right = (row < NEAR) | (row >= 2 * HALO - FAR)
    straight = (lane >= HALO) & (lane < TILE - HALO)
    seam = (lane < HALO) | (lane >= TILE - HALO)
    top = (lane >= UPPER + HALO) & (lane < UPPER + 2 * HALO)
    bottom = (lane >= LOWER + INNER) & (lane < LOWER + INNER + HALO)
    dens = jnp.concatenate(
        [
            jnp.where(right & straight, side(0) + side(1), 0.0),
            jnp.where(right & (seam | top | bottom), side(2), 0.0),
        ],
        axis=1,
    )
    half = lax.dot_general(
        basis_rows[...], split(dens, 1), (((1,), (1,)), ((), ())), preferred_element_type=F32
    )
    high = half.astype(jnp.bfloat16)
    low = (half - high.astype(F32)).astype(jnp.bfloat16)
    both = jnp.dot(jnp.concatenate([high, low], axis=0), basis_cols[:INNER], preferred_element_type=F32)
    rest = jnp.dot(high, basis_cols[INNER:], preferred_element_type=F32)
    wide = wide_in[...] + (both[:MODES] + (both[MODES:] + rest))
    lane = lanes()
    which = lax.div(lane, MODES)
    flat = wide[:SUB]
    for j in range(1, MODES // SUB):
        flat = jnp.where(which == j, wide[SUB * j : SUB * (j + 1)], flat)
    mark = jnp.broadcast_to(block[:1, :].astype(F32), (SUB, TILE))
    row = lax.broadcasted_iota(jnp.int32, (SUB, TILE), 0)
    moved = [flat] + [pltpu.roll(flat, r, 0) for r in range(1, SUB)] + [flat]
    lines = [flat] + [
        jnp.where(row < r - 1, moved[r - 1], jnp.where(row == r - 1, mark, moved[r])) for r in range(1, SUB + 1)
    ]
    cycle = SUB * (SUB + 1)
    chunk = min(4, coef.shape[0] // cycle)

    def spread(d, carry):
        for e in range(chunk):
            for r, line in enumerate(lines):
                coef[pl.ds(pl.multiple_of((d * chunk + e) * cycle + SUB * r, SUB), SUB), :] = line
        return carry

    lax.fori_loop(0, coef.shape[0] // cycle // chunk, spread, 0)


def join_kernel(v0, v1, vel_ends, strips, vel, turned):
    rows = vel.shape[1]
    span = rows // SUB
    middle = jnp.zeros((TILE - 2 * HALO, TILE), F32)
    side = beside()
    for k, v in enumerate((v0, v1)):
        for part in range(PARTS):
            base = STRIP * (2 * part + 1 - k)
            first, last = (strips[base + at : base + at + HALO, :] for at in OUTER)
            at = TILE * (2 * part + k)
            turned[at : at + TILE, :] = jnp.concatenate([first, middle, last], axis=0).T
        for row in range(0, rows, SUB):
            value = v[pl.ds(SUB * (row % span) + row // span, SUB, stride=SUB), :]
            if row in (0, rows - SUB):
                at = HALO * (2 * k + (row > 0))
                value = jnp.where(ends(row > 0), vel_ends[at : at + HALO, :], value)
            part, lane = right_part(row)
            at = TILE * (2 * part + k) + lane
            vel[k, row : row + SUB, :] = jnp.where(side, turned[at : at + SUB, :], value)


def bases():
    places = np.arange(TILE) + 0.5
    basis = np.cos(math.pi * places[:, None] * np.arange(MODES)[None, :] / TILE)
    groups = MODES // SUB
    order = np.arange(MODES).reshape(SUB, groups).T.reshape(-1)
    rows = basis[:, order] / TILE
    cols = np.tile(basis, (1, groups))
    placed = np.zeros((2 * TILE, MODES))
    for row in range(0, 2 * TILE, SUB):
        part, lane = right_part(row)
        at = lane + (TILE if part == 2 else 0)
        placed[at : at + SUB] = rows[row % TILE : row % TILE + SUB]
    outer = np.concatenate([cols[:HALO], cols[TILE - HALO :]])
    return jnp.asarray(rows.T, F32), jnp.asarray(cols, F32), split_constant(placed.T, 1), split_constant(outer, 0)[: 2 * INNER]


def pick_kernel(owners, every, out):
    mine = out.shape[1]
    own = lax.axis_index("own")
    wanted = [owners[pl.ds(own, 1), k : k + 1].astype(F32) for k in range(mine)]
    lines = SUB + 1
    devices = every.shape[0] // lines
    chunk = min(4, devices // SUB)

    def body(d, sums):
        sums = list(sums)
        for e in range(chunk):
            base = (d * chunk + e) * SUB * lines
            mark = every[pl.ds(base + SUB, SUB, stride=lines), :]
            hits = [mark == wanted[k] for k in range(mine)]
            for r in range(SUB):
                part = every[pl.ds(base + r, SUB, stride=lines), :]
                for k in range(mine):
                    sums[SUB * k + r] += jnp.where(hits[k], part, 0.0)
        return tuple(sums)

    start = (jnp.zeros((SUB, TILE), F32),) * (mine * SUB)
    sums = lax.fori_loop(0, devices // SUB // chunk, body, start)
    for k in range(mine):
        for r in range(SUB):
            total = jnp.sum(sums[SUB * k + r], axis=0, keepdims=True)
            out[0, k : k + 1, TILE * r : TILE * (r + 1)] = total


def local(viscosity, friction, driving, observed, ice_mask, tile_block, owner_list):
    rows, cols = viscosity.shape
    assert (rows, cols) == (2 * TILE, TILE)
    inputs = (viscosity, friction, driving, ice_mask, observed)
    far = [pltpu.with_memory_space_constraint(x, pltpu.HBM) for x in inputs]
    basis_p, basis_q, basis_rows, basis_cols = bases()
    to_b, to_a = call(
        ends_kernel,
        "ends",
        (vmem(EDGE, cols), vmem(EDGE, cols)),
        [
            vmem(2, 2, HALO, cols),
            vmem(2, 2, 2, HALO, cols),
            pltpu.VMEM((2, HALO, cols), jnp.int32),
            pltpu.SemaphoreType.DMA((2, 5)),
        ],
        10**6,
        *far,
    )
    row_b = swap(to_b, 0, 1)
    row_a = swap(to_a, 0, 0)
    every, edge = call(
        load_kernel,
        "load",
        (vmem(ARRAYS * rows, cols), vmem(2 * PARTS * TILE, TILE)),
        [pltpu.VMEM((rows, cols), jnp.int32), pltpu.SemaphoreType.DMA((ARRAYS,))],
        8 * 10**6,
        *far,
        to_b,
    )
    to_b, to_a, turned = call(
        columns_kernel,
        "columns",
        (vmem(SENT, TILE), vmem(SENT, TILE), vmem(SLOT, TILE)),
        [],
        10**5,
        row_b,
        row_a,
        edge,
    )
    col_b = swap(to_b, 1, 1)
    col_a = swap(to_a, 1, 0)
    vel_ends, wide, sides, seams, *vel_inner = call(
        adjoint_kernel,
        "adjoint",
        (
            vmem(4 * HALO, cols),
            vmem(MODES, TILE),
            vmem(PARTS * ARRAYS * STRIP, TILE),
            vmem(PARTS * SUB, TILE),
            vmem(rows, cols),
            vmem(rows, cols),
        ),
        [vmem(ARRAYS * STRIP, cols), vmem(2 * STRIP, cols), vmem(rows + STRIP, cols), vmem(TILE, cols)]
        + [vmem(STRIP, cols)] * STRIP_FIELDS
        + [vmem(rows, cols)] * FIELDS,
        8 * 10**6,
        row_b,
        row_a,
        every,
        basis_p,
        basis_q,
        edge,
        turned,
    )
    devices = lax.axis_size(ROW_AXES + COL_AXES)
    _, strips, coef = call(
        left_right_kernel,
        "left_right",
        (
            vmem(PARTS * ARRAYS * STRIP, TILE),
            vmem(PARTS * 2 * STRIP, TILE),
            vmem(devices * (SUB + 1), TILE),
        ),
        [vmem(PARTS * STRIP, TILE)] * (STRIP_FIELDS + 1),
        4 * 10**6,
        sides,
        seams,
        col_b,
        col_a,
        wide,
        tile_block,
        basis_rows,
        basis_cols,
        aliases={0: 0},
    )
    coef = coef.reshape(devices, 1, (SUB + 1) * TILE)
    parts = lax.all_to_all(coef, ROW_AXES + COL_AXES, 0, 0, tiled=True)
    state = call(
        join_kernel,
        "join",
        jax.ShapeDtypeStruct((2, rows, cols), F32),
        [vmem(2 * PARTS * TILE, TILE)],
        4 * 10**6,
        *vel_inner,
        vel_ends,
        strips,
    )
    owners = owner_list.reshape(lax.axis_size("own"), -1)
    picked = call(
        pick_kernel,
        "pick",
        jax.ShapeDtypeStruct((1, owners.shape[1], MODES * MODES), F32),
        [],
        10**5,
        owners,
        parts.reshape(-1, TILE),
    )
    return (state, picked)


def solution(mesh):
    return jax.shard_map(
        local,
        mesh=mesh,
        in_specs=(
            P(("row", "own"), "col"),
            P(("row", "own"), "col"),
            P(None, ("row", "own"), "col"),
            P(None, ("row", "own"), "col"),
            P(("row", "own"), "col"),
            P(("row", "own"), "col"),
            P(),
        ),
        out_specs=(P(None, ("row", "own"), "col"), P("own", None, None)),
        check_vma=False,
    )
```

```python
import math

import jax
import jax.numpy as jnp
import numpy as np
from jax import lax
from jax.experimental import pallas as pl
from jax.experimental.pallas import tpu as pltpu
from jax.sharding import PartitionSpec as P

TILE = 128
MODES = 32
SWEEPS = 3
SUB = 8
HALO = 8
INNER = 2 * HALO
STRIP = 40
LEAD = HALO - 1
KEPT = 12
OUTER = (LEAD, STRIP - 2 * HALO)
NEAR, FAR = 7, 6
ARRAYS = 7
VISC, FRIC, DRIV, MASK, OBS = 0, 1, 2, 4, 5
EDGE = ARRAYS * HALO
SLOT = 2 * INNER
PER = TILE // SLOT
GROUPS = 5
SENT = 2 * GROUPS * HALO + HALO
PARTS = 3
UPPER, LOWER = 32, 64
ROW_AXES = ("row", "own")
COL_AXES = ("col",)
F32 = jnp.float32
LIMIT = 40 * 1024 * 1024


def swap(x, axis, first):
    sizes = lax.axis_size(ROW_AXES), lax.axis_size(COL_AXES)
    owners = lax.axis_size("own")

    def device(i, j):
        return (i // owners * sizes[1] + j) * owners + i % owners

    pairs = []
    for i in range(sizes[0]):
        for j in range(sizes[1]):
            place = [i, j]
            if first and place[axis] in (0, sizes[axis] - 1):
                place[1 - axis] ^= 1
            else:
                place[axis] = ((place[axis] + first) ^ 1) - first
            pairs.append((device(i, j), device(*place)))
    return lax.ppermute(x, ("row", "col", "own"), pairs)


def position(axes):
    index, size = 0, 1
    for axis in axes:
        index = index * lax.axis_size(axis) + lax.axis_index(axis)
        size *= lax.axis_size(axis)
    assert size % 2 == 0
    return lax.rem(index, 2) == 0, (index == 0) | (index == size - 1)


def is_even(axes):
    return position(axes)[0]


def lanes():
    return lax.broadcasted_iota(jnp.int32, (SUB, TILE), 1)


def call(kernel, name, outs, scratch, cost, *args, aliases={}):
    return pl.pallas_call(
        kernel,
        out_shape=outs,
        scratch_shapes=scratch,
        input_output_aliases=aliases,
        compiler_params=pltpu.CompilerParams(vmem_limit_bytes=LIMIT),
        cost_estimate=pl.CostEstimate(flops=cost, bytes_accessed=cost, transcendentals=0),
        name=name,
    )(*args)


def vmem(*shape):
    return pltpu.VMEM(shape, F32)


FIELDS = 14
STRIP_FIELDS = 24


class Domain:
    def __init__(self, refs, base, span, source, seam=None):
        self.refs, self.base, self.span, self.source, self.seam = refs, base, span, source, seam

    def at(self, j):
        return pl.ds(self.base + SUB * j, SUB)

    def prepare(self, flipped):
        n2, n4, c, i = self.refs[:4]
        visc = [self.source(VISC, j) for j in range(self.span)]
        for j in range(self.span):
            at = self.at(j)
            before = visc[j - 1] if j else pltpu.roll(visc[-1], 1, 0)
            if self.seam and not j:
                row = lax.broadcasted_iota(jnp.int32, (SUB, TILE), 0)
                before = jnp.where(row == SUB // 2, self.seam(), before)
            pair = visc[j] + before
            fric = self.source(FRIC, j)
            diag = 1.25 * (pair + pltpu.roll(pair, 1, 1)) + fric
            on = self.source(MASK, j) > 0.0
            inv = jnp.where(on, 0.5 / jnp.where(on, diag, 1.0), 0.0)
            half = 0.5 * visc[j]
            n2[at, :] = half
            n4[at, :] = 0.5 * half
            c[at, :] = 1.0 - fric * inv
            i[at, :] = inv
            for k in range(2):
                self.start(k, at, inv * self.source(DRIV + (1 - k if flipped else k), j))

    def start(self, k, at, value):
        self.refs[4 + k][at, :] = value
        self.write(k, at, value + value)

    def write(self, k, at, value):
        self.refs[6 + k][at, :] = value
        self.refs[8 + k][at, :] = pltpu.roll(value, TILE - 1, 1)

    def retarget(self, flipped, velocity=None):
        i = self.refs[3]
        velocity = velocity or self.refs[6:8]
        for j in range(self.span):
            at = self.at(j)
            for k in range(2):
                seen = self.source(OBS + (1 - k if flipped else k), j)
                self.start(k, at, i[at, :] * (velocity[k][at, :] - seen))

    def differences(self):
        n2, n4 = self.refs[:2]
        fields = self.refs[6:10]
        parts = self.refs[10:14]

        def corners(j, here, below):
            w0, w1, r0, r1 = here
            v0, v1, s0, s1 = below
            a1, a2 = s0 - w0, v0 - r0
            e1, e2 = s1 - w1, v1 - r1
            x, y = a1 + a2, e1 - e2
            q = (a1 - a2) + (e1 + e2)
            both = x + y
            at = self.at(j)
            half = n2[at, :]
            return half * (both + x), n4[at, :] * q, half * (both + y)

        def load(j):
            at = self.at(j)
            return [field[at, :] for field in fields]

        top = load(0)
        last = corners(self.span - 1, load(self.span - 1), [pltpu.roll(v, SUB - 1, 0) for v in top])
        up = [pltpu.roll(v, 1, 0) for v in last]
        here = top
        for j in range(self.span):
            at = self.at(j)
            if j < self.span - 1:
                below = load(j + 1)
                p, q, r = corners(j, here, below)
                here = below
            else:
                p, q, r = last
            g, t = up[0] - p, up[1] + q
            gq, tr = up[1] - q, up[2] + r
            parts[0][at, :] = g - t
            parts[1][at, :] = gq - tr
            parts[2][at, :] = pltpu.roll(g + t, 1, 1)
            parts[3][at, :] = pltpu.roll(gq + tr, 1, 1)
            up = (p, q, r)

    def update(self):
        c, i, b0, b1, w0, w1 = self.refs[2:8]
        parts = self.refs[10:14]
        for j in range(self.span):
            at = self.at(j)
            cv, iv = c[at, :], i[at, :]
            for k, (b, w) in enumerate(((b0, w0), (b1, w1))):
                value = (cv * w[at, :] + b[at, :]) - iv * (parts[k][at, :] + parts[k + 2][at, :])
                self.write(k, at, value)


class Strips(Domain):
    def prepare(self, flipped):
        super().prepare(flipped)
        for j in range(self.span):
            at = self.at(j)
            for now, later in zip(self.refs[2:4], self.refs[10:12]):
                later[at, :] = pltpu.roll(now[at, :], TILE - 1, 1)
        for now, before in zip(self.refs[:2], self.refs[14:16]):
            before[self.at(0), :] = pltpu.roll(now[self.at(self.span - 1), :], 1, 0)

    def start(self, k, at, value):
        b, w, r, later = (self.refs[n + k] for n in (4, 6, 8, 12))
        b[at, :] = value
        w[at, :] = value + value
        turned = pltpu.roll(value, TILE - 1, 1)
        later[at, :] = turned
        r[at, :] = turned + turned

    def differences(self):
        fields = self.refs[6:10]
        kept, turned, kept_next, turned_next = (self.refs[16 + 2 * k : 18 + 2 * k] for k in range(4))

        def corners(halves, quarters, j, here, below):
            w0, w1, r0, r1 = here
            v0, v1, s0, s1 = below
            a1, a2 = s0 - w0, v0 - r0
            e1, e2 = s1 - w1, v1 - r1
            x, y = a1 + a2, e1 - e2
            q = (a1 - a2) + (e1 + e2)
            both = x + y
            at = self.at(j)
            half = halves[at, :]
            return half * (both + x), quarters[at, :] * q, half * (both + y)

        def load(j):
            at = self.at(j)
            return [field[at, :] for field in fields]

        top, end = load(0), load(self.span - 1)
        up = corners(*self.refs[14:16], 0, [pltpu.roll(v, 1, 0) for v in end], top)
        here = top
        for j in range(self.span):
            at = self.at(j)
            below = load(j + 1) if j < self.span - 1 else [pltpu.roll(v, SUB - 1, 0) for v in top]
            p, q, r = corners(*self.refs[:2], j, here, below)
            g, t = up[0] - p, up[1] + q
            gq, tr = up[1] - q, up[2] + r
            for k, (stay, move) in enumerate(((g - t, g + t), (gq - tr, gq + tr))):
                kept[k][at, :] = stay
                turned_next[k][at, :] = move
                turned[k][at, :] = pltpu.roll(move, 1, 1)
                kept_next[k][at, :] = pltpu.roll(stay, TILE - 1, 1)
            up, here = (p, q, r), below

    def update(self):
        for first, offset, parts in ((2, 6, (16, 18)), (10, 8, (20, 22))):
            c, i, *b = self.refs[first : first + 4]
            for j in range(self.span):
                at = self.at(j)
                cv, iv = c[at, :], i[at, :]
                for k in range(2):
                    w = self.refs[offset + k]
                    change = self.refs[parts[0] + k][at, :] + self.refs[parts[1] + k][at, :]
                    w[at, :] = (cv * w[at, :] + b[k][at, :]) - iv * change


def run(domains, written_out=False):
    def body(_, carry):
        for domain in domains:
            domain.differences()
        for domain in domains:
            domain.update()
        return carry

    if written_out:
        for k in range(SWEEPS):
            body(k, 0)
    else:
        lax.fori_loop(0, SWEEPS, body, 0)


def ends_kernel(visc, fric, driv, mask, obs, to_b, to_a, one, two, flags, sems):
    rows = visc.shape[0]
    copies = []
    for e, first in enumerate((0, rows - HALO)):
        at = pl.ds(first, HALO)
        pieces = [
            (visc.at[at], one.at[e, 0]),
            (fric.at[at], one.at[e, 1]),
            (driv.at[:, at], two.at[e, 0]),
            (mask.at[at], flags.at[e]),
            (obs.at[:, at], two.at[e, 1]),
        ]
        for n, (source, place) in enumerate(pieces):
            copies.append(pltpu.make_async_copy(source, place, sems.at[e, n]))
    for copy in copies:
        copy.start()
    for copy in copies:
        copy.wait()
    even, at_end = position(ROW_AXES)

    def edge(e):
        return [one[e, 0], one[e, 1], two[e, 0, 0], two[e, 0, 1], flags[e].astype(F32), two[e, 1, 0], two[e, 1, 1]]

    for a, (head, tail) in enumerate(zip(edge(0), edge(1))):
        at = slice(HALO * a, HALO * (a + 1))
        to_a[at, :] = jnp.where(even, tail, head)
        to_b[at, :] = jnp.where(at_end, 0.0, jnp.where(even, head, tail))


def field_of(visc, fric, driv, mask, obs):
    def field(a, at):
        if a == MASK:
            return mask[at, :].astype(F32)
        if a >= OBS:
            return obs[a - OBS, at, :]
        if a >= DRIV:
            return driv[a - DRIV, at, :]
        return (visc, fric)[a][at, :]

    return field


def first_row(part, lane):
    if part < 2:
        return TILE * part + lane
    if lane < INNER + HALO:
        return TILE + lane
    if lane >= TILE - INNER - HALO:
        return lane
    if UPPER + HALO <= lane < UPPER + SLOT:
        return lane - UPPER - HALO
    if LOWER <= lane < LOWER + INNER + HALO:
        return 2 * TILE - INNER - HALO + lane - LOWER
    return None


def right_part(row):
    seam = TILE - HALO <= row < TILE + HALO
    part = 2 if seam or row == 0 or row == 2 * TILE - HALO else row // TILE
    return part, [lane for lane in range(0, TILE, SUB) if first_row(part, lane) == row][-1]


def slot(part, a):
    return TILE * (2 * part + a // PER) + SLOT * (a % PER)


def interior_kernel(visc, fric, driv, mask, obs, edge, n2, n4, c, i, v0, v1, *refs):
    span = visc.shape[0] // SUB
    field = field_of(visc, fric, driv, mask, obs)
    lane = lanes()
    for part in range(PARTS):
        for m in range(-(-ARRAYS // PER)):
            strips = []
            for at in range(0, TILE, SUB):
                row = first_row(part, at)
                packed = jnp.zeros((SUB, TILE), F32)
                if row is not None:
                    for k in range(min(PER, ARRAYS - PER * m)):
                        value = field(PER * m + k, slice(row, row + SUB))
                        moved = pltpu.roll(value, (SLOT * k + INNER) % TILE, 1)
                        packed = jnp.where(lax.div(lane, SLOT) == k, moved, packed)
                strips.append(packed)
            base = TILE * (2 * part + m)
            edge[base : base + TILE, :] = jnp.concatenate(strips, axis=0).T
    refs = (n2, n4, c, i, *refs[:2], v0, v1, *refs[2:])
    domain = Domain(refs, 0, span, lambda a, j: field(a, pl.ds(j, SUB, stride=span)))
    domain.prepare(False)
    run([domain])


def columns_kernel(row_b, row_a, edge, to_b, to_a, turned):
    even = is_even(ROW_AXES)
    above = jnp.where(even, row_b[...], row_a[...])
    below = jnp.where(even, row_a[...], row_b[...])
    halo = jnp.concatenate([above, below, jnp.zeros((TILE - 2 * EDGE, TILE), F32)], axis=0).T
    turned[:INNER, :] = halo[TILE - INNER :]
    turned[INNER:, :] = halo[:INNER]
    even, at_end = position(COL_AXES)
    row = lax.broadcasted_iota(jnp.int32, (SUB, TILE), 0)

    def put(out, right, left):
        right = pltpu.roll(right, LEAD, 0)
        to_a[out : out + HALO, :] = jnp.where(even, right, left)
        to_b[out : out + HALO, :] = jnp.where(at_end, 0.0, jnp.where(even, left, right))

    for part in range(2):
        right, left = [], []
        for a in range(ARRAYS):
            at = slot(part, a) + INNER
            right.append(edge[at - HALO : at, :])
            left.append(edge[at : at + HALO, :])
        for k in range(2):
            seen_r, seen_l = right[OBS + k], left[OBS + k]
            g = 1 + 2 * k
            right[g] = jnp.where(row < 2, pltpu.roll(seen_r, 2, 0), right[g])
            right[g + 1] = jnp.where(row < 2, pltpu.roll(seen_r, 4, 0), right[g + 1])
            left[g] = jnp.where(row >= 6, pltpu.roll(seen_l, 6, 0), left[g])
            left[g + 1] = jnp.where(row >= 6, pltpu.roll(seen_l, 4, 0), left[g + 1])
        for g in range(GROUPS):
            put(HALO * (GROUPS * part + g), right[g], left[g])
    put(2 * GROUPS * HALO, halo[TILE - HALO :], halo[:HALO])


def strided(stack, base):
    span = STRIP // SUB
    return lambda a, j: stack[pl.ds(base + STRIP * a + j, SUB, stride=span), :]


def fill(stack, base, first, last):
    row = lax.broadcasted_iota(jnp.int32, (SUB, TILE), 0)
    one, two = (pltpu.roll(value, LEAD, 0) for value in first)
    mixed = [jnp.where(row == LEAD, two, one), jnp.where(row < SUB // 2, two, last[0])]
    for k, value in enumerate((one, *mixed, last[1])):
        stack[base + SUB * k : base + SUB * (k + 1), :] = value


def velocity(domain, plain, base):
    for j in range(domain.span):
        at = domain.at(j)
        for k in range(2):
            plain[pl.ds(base + STRIP * k + j, SUB, stride=domain.span), :] = domain.refs[6 + k][at, :]


def density(domain, plain, base, out, place):
    w0, w1 = domain.refs[6:8]
    for j in range(domain.span):
        at = domain.at(j)
        v0, v1 = (plain[pl.ds(base + STRIP * k + j, SUB, stride=domain.span), :] for k in range(2))
        value = -domain.source(FRIC, j) * (w0[at, :] * v0 + w1[at, :] * v1)
        out[pl.ds(place + j, SUB, stride=domain.span), :] = value


def beside():
    lane = lanes()
    return (lane < NEAR) | (lane >= TILE - FAR)


def ends(second):
    row = lax.broadcasted_iota(jnp.int32, (SUB, TILE), 0)
    return row >= SUB - FAR if second else row < NEAR


def adjoint_kernel(
    row_b, row_a, visc, fric, driv, mask, obs, n2, n4, c, i, v0, v1, basis_p, basis_q, edge, turned,
    vel, wide, sides, seams,
    stack, plain, dens, total, *refs,
):
    rows = visc.shape[0]
    span = rows // SUB
    even = is_even(ROW_AXES)
    field = field_of(visc, fric, driv, mask, obs)
    for a in range(ARRAYS):
        at = slice(HALO * a, HALO * (a + 1))
        got_a, got_b = row_a[at, :], row_b[at, :]
        base = STRIP * a
        first = [field(a, slice(at, at + SUB)) for at in (0, SUB)]
        last = [field(a, slice(at, at + SUB)) for at in (rows - 2 * SUB, rows - SUB)]
        fill(stack, base, first, last)
        stack[base : base + LEAD, :] = jnp.where(even, got_b, got_a)[HALO - LEAD :]
        stack[base + STRIP - HALO : base + STRIP, :] = jnp.where(even, got_a, got_b)
    strips = Strips(refs[:STRIP_FIELDS], 0, STRIP // SUB, strided(stack, 0), lambda: visc[rows - KEPT - 1 : rows - KEPT, :])
    strips.prepare(False)
    run([strips])
    velocity(strips, plain, 0)
    for k in range(2):
        for e in range(2):
            out = HALO * (2 * k + e)
            vel[out : out + HALO, :] = plain[STRIP * k + OUTER[e] : STRIP * k + OUTER[e] + HALO, :]
    interior = Domain(
        (n2, n4, c, i, *refs[STRIP_FIELDS:]), 0, span, lambda a, j: field(a, pl.ds(j, SUB, stride=span))
    )
    strips.retarget(False)
    interior.retarget(False, (v0, v1))
    run([interior, strips])
    w0, w1 = interior.refs[6:8]
    for j in range(span):
        at = interior.at(j)
        value = -interior.source(FRIC, j) * (w0[at, :] * v0[at, :] + w1[at, :] * v1[at, :])
        dens[pl.ds(j, SUB, stride=span), :] = value
    density(strips, plain, 0, dens, rows)

    side = beside()
    for s in range(0, TILE, SUB):
        summed = jnp.zeros((SUB, TILE), F32)
        for row in range(s, rows, TILE):
            value = dens[row : row + SUB, :]
            if row in (0, rows - SUB):
                at = rows + OUTER[row > 0]
                value = jnp.where(ends(row > 0), dens[at : at + SUB, :], value)
            summed += value
        total[s : s + SUB, :] = jnp.where(side, 0.0, summed)
    exact = dict(precision=lax.Precision.HIGHEST, preferred_element_type=F32)
    half = jnp.dot(basis_p[...], total[...], **exact)
    wide[...] = jnp.dot(half, basis_q[...], **exact)

    corner = corners()
    for part in range(PARTS):
        for a in range(ARRAYS):
            columns = []
            for r in range(0, SLOT, SUB):
                value = edge[slot(part, a) + r : slot(part, a) + r + SUB, :]
                if part == 2:
                    moved = pltpu.roll(turned[r : r + SUB, :], (UPPER - HALO * a) % TILE, 1)
                    value = jnp.where(corner, moved, value)
                columns.append(value)
            fill(sides, strip(part, a), columns[2:], columns[:2])
            if a == VISC:
                seams[SUB * part : SUB * (part + 1), :] = columns[0]


def strip(part, a):
    return STRIP * (ARRAYS * part + a)


def corners():
    lane = lanes()
    above = (lane >= UPPER) & (lane < UPPER + HALO)
    return above | ((lane >= LOWER + INNER + HALO) & (lane < LOWER + SLOT))


def split(x, axis):
    high = x.astype(jnp.bfloat16)
    low = (x - high.astype(F32)).astype(jnp.bfloat16)
    return jnp.concatenate([high, high, low], axis=axis)


def split_constant(x, axis):
    x = np.asarray(x, np.float32)
    high = np.asarray(x, jnp.bfloat16)
    low = np.asarray(x - np.asarray(high, np.float32), jnp.bfloat16)
    return jnp.asarray(np.concatenate([high, low, high], axis=axis))


def left_right_kernel(
    _, seams, col_b, col_a, wide_in, block, basis_rows, basis_cols,
    stack, strips, coef,
    plain, *refs,
):
    even = is_even(COL_AXES)
    lane = lanes()
    row = lax.broadcasted_iota(jnp.int32, (SUB, TILE), 0)
    upper = (lane >= UPPER + HALO) & (lane < UPPER + SLOT)
    lower = (lane >= LOWER) & (lane < LOWER + INNER + HALO)
    seam_t0 = lane >= TILE - INNER - HALO
    seam_t1 = lane < INNER + HALO
    corner = corners()
    for from_left in (True, False):
        groups = []
        for g in range(2 * GROUPS + 1):
            got_a, got_b = col_a[HALO * g : HALO * (g + 1), :], col_b[HALO * g : HALO * (g + 1), :]
            groups.append(jnp.where(even, got_b, got_a) if from_left else jnp.where(even, got_a, got_b))
        tiles = []
        for part in range(2):
            tile = groups[GROUPS * part : GROUPS * (part + 1)]
            for k in range(2):
                g, h = tile[1 + 2 * k], tile[2 + 2 * k]
                if from_left:
                    tile.append(jnp.where(row >= 5, pltpu.roll(g, 6, 0), pltpu.roll(h, 4, 0)))
                else:
                    tile.append(jnp.where(row < 2, pltpu.roll(g, 2, 0), pltpu.roll(h, 4, 0)))
            tiles.append(tile)
        for a in range(ARRAYS):
            t0, t1 = tiles[0][a], tiles[1][a]
            third = jnp.where(corner, pltpu.roll(groups[-1], (UPPER - HALO * a) % TILE, 1), 0.0)
            third = jnp.where(upper, pltpu.roll(t0, UPPER + HALO, 1), third)
            third = jnp.where(lower, pltpu.roll(t1, LOWER + INNER + HALO, 1), third)
            third = jnp.where(seam_t0, t0, jnp.where(seam_t1, t1, third))
            for part, value in enumerate((t0, t1, third)):
                base = strip(part, a)
                if from_left:
                    stack[base : base + LEAD, :] = value[:LEAD]
                else:
                    stack[base + STRIP - HALO : base + STRIP, :] = value
    last = INNER - KEPT - 1
    before = [lambda at=SUB * part + last: seams[at : at + 1, :] for part in range(PARTS)]
    domains = [
        Strips(refs, STRIP * part, STRIP // SUB, strided(stack, strip(part, 0)), seam)
        for part, seam in enumerate(before)
    ]
    for domain in domains:
        domain.prepare(True)
    run(domains, True)
    for part, domain in enumerate(domains):
        velocity(domain, strips, 2 * STRIP * part)
        domain.retarget(True)
    run(domains, True)
    for part, domain in enumerate(domains):
        density(domain, strips, 2 * STRIP * part, plain, STRIP * part)

    def side(part):
        base = STRIP * part
        return jnp.concatenate(
            [plain[base + at : base + at + HALO, :] for at in OUTER], axis=0
        )

    lane = lax.broadcasted_iota(jnp.int32, (2 * HALO, TILE), 1)
    row = lax.broadcasted_iota(jnp.int32, (2 * HALO, TILE), 0)
    right = (row < NEAR) | (row >= 2 * HALO - FAR)
    straight = (lane >= HALO) & (lane < TILE - HALO)
    seam = (lane < HALO) | (lane >= TILE - HALO)
    top = (lane >= UPPER + HALO) & (lane < UPPER + 2 * HALO)
    bottom = (lane >= LOWER + INNER) & (lane < LOWER + INNER + HALO)
    dens = jnp.concatenate(
        [
            jnp.where(right & straight, side(0) + side(1), 0.0),
            jnp.where(right & (seam | top | bottom), side(2), 0.0),
        ],
        axis=1,
    )
    half = lax.dot_general(
        basis_rows[...], split(dens, 1), (((1,), (1,)), ((), ())), preferred_element_type=F32
    )
    high = half.astype(jnp.bfloat16)
    low = (half - high.astype(F32)).astype(jnp.bfloat16)
    both = jnp.dot(jnp.concatenate([high, low], axis=0), basis_cols[:INNER], preferred_element_type=F32)
    rest = jnp.dot(high, basis_cols[INNER:], preferred_element_type=F32)
    wide = wide_in[...] + (both[:MODES] + (both[MODES:] + rest))
    lane = lanes()
    which = lax.div(lane, MODES)
    flat = wide[:SUB]
    for j in range(1, MODES // SUB):
        flat = jnp.where(which == j, wide[SUB * j : SUB * (j + 1)], flat)
    mark = jnp.broadcast_to(block[:1, :].astype(F32), (SUB, TILE))
    row = lax.broadcasted_iota(jnp.int32, (SUB, TILE), 0)
    moved = [flat] + [pltpu.roll(flat, r, 0) for r in range(1, SUB)] + [flat]
    lines = [flat] + [
        jnp.where(row < r - 1, moved[r - 1], jnp.where(row == r - 1, mark, moved[r])) for r in range(1, SUB + 1)
    ]
    cycle = SUB * (SUB + 1)
    chunk = min(4, coef.shape[0] // cycle)

    def spread(d, carry):
        for e in range(chunk):
            for r, line in enumerate(lines):
                coef[pl.ds(pl.multiple_of((d * chunk + e) * cycle + SUB * r, SUB), SUB), :] = line
        return carry

    lax.fori_loop(0, coef.shape[0] // cycle // chunk, spread, 0)


def join_kernel(v0, v1, vel_ends, strips, vel, turned):
    rows = vel.shape[1]
    span = rows // SUB
    middle = jnp.zeros((TILE - 2 * HALO, TILE), F32)
    side = beside()
    for k, v in enumerate((v0, v1)):
        for part in range(PARTS):
            base = STRIP * (2 * part + 1 - k)
            first, last = (strips[base + at : base + at + HALO, :] for at in OUTER)
            at = TILE * (2 * part + k)
            turned[at : at + TILE, :] = jnp.concatenate([first, middle, last], axis=0).T
        for row in range(0, rows, SUB):
            value = v[pl.ds(SUB * (row % span) + row // span, SUB, stride=SUB), :]
            if row in (0, rows - SUB):
                at = HALO * (2 * k + (row > 0))
                value = jnp.where(ends(row > 0), vel_ends[at : at + HALO, :], value)
            part, lane = right_part(row)
            at = TILE * (2 * part + k) + lane
            vel[k, row : row + SUB, :] = jnp.where(side, turned[at : at + SUB, :], value)


def bases():
    places = np.arange(TILE) + 0.5
    basis = np.cos(math.pi * places[:, None] * np.arange(MODES)[None, :] / TILE)
    groups = MODES // SUB
    order = np.arange(MODES).reshape(SUB, groups).T.reshape(-1)
    rows = basis[:, order] / TILE
    cols = np.tile(basis, (1, groups))
    placed = np.zeros((2 * TILE, MODES))
    for row in range(0, 2 * TILE, SUB):
        part, lane = right_part(row)
        at = lane + (TILE if part == 2 else 0)
        placed[at : at + SUB] = rows[row % TILE : row % TILE + SUB]
    outer = np.concatenate([cols[:HALO], cols[TILE - HALO :]])
    return jnp.asarray(rows.T, F32), jnp.asarray(cols, F32), split_constant(placed.T, 1), split_constant(outer, 0)[: 2 * INNER]


def gather_kernel(owners, every, kept, given):
    mine = owners.shape[1]
    own = lax.axis_index("own")
    wanted = [
        owners[pl.ds(owner, 1), k : k + 1].astype(F32) for owner in (own, own ^ 1) for k in range(mine)
    ]
    cycle = SUB * (SUB + 1)

    def body(d, sums):
        block = every[pl.ds(pl.multiple_of(d * cycle, SUB), cycle), :]
        totals = [None] * len(wanted)
        for e in range(SUB):
            part = block[(SUB + 1) * e : (SUB + 1) * e + SUB]
            mark = block[(SUB + 1) * e + SUB : (SUB + 1) * (e + 1)]
            for k, want in enumerate(wanted):
                value = jnp.where(jnp.broadcast_to(mark == want, (SUB, TILE)), part, 0.0)
                totals[k] = value if e == 0 else totals[k] + value
        return tuple(x + y for x, y in zip(sums, totals))

    sums = (jnp.zeros((SUB, TILE), F32),) * len(wanted)
    count = every.shape[0] // cycle
    if count <= 4:
        for d in range(count):
            sums = body(d, sums)
    else:
        sums = lax.fori_loop(0, count, body, sums)
    for k in range(mine):
        kept[SUB * k : SUB * (k + 1), :] = sums[k]
        given[SUB * k : SUB * (k + 1), :] = sums[mine + k]


def pick_kernel(kept, got, out):
    for k in range(out.shape[1]):
        total = kept[SUB * k : SUB * (k + 1), :] + got[SUB * k : SUB * (k + 1), :]
        for r in range(SUB):
            out[0, k : k + 1, TILE * r : TILE * (r + 1)] = total[r : r + 1]


def local(viscosity, friction, driving, observed, ice_mask, tile_block, owner_list):
    rows, cols = viscosity.shape
    assert (rows, cols) == (2 * TILE, TILE)
    inputs = (viscosity, friction, driving, ice_mask, observed)
    near = [pltpu.with_memory_space_constraint(x, pltpu.VMEM) for x in inputs]
    basis_p, basis_q, basis_rows, basis_cols = bases()
    to_b, to_a = call(
        ends_kernel,
        "ends",
        (vmem(EDGE, cols), vmem(EDGE, cols)),
        [
            vmem(2, 2, HALO, cols),
            vmem(2, 2, 2, HALO, cols),
            pltpu.VMEM((2, HALO, cols), jnp.int32),
            pltpu.SemaphoreType.DMA((2, 5)),
        ],
        10**6,
        *(pltpu.with_memory_space_constraint(x, pltpu.HBM) for x in inputs),
    )
    row_b = swap(to_b, 0, 1)
    row_a = swap(to_a, 0, 0)
    edge, *forward = call(
        interior_kernel,
        "interior",
        (vmem(2 * PARTS * TILE, TILE),) + (vmem(rows, cols),) * 6,
        [vmem(rows, cols)] * (FIELDS - 6),
        8 * 10**6,
        *near,
    )
    to_b, to_a, turned = call(
        columns_kernel,
        "columns",
        (vmem(SENT, TILE), vmem(SENT, TILE), vmem(SLOT, TILE)),
        [],
        10**5,
        row_b,
        row_a,
        edge,
    )
    col_b = swap(to_b, 1, 1)
    col_a = swap(to_a, 1, 0)
    vel_ends, wide, sides, seams = call(
        adjoint_kernel,
        "adjoint",
        (
            vmem(4 * HALO, cols),
            vmem(MODES, TILE),
            vmem(PARTS * ARRAYS * STRIP, TILE),
            vmem(PARTS * SUB, TILE),
        ),
        [vmem(ARRAYS * STRIP, cols), vmem(2 * STRIP, cols), vmem(rows + STRIP, cols), vmem(TILE, cols)]
        + [vmem(STRIP, cols)] * STRIP_FIELDS
        + [vmem(rows, cols)] * (FIELDS - 4),
        8 * 10**6,
        row_b,
        row_a,
        *near,
        *forward,
        basis_p,
        basis_q,
        edge,
        turned,
    )
    devices = lax.axis_size(ROW_AXES + COL_AXES)
    _, strips, coef = call(
        left_right_kernel,
        "left_right",
        (
            vmem(PARTS * ARRAYS * STRIP, TILE),
            vmem(PARTS * 2 * STRIP, TILE),
            vmem(devices // 2 * (SUB + 1), TILE),
        ),
        [vmem(PARTS * STRIP, TILE)] * (STRIP_FIELDS + 1),
        4 * 10**6,
        sides,
        seams,
        col_b,
        col_a,
        wide,
        tile_block,
        basis_rows,
        basis_cols,
        aliases={0: 0},
    )
    coef = coef.reshape(devices // 2, 1, (SUB + 1) * TILE)
    members = [[d for d in range(devices) if d % 2 == core] for core in range(2)]
    parts = lax.all_to_all(coef, ("row", "col", "own"), 0, 0, axis_index_groups=members, tiled=True)
    state = call(
        join_kernel,
        "join",
        jax.ShapeDtypeStruct((2, rows, cols), F32),
        [vmem(2 * PARTS * TILE, TILE)],
        4 * 10**6,
        *forward[4:],
        vel_ends,
        strips,
    )
    owners = owner_list.reshape(lax.axis_size("own"), -1)
    mine = owners.shape[1]
    kept, given = call(
        gather_kernel,
        "gather",
        (vmem(mine * SUB, TILE),) * 2,
        [],
        10**5,
        owners,
        parts.reshape(-1, TILE),
    )
    picked = call(
        pick_kernel,
        "pick",
        jax.ShapeDtypeStruct((1, mine, MODES * MODES), F32),
        [],
        10**5,
        kept,
        swap(given, 0, 0),
    )
    return (state, picked)


def solution(mesh):
    return jax.shard_map(
        local,
        mesh=mesh,
        in_specs=(
            P(("row", "own"), "col"),
            P(("row", "own"), "col"),
            P(None, ("row", "own"), "col"),
            P(None, ("row", "own"), "col"),
            P(("row", "own"), "col"),
            P(("row", "own"), "col"),
            P(),
        ),
        out_specs=(P(None, ("row", "own"), "col"), P("own", None, None)),
        check_vma=False,
    )
```

```python
import math

import jax
import jax.numpy as jnp
import numpy as np
from jax import lax
from jax.experimental import pallas as pl
from jax.experimental.pallas import tpu as pltpu
from jax.sharding import PartitionSpec as P

TILE = 128
MODES = 32
SWEEPS = 3
SUB = 8
HALO = 8
INNER = 2 * HALO
STRIP = 40
LEAD = HALO - 1
KEPT = 12
OUTER = (LEAD, STRIP - 2 * HALO)
NEAR, FAR = 7, 6
ARRAYS = 7
VISC, FRIC, DRIV, MASK, OBS = 0, 1, 2, 4, 5
EDGE = ARRAYS * HALO
SLOT = 2 * INNER
PER = TILE // SLOT
GROUPS = 5
SENT = 2 * GROUPS * HALO + HALO
PARTS = 3
UPPER, LOWER = 32, 64
ROW_AXES = ("row", "own")
COL_AXES = ("col",)
F32 = jnp.float32
LIMIT = 40 * 1024 * 1024


def swap(x, axis, first):
    sizes = lax.axis_size(ROW_AXES), lax.axis_size(COL_AXES)
    owners = lax.axis_size("own")

    def device(i, j):
        return (i // owners * sizes[1] + j) * owners + i % owners

    pairs = []
    for i in range(sizes[0]):
        for j in range(sizes[1]):
            place = [i, j]
            if first and place[axis] in (0, sizes[axis] - 1):
                place[1 - axis] ^= 1
            else:
                place[axis] = ((place[axis] + first) ^ 1) - first
            pairs.append((device(i, j), device(*place)))
    return lax.ppermute(x, ("row", "col", "own"), pairs)


def position(axes):
    index, size = 0, 1
    for axis in axes:
        index = index * lax.axis_size(axis) + lax.axis_index(axis)
        size *= lax.axis_size(axis)
    assert size % 2 == 0
    return lax.rem(index, 2) == 0, (index == 0) | (index == size - 1)


def is_even(axes):
    return position(axes)[0]


def lanes():
    return lax.broadcasted_iota(jnp.int32, (SUB, TILE), 1)


def call(kernel, name, outs, scratch, cost, *args, aliases={}):
    return pl.pallas_call(
        kernel,
        out_shape=outs,
        scratch_shapes=scratch,
        input_output_aliases=aliases,
        compiler_params=pltpu.CompilerParams(vmem_limit_bytes=LIMIT),
        cost_estimate=pl.CostEstimate(flops=cost, bytes_accessed=cost, transcendentals=0),
        name=name,
    )(*args)


def vmem(*shape):
    return pltpu.VMEM(shape, F32)


FIELDS = 14
STRIP_FIELDS = 24


class Domain:
    def __init__(self, refs, base, span, source, seam=None):
        self.refs, self.base, self.span, self.source, self.seam = refs, base, span, source, seam

    def at(self, j):
        return pl.ds(self.base + SUB * j, SUB)

    def prepare(self, flipped):
        n2, n4, c, i = self.refs[:4]
        visc = [self.source(VISC, j) for j in range(self.span)]
        for j in range(self.span):
            at = self.at(j)
            before = visc[j - 1] if j else pltpu.roll(visc[-1], 1, 0)
            if self.seam and not j:
                row = lax.broadcasted_iota(jnp.int32, (SUB, TILE), 0)
                before = jnp.where(row == SUB // 2, self.seam(), before)
            pair = visc[j] + before
            fric = self.source(FRIC, j)
            diag = 1.25 * (pair + pltpu.roll(pair, 1, 1)) + fric
            on = self.source(MASK, j) > 0.0
            inv = jnp.where(on, 0.5 / jnp.where(on, diag, 1.0), 0.0)
            half = 0.5 * visc[j]
            n2[at, :] = half
            n4[at, :] = 0.5 * half
            c[at, :] = 1.0 - fric * inv
            i[at, :] = inv
            for k in range(2):
                self.start(k, at, inv * self.source(DRIV + (1 - k if flipped else k), j))

    def start(self, k, at, value):
        self.refs[4 + k][at, :] = value
        self.write(k, at, value + value)

    def write(self, k, at, value):
        self.refs[6 + k][at, :] = value
        self.refs[8 + k][at, :] = pltpu.roll(value, TILE - 1, 1)

    def retarget(self, flipped, velocity=None):
        i = self.refs[3]
        velocity = velocity or self.refs[6:8]
        for j in range(self.span):
            at = self.at(j)
            for k in range(2):
                seen = self.source(OBS + (1 - k if flipped else k), j)
                self.start(k, at, i[at, :] * (velocity[k][at, :] - seen))

    def differences(self):
        n2, n4 = self.refs[:2]
        fields = self.refs[6:10]
        parts = self.refs[10:14]

        def corners(j, here, below):
            w0, w1, r0, r1 = here
            v0, v1, s0, s1 = below
            a1, a2 = s0 - w0, v0 - r0
            e1, e2 = s1 - w1, v1 - r1
            x, y = a1 + a2, e1 - e2
            q = (a1 - a2) + (e1 + e2)
            both = x + y
            at = self.at(j)
            half = n2[at, :]
            return half * (both + x), n4[at, :] * q, half * (both + y)

        def load(j):
            at = self.at(j)
            return [field[at, :] for field in fields]

        top = load(0)
        last = corners(self.span - 1, load(self.span - 1), [pltpu.roll(v, SUB - 1, 0) for v in top])
        up = [pltpu.roll(v, 1, 0) for v in last]
        here = top
        for j in range(self.span):
            at = self.at(j)
            if j < self.span - 1:
                below = load(j + 1)
                p, q, r = corners(j, here, below)
                here = below
            else:
                p, q, r = last
            g, t = up[0] - p, up[1] + q
            gq, tr = up[1] - q, up[2] + r
            parts[0][at, :] = g - t
            parts[1][at, :] = gq - tr
            parts[2][at, :] = pltpu.roll(g + t, 1, 1)
            parts[3][at, :] = pltpu.roll(gq + tr, 1, 1)
            up = (p, q, r)

    def update(self):
        c, i, b0, b1, w0, w1 = self.refs[2:8]
        parts = self.refs[10:14]
        for j in range(self.span):
            at = self.at(j)
            cv, iv = c[at, :], i[at, :]
            for k, (b, w) in enumerate(((b0, w0), (b1, w1))):
                value = (cv * w[at, :] + b[at, :]) - iv * (parts[k][at, :] + parts[k + 2][at, :])
                self.write(k, at, value)


class Strips(Domain):
    def prepare(self, flipped):
        super().prepare(flipped)
        for j in range(self.span):
            at = self.at(j)
            for now, later in zip(self.refs[2:4], self.refs[10:12]):
                later[at, :] = pltpu.roll(now[at, :], TILE - 1, 1)
        for now, before in zip(self.refs[:2], self.refs[14:16]):
            before[self.at(0), :] = pltpu.roll(now[self.at(self.span - 1), :], 1, 0)

    def start(self, k, at, value):
        b, w, r, later = (self.refs[n + k] for n in (4, 6, 8, 12))
        b[at, :] = value
        w[at, :] = value + value
        turned = pltpu.roll(value, TILE - 1, 1)
        later[at, :] = turned
        r[at, :] = turned + turned

    def differences(self):
        fields = self.refs[6:10]
        kept, turned, kept_next, turned_next = (self.refs[16 + 2 * k : 18 + 2 * k] for k in range(4))

        def corners(halves, quarters, j, here, below):
            w0, w1, r0, r1 = here
            v0, v1, s0, s1 = below
            a1, a2 = s0 - w0, v0 - r0
            e1, e2 = s1 - w1, v1 - r1
            x, y = a1 + a2, e1 - e2
            q = (a1 - a2) + (e1 + e2)
            both = x + y
            at = self.at(j)
            half = halves[at, :]
            return half * (both + x), quarters[at, :] * q, half * (both + y)

        def load(j):
            at = self.at(j)
            return [field[at, :] for field in fields]

        top, end = load(0), load(self.span - 1)
        up = corners(*self.refs[14:16], 0, [pltpu.roll(v, 1, 0) for v in end], top)
        here = top
        for j in range(self.span):
            at = self.at(j)
            below = load(j + 1) if j < self.span - 1 else [pltpu.roll(v, SUB - 1, 0) for v in top]
            p, q, r = corners(*self.refs[:2], j, here, below)
            g, t = up[0] - p, up[1] + q
            gq, tr = up[1] - q, up[2] + r
            for k, (stay, move) in enumerate(((g - t, g + t), (gq - tr, gq + tr))):
                kept[k][at, :] = stay
                turned_next[k][at, :] = move
                turned[k][at, :] = pltpu.roll(move, 1, 1)
                kept_next[k][at, :] = pltpu.roll(stay, TILE - 1, 1)
            up, here = (p, q, r), below

    def update(self):
        for first, offset, parts in ((2, 6, (16, 18)), (10, 8, (20, 22))):
            c, i, *b = self.refs[first : first + 4]
            for j in range(self.span):
                at = self.at(j)
                cv, iv = c[at, :], i[at, :]
                for k in range(2):
                    w = self.refs[offset + k]
                    change = self.refs[parts[0] + k][at, :] + self.refs[parts[1] + k][at, :]
                    w[at, :] = (cv * w[at, :] + b[k][at, :]) - iv * change


def run(domains, written_out=False):
    def body(_, carry):
        for domain in domains:
            domain.differences()
        for domain in domains:
            domain.update()
        return carry

    if written_out:
        for k in range(SWEEPS):
            body(k, 0)
    else:
        lax.fori_loop(0, SWEEPS, body, 0)


def ends_kernel(visc, fric, driv, mask, obs, to_b, to_a, one, two, flags, sems):
    rows = visc.shape[0]
    copies = []
    for e, first in enumerate((0, rows - HALO)):
        at = pl.ds(first, HALO)
        pieces = [
            (visc.at[at], one.at[e, 0]),
            (fric.at[at], one.at[e, 1]),
            (driv.at[:, at], two.at[e, 0]),
            (mask.at[at], flags.at[e]),
            (obs.at[:, at], two.at[e, 1]),
        ]
        for n, (source, place) in enumerate(pieces):
            copies.append(pltpu.make_async_copy(source, place, sems.at[e, n]))
    for copy in copies:
        copy.start()
    for copy in copies:
        copy.wait()
    even, at_end = position(ROW_AXES)

    def edge(e):
        return [one[e, 0], one[e, 1], two[e, 0, 0], two[e, 0, 1], flags[e].astype(F32), two[e, 1, 0], two[e, 1, 1]]

    for a, (head, tail) in enumerate(zip(edge(0), edge(1))):
        at = slice(HALO * a, HALO * (a + 1))
        to_a[at, :] = jnp.where(even, tail, head)
        to_b[at, :] = jnp.where(at_end, 0.0, jnp.where(even, head, tail))


def field_of(visc, fric, driv, mask, obs):
    def field(a, at):
        if a == MASK:
            return mask[at, :].astype(F32)
        if a >= OBS:
            return obs[a - OBS, at, :]
        if a >= DRIV:
            return driv[a - DRIV, at, :]
        return (visc, fric)[a][at, :]

    return field


def first_row(part, lane):
    if part < 2:
        return TILE * part + lane
    if lane < INNER + HALO:
        return TILE + lane
    if lane >= TILE - INNER - HALO:
        return lane
    if UPPER + HALO <= lane < UPPER + SLOT:
        return lane - UPPER - HALO
    if LOWER <= lane < LOWER + INNER + HALO:
        return 2 * TILE - INNER - HALO + lane - LOWER
    return None


def right_part(row):
    seam = TILE - HALO <= row < TILE + HALO
    part = 2 if seam or row == 0 or row == 2 * TILE - HALO else row // TILE
    return part, [lane for lane in range(0, TILE, SUB) if first_row(part, lane) == row][-1]


def slot(part, a):
    return TILE * (2 * part + a // PER) + SLOT * (a % PER)


def interior_kernel(visc, fric, driv, mask, obs, edge, n2, n4, c, i, v0, v1, *refs):
    span = visc.shape[0] // SUB
    field = field_of(visc, fric, driv, mask, obs)
    lane = lanes()
    for part in range(PARTS):
        for m in range(-(-ARRAYS // PER)):
            strips = []
            for at in range(0, TILE, SUB):
                row = first_row(part, at)
                packed = jnp.zeros((SUB, TILE), F32)
                if row is not None:
                    for k in range(min(PER, ARRAYS - PER * m)):
                        value = field(PER * m + k, slice(row, row + SUB))
                        moved = pltpu.roll(value, (SLOT * k + INNER) % TILE, 1)
                        packed = jnp.where(lax.div(lane, SLOT) == k, moved, packed)
                strips.append(packed)
            base = TILE * (2 * part + m)
            edge[base : base + TILE, :] = jnp.concatenate(strips, axis=0).T
    refs = (n2, n4, c, i, *refs[:2], v0, v1, *refs[2:])
    domain = Domain(refs, 0, span, lambda a, j: field(a, pl.ds(j, SUB, stride=span)))
    domain.prepare(False)
    run([domain])


def columns_kernel(row_b, row_a, edge, to_b, to_a, turned):
    even = is_even(ROW_AXES)
    above = jnp.where(even, row_b[...], row_a[...])
    below = jnp.where(even, row_a[...], row_b[...])
    halo = jnp.concatenate([above, below, jnp.zeros((TILE - 2 * EDGE, TILE), F32)], axis=0).T
    turned[:INNER, :] = halo[TILE - INNER :]
    turned[INNER:, :] = halo[:INNER]
    even, at_end = position(COL_AXES)
    row = lax.broadcasted_iota(jnp.int32, (SUB, TILE), 0)

    def put(out, right, left):
        right = pltpu.roll(right, LEAD, 0)
        to_a[out : out + HALO, :] = jnp.where(even, right, left)
        to_b[out : out + HALO, :] = jnp.where(at_end, 0.0, jnp.where(even, left, right))

    for part in range(2):
        right, left = [], []
        for a in range(ARRAYS):
            at = slot(part, a) + INNER
            right.append(edge[at - HALO : at, :])
            left.append(edge[at : at + HALO, :])
        for k in range(2):
            seen_r, seen_l = right[OBS + k], left[OBS + k]
            g = 1 + 2 * k
            right[g] = jnp.where(row < 2, pltpu.roll(seen_r, 2, 0), right[g])
            right[g + 1] = jnp.where(row < 2, pltpu.roll(seen_r, 4, 0), right[g + 1])
            left[g] = jnp.where(row >= 6, pltpu.roll(seen_l, 6, 0), left[g])
            left[g + 1] = jnp.where(row >= 6, pltpu.roll(seen_l, 4, 0), left[g + 1])
        for g in range(GROUPS):
            put(HALO * (GROUPS * part + g), right[g], left[g])
    put(2 * GROUPS * HALO, halo[TILE - HALO :], halo[:HALO])


def strided(stack, base):
    span = STRIP // SUB
    return lambda a, j: stack[pl.ds(base + STRIP * a + j, SUB, stride=span), :]


def fill(stack, base, first, last):
    row = lax.broadcasted_iota(jnp.int32, (SUB, TILE), 0)
    one, two = (pltpu.roll(value, LEAD, 0) for value in first)
    mixed = [jnp.where(row == LEAD, two, one), jnp.where(row < SUB // 2, two, last[0])]
    for k, value in enumerate((one, *mixed, last[1])):
        stack[base + SUB * k : base + SUB * (k + 1), :] = value


def velocity(domain, plain, base):
    for j in range(domain.span):
        at = domain.at(j)
        for k in range(2):
            plain[pl.ds(base + STRIP * k + j, SUB, stride=domain.span), :] = domain.refs[6 + k][at, :]


def density(domain, plain, base, out, place):
    w0, w1 = domain.refs[6:8]
    for j in range(domain.span):
        at = domain.at(j)
        v0, v1 = (plain[pl.ds(base + STRIP * k + j, SUB, stride=domain.span), :] for k in range(2))
        value = -domain.source(FRIC, j) * (w0[at, :] * v0 + w1[at, :] * v1)
        out[pl.ds(place + j, SUB, stride=domain.span), :] = value


def beside():
    lane = lanes()
    return (lane < NEAR) | (lane >= TILE - FAR)


def ends(second):
    row = lax.broadcasted_iota(jnp.int32, (SUB, TILE), 0)
    return row >= SUB - FAR if second else row < NEAR


def adjoint_kernel(
    row_b, row_a, visc, fric, driv, mask, obs, n2, n4, c, i, v0, v1, basis_p, basis_q, edge, turned,
    vel, wide, sides, seams,
    stack, plain, dens, total, *refs,
):
    rows = visc.shape[0]
    span = rows // SUB
    even = is_even(ROW_AXES)
    field = field_of(visc, fric, driv, mask, obs)
    for a in range(ARRAYS):
        at = slice(HALO * a, HALO * (a + 1))
        got_a, got_b = row_a[at, :], row_b[at, :]
        base = STRIP * a
        first = [field(a, slice(at, at + SUB)) for at in (0, SUB)]
        last = [field(a, slice(at, at + SUB)) for at in (rows - 2 * SUB, rows - SUB)]
        fill(stack, base, first, last)
        stack[base : base + LEAD, :] = jnp.where(even, got_b, got_a)[HALO - LEAD :]
        stack[base + STRIP - HALO : base + STRIP, :] = jnp.where(even, got_a, got_b)
    strips = Strips(refs[:STRIP_FIELDS], 0, STRIP // SUB, strided(stack, 0), lambda: visc[rows - KEPT - 1 : rows - KEPT, :])
    strips.prepare(False)
    run([strips])
    velocity(strips, plain, 0)
    for k in range(2):
        for e in range(2):
            out = HALO * (2 * k + e)
            vel[out : out + HALO, :] = plain[STRIP * k + OUTER[e] : STRIP * k + OUTER[e] + HALO, :]
    interior = Domain(
        (n2, n4, c, i, *refs[STRIP_FIELDS:]), 0, span, lambda a, j: field(a, pl.ds(j, SUB, stride=span))
    )
    strips.retarget(False)
    interior.retarget(False, (v0, v1))
    run([interior, strips])
    w0, w1 = interior.refs[6:8]
    for j in range(span):
        at = interior.at(j)
        value = -interior.source(FRIC, j) * (w0[at, :] * v0[at, :] + w1[at, :] * v1[at, :])
        dens[pl.ds(j, SUB, stride=span), :] = value
    density(strips, plain, 0, dens, rows)

    side = beside()
    for s in range(0, TILE, SUB):
        summed = jnp.zeros((SUB, TILE), F32)
        for row in range(s, rows, TILE):
            value = dens[row : row + SUB, :]
            if row in (0, rows - SUB):
                at = rows + OUTER[row > 0]
                value = jnp.where(ends(row > 0), dens[at : at + SUB, :], value)
            summed += value
        total[s : s + SUB, :] = jnp.where(side, 0.0, summed)
    exact = dict(precision=lax.Precision.HIGHEST, preferred_element_type=F32)
    half = jnp.dot(basis_p[...], total[...], **exact)
    wide[...] = jnp.dot(half, basis_q[...], **exact)

    corner = corners()
    for part in range(PARTS):
        for a in range(ARRAYS):
            columns = []
            for r in range(0, SLOT, SUB):
                value = edge[slot(part, a) + r : slot(part, a) + r + SUB, :]
                if part == 2:
                    moved = pltpu.roll(turned[r : r + SUB, :], (UPPER - HALO * a) % TILE, 1)
                    value = jnp.where(corner, moved, value)
                columns.append(value)
            fill(sides, strip(part, a), columns[2:], columns[:2])
            if a == VISC:
                seams[SUB * part : SUB * (part + 1), :] = columns[0]


def strip(part, a):
    return STRIP * (ARRAYS * part + a)


def corners():
    lane = lanes()
    above = (lane >= UPPER) & (lane < UPPER + HALO)
    return above | ((lane >= LOWER + INNER + HALO) & (lane < LOWER + SLOT))


def split(x, axis):
    high = x.astype(jnp.bfloat16)
    low = (x - high.astype(F32)).astype(jnp.bfloat16)
    return jnp.concatenate([high, high, low], axis=axis)


def split_constant(x, axis):
    x = np.asarray(x, np.float32)
    high = np.asarray(x, jnp.bfloat16)
    low = np.asarray(x - np.asarray(high, np.float32), jnp.bfloat16)
    return jnp.asarray(np.concatenate([high, low, high], axis=axis))


def left_right_kernel(
    _, seams, col_b, col_a, wide_in, block, basis_rows, basis_cols,
    stack, strips, coef,
    plain, *refs,
):
    even = is_even(COL_AXES)
    lane = lanes()
    row = lax.broadcasted_iota(jnp.int32, (SUB, TILE), 0)
    upper = (lane >= UPPER + HALO) & (lane < UPPER + SLOT)
    lower = (lane >= LOWER) & (lane < LOWER + INNER + HALO)
    seam_t0 = lane >= TILE - INNER - HALO
    seam_t1 = lane < INNER + HALO
    corner = corners()
    for from_left in (True, False):
        groups = []
        for g in range(2 * GROUPS + 1):
            got_a, got_b = col_a[HALO * g : HALO * (g + 1), :], col_b[HALO * g : HALO * (g + 1), :]
            groups.append(jnp.where(even, got_b, got_a) if from_left else jnp.where(even, got_a, got_b))
        tiles = []
        for part in range(2):
            tile = groups[GROUPS * part : GROUPS * (part + 1)]
            for k in range(2):
                g, h = tile[1 + 2 * k], tile[2 + 2 * k]
                if from_left:
                    tile.append(jnp.where(row >= 5, pltpu.roll(g, 6, 0), pltpu.roll(h, 4, 0)))
                else:
                    tile.append(jnp.where(row < 2, pltpu.roll(g, 2, 0), pltpu.roll(h, 4, 0)))
            tiles.append(tile)
        for a in range(ARRAYS):
            t0, t1 = tiles[0][a], tiles[1][a]
            third = jnp.where(corner, pltpu.roll(groups[-1], (UPPER - HALO * a) % TILE, 1), 0.0)
            third = jnp.where(upper, pltpu.roll(t0, UPPER + HALO, 1), third)
            third = jnp.where(lower, pltpu.roll(t1, LOWER + INNER + HALO, 1), third)
            third = jnp.where(seam_t0, t0, jnp.where(seam_t1, t1, third))
            for part, value in enumerate((t0, t1, third)):
                base = strip(part, a)
                if from_left:
                    stack[base : base + LEAD, :] = value[:LEAD]
                else:
                    stack[base + STRIP - HALO : base + STRIP, :] = value
    last = INNER - KEPT - 1
    before = [lambda at=SUB * part + last: seams[at : at + 1, :] for part in range(PARTS)]
    domains = [
        Strips(refs, STRIP * part, STRIP // SUB, strided(stack, strip(part, 0)), seam)
        for part, seam in enumerate(before)
    ]
    for domain in domains:
        domain.prepare(True)
    run(domains, True)
    for part, domain in enumerate(domains):
        velocity(domain, strips, 2 * STRIP * part)
        domain.retarget(True)
    run(domains, True)
    for part, domain in enumerate(domains):
        density(domain, strips, 2 * STRIP * part, plain, STRIP * part)

    def side(part):
        base = STRIP * part
        return jnp.concatenate(
            [plain[base + at : base + at + HALO, :] for at in OUTER], axis=0
        )

    lane = lax.broadcasted_iota(jnp.int32, (2 * HALO, TILE), 1)
    row = lax.broadcasted_iota(jnp.int32, (2 * HALO, TILE), 0)
    right = (row < NEAR) | (row >= 2 * HALO - FAR)
    straight = (lane >= HALO) & (lane < TILE - HALO)
    seam = (lane < HALO) | (lane >= TILE - HALO)
    top = (lane >= UPPER + HALO) & (lane < UPPER + 2 * HALO)
    bottom = (lane >= LOWER + INNER) & (lane < LOWER + INNER + HALO)
    dens = jnp.concatenate(
        [
            jnp.where(right & straight, side(0) + side(1), 0.0),
            jnp.where(right & (seam | top | bottom), side(2), 0.0),
        ],
        axis=1,
    )
    half = lax.dot_general(
        basis_rows[...], split(dens, 1), (((1,), (1,)), ((), ())), preferred_element_type=F32
    )
    high = half.astype(jnp.bfloat16)
    low = (half - high.astype(F32)).astype(jnp.bfloat16)
    both = jnp.dot(jnp.concatenate([high, low], axis=0), basis_cols[:INNER], preferred_element_type=F32)
    rest = jnp.dot(high, basis_cols[INNER:], preferred_element_type=F32)
    wide = wide_in[...] + (both[:MODES] + (both[MODES:] + rest))
    lane = lanes()
    which = lax.div(lane, MODES)
    flat = wide[:SUB]
    for j in range(1, MODES // SUB):
        flat = jnp.where(which == j, wide[SUB * j : SUB * (j + 1)], flat)
    mark = jnp.broadcast_to(block[:1, :].astype(F32), (SUB, TILE))
    row = lax.broadcasted_iota(jnp.int32, (SUB, TILE), 0)
    moved = [flat] + [pltpu.roll(flat, r, 0) for r in range(1, SUB)] + [flat]
    lines = [flat] + [
        jnp.where(row < r - 1, moved[r - 1], jnp.where(row == r - 1, mark, moved[r])) for r in range(1, SUB + 1)
    ]
    cycle = SUB * (SUB + 1)
    chunk = min(4, coef.shape[0] // cycle)

    def spread(d, carry):
        for e in range(chunk):
            for r, line in enumerate(lines):
                coef[pl.ds(pl.multiple_of((d * chunk + e) * cycle + SUB * r, SUB), SUB), :] = line
        return carry

    lax.fori_loop(0, coef.shape[0] // cycle // chunk, spread, 0)


def join_kernel(v0, v1, vel_ends, strips, vel, turned):
    rows = vel.shape[1]
    span = rows // SUB
    middle = jnp.zeros((TILE - 2 * HALO, TILE), F32)
    side = beside()
    for k, v in enumerate((v0, v1)):
        for part in range(PARTS):
            base = STRIP * (2 * part + 1 - k)
            first, last = (strips[base + at : base + at + HALO, :] for at in OUTER)
            at = TILE * (2 * part + k)
            turned[at : at + TILE, :] = jnp.concatenate([first, middle, last], axis=0).T
        for row in range(0, rows, SUB):
            value = v[pl.ds(SUB * (row % span) + row // span, SUB, stride=SUB), :]
            if row in (0, rows - SUB):
                at = HALO * (2 * k + (row > 0))
                value = jnp.where(ends(row > 0), vel_ends[at : at + HALO, :], value)
            part, lane = right_part(row)
            at = TILE * (2 * part + k) + lane
            vel[k, row : row + SUB, :] = jnp.where(side, turned[at : at + SUB, :], value)


def bases():
    places = np.arange(TILE) + 0.5
    basis = np.cos(math.pi * places[:, None] * np.arange(MODES)[None, :] / TILE)
    groups = MODES // SUB
    order = np.arange(MODES).reshape(SUB, groups).T.reshape(-1)
    rows = basis[:, order] / TILE
    cols = np.tile(basis, (1, groups))
    placed = np.zeros((2 * TILE, MODES))
    for row in range(0, 2 * TILE, SUB):
        part, lane = right_part(row)
        at = lane + (TILE if part == 2 else 0)
        placed[at : at + SUB] = rows[row % TILE : row % TILE + SUB]
    outer = np.concatenate([cols[:HALO], cols[TILE - HALO :]])
    return jnp.asarray(rows.T, F32), jnp.asarray(cols, F32), split_constant(placed.T, 1), split_constant(outer, 0)[: 2 * INNER]


def pick_kernel(owners, every, out):
    mine = out.shape[1]
    own = lax.axis_index("own")
    wanted = [owners[pl.ds(own, 1), k : k + 1].astype(F32) for k in range(mine)]
    lines = SUB + 1
    devices = every.shape[0] // lines
    chunk = min(4, devices // SUB)

    def body(d, sums):
        sums = list(sums)
        for e in range(chunk):
            base = (d * chunk + e) * SUB * lines
            mark = every[pl.ds(base + SUB, SUB, stride=lines), :]
            hits = [mark == wanted[k] for k in range(mine)]
            for r in range(SUB):
                part = every[pl.ds(base + r, SUB, stride=lines), :]
                for k in range(mine):
                    sums[SUB * k + r] += jnp.where(hits[k], part, 0.0)
        return tuple(sums)

    start = (jnp.zeros((SUB, TILE), F32),) * (mine * SUB)
    sums = lax.fori_loop(0, devices // SUB // chunk, body, start)
    for k in range(mine):
        for r in range(SUB):
            total = jnp.sum(sums[SUB * k + r], axis=0, keepdims=True)
            out[0, k : k + 1, TILE * r : TILE * (r + 1)] = total


def local(viscosity, friction, driving, observed, ice_mask, tile_block, owner_list):
    rows, cols = viscosity.shape
    assert (rows, cols) == (2 * TILE, TILE)
    inputs = (viscosity, friction, driving, ice_mask, observed)
    near = [pltpu.with_memory_space_constraint(x, pltpu.VMEM) for x in inputs]
    basis_p, basis_q, basis_rows, basis_cols = bases()
    to_b, to_a = call(
        ends_kernel,
        "ends",
        (vmem(EDGE, cols), vmem(EDGE, cols)),
        [
            vmem(2, 2, HALO, cols),
            vmem(2, 2, 2, HALO, cols),
            pltpu.VMEM((2, HALO, cols), jnp.int32),
            pltpu.SemaphoreType.DMA((2, 5)),
        ],
        10**6,
        *(pltpu.with_memory_space_constraint(x, pltpu.HBM) for x in inputs),
    )
    row_b = swap(to_b, 0, 1)
    row_a = swap(to_a, 0, 0)
    edge, *forward = call(
        interior_kernel,
        "interior",
        (vmem(2 * PARTS * TILE, TILE),) + (vmem(rows, cols),) * 6,
        [vmem(rows, cols)] * (FIELDS - 6),
        8 * 10**6,
        *near,
    )
    to_b, to_a, turned = call(
        columns_kernel,
        "columns",
        (vmem(SENT, TILE), vmem(SENT, TILE), vmem(SLOT, TILE)),
        [],
        10**5,
        row_b,
        row_a,
        edge,
    )
    col_b = swap(to_b, 1, 1)
    col_a = swap(to_a, 1, 0)
    vel_ends, wide, sides, seams = call(
        adjoint_kernel,
        "adjoint",
        (
            vmem(4 * HALO, cols),
            vmem(MODES, TILE),
            vmem(PARTS * ARRAYS * STRIP, TILE),
            vmem(PARTS * SUB, TILE),
        ),
        [vmem(ARRAYS * STRIP, cols), vmem(2 * STRIP, cols), vmem(rows + STRIP, cols), vmem(TILE, cols)]
        + [vmem(STRIP, cols)] * STRIP_FIELDS
        + [vmem(rows, cols)] * (FIELDS - 4),
        8 * 10**6,
        row_b,
        row_a,
        *near,
        *forward,
        basis_p,
        basis_q,
        edge,
        turned,
    )
    devices = lax.axis_size(ROW_AXES + COL_AXES)
    _, strips, coef = call(
        left_right_kernel,
        "left_right",
        (
            vmem(PARTS * ARRAYS * STRIP, TILE),
            vmem(PARTS * 2 * STRIP, TILE),
            vmem(devices * (SUB + 1), TILE),
        ),
        [vmem(PARTS * STRIP, TILE)] * (STRIP_FIELDS + 1),
        4 * 10**6,
        sides,
        seams,
        col_b,
        col_a,
        wide,
        tile_block,
        basis_rows,
        basis_cols,
        aliases={0: 0},
    )
    coef = coef.reshape(devices, 1, (SUB + 1) * TILE)
    sizes = [lax.axis_size(axis) for axis in ("col", "row", "own")]
    members = [
        (row * sizes[0] + col) * sizes[2] + own
        for col in range(sizes[0])
        for row in range(sizes[1])
        for own in range(sizes[2])
    ]
    parts = lax.all_to_all(coef, ("row", "col", "own"), 0, 0, axis_index_groups=[members], tiled=True)
    state = call(
        join_kernel,
        "join",
        jax.ShapeDtypeStruct((2, rows, cols), F32),
        [vmem(2 * PARTS * TILE, TILE)],
        4 * 10**6,
        *forward[4:],
        vel_ends,
        strips,
    )
    owners = owner_list.reshape(lax.axis_size("own"), -1)
    picked = call(
        pick_kernel,
        "pick",
        jax.ShapeDtypeStruct((1, owners.shape[1], MODES * MODES), F32),
        [],
        10**5,
        owners,
        parts.reshape(-1, TILE),
    )
    return (state, picked)


def solution(mesh):
    return jax.shard_map(
        local,
        mesh=mesh,
        in_specs=(
            P(("row", "own"), "col"),
            P(("row", "own"), "col"),
            P(None, ("row", "own"), "col"),
            P(None, ("row", "own"), "col"),
            P(("row", "own"), "col"),
            P(("row", "own"), "col"),
            P(),
        ),
        out_specs=(P(None, ("row", "own"), "col"), P("own", None, None)),
        check_vma=False,
    )
```

```python
import math

import jax
import jax.numpy as jnp
import numpy as np
from jax import lax
from jax.experimental import pallas as pl
from jax.experimental.pallas import tpu as pltpu
from jax.sharding import PartitionSpec as P

TILE = 128
MODES = 32
SWEEPS = 3
SUB = 8
HALO = 8
INNER = 2 * HALO
STRIP = 40
LEAD = HALO - 1
KEPT = 12
OUTER = (LEAD, STRIP - 2 * HALO)
NEAR, FAR = 7, 6
ARRAYS = 7
VISC, FRIC, DRIV, MASK, OBS = 0, 1, 2, 4, 5
EDGE = ARRAYS * HALO
SLOT = 2 * INNER
PER = TILE // SLOT
GROUPS = 5
SENT = 2 * GROUPS * HALO + HALO
PARTS = 3
UPPER, LOWER = 32, 64
ROW_AXES = ("row", "own")
COL_AXES = ("col",)
F32 = jnp.float32
LIMIT = 40 * 1024 * 1024


def swap(x, axis, first):
    sizes = lax.axis_size(ROW_AXES), lax.axis_size(COL_AXES)
    owners = lax.axis_size("own")

    def device(i, j):
        return (i // owners * sizes[1] + j) * owners + i % owners

    pairs = []
    for i in range(sizes[0]):
        for j in range(sizes[1]):
            place = [i, j]
            if first and place[axis] in (0, sizes[axis] - 1):
                place[1 - axis] ^= 1
            else:
                place[axis] = ((place[axis] + first) ^ 1) - first
            pairs.append((device(i, j), device(*place)))
    return lax.ppermute(x, ("row", "col", "own"), pairs)


def position(axes):
    index, size = 0, 1
    for axis in axes:
        index = index * lax.axis_size(axis) + lax.axis_index(axis)
        size *= lax.axis_size(axis)
    assert size % 2 == 0
    return lax.rem(index, 2) == 0, (index == 0) | (index == size - 1)


def is_even(axes):
    return position(axes)[0]


def lanes():
    return lax.broadcasted_iota(jnp.int32, (SUB, TILE), 1)


def call(kernel, name, outs, scratch, cost, *args, aliases={}):
    return pl.pallas_call(
        kernel,
        out_shape=outs,
        scratch_shapes=scratch,
        input_output_aliases=aliases,
        compiler_params=pltpu.CompilerParams(vmem_limit_bytes=LIMIT),
        cost_estimate=pl.CostEstimate(flops=cost, bytes_accessed=cost, transcendentals=0),
        name=name,
    )(*args)


def vmem(*shape):
    return pltpu.VMEM(shape, F32)


FIELDS = 14
STRIP_FIELDS = 24


class Domain:
    def __init__(self, refs, base, span, source, seam=None):
        self.refs, self.base, self.span, self.source, self.seam = refs, base, span, source, seam

    def at(self, j):
        return pl.ds(self.base + SUB * j, SUB)

    def prepare(self, flipped):
        n2, n4, c, i = self.refs[:4]
        visc = [self.source(VISC, j) for j in range(self.span)]
        for j in range(self.span):
            at = self.at(j)
            before = visc[j - 1] if j else pltpu.roll(visc[-1], 1, 0)
            if self.seam and not j:
                row = lax.broadcasted_iota(jnp.int32, (SUB, TILE), 0)
                before = jnp.where(row == SUB // 2, self.seam(), before)
            pair = visc[j] + before
            fric = self.source(FRIC, j)
            diag = 1.25 * (pair + pltpu.roll(pair, 1, 1)) + fric
            on = self.source(MASK, j) > 0.0
            inv = jnp.where(on, 0.5 / jnp.where(on, diag, 1.0), 0.0)
            half = 0.5 * visc[j]
            n2[at, :] = half
            n4[at, :] = 0.5 * half
            c[at, :] = 1.0 - fric * inv
            i[at, :] = inv
            for k in range(2):
                self.start(k, at, inv * self.source(DRIV + (1 - k if flipped else k), j))

    def start(self, k, at, value):
        self.refs[4 + k][at, :] = value
        self.write(k, at, value + value)

    def write(self, k, at, value):
        self.refs[6 + k][at, :] = value
        self.refs[8 + k][at, :] = pltpu.roll(value, TILE - 1, 1)

    def retarget(self, flipped, velocity=None):
        i = self.refs[3]
        velocity = velocity or self.refs[6:8]
        for j in range(self.span):
            at = self.at(j)
            for k in range(2):
                seen = self.source(OBS + (1 - k if flipped else k), j)
                self.start(k, at, i[at, :] * (velocity[k][at, :] - seen))

    def differences(self):
        n2, n4 = self.refs[:2]
        fields = self.refs[6:10]
        parts = self.refs[10:14]

        def corners(j, here, below):
            w0, w1, r0, r1 = here
            v0, v1, s0, s1 = below
            a1, a2 = s0 - w0, v0 - r0
            e1, e2 = s1 - w1, v1 - r1
            x, y = a1 + a2, e1 - e2
            q = (a1 - a2) + (e1 + e2)
            both = x + y
            at = self.at(j)
            half = n2[at, :]
            return half * (both + x), n4[at, :] * q, half * (both + y)

        def load(j):
            at = self.at(j)
            return [field[at, :] for field in fields]

        top = load(0)
        last = corners(self.span - 1, load(self.span - 1), [pltpu.roll(v, SUB - 1, 0) for v in top])
        up = [pltpu.roll(v, 1, 0) for v in last]
        here = top
        for j in range(self.span):
            at = self.at(j)
            if j < self.span - 1:
                below = load(j + 1)
                p, q, r = corners(j, here, below)
                here = below
            else:
                p, q, r = last
            g, t = up[0] - p, up[1] + q
            gq, tr = up[1] - q, up[2] + r
            parts[0][at, :] = g - t
            parts[1][at, :] = gq - tr
            parts[2][at, :] = pltpu.roll(g + t, 1, 1)
            parts[3][at, :] = pltpu.roll(gq + tr, 1, 1)
            up = (p, q, r)

    def update(self):
        c, i, b0, b1, w0, w1 = self.refs[2:8]
        parts = self.refs[10:14]
        for j in range(self.span):
            at = self.at(j)
            cv, iv = c[at, :], i[at, :]
            for k, (b, w) in enumerate(((b0, w0), (b1, w1))):
                value = (cv * w[at, :] + b[at, :]) - iv * (parts[k][at, :] + parts[k + 2][at, :])
                self.write(k, at, value)


class Strips(Domain):
    def prepare(self, flipped):
        super().prepare(flipped)
        for j in range(self.span):
            at = self.at(j)
            for now, later in zip(self.refs[2:4], self.refs[10:12]):
                later[at, :] = pltpu.roll(now[at, :], TILE - 1, 1)
        for now, before in zip(self.refs[:2], self.refs[14:16]):
            before[self.at(0), :] = pltpu.roll(now[self.at(self.span - 1), :], 1, 0)

    def start(self, k, at, value):
        b, w, r, later = (self.refs[n + k] for n in (4, 6, 8, 12))
        b[at, :] = value
        w[at, :] = value + value
        turned = pltpu.roll(value, TILE - 1, 1)
        later[at, :] = turned
        r[at, :] = turned + turned

    def differences(self):
        fields = self.refs[6:10]
        kept, turned, kept_next, turned_next = (self.refs[16 + 2 * k : 18 + 2 * k] for k in range(4))

        def corners(halves, quarters, j, here, below):
            w0, w1, r0, r1 = here
            v0, v1, s0, s1 = below
            a1, a2 = s0 - w0, v0 - r0
            e1, e2 = s1 - w1, v1 - r1
            x, y = a1 + a2, e1 - e2
            q = (a1 - a2) + (e1 + e2)
            both = x + y
            at = self.at(j)
            half = halves[at, :]
            return half * (both + x), quarters[at, :] * q, half * (both + y)

        def load(j):
            at = self.at(j)
            return [field[at, :] for field in fields]

        top, end = load(0), load(self.span - 1)
        up = corners(*self.refs[14:16], 0, [pltpu.roll(v, 1, 0) for v in end], top)
        here = top
        for j in range(self.span):
            at = self.at(j)
            below = load(j + 1) if j < self.span - 1 else [pltpu.roll(v, SUB - 1, 0) for v in top]
            p, q, r = corners(*self.refs[:2], j, here, below)
            g, t = up[0] - p, up[1] + q
            gq, tr = up[1] - q, up[2] + r
            for k, (stay, move) in enumerate(((g - t, g + t), (gq - tr, gq + tr))):
                kept[k][at, :] = stay
                turned_next[k][at, :] = move
                turned[k][at, :] = pltpu.roll(move, 1, 1)
                kept_next[k][at, :] = pltpu.roll(stay, TILE - 1, 1)
            up, here = (p, q, r), below

    def update(self):
        for first, offset, parts in ((2, 6, (16, 18)), (10, 8, (20, 22))):
            c, i, *b = self.refs[first : first + 4]
            for j in range(self.span):
                at = self.at(j)
                cv, iv = c[at, :], i[at, :]
                for k in range(2):
                    w = self.refs[offset + k]
                    change = self.refs[parts[0] + k][at, :] + self.refs[parts[1] + k][at, :]
                    w[at, :] = (cv * w[at, :] + b[k][at, :]) - iv * change


def run(domains, written_out=False):
    def body(_, carry):
        for domain in domains:
            domain.differences()
        for domain in domains:
            domain.update()
        return carry

    if written_out:
        for k in range(SWEEPS):
            body(k, 0)
    else:
        lax.fori_loop(0, SWEEPS, body, 0)


def ends_kernel(visc, fric, driv, mask, obs, to_b, to_a, one, two, flags, sems):
    rows = visc.shape[0]
    copies = []
    for e, first in enumerate((0, rows - HALO)):
        at = pl.ds(first, HALO)
        pieces = [
            (visc.at[at], one.at[e, 0]),
            (fric.at[at], one.at[e, 1]),
            (driv.at[:, at], two.at[e, 0]),
            (mask.at[at], flags.at[e]),
            (obs.at[:, at], two.at[e, 1]),
        ]
        for n, (source, place) in enumerate(pieces):
            copies.append(pltpu.make_async_copy(source, place, sems.at[e, n]))
    for copy in copies:
        copy.start()
    for copy in copies:
        copy.wait()
    even, at_end = position(ROW_AXES)

    def edge(e):
        return [one[e, 0], one[e, 1], two[e, 0, 0], two[e, 0, 1], flags[e].astype(F32), two[e, 1, 0], two[e, 1, 1]]

    for a, (head, tail) in enumerate(zip(edge(0), edge(1))):
        at = slice(HALO * a, HALO * (a + 1))
        to_a[at, :] = jnp.where(even, tail, head)
        to_b[at, :] = jnp.where(at_end, 0.0, jnp.where(even, head, tail))


def field_of(visc, fric, driv, mask, obs):
    def field(a, at):
        if a == MASK:
            return mask[at, :].astype(F32)
        if a >= OBS:
            return obs[a - OBS, at, :]
        if a >= DRIV:
            return driv[a - DRIV, at, :]
        return (visc, fric)[a][at, :]

    return field


def first_row(part, lane):
    if part < 2:
        return TILE * part + lane
    if lane < INNER + HALO:
        return TILE + lane
    if lane >= TILE - INNER - HALO:
        return lane
    if UPPER + HALO <= lane < UPPER + SLOT:
        return lane - UPPER - HALO
    if LOWER <= lane < LOWER + INNER + HALO:
        return 2 * TILE - INNER - HALO + lane - LOWER
    return None


def right_part(row):
    seam = TILE - HALO <= row < TILE + HALO
    part = 2 if seam or row == 0 or row == 2 * TILE - HALO else row // TILE
    return part, [lane for lane in range(0, TILE, SUB) if first_row(part, lane) == row][-1]


def slot(part, a):
    return TILE * (2 * part + a // PER) + SLOT * (a % PER)


def interior_kernel(visc, fric, driv, mask, obs, edge, n2, n4, c, i, v0, v1, *refs):
    span = visc.shape[0] // SUB
    field = field_of(visc, fric, driv, mask, obs)
    lane = lanes()
    for part in range(PARTS):
        for m in range(-(-ARRAYS // PER)):
            strips = []
            for at in range(0, TILE, SUB):
                row = first_row(part, at)
                packed = jnp.zeros((SUB, TILE), F32)
                if row is not None:
                    for k in range(min(PER, ARRAYS - PER * m)):
                        value = field(PER * m + k, slice(row, row + SUB))
                        moved = pltpu.roll(value, (SLOT * k + INNER) % TILE, 1)
                        packed = jnp.where(lax.div(lane, SLOT) == k, moved, packed)
                strips.append(packed)
            base = TILE * (2 * part + m)
            edge[base : base + TILE, :] = jnp.concatenate(strips, axis=0).T
    refs = (n2, n4, c, i, *refs[:2], v0, v1, *refs[2:])
    domain = Domain(refs, 0, span, lambda a, j: field(a, pl.ds(j, SUB, stride=span)))
    domain.prepare(False)
    run([domain])


def columns_kernel(row_b, row_a, edge, to_b, to_a, turned):
    even = is_even(ROW_AXES)
    above = jnp.where(even, row_b[...], row_a[...])
    below = jnp.where(even, row_a[...], row_b[...])
    halo = jnp.concatenate([above, below, jnp.zeros((TILE - 2 * EDGE, TILE), F32)], axis=0).T
    turned[:INNER, :] = halo[TILE - INNER :]
    turned[INNER:, :] = halo[:INNER]
    even, at_end = position(COL_AXES)
    row = lax.broadcasted_iota(jnp.int32, (SUB, TILE), 0)

    def put(out, right, left):
        right = pltpu.roll(right, LEAD, 0)
        to_a[out : out + HALO, :] = jnp.where(even, right, left)
        to_b[out : out + HALO, :] = jnp.where(at_end, 0.0, jnp.where(even, left, right))

    for part in range(2):
        right, left = [], []
        for a in range(ARRAYS):
            at = slot(part, a) + INNER
            right.append(edge[at - HALO : at, :])
            left.append(edge[at : at + HALO, :])
        for k in range(2):
            seen_r, seen_l = right[OBS + k], left[OBS + k]
            g = 1 + 2 * k
            right[g] = jnp.where(row < 2, pltpu.roll(seen_r, 2, 0), right[g])
            right[g + 1] = jnp.where(row < 2, pltpu.roll(seen_r, 4, 0), right[g + 1])
            left[g] = jnp.where(row >= 6, pltpu.roll(seen_l, 6, 0), left[g])
            left[g + 1] = jnp.where(row >= 6, pltpu.roll(seen_l, 4, 0), left[g + 1])
        for g in range(GROUPS):
            put(HALO * (GROUPS * part + g), right[g], left[g])
    put(2 * GROUPS * HALO, halo[TILE - HALO :], halo[:HALO])


def strided(stack, base):
    span = STRIP // SUB
    return lambda a, j: stack[pl.ds(base + STRIP * a + j, SUB, stride=span), :]


def fill(stack, base, first, last):
    row = lax.broadcasted_iota(jnp.int32, (SUB, TILE), 0)
    one, two = (pltpu.roll(value, LEAD, 0) for value in first)
    mixed = [jnp.where(row == LEAD, two, one), jnp.where(row < SUB // 2, two, last[0])]
    for k, value in enumerate((one, *mixed, last[1])):
        stack[base + SUB * k : base + SUB * (k + 1), :] = value


def velocity(domain, plain, base):
    for j in range(domain.span):
        at = domain.at(j)
        for k in range(2):
            plain[pl.ds(base + STRIP * k + j, SUB, stride=domain.span), :] = domain.refs[6 + k][at, :]


def density(domain, plain, base, out, place):
    w0, w1 = domain.refs[6:8]
    for j in range(domain.span):
        at = domain.at(j)
        v0, v1 = (plain[pl.ds(base + STRIP * k + j, SUB, stride=domain.span), :] for k in range(2))
        value = -domain.source(FRIC, j) * (w0[at, :] * v0 + w1[at, :] * v1)
        out[pl.ds(place + j, SUB, stride=domain.span), :] = value


def beside():
    lane = lanes()
    return (lane < NEAR) | (lane >= TILE - FAR)


def ends(second):
    row = lax.broadcasted_iota(jnp.int32, (SUB, TILE), 0)
    return row >= SUB - FAR if second else row < NEAR


def adjoint_kernel(
    row_b, row_a, visc, fric, driv, mask, obs, n2, n4, c, i, v0, v1, basis_p, basis_q, edge, turned,
    vel, wide, sides, seams,
    stack, plain, dens, total, *refs,
):
    rows = visc.shape[0]
    span = rows // SUB
    even = is_even(ROW_AXES)
    field = field_of(visc, fric, driv, mask, obs)
    for a in range(ARRAYS):
        at = slice(HALO * a, HALO * (a + 1))
        got_a, got_b = row_a[at, :], row_b[at, :]
        base = STRIP * a
        first = [field(a, slice(at, at + SUB)) for at in (0, SUB)]
        last = [field(a, slice(at, at + SUB)) for at in (rows - 2 * SUB, rows - SUB)]
        fill(stack, base, first, last)
        stack[base : base + LEAD, :] = jnp.where(even, got_b, got_a)[HALO - LEAD :]
        stack[base + STRIP - HALO : base + STRIP, :] = jnp.where(even, got_a, got_b)
    strips = Strips(refs[:STRIP_FIELDS], 0, STRIP // SUB, strided(stack, 0), lambda: visc[rows - KEPT - 1 : rows - KEPT, :])
    strips.prepare(False)
    run([strips])
    velocity(strips, plain, 0)
    for k in range(2):
        for e in range(2):
            out = HALO * (2 * k + e)
            vel[out : out + HALO, :] = plain[STRIP * k + OUTER[e] : STRIP * k + OUTER[e] + HALO, :]
    interior = Domain(
        (n2, n4, c, i, *refs[STRIP_FIELDS:]), 0, span, lambda a, j: field(a, pl.ds(j, SUB, stride=span))
    )
    strips.retarget(False)
    interior.retarget(False, (v0, v1))
    run([interior, strips])
    w0, w1 = interior.refs[6:8]
    for j in range(span):
        at = interior.at(j)
        value = -interior.source(FRIC, j) * (w0[at, :] * v0[at, :] + w1[at, :] * v1[at, :])
        dens[pl.ds(j, SUB, stride=span), :] = value
    density(strips, plain, 0, dens, rows)

    side = beside()
    for s in range(0, TILE, SUB):
        summed = jnp.zeros((SUB, TILE), F32)
        for row in range(s, rows, TILE):
            value = dens[row : row + SUB, :]
            if row in (0, rows - SUB):
                at = rows + OUTER[row > 0]
                value = jnp.where(ends(row > 0), dens[at : at + SUB, :], value)
            summed += value
        total[s : s + SUB, :] = jnp.where(side, 0.0, summed)
    exact = dict(precision=lax.Precision.HIGHEST, preferred_element_type=F32)
    half = jnp.dot(basis_p[...], total[...], **exact)
    wide[...] = jnp.dot(half, basis_q[...], **exact)

    corner = corners()
    for part in range(PARTS):
        for a in range(ARRAYS):
            columns = []
            for r in range(0, SLOT, SUB):
                value = edge[slot(part, a) + r : slot(part, a) + r + SUB, :]
                if part == 2:
                    moved = pltpu.roll(turned[r : r + SUB, :], (UPPER - HALO * a) % TILE, 1)
                    value = jnp.where(corner, moved, value)
                columns.append(value)
            fill(sides, strip(part, a), columns[2:], columns[:2])
            if a == VISC:
                seams[SUB * part : SUB * (part + 1), :] = columns[0]


def strip(part, a):
    return STRIP * (ARRAYS * part + a)


def corners():
    lane = lanes()
    above = (lane >= UPPER) & (lane < UPPER + HALO)
    return above | ((lane >= LOWER + INNER + HALO) & (lane < LOWER + SLOT))


def split(x, axis):
    high = x.astype(jnp.bfloat16)
    low = (x - high.astype(F32)).astype(jnp.bfloat16)
    return jnp.concatenate([high, high, low], axis=axis)


def split_constant(x, axis):
    x = np.asarray(x, np.float32)
    high = np.asarray(x, jnp.bfloat16)
    low = np.asarray(x - np.asarray(high, np.float32), jnp.bfloat16)
    return jnp.asarray(np.concatenate([high, low, high], axis=axis))


def left_right_kernel(
    _, seams, col_b, col_a, wide_in, block, basis_rows, basis_cols,
    stack, strips, coef,
    plain, *refs,
):
    even = is_even(COL_AXES)
    lane = lanes()
    row = lax.broadcasted_iota(jnp.int32, (SUB, TILE), 0)
    upper = (lane >= UPPER + HALO) & (lane < UPPER + SLOT)
    lower = (lane >= LOWER) & (lane < LOWER + INNER + HALO)
    seam_t0 = lane >= TILE - INNER - HALO
    seam_t1 = lane < INNER + HALO
    corner = corners()
    for from_left in (True, False):
        groups = []
        for g in range(2 * GROUPS + 1):
            got_a, got_b = col_a[HALO * g : HALO * (g + 1), :], col_b[HALO * g : HALO * (g + 1), :]
            groups.append(jnp.where(even, got_b, got_a) if from_left else jnp.where(even, got_a, got_b))
        tiles = []
        for part in range(2):
            tile = groups[GROUPS * part : GROUPS * (part + 1)]
            for k in range(2):
                g, h = tile[1 + 2 * k], tile[2 + 2 * k]
                if from_left:
                    tile.append(jnp.where(row >= 5, pltpu.roll(g, 6, 0), pltpu.roll(h, 4, 0)))
                else:
                    tile.append(jnp.where(row < 2, pltpu.roll(g, 2, 0), pltpu.roll(h, 4, 0)))
            tiles.append(tile)
        for a in range(ARRAYS):
            t0, t1 = tiles[0][a], tiles[1][a]
            third = jnp.where(corner, pltpu.roll(groups[-1], (UPPER - HALO * a) % TILE, 1), 0.0)
            third = jnp.where(upper, pltpu.roll(t0, UPPER + HALO, 1), third)
            third = jnp.where(lower, pltpu.roll(t1, LOWER + INNER + HALO, 1), third)
            third = jnp.where(seam_t0, t0, jnp.where(seam_t1, t1, third))
            for part, value in enumerate((t0, t1, third)):
                base = strip(part, a)
                if from_left:
                    stack[base : base + LEAD, :] = value[:LEAD]
                else:
                    stack[base + STRIP - HALO : base + STRIP, :] = value
    last = INNER - KEPT - 1
    before = [lambda at=SUB * part + last: seams[at : at + 1, :] for part in range(PARTS)]
    domains = [
        Strips(refs, STRIP * part, STRIP // SUB, strided(stack, strip(part, 0)), seam)
        for part, seam in enumerate(before)
    ]
    for domain in domains:
        domain.prepare(True)
    run(domains, True)
    for part, domain in enumerate(domains):
        velocity(domain, strips, 2 * STRIP * part)
        domain.retarget(True)
    run(domains, True)
    for part, domain in enumerate(domains):
        density(domain, strips, 2 * STRIP * part, plain, STRIP * part)

    def side(part):
        base = STRIP * part
        return jnp.concatenate(
            [plain[base + at : base + at + HALO, :] for at in OUTER], axis=0
        )

    lane = lax.broadcasted_iota(jnp.int32, (2 * HALO, TILE), 1)
    row = lax.broadcasted_iota(jnp.int32, (2 * HALO, TILE), 0)
    right = (row < NEAR) | (row >= 2 * HALO - FAR)
    straight = (lane >= HALO) & (lane < TILE - HALO)
    seam = (lane < HALO) | (lane >= TILE - HALO)
    top = (lane >= UPPER + HALO) & (lane < UPPER + 2 * HALO)
    bottom = (lane >= LOWER + INNER) & (lane < LOWER + INNER + HALO)
    dens = jnp.concatenate(
        [
            jnp.where(right & straight, side(0) + side(1), 0.0),
            jnp.where(right & (seam | top | bottom), side(2), 0.0),
        ],
        axis=1,
    )
    half = lax.dot_general(
        basis_rows[...], split(dens, 1), (((1,), (1,)), ((), ())), preferred_element_type=F32
    )
    high = half.astype(jnp.bfloat16)
    low = (half - high.astype(F32)).astype(jnp.bfloat16)
    both = jnp.dot(jnp.concatenate([high, low], axis=0), basis_cols[:INNER], preferred_element_type=F32)
    rest = jnp.dot(high, basis_cols[INNER:], preferred_element_type=F32)
    wide = wide_in[...] + (both[:MODES] + (both[MODES:] + rest))
    lane = lanes()
    which = lax.div(lane, MODES)
    flat = wide[:SUB]
    for j in range(1, MODES // SUB):
        flat = jnp.where(which == j, wide[SUB * j : SUB * (j + 1)], flat)
    mark = jnp.broadcast_to(block[:1, :].astype(F32), (SUB, TILE))
    row = lax.broadcasted_iota(jnp.int32, (SUB, TILE), 0)
    moved = [flat] + [pltpu.roll(flat, r, 0) for r in range(1, SUB)] + [flat]
    lines = [flat] + [
        jnp.where(row < r - 1, moved[r - 1], jnp.where(row == r - 1, mark, moved[r])) for r in range(1, SUB + 1)
    ]
    cycle = SUB * (SUB + 1)
    chunk = min(4, coef.shape[0] // cycle)

    def spread(d, carry):
        for e in range(chunk):
            for r, line in enumerate(lines):
                coef[pl.ds(pl.multiple_of((d * chunk + e) * cycle + SUB * r, SUB), SUB), :] = line
        return carry

    lax.fori_loop(0, coef.shape[0] // cycle // chunk, spread, 0)


def join_kernel(v0, v1, vel_ends, strips, vel, turned):
    rows = vel.shape[1]
    span = rows // SUB
    middle = jnp.zeros((TILE - 2 * HALO, TILE), F32)
    side = beside()
    for k, v in enumerate((v0, v1)):
        for part in range(PARTS):
            base = STRIP * (2 * part + 1 - k)
            first, last = (strips[base + at : base + at + HALO, :] for at in OUTER)
            at = TILE * (2 * part + k)
            turned[at : at + TILE, :] = jnp.concatenate([first, middle, last], axis=0).T
        for row in range(0, rows, SUB):
            value = v[pl.ds(SUB * (row % span) + row // span, SUB, stride=SUB), :]
            if row in (0, rows - SUB):
                at = HALO * (2 * k + (row > 0))
                value = jnp.where(ends(row > 0), vel_ends[at : at + HALO, :], value)
            part, lane = right_part(row)
            at = TILE * (2 * part + k) + lane
            vel[k, row : row + SUB, :] = jnp.where(side, turned[at : at + SUB, :], value)


def bases():
    places = np.arange(TILE) + 0.5
    basis = np.cos(math.pi * places[:, None] * np.arange(MODES)[None, :] / TILE)
    groups = MODES // SUB
    order = np.arange(MODES).reshape(SUB, groups).T.reshape(-1)
    rows = basis[:, order] / TILE
    cols = np.tile(basis, (1, groups))
    placed = np.zeros((2 * TILE, MODES))
    for row in range(0, 2 * TILE, SUB):
        part, lane = right_part(row)
        at = lane + (TILE if part == 2 else 0)
        placed[at : at + SUB] = rows[row % TILE : row % TILE + SUB]
    outer = np.concatenate([cols[:HALO], cols[TILE - HALO :]])
    return jnp.asarray(rows.T, F32), jnp.asarray(cols, F32), split_constant(placed.T, 1), split_constant(outer, 0)[: 2 * INNER]


def pick_kernel(owners, every, out):
    mine = out.shape[1]
    own = lax.axis_index("own")
    wanted = [owners[pl.ds(own, 1), k : k + 1].astype(F32) for k in range(mine)]
    lines = SUB + 1
    devices = every.shape[0] // lines
    chunk = min(4, devices // SUB)

    def body(d, sums):
        sums = list(sums)
        for e in range(chunk):
            base = (d * chunk + e) * SUB * lines
            mark = every[pl.ds(base + SUB, SUB, stride=lines), :]
            hits = [mark == wanted[k] for k in range(mine)]
            for r in range(SUB):
                part = every[pl.ds(base + r, SUB, stride=lines), :]
                for k in range(mine):
                    sums[SUB * k + r] += jnp.where(hits[k], part, 0.0)
        return tuple(sums)

    start = (jnp.zeros((SUB, TILE), F32),) * (mine * SUB)
    sums = lax.fori_loop(0, devices // SUB // chunk, body, start)
    for k in range(mine):
        for r in range(SUB):
            total = jnp.sum(sums[SUB * k + r], axis=0, keepdims=True)
            out[0, k : k + 1, TILE * r : TILE * (r + 1)] = total


def local(viscosity, friction, driving, observed, ice_mask, tile_block, owner_list):
    rows, cols = viscosity.shape
    assert (rows, cols) == (2 * TILE, TILE)
    inputs = (viscosity, friction, driving, ice_mask, observed)
    near = [pltpu.with_memory_space_constraint(x, pltpu.VMEM) for x in inputs]
    basis_p, basis_q, basis_rows, basis_cols = bases()
    to_b, to_a = call(
        ends_kernel,
        "ends",
        (vmem(EDGE, cols), vmem(EDGE, cols)),
        [
            vmem(2, 2, HALO, cols),
            vmem(2, 2, 2, HALO, cols),
            pltpu.VMEM((2, HALO, cols), jnp.int32),
            pltpu.SemaphoreType.DMA((2, 5)),
        ],
        10**6,
        *(pltpu.with_memory_space_constraint(x, pltpu.HBM) for x in inputs),
    )
    row_b = swap(to_b, 0, 1)
    row_a = swap(to_a, 0, 0)
    edge, *forward = call(
        interior_kernel,
        "interior",
        (vmem(2 * PARTS * TILE, TILE),) + (vmem(rows, cols),) * 6,
        [vmem(rows, cols)] * (FIELDS - 6),
        8 * 10**6,
        *near,
    )
    to_b, to_a, turned = call(
        columns_kernel,
        "columns",
        (vmem(SENT, TILE), vmem(SENT, TILE), vmem(SLOT, TILE)),
        [],
        10**5,
        row_b,
        row_a,
        edge,
    )
    col_b = swap(to_b, 1, 1)
    col_a = swap(to_a, 1, 0)
    vel_ends, wide, sides, seams = call(
        adjoint_kernel,
        "adjoint",
        (
            vmem(4 * HALO, cols),
            vmem(MODES, TILE),
            vmem(PARTS * ARRAYS * STRIP, TILE),
            vmem(PARTS * SUB, TILE),
        ),
        [vmem(ARRAYS * STRIP, cols), vmem(2 * STRIP, cols), vmem(rows + STRIP, cols), vmem(TILE, cols)]
        + [vmem(STRIP, cols)] * STRIP_FIELDS
        + [vmem(rows, cols)] * (FIELDS - 4),
        8 * 10**6,
        row_b,
        row_a,
        *near,
        *forward,
        basis_p,
        basis_q,
        edge,
        turned,
    )
    devices = lax.axis_size(ROW_AXES + COL_AXES)
    _, strips, coef = call(
        left_right_kernel,
        "left_right",
        (
            vmem(PARTS * ARRAYS * STRIP, TILE),
            vmem(PARTS * 2 * STRIP, TILE),
            vmem(devices * (SUB + 1), TILE),
        ),
        [vmem(PARTS * STRIP, TILE)] * (STRIP_FIELDS + 1),
        4 * 10**6,
        sides,
        seams,
        col_b,
        col_a,
        wide,
        tile_block,
        basis_rows,
        basis_cols,
        aliases={0: 0},
    )
    coef = coef.reshape(devices, 1, (SUB + 1) * TILE)
    sizes = [lax.axis_size(axis) for axis in ("col", "row", "own")]
    members = [
        (row * sizes[0] + col) * sizes[2] + own
        for col in reversed(range(sizes[0]))
        for row in range(sizes[1])
        for own in range(sizes[2])
    ]
    parts = lax.all_to_all(coef, ("row", "col", "own"), 0, 0, axis_index_groups=[members], tiled=True)
    state = call(
        join_kernel,
        "join",
        jax.ShapeDtypeStruct((2, rows, cols), F32),
        [vmem(2 * PARTS * TILE, TILE)],
        4 * 10**6,
        *forward[4:],
        vel_ends,
        strips,
    )
    owners = owner_list.reshape(lax.axis_size("own"), -1)
    picked = call(
        pick_kernel,
        "pick",
        jax.ShapeDtypeStruct((1, owners.shape[1], MODES * MODES), F32),
        [],
        10**5,
        owners,
        parts.reshape(-1, TILE),
    )
    return (state, picked)


def solution(mesh):
    return jax.shard_map(
        local,
        mesh=mesh,
        in_specs=(
            P(("row", "own"), "col"),
            P(("row", "own"), "col"),
            P(None, ("row", "own"), "col"),
            P(None, ("row", "own"), "col"),
            P(("row", "own"), "col"),
            P(("row", "own"), "col"),
            P(),
        ),
        out_specs=(P(None, ("row", "own"), "col"), P("own", None, None)),
        check_vma=False,
    )
```

```python
import math

import jax
import jax.numpy as jnp
import numpy as np
from jax import lax
from jax.experimental import pallas as pl
from jax.experimental.pallas import tpu as pltpu
from jax.sharding import PartitionSpec as P

TILE = 128
MODES = 32
SWEEPS = 3
SUB = 8
HALO = 8
INNER = 2 * HALO
STRIP = 40
LEAD = HALO - 1
KEPT = 12
OUTER = (LEAD, STRIP - 2 * HALO)
NEAR, FAR = 7, 6
ARRAYS = 7
VISC, FRIC, DRIV, MASK, OBS = 0, 1, 2, 4, 5
EDGE = ARRAYS * HALO
SLOT = 2 * INNER
PER = TILE // SLOT
GROUPS = 5
SENT = 2 * GROUPS * HALO + HALO
PARTS = 3
UPPER, LOWER = 32, 64
ROW_AXES = ("row", "own")
COL_AXES = ("col",)
F32 = jnp.float32
LIMIT = 40 * 1024 * 1024


def swap(x, axis, first):
    sizes = lax.axis_size(ROW_AXES), lax.axis_size(COL_AXES)
    owners = lax.axis_size("own")

    def device(i, j):
        return (i // owners * sizes[1] + j) * owners + i % owners

    pairs = []
    for i in range(sizes[0]):
        for j in range(sizes[1]):
            place = [i, j]
            if first and place[axis] in (0, sizes[axis] - 1):
                place[1 - axis] ^= 1
            else:
                place[axis] = ((place[axis] + first) ^ 1) - first
            pairs.append((device(i, j), device(*place)))
    return lax.ppermute(x, ("row", "col", "own"), pairs)


def position(axes):
    index, size = 0, 1
    for axis in axes:
        index = index * lax.axis_size(axis) + lax.axis_index(axis)
        size *= lax.axis_size(axis)
    assert size % 2 == 0
    return lax.rem(index, 2) == 0, (index == 0) | (index == size - 1)


def is_even(axes):
    return position(axes)[0]


def lanes():
    return lax.broadcasted_iota(jnp.int32, (SUB, TILE), 1)


def call(kernel, name, outs, scratch, cost, *args, aliases={}):
    return pl.pallas_call(
        kernel,
        out_shape=outs,
        scratch_shapes=scratch,
        input_output_aliases=aliases,
        compiler_params=pltpu.CompilerParams(vmem_limit_bytes=LIMIT),
        cost_estimate=pl.CostEstimate(flops=cost, bytes_accessed=cost, transcendentals=0),
        name=name,
    )(*args)


def vmem(*shape):
    return pltpu.VMEM(shape, F32)


FIELDS = 14
STRIP_FIELDS = 24


class Domain:
    def __init__(self, refs, base, span, source, seam=None):
        self.refs, self.base, self.span, self.source, self.seam = refs, base, span, source, seam

    def at(self, j):
        return pl.ds(self.base + SUB * j, SUB)

    def prepare(self, flipped):
        n2, n4, c, i = self.refs[:4]
        visc = [self.source(VISC, j) for j in range(self.span)]
        for j in range(self.span):
            at = self.at(j)
            before = visc[j - 1] if j else pltpu.roll(visc[-1], 1, 0)
            if self.seam and not j:
                row = lax.broadcasted_iota(jnp.int32, (SUB, TILE), 0)
                before = jnp.where(row == SUB // 2, self.seam(), before)
            pair = visc[j] + before
            fric = self.source(FRIC, j)
            diag = 1.25 * (pair + pltpu.roll(pair, 1, 1)) + fric
            on = self.source(MASK, j) > 0.0
            inv = jnp.where(on, 0.5 / jnp.where(on, diag, 1.0), 0.0)
            half = 0.5 * visc[j]
            n2[at, :] = half
            n4[at, :] = 0.5 * half
            c[at, :] = 1.0 - fric * inv
            i[at, :] = inv
            for k in range(2):
                self.start(k, at, inv * self.source(DRIV + (1 - k if flipped else k), j))

    def start(self, k, at, value):
        self.refs[4 + k][at, :] = value
        self.write(k, at, value + value)

    def write(self, k, at, value):
        self.refs[6 + k][at, :] = value
        self.refs[8 + k][at, :] = pltpu.roll(value, TILE - 1, 1)

    def retarget(self, flipped, velocity=None):
        i = self.refs[3]
        velocity = velocity or self.refs[6:8]
        for j in range(self.span):
            at = self.at(j)
            for k in range(2):
                seen = self.source(OBS + (1 - k if flipped else k), j)
                self.start(k, at, i[at, :] * (velocity[k][at, :] - seen))

    def differences(self):
        n2, n4 = self.refs[:2]
        fields = self.refs[6:10]
        parts = self.refs[10:14]

        def corners(j, here, below):
            w0, w1, r0, r1 = here
            v0, v1, s0, s1 = below
            a1, a2 = s0 - w0, v0 - r0
            e1, e2 = s1 - w1, v1 - r1
            x, y = a1 + a2, e1 - e2
            q = (a1 - a2) + (e1 + e2)
            both = x + y
            at = self.at(j)
            half = n2[at, :]
            return half * (both + x), n4[at, :] * q, half * (both + y)

        def load(j):
            at = self.at(j)
            return [field[at, :] for field in fields]

        top = load(0)
        last = corners(self.span - 1, load(self.span - 1), [pltpu.roll(v, SUB - 1, 0) for v in top])
        up = [pltpu.roll(v, 1, 0) for v in last]
        here = top
        for j in range(self.span):
            at = self.at(j)
            if j < self.span - 1:
                below = load(j + 1)
                p, q, r = corners(j, here, below)
                here = below
            else:
                p, q, r = last
            g, t = up[0] - p, up[1] + q
            gq, tr = up[1] - q, up[2] + r
            parts[0][at, :] = g - t
            parts[1][at, :] = gq - tr
            parts[2][at, :] = pltpu.roll(g + t, 1, 1)
            parts[3][at, :] = pltpu.roll(gq + tr, 1, 1)
            up = (p, q, r)

    def update(self):
        c, i, b0, b1, w0, w1 = self.refs[2:8]
        parts = self.refs[10:14]
        for j in range(self.span):
            at = self.at(j)
            cv, iv = c[at, :], i[at, :]
            for k, (b, w) in enumerate(((b0, w0), (b1, w1))):
                value = (cv * w[at, :] + b[at, :]) - iv * (parts[k][at, :] + parts[k + 2][at, :])
                self.write(k, at, value)


class Strips(Domain):
    def prepare(self, flipped):
        super().prepare(flipped)
        for j in range(self.span):
            at = self.at(j)
            for now, later in zip(self.refs[2:4], self.refs[10:12]):
                later[at, :] = pltpu.roll(now[at, :], TILE - 1, 1)
        for now, before in zip(self.refs[:2], self.refs[14:16]):
            before[self.at(0), :] = pltpu.roll(now[self.at(self.span - 1), :], 1, 0)

    def start(self, k, at, value):
        b, w, r, later = (self.refs[n + k] for n in (4, 6, 8, 12))
        b[at, :] = value
        w[at, :] = value + value
        turned = pltpu.roll(value, TILE - 1, 1)
        later[at, :] = turned
        r[at, :] = turned + turned

    def differences(self):
        fields = self.refs[6:10]
        kept, turned, kept_next, turned_next = (self.refs[16 + 2 * k : 18 + 2 * k] for k in range(4))

        def corners(halves, quarters, j, here, below):
            w0, w1, r0, r1 = here
            v0, v1, s0, s1 = below
            a1, a2 = s0 - w0, v0 - r0
            e1, e2 = s1 - w1, v1 - r1
            x, y = a1 + a2, e1 - e2
            q = (a1 - a2) + (e1 + e2)
            both = x + y
            at = self.at(j)
            half = halves[at, :]
            return half * (both + x), quarters[at, :] * q, half * (both + y)

        def load(j):
            at = self.at(j)
            return [field[at, :] for field in fields]

        top, end = load(0), load(self.span - 1)
        up = corners(*self.refs[14:16], 0, [pltpu.roll(v, 1, 0) for v in end], top)
        here = top
        for j in range(self.span):
            at = self.at(j)
            below = load(j + 1) if j < self.span - 1 else [pltpu.roll(v, SUB - 1, 0) for v in top]
            p, q, r = corners(*self.refs[:2], j, here, below)
            g, t = up[0] - p, up[1] + q
            gq, tr = up[1] - q, up[2] + r
            for k, (stay, move) in enumerate(((g - t, g + t), (gq - tr, gq + tr))):
                kept[k][at, :] = stay
                turned_next[k][at, :] = move
                turned[k][at, :] = pltpu.roll(move, 1, 1)
                kept_next[k][at, :] = pltpu.roll(stay, TILE - 1, 1)
            up, here = (p, q, r), below

    def update(self):
        for first, offset, parts in ((2, 6, (16, 18)), (10, 8, (20, 22))):
            c, i, *b = self.refs[first : first + 4]
            for j in range(self.span):
                at = self.at(j)
                cv, iv = c[at, :], i[at, :]
                for k in range(2):
                    w = self.refs[offset + k]
                    change = self.refs[parts[0] + k][at, :] + self.refs[parts[1] + k][at, :]
                    w[at, :] = (cv * w[at, :] + b[k][at, :]) - iv * change


def run(domains, written_out=False):
    def body(_, carry):
        for domain in domains:
            domain.differences()
        for domain in domains:
            domain.update()
        return carry

    if written_out:
        for k in range(SWEEPS):
            body(k, 0)
    else:
        lax.fori_loop(0, SWEEPS, body, 0)


def ends_kernel(visc, fric, driv, mask, obs, to_b, to_a, one, two, flags, sems):
    rows = visc.shape[0]
    copies = []
    for n in range(5):
        for e, first in enumerate((0, rows - HALO)):
            at = pl.ds(first, HALO)
            source, place = [
                (visc.at[at], one.at[e, 0]),
                (fric.at[at], one.at[e, 1]),
                (mask.at[at], flags.at[e]),
                (driv.at[:, at], two.at[e, 0]),
                (obs.at[:, at], two.at[e, 1]),
            ][n]
            copies.append(pltpu.make_async_copy(source, place, sems.at[e, n]))
    for copy in copies:
        copy.start()
    even, at_end = position(ROW_AXES)

    def put(a, head, tail):
        at = slice(HALO * a, HALO * (a + 1))
        to_a[at, :] = jnp.where(even, tail, head)
        to_b[at, :] = jnp.where(at_end, 0.0, jnp.where(even, head, tail))

    for n in range(5):
        copies[2 * n].wait()
        copies[2 * n + 1].wait()
        if n < 2:
            put((VISC, FRIC)[n], one[0, n], one[1, n])
        elif n == 2:
            put(MASK, flags[0].astype(F32), flags[1].astype(F32))
        else:
            for k in range(2):
                put((DRIV, OBS)[n - 3] + k, two[0, n - 3, k], two[1, n - 3, k])


def field_of(visc, fric, driv, mask, obs):
    def field(a, at):
        if a == MASK:
            return mask[at, :].astype(F32)
        if a >= OBS:
            return obs[a - OBS, at, :]
        if a >= DRIV:
            return driv[a - DRIV, at, :]
        return (visc, fric)[a][at, :]

    return field


def first_row(part, lane):
    if part < 2:
        return TILE * part + lane
    if lane < INNER + HALO:
        return TILE + lane
    if lane >= TILE - INNER - HALO:
        return lane
    if UPPER + HALO <= lane < UPPER + SLOT:
        return lane - UPPER - HALO
    if LOWER <= lane < LOWER + INNER + HALO:
        return 2 * TILE - INNER - HALO + lane - LOWER
    return None


def right_part(row):
    seam = TILE - HALO <= row < TILE + HALO
    part = 2 if seam or row == 0 or row == 2 * TILE - HALO else row // TILE
    return part, [lane for lane in range(0, TILE, SUB) if first_row(part, lane) == row][-1]


def slot(part, a):
    return TILE * (2 * part + a // PER) + SLOT * (a % PER)


def interior_kernel(visc, fric, driv, mask, obs, edge, n2, n4, c, i, v0, v1, *refs):
    span = visc.shape[0] // SUB
    field = field_of(visc, fric, driv, mask, obs)
    lane = lanes()
    for part in range(PARTS):
        for m in range(-(-ARRAYS // PER)):
            strips = []
            for at in range(0, TILE, SUB):
                row = first_row(part, at)
                packed = jnp.zeros((SUB, TILE), F32)
                if row is not None:
                    for k in range(min(PER, ARRAYS - PER * m)):
                        value = field(PER * m + k, slice(row, row + SUB))
                        moved = pltpu.roll(value, (SLOT * k + INNER) % TILE, 1)
                        packed = jnp.where(lax.div(lane, SLOT) == k, moved, packed)
                strips.append(packed)
            base = TILE * (2 * part + m)
            edge[base : base + TILE, :] = jnp.concatenate(strips, axis=0).T
    refs = (n2, n4, c, i, *refs[:2], v0, v1, *refs[2:])
    domain = Domain(refs, 0, span, lambda a, j: field(a, pl.ds(j, SUB, stride=span)))
    domain.prepare(False)
    run([domain])


def columns_kernel(row_b, row_a, edge, to_b, to_a, turned):
    even = is_even(ROW_AXES)
    above = jnp.where(even, row_b[...], row_a[...])
    below = jnp.where(even, row_a[...], row_b[...])
    halo = jnp.concatenate([above, below, jnp.zeros((TILE - 2 * EDGE, TILE), F32)], axis=0).T
    turned[:INNER, :] = halo[TILE - INNER :]
    turned[INNER:, :] = halo[:INNER]
    even, at_end = position(COL_AXES)
    row = lax.broadcasted_iota(jnp.int32, (SUB, TILE), 0)

    def put(out, right, left):
        right = pltpu.roll(right, LEAD, 0)
        to_a[out : out + HALO, :] = jnp.where(even, right, left)
        to_b[out : out + HALO, :] = jnp.where(at_end, 0.0, jnp.where(even, left, right))

    for part in range(2):
        right, left = [], []
        for a in range(ARRAYS):
            at = slot(part, a) + INNER
            right.append(edge[at - HALO : at, :])
            left.append(edge[at : at + HALO, :])
        for k in range(2):
            seen_r, seen_l = right[OBS + k], left[OBS + k]
            g = 1 + 2 * k
            right[g] = jnp.where(row < 2, pltpu.roll(seen_r, 2, 0), right[g])
            right[g + 1] = jnp.where(row < 2, pltpu.roll(seen_r, 4, 0), right[g + 1])
            left[g] = jnp.where(row >= 6, pltpu.roll(seen_l, 6, 0), left[g])
            left[g + 1] = jnp.where(row >= 6, pltpu.roll(seen_l, 4, 0), left[g + 1])
        for g in range(GROUPS):
            put(HALO * (GROUPS * part + g), right[g], left[g])
    put(2 * GROUPS * HALO, halo[TILE - HALO :], halo[:HALO])


def strided(stack, base):
    span = STRIP // SUB
    return lambda a, j: stack[pl.ds(base + STRIP * a + j, SUB, stride=span), :]


def fill(stack, base, first, last):
    row = lax.broadcasted_iota(jnp.int32, (SUB, TILE), 0)
    one, two = (pltpu.roll(value, LEAD, 0) for value in first)
    mixed = [jnp.where(row == LEAD, two, one), jnp.where(row < SUB // 2, two, last[0])]
    for k, value in enumerate((one, *mixed, last[1])):
        stack[base + SUB * k : base + SUB * (k + 1), :] = value


def velocity(domain, plain, base):
    for j in range(domain.span):
        at = domain.at(j)
        for k in range(2):
            plain[pl.ds(base + STRIP * k + j, SUB, stride=domain.span), :] = domain.refs[6 + k][at, :]


def density(domain, plain, base, out, place):
    w0, w1 = domain.refs[6:8]
    for j in range(domain.span):
        at = domain.at(j)
        v0, v1 = (plain[pl.ds(base + STRIP * k + j, SUB, stride=domain.span), :] for k in range(2))
        value = -domain.source(FRIC, j) * (w0[at, :] * v0 + w1[at, :] * v1)
        out[pl.ds(place + j, SUB, stride=domain.span), :] = value


def beside():
    lane = lanes()
    return (lane < NEAR) | (lane >= TILE - FAR)


def ends(second):
    row = lax.broadcasted_iota(jnp.int32, (SUB, TILE), 0)
    return row >= SUB - FAR if second else row < NEAR


def adjoint_kernel(
    row_b, row_a, visc, fric, driv, mask, obs, n2, n4, c, i, v0, v1, basis_p, basis_q, edge, turned,
    vel, wide, sides, seams,
    stack, plain, dens, total, *refs,
):
    rows = visc.shape[0]
    span = rows // SUB
    even = is_even(ROW_AXES)
    field = field_of(visc, fric, driv, mask, obs)
    for a in range(ARRAYS):
        at = slice(HALO * a, HALO * (a + 1))
        got_a, got_b = row_a[at, :], row_b[at, :]
        base = STRIP * a
        first = [field(a, slice(at, at + SUB)) for at in (0, SUB)]
        last = [field(a, slice(at, at + SUB)) for at in (rows - 2 * SUB, rows - SUB)]
        fill(stack, base, first, last)
        stack[base : base + LEAD, :] = jnp.where(even, got_b, got_a)[HALO - LEAD :]
        stack[base + STRIP - HALO : base + STRIP, :] = jnp.where(even, got_a, got_b)
    strips = Strips(refs[:STRIP_FIELDS], 0, STRIP // SUB, strided(stack, 0), lambda: visc[rows - KEPT - 1 : rows - KEPT, :])
    strips.prepare(False)
    run([strips])
    velocity(strips, plain, 0)
    for k in range(2):
        for e in range(2):
            out = HALO * (2 * k + e)
            vel[out : out + HALO, :] = plain[STRIP * k + OUTER[e] : STRIP * k + OUTER[e] + HALO, :]
    interior = Domain(
        (n2, n4, c, i, *refs[STRIP_FIELDS:]), 0, span, lambda a, j: field(a, pl.ds(j, SUB, stride=span))
    )
    strips.retarget(False)
    interior.retarget(False, (v0, v1))
    run([interior, strips])
    w0, w1 = interior.refs[6:8]
    for j in range(span):
        at = interior.at(j)
        value = -interior.source(FRIC, j) * (w0[at, :] * v0[at, :] + w1[at, :] * v1[at, :])
        dens[pl.ds(j, SUB, stride=span), :] = value
    density(strips, plain, 0, dens, rows)

    side = beside()
    for s in range(0, TILE, SUB):
        summed = jnp.zeros((SUB, TILE), F32)
        for row in range(s, rows, TILE):
            value = dens[row : row + SUB, :]
            if row in (0, rows - SUB):
                at = rows + OUTER[row > 0]
                value = jnp.where(ends(row > 0), dens[at : at + SUB, :], value)
            summed += value
        total[s : s + SUB, :] = jnp.where(side, 0.0, summed)
    exact = dict(precision=lax.Precision.HIGHEST, preferred_element_type=F32)
    half = jnp.dot(basis_p[...], total[...], **exact)
    wide[...] = jnp.dot(half, basis_q[...], **exact)

    corner = corners()
    for part in range(PARTS):
        for a in range(ARRAYS):
            columns = []
            for r in range(0, SLOT, SUB):
                value = edge[slot(part, a) + r : slot(part, a) + r + SUB, :]
                if part == 2:
                    moved = pltpu.roll(turned[r : r + SUB, :], (UPPER - HALO * a) % TILE, 1)
                    value = jnp.where(corner, moved, value)
                columns.append(value)
            fill(sides, strip(part, a), columns[2:], columns[:2])
            if a == VISC:
                seams[SUB * part : SUB * (part + 1), :] = columns[0]


def strip(part, a):
    return STRIP * (ARRAYS * part + a)


def corners():
    lane = lanes()
    above = (lane >= UPPER) & (lane < UPPER + HALO)
    return above | ((lane >= LOWER + INNER + HALO) & (lane < LOWER + SLOT))


def split(x, axis):
    high = x.astype(jnp.bfloat16)
    low = (x - high.astype(F32)).astype(jnp.bfloat16)
    return jnp.concatenate([high, high, low], axis=axis)


def split_constant(x, axis):
    x = np.asarray(x, np.float32)
    high = np.asarray(x, jnp.bfloat16)
    low = np.asarray(x - np.asarray(high, np.float32), jnp.bfloat16)
    return jnp.asarray(np.concatenate([high, low, high], axis=axis))


def left_right_kernel(
    _, seams, col_b, col_a, wide_in, block, basis_rows, basis_cols,
    stack, strips, coef,
    plain, *refs,
):
    even = is_even(COL_AXES)
    lane = lanes()
    row = lax.broadcasted_iota(jnp.int32, (SUB, TILE), 0)
    upper = (lane >= UPPER + HALO) & (lane < UPPER + SLOT)
    lower = (lane >= LOWER) & (lane < LOWER + INNER + HALO)
    seam_t0 = lane >= TILE - INNER - HALO
    seam_t1 = lane < INNER + HALO
    corner = corners()
    for from_left in (True, False):
        groups = []
        for g in range(2 * GROUPS + 1):
            got_a, got_b = col_a[HALO * g : HALO * (g + 1), :], col_b[HALO * g : HALO * (g + 1), :]
            groups.append(jnp.where(even, got_b, got_a) if from_left else jnp.where(even, got_a, got_b))
        tiles = []
        for part in range(2):
            tile = groups[GROUPS * part : GROUPS * (part + 1)]
            for k in range(2):
                g, h = tile[1 + 2 * k], tile[2 + 2 * k]
                if from_left:
                    tile.append(jnp.where(row >= 5, pltpu.roll(g, 6, 0), pltpu.roll(h, 4, 0)))
                else:
                    tile.append(jnp.where(row < 2, pltpu.roll(g, 2, 0), pltpu.roll(h, 4, 0)))
            tiles.append(tile)
        for a in range(ARRAYS):
            t0, t1 = tiles[0][a], tiles[1][a]
            third = jnp.where(corner, pltpu.roll(groups[-1], (UPPER - HALO * a) % TILE, 1), 0.0)
            third = jnp.where(upper, pltpu.roll(t0, UPPER + HALO, 1), third)
            third = jnp.where(lower, pltpu.roll(t1, LOWER + INNER + HALO, 1), third)
            third = jnp.where(seam_t0, t0, jnp.where(seam_t1, t1, third))
            for part, value in enumerate((t0, t1, third)):
                base = strip(part, a)
                if from_left:
                    stack[base : base + LEAD, :] = value[:LEAD]
                else:
                    stack[base + STRIP - HALO : base + STRIP, :] = value
    last = INNER - KEPT - 1
    before = [lambda at=SUB * part + last: seams[at : at + 1, :] for part in range(PARTS)]
    domains = [
        Strips(refs, STRIP * part, STRIP // SUB, strided(stack, strip(part, 0)), seam)
        for part, seam in enumerate(before)
    ]
    for domain in domains:
        domain.prepare(True)
    run(domains, True)
    for part, domain in enumerate(domains):
        velocity(domain, strips, 2 * STRIP * part)
        domain.retarget(True)
    run(domains, True)
    for part, domain in enumerate(domains):
        density(domain, strips, 2 * STRIP * part, plain, STRIP * part)

    def side(part):
        base = STRIP * part
        return jnp.concatenate(
            [plain[base + at : base + at + HALO, :] for at in OUTER], axis=0
        )

    lane = lax.broadcasted_iota(jnp.int32, (2 * HALO, TILE), 1)
    row = lax.broadcasted_iota(jnp.int32, (2 * HALO, TILE), 0)
    right = (row < NEAR) | (row >= 2 * HALO - FAR)
    straight = (lane >= HALO) & (lane < TILE - HALO)
    seam = (lane < HALO) | (lane >= TILE - HALO)
    top = (lane >= UPPER + HALO) & (lane < UPPER + 2 * HALO)
    bottom = (lane >= LOWER + INNER) & (lane < LOWER + INNER + HALO)
    dens = jnp.concatenate(
        [
            jnp.where(right & straight, side(0) + side(1), 0.0),
            jnp.where(right & (seam | top | bottom), side(2), 0.0),
        ],
        axis=1,
    )
    half = lax.dot_general(
        basis_rows[...], split(dens, 1), (((1,), (1,)), ((), ())), preferred_element_type=F32
    )
    high = half.astype(jnp.bfloat16)
    low = (half - high.astype(F32)).astype(jnp.bfloat16)
    both = jnp.dot(jnp.concatenate([high, low], axis=0), basis_cols[:INNER], preferred_element_type=F32)
    rest = jnp.dot(high, basis_cols[INNER:], preferred_element_type=F32)
    wide = wide_in[...] + (both[:MODES] + (both[MODES:] + rest))
    lane = lanes()
    which = lax.div(lane, MODES)
    flat = wide[:SUB]
    for j in range(1, MODES // SUB):
        flat = jnp.where(which == j, wide[SUB * j : SUB * (j + 1)], flat)
    mark = jnp.broadcast_to(block[:1, :].astype(F32), (SUB, TILE))
    row = lax.broadcasted_iota(jnp.int32, (SUB, TILE), 0)
    moved = [flat] + [pltpu.roll(flat, r, 0) for r in range(1, SUB)] + [flat]
    lines = [flat] + [
        jnp.where(row < r - 1, moved[r - 1], jnp.where(row == r - 1, mark, moved[r])) for r in range(1, SUB + 1)
    ]
    cycle = SUB * (SUB + 1)
    chunk = min(4, coef.shape[0] // cycle)

    def spread(d, carry):
        for e in range(chunk):
            for r, line in enumerate(lines):
                coef[pl.ds(pl.multiple_of((d * chunk + e) * cycle + SUB * r, SUB), SUB), :] = line
        return carry

    lax.fori_loop(0, coef.shape[0] // cycle // chunk, spread, 0)


def join_kernel(v0, v1, vel_ends, strips, vel, turned):
    rows = vel.shape[1]
    span = rows // SUB
    middle = jnp.zeros((TILE - 2 * HALO, TILE), F32)
    side = beside()
    for k, v in enumerate((v0, v1)):
        for part in range(PARTS):
            base = STRIP * (2 * part + 1 - k)
            first, last = (strips[base + at : base + at + HALO, :] for at in OUTER)
            at = TILE * (2 * part + k)
            turned[at : at + TILE, :] = jnp.concatenate([first, middle, last], axis=0).T
        for row in range(0, rows, SUB):
            value = v[pl.ds(SUB * (row % span) + row // span, SUB, stride=SUB), :]
            if row in (0, rows - SUB):
                at = HALO * (2 * k + (row > 0))
                value = jnp.where(ends(row > 0), vel_ends[at : at + HALO, :], value)
            part, lane = right_part(row)
            at = TILE * (2 * part + k) + lane
            vel[k, row : row + SUB, :] = jnp.where(side, turned[at : at + SUB, :], value)


def bases():
    places = np.arange(TILE) + 0.5
    basis = np.cos(math.pi * places[:, None] * np.arange(MODES)[None, :] / TILE)
    groups = MODES // SUB
    order = np.arange(MODES).reshape(SUB, groups).T.reshape(-1)
    rows = basis[:, order] / TILE
    cols = np.tile(basis, (1, groups))
    placed = np.zeros((2 * TILE, MODES))
    for row in range(0, 2 * TILE, SUB):
        part, lane = right_part(row)
        at = lane + (TILE if part == 2 else 0)
        placed[at : at + SUB] = rows[row % TILE : row % TILE + SUB]
    outer = np.concatenate([cols[:HALO], cols[TILE - HALO :]])
    return jnp.asarray(rows.T, F32), jnp.asarray(cols, F32), split_constant(placed.T, 1), split_constant(outer, 0)[: 2 * INNER]


def pick_kernel(owners, every, out):
    mine = out.shape[1]
    own = lax.axis_index("own")
    wanted = [owners[pl.ds(own, 1), k : k + 1].astype(F32) for k in range(mine)]
    lines = SUB + 1
    devices = every.shape[0] // lines
    chunk = min(4, devices // SUB)

    def body(d, sums):
        sums = list(sums)
        for e in range(chunk):
            base = (d * chunk + e) * SUB * lines
            mark = every[pl.ds(base + SUB, SUB, stride=lines), :]
            hits = [mark == wanted[k] for k in range(mine)]
            for r in range(SUB):
                part = every[pl.ds(base + r, SUB, stride=lines), :]
                for k in range(mine):
                    sums[SUB * k + r] += jnp.where(hits[k], part, 0.0)
        return tuple(sums)

    start = (jnp.zeros((SUB, TILE), F32),) * (mine * SUB)
    sums = lax.fori_loop(0, devices // SUB // chunk, body, start)
    for k in range(mine):
        for r in range(SUB):
            total = jnp.sum(sums[SUB * k + r], axis=0, keepdims=True)
            out[0, k : k + 1, TILE * r : TILE * (r + 1)] = total


def local(viscosity, friction, driving, observed, ice_mask, tile_block, owner_list):
    rows, cols = viscosity.shape
    assert (rows, cols) == (2 * TILE, TILE)
    inputs = (viscosity, friction, driving, ice_mask, observed)
    near = [pltpu.with_memory_space_constraint(x, pltpu.VMEM) for x in inputs]
    basis_p, basis_q, basis_rows, basis_cols = bases()
    to_b, to_a = call(
        ends_kernel,
        "ends",
        (vmem(EDGE, cols), vmem(EDGE, cols)),
        [
            vmem(2, 2, HALO, cols),
            vmem(2, 2, 2, HALO, cols),
            pltpu.VMEM((2, HALO, cols), jnp.int32),
            pltpu.SemaphoreType.DMA((2, 5)),
        ],
        10**6,
        *(pltpu.with_memory_space_constraint(x, pltpu.HBM) for x in inputs),
    )
    row_b = swap(to_b, 0, 1)
    row_a = swap(to_a, 0, 0)
    edge, *forward = call(
        interior_kernel,
        "interior",
        (vmem(2 * PARTS * TILE, TILE),) + (vmem(rows, cols),) * 6,
        [vmem(rows, cols)] * (FIELDS - 6),
        8 * 10**6,
        *near,
    )
    to_b, to_a, turned = call(
        columns_kernel,
        "columns",
        (vmem(SENT, TILE), vmem(SENT, TILE), vmem(SLOT, TILE)),
        [],
        10**5,
        row_b,
        row_a,
        edge,
    )
    col_b = swap(to_b, 1, 1)
    col_a = swap(to_a, 1, 0)
    vel_ends, wide, sides, seams = call(
        adjoint_kernel,
        "adjoint",
        (
            vmem(4 * HALO, cols),
            vmem(MODES, TILE),
            vmem(PARTS * ARRAYS * STRIP, TILE),
            vmem(PARTS * SUB, TILE),
        ),
        [vmem(ARRAYS * STRIP, cols), vmem(2 * STRIP, cols), vmem(rows + STRIP, cols), vmem(TILE, cols)]
        + [vmem(STRIP, cols)] * STRIP_FIELDS
        + [vmem(rows, cols)] * (FIELDS - 4),
        8 * 10**6,
        row_b,
        row_a,
        *near,
        *forward,
        basis_p,
        basis_q,
        edge,
        turned,
    )
    devices = lax.axis_size(ROW_AXES + COL_AXES)
    _, strips, coef = call(
        left_right_kernel,
        "left_right",
        (
            vmem(PARTS * ARRAYS * STRIP, TILE),
            vmem(PARTS * 2 * STRIP, TILE),
            vmem(devices * (SUB + 1), TILE),
        ),
        [vmem(PARTS * STRIP, TILE)] * (STRIP_FIELDS + 1),
        4 * 10**6,
        sides,
        seams,
        col_b,
        col_a,
        wide,
        tile_block,
        basis_rows,
        basis_cols,
        aliases={0: 0},
    )
    coef = coef.reshape(devices, 1, (SUB + 1) * TILE)
    sizes = [lax.axis_size(axis) for axis in ("col", "row", "own")]
    members = [
        (row * sizes[0] + col) * sizes[2] + own
        for col in range(sizes[0])
        for row in range(sizes[1])
        for own in range(sizes[2])
    ]
    parts = lax.all_to_all(coef, ("row", "col", "own"), 0, 0, axis_index_groups=[members], tiled=True)
    state = call(
        join_kernel,
        "join",
        jax.ShapeDtypeStruct((2, rows, cols), F32),
        [vmem(2 * PARTS * TILE, TILE)],
        4 * 10**6,
        *forward[4:],
        vel_ends,
        strips,
    )
    owners = owner_list.reshape(lax.axis_size("own"), -1)
    picked = call(
        pick_kernel,
        "pick",
        jax.ShapeDtypeStruct((1, owners.shape[1], MODES * MODES), F32),
        [],
        10**5,
        owners,
        parts.reshape(-1, TILE),
    )
    return (state, picked)


def solution(mesh):
    return jax.shard_map(
        local,
        mesh=mesh,
        in_specs=(
            P(("row", "own"), "col"),
            P(("row", "own"), "col"),
            P(None, ("row", "own"), "col"),
            P(None, ("row", "own"), "col"),
            P(("row", "own"), "col"),
            P(("row", "own"), "col"),
            P(),
        ),
        out_specs=(P(None, ("row", "own"), "col"), P("own", None, None)),
        check_vma=False,
    )
```

```python
import math

import jax
import jax.numpy as jnp
import numpy as np
from jax import lax
from jax.experimental import pallas as pl
from jax.experimental.pallas import tpu as pltpu
from jax.sharding import PartitionSpec as P

TILE = 128
MODES = 32
SWEEPS = 3
SUB = 8
HALO = 8
INNER = 2 * HALO
STRIP = 40
LEAD = HALO - 1
KEPT = 12
OUTER = (LEAD, STRIP - 2 * HALO)
NEAR, FAR = 7, 6
ARRAYS = 7
VISC, FRIC, DRIV, MASK, OBS = 0, 1, 2, 4, 5
EDGE = ARRAYS * HALO
SLOT = 2 * INNER
PER = TILE // SLOT
GROUPS = 5
SENT = 2 * GROUPS * HALO + HALO
PARTS = 3
UPPER, LOWER = 32, 64
ROW_AXES = ("row", "own")
COL_AXES = ("col",)
F32 = jnp.float32
LIMIT = 40 * 1024 * 1024


def swap(x, axis, first):
    sizes = lax.axis_size(ROW_AXES), lax.axis_size(COL_AXES)
    owners = lax.axis_size("own")

    def device(i, j):
        return (i // owners * sizes[1] + j) * owners + i % owners

    pairs = []
    for i in range(sizes[0]):
        for j in range(sizes[1]):
            place = [i, j]
            if first and place[axis] in (0, sizes[axis] - 1):
                place[1 - axis] ^= 1
            else:
                place[axis] = ((place[axis] + first) ^ 1) - first
            pairs.append((device(i, j), device(*place)))
    return lax.ppermute(x, ("row", "col", "own"), pairs)


def position(axes):
    index, size = 0, 1
    for axis in axes:
        index = index * lax.axis_size(axis) + lax.axis_index(axis)
        size *= lax.axis_size(axis)
    assert size % 2 == 0
    return lax.rem(index, 2) == 0, (index == 0) | (index == size - 1)


def is_even(axes):
    return position(axes)[0]


def lanes():
    return lax.broadcasted_iota(jnp.int32, (SUB, TILE), 1)


def call(kernel, name, outs, scratch, cost, *args, aliases={}):
    return pl.pallas_call(
        kernel,
        out_shape=outs,
        scratch_shapes=scratch,
        input_output_aliases=aliases,
        compiler_params=pltpu.CompilerParams(vmem_limit_bytes=LIMIT),
        cost_estimate=pl.CostEstimate(flops=cost, bytes_accessed=cost, transcendentals=0),
        name=name,
    )(*args)


def vmem(*shape):
    return pltpu.VMEM(shape, F32)


FIELDS = 14
STRIP_FIELDS = 24


class Domain:
    def __init__(self, refs, base, span, source, seam=None):
        self.refs, self.base, self.span, self.source, self.seam = refs, base, span, source, seam

    def at(self, j):
        return pl.ds(self.base + SUB * j, SUB)

    def prepare(self, flipped):
        n2, n4, c, i = self.refs[:4]
        visc = [self.source(VISC, j) for j in range(self.span)]
        for j in range(self.span):
            at = self.at(j)
            before = visc[j - 1] if j else pltpu.roll(visc[-1], 1, 0)
            if self.seam and not j:
                row = lax.broadcasted_iota(jnp.int32, (SUB, TILE), 0)
                before = jnp.where(row == SUB // 2, self.seam(), before)
            pair = visc[j] + before
            fric = self.source(FRIC, j)
            diag = 1.25 * (pair + pltpu.roll(pair, 1, 1)) + fric
            on = self.source(MASK, j) > 0.0
            inv = jnp.where(on, 0.5 / jnp.where(on, diag, 1.0), 0.0)
            half = 0.5 * visc[j]
            n2[at, :] = half
            n4[at, :] = 0.5 * half
            c[at, :] = 1.0 - fric * inv
            i[at, :] = inv
            for k in range(2):
                self.start(k, at, inv * self.source(DRIV + (1 - k if flipped else k), j))

    def start(self, k, at, value):
        self.refs[4 + k][at, :] = value
        self.write(k, at, value + value)

    def write(self, k, at, value):
        self.refs[6 + k][at, :] = value
        self.refs[8 + k][at, :] = pltpu.roll(value, TILE - 1, 1)

    def retarget(self, flipped, velocity=None):
        i = self.refs[3]
        velocity = velocity or self.refs[6:8]
        for j in range(self.span):
            at = self.at(j)
            for k in range(2):
                seen = self.source(OBS + (1 - k if flipped else k), j)
                self.start(k, at, i[at, :] * (velocity[k][at, :] - seen))

    def differences(self):
        n2, n4 = self.refs[:2]
        fields = self.refs[6:10]
        parts = self.refs[10:14]

        def corners(j, here, below):
            w0, w1, r0, r1 = here
            v0, v1, s0, s1 = below
            a1, a2 = s0 - w0, v0 - r0
            e1, e2 = s1 - w1, v1 - r1
            x, y = a1 + a2, e1 - e2
            q = (a1 - a2) + (e1 + e2)
            both = x + y
            at = self.at(j)
            half = n2[at, :]
            return half * (both + x), n4[at, :] * q, half * (both + y)

        def load(j):
            at = self.at(j)
            return [field[at, :] for field in fields]

        top = load(0)
        last = corners(self.span - 1, load(self.span - 1), [pltpu.roll(v, SUB - 1, 0) for v in top])
        up = [pltpu.roll(v, 1, 0) for v in last]
        here = top
        for j in range(self.span):
            at = self.at(j)
            if j < self.span - 1:
                below = load(j + 1)
                p, q, r = corners(j, here, below)
                here = below
            else:
                p, q, r = last
            g, t = up[0] - p, up[1] + q
            gq, tr = up[1] - q, up[2] + r
            parts[0][at, :] = g - t
            parts[1][at, :] = gq - tr
            parts[2][at, :] = pltpu.roll(g + t, 1, 1)
            parts[3][at, :] = pltpu.roll(gq + tr, 1, 1)
            up = (p, q, r)

    def update(self):
        c, i, b0, b1, w0, w1 = self.refs[2:8]
        parts = self.refs[10:14]
        for j in range(self.span):
            at = self.at(j)
            cv, iv = c[at, :], i[at, :]
            for k, (b, w) in enumerate(((b0, w0), (b1, w1))):
                value = (cv * w[at, :] + b[at, :]) - iv * (parts[k][at, :] + parts[k + 2][at, :])
                self.write(k, at, value)


class Strips(Domain):
    def prepare(self, flipped):
        super().prepare(flipped)
        for j in range(self.span):
            at = self.at(j)
            for now, later in zip(self.refs[2:4], self.refs[10:12]):
                later[at, :] = pltpu.roll(now[at, :], TILE - 1, 1)
        for now, before in zip(self.refs[:2], self.refs[14:16]):
            before[self.at(0), :] = pltpu.roll(now[self.at(self.span - 1), :], 1, 0)

    def start(self, k, at, value):
        b, w, r, later = (self.refs[n + k] for n in (4, 6, 8, 12))
        b[at, :] = value
        w[at, :] = value + value
        turned = pltpu.roll(value, TILE - 1, 1)
        later[at, :] = turned
        r[at, :] = turned + turned

    def differences(self):
        fields = self.refs[6:10]
        kept, turned, kept_next, turned_next = (self.refs[16 + 2 * k : 18 + 2 * k] for k in range(4))

        def corners(halves, quarters, j, here, below):
            w0, w1, r0, r1 = here
            v0, v1, s0, s1 = below
            a1, a2 = s0 - w0, v0 - r0
            e1, e2 = s1 - w1, v1 - r1
            x, y = a1 + a2, e1 - e2
            q = (a1 - a2) + (e1 + e2)
            both = x + y
            at = self.at(j)
            half = halves[at, :]
            return half * (both + x), quarters[at, :] * q, half * (both + y)

        def load(j):
            at = self.at(j)
            return [field[at, :] for field in fields]

        top, end = load(0), load(self.span - 1)
        up = corners(*self.refs[14:16], 0, [pltpu.roll(v, 1, 0) for v in end], top)
        here = top
        for j in range(self.span):
            at = self.at(j)
            below = load(j + 1) if j < self.span - 1 else [pltpu.roll(v, SUB - 1, 0) for v in top]
            p, q, r = corners(*self.refs[:2], j, here, below)
            g, t = up[0] - p, up[1] + q
            gq, tr = up[1] - q, up[2] + r
            for k, (stay, move) in enumerate(((g - t, g + t), (gq - tr, gq + tr))):
                kept[k][at, :] = stay
                turned_next[k][at, :] = move
                turned[k][at, :] = pltpu.roll(move, 1, 1)
                kept_next[k][at, :] = pltpu.roll(stay, TILE - 1, 1)
            up, here = (p, q, r), below

    def update(self):
        for first, offset, parts in ((2, 6, (16, 18)), (10, 8, (20, 22))):
            c, i, *b = self.refs[first : first + 4]
            for j in range(self.span):
                at = self.at(j)
                cv, iv = c[at, :], i[at, :]
                for k in range(2):
                    w = self.refs[offset + k]
                    change = self.refs[parts[0] + k][at, :] + self.refs[parts[1] + k][at, :]
                    w[at, :] = (cv * w[at, :] + b[k][at, :]) - iv * change


def run(domains, written_out=False):
    def body(_, carry):
        for domain in domains:
            domain.differences()
        for domain in domains:
            domain.update()
        return carry

    if written_out:
        for k in range(SWEEPS):
            body(k, 0)
    else:
        lax.fori_loop(0, SWEEPS, body, 0)


def ends_kernel(visc, fric, driv, mask, obs, to_b, to_a, one, two, flags, sems):
    rows = visc.shape[0]
    copies = []
    for e, first in enumerate((0, rows - HALO)):
        at = pl.ds(first, HALO)
        pieces = [
            (visc.at[at], one.at[e, 0]),
            (fric.at[at], one.at[e, 1]),
            (driv.at[:, at], two.at[e, 0]),
            (mask.at[at], flags.at[e]),
            (obs.at[:, at], two.at[e, 1]),
        ]
        for n, (source, place) in enumerate(pieces):
            copies.append(pltpu.make_async_copy(source, place, sems.at[e, n]))
    for copy in copies:
        copy.start()
    for copy in copies:
        copy.wait()
    even, at_end = position(ROW_AXES)

    def edge(e):
        return [one[e, 0], one[e, 1], two[e, 0, 0], two[e, 0, 1], flags[e].astype(F32), two[e, 1, 0], two[e, 1, 1]]

    for a, (head, tail) in enumerate(zip(edge(0), edge(1))):
        at = slice(HALO * a, HALO * (a + 1))
        to_a[at, :] = jnp.where(even, tail, head)
        to_b[at, :] = jnp.where(at_end, 0.0, jnp.where(even, head, tail))


def field_of(visc, fric, driv, mask, obs):
    def field(a, at):
        if a == MASK:
            return mask[at, :].astype(F32)
        if a >= OBS:
            return obs[a - OBS, at, :]
        if a >= DRIV:
            return driv[a - DRIV, at, :]
        return (visc, fric)[a][at, :]

    return field


def first_row(part, lane):
    if part < 2:
        return TILE * part + lane
    if lane < INNER + HALO:
        return TILE + lane
    if lane >= TILE - INNER - HALO:
        return lane
    if UPPER + HALO <= lane < UPPER + SLOT:
        return lane - UPPER - HALO
    if LOWER <= lane < LOWER + INNER + HALO:
        return 2 * TILE - INNER - HALO + lane - LOWER
    return None


def right_part(row):
    seam = TILE - HALO <= row < TILE + HALO
    part = 2 if seam or row == 0 or row == 2 * TILE - HALO else row // TILE
    return part, [lane for lane in range(0, TILE, SUB) if first_row(part, lane) == row][-1]


def slot(part, a):
    return TILE * (2 * part + a // PER) + SLOT * (a % PER)


def interior_kernel(visc, fric, driv, mask, obs, edge, n2, n4, c, i, v0, v1, *refs):
    span = visc.shape[0] // SUB
    field = field_of(visc, fric, driv, mask, obs)
    lane = lanes()
    for part in range(PARTS):
        for m in range(-(-ARRAYS // PER)):
            strips = []
            for at in range(0, TILE, SUB):
                row = first_row(part, at)
                packed = jnp.zeros((SUB, TILE), F32)
                if row is not None:
                    for k in range(min(PER, ARRAYS - PER * m)):
                        value = field(PER * m + k, slice(row, row + SUB))
                        moved = pltpu.roll(value, (SLOT * k + INNER) % TILE, 1)
                        packed = jnp.where(lax.div(lane, SLOT) == k, moved, packed)
                strips.append(packed)
            base = TILE * (2 * part + m)
            edge[base : base + TILE, :] = jnp.concatenate(strips, axis=0).T
    refs = (n2, n4, c, i, *refs[:2], v0, v1, *refs[2:])
    domain = Domain(refs, 0, span, lambda a, j: field(a, pl.ds(j, SUB, stride=span)))
    domain.prepare(False)
    run([domain])


def columns_kernel(row_b, row_a, edge, to_b, to_a, turned):
    even = is_even(ROW_AXES)
    above = jnp.where(even, row_b[...], row_a[...])
    below = jnp.where(even, row_a[...], row_b[...])
    halo = jnp.concatenate([above, below, jnp.zeros((TILE - 2 * EDGE, TILE), F32)], axis=0).T
    turned[:INNER, :] = halo[TILE - INNER :]
    turned[INNER:, :] = halo[:INNER]
    even, at_end = position(COL_AXES)
    row = lax.broadcasted_iota(jnp.int32, (SUB, TILE), 0)

    def put(out, right, left):
        right = pltpu.roll(right, LEAD, 0)
        to_a[out : out + HALO, :] = jnp.where(even, right, left)
        to_b[out : out + HALO, :] = jnp.where(at_end, 0.0, jnp.where(even, left, right))

    for part in range(2):
        right, left = [], []
        for a in range(ARRAYS):
            at = slot(part, a) + INNER
            right.append(edge[at - HALO : at, :])
            left.append(edge[at : at + HALO, :])
        for k in range(2):
            seen_r, seen_l = right[OBS + k], left[OBS + k]
            g = 1 + 2 * k
            right[g] = jnp.where(row < 2, pltpu.roll(seen_r, 2, 0), right[g])
            right[g + 1] = jnp.where(row < 2, pltpu.roll(seen_r, 4, 0), right[g + 1])
            left[g] = jnp.where(row >= 6, pltpu.roll(seen_l, 6, 0), left[g])
            left[g + 1] = jnp.where(row >= 6, pltpu.roll(seen_l, 4, 0), left[g + 1])
        for g in range(GROUPS):
            put(HALO * (GROUPS * part + g), right[g], left[g])
    put(2 * GROUPS * HALO, halo[TILE - HALO :], halo[:HALO])


def strided(stack, base):
    span = STRIP // SUB
    return lambda a, j: stack[pl.ds(base + STRIP * a + j, SUB, stride=span), :]


def fill(stack, base, first, last):
    row = lax.broadcasted_iota(jnp.int32, (SUB, TILE), 0)
    one, two = (pltpu.roll(value, LEAD, 0) for value in first)
    mixed = [jnp.where(row == LEAD, two, one), jnp.where(row < SUB // 2, two, last[0])]
    for k, value in enumerate((one, *mixed, last[1])):
        stack[base + SUB * k : base + SUB * (k + 1), :] = value


def velocity(domain, plain, base):
    for j in range(domain.span):
        at = domain.at(j)
        for k in range(2):
            plain[pl.ds(base + STRIP * k + j, SUB, stride=domain.span), :] = domain.refs[6 + k][at, :]


def density(domain, plain, base, out, place):
    w0, w1 = domain.refs[6:8]
    for j in range(domain.span):
        at = domain.at(j)
        v0, v1 = (plain[pl.ds(base + STRIP * k + j, SUB, stride=domain.span), :] for k in range(2))
        value = -domain.source(FRIC, j) * (w0[at, :] * v0 + w1[at, :] * v1)
        out[pl.ds(place + j, SUB, stride=domain.span), :] = value


def beside():
    lane = lanes()
    return (lane < NEAR) | (lane >= TILE - FAR)


def ends(second):
    row = lax.broadcasted_iota(jnp.int32, (SUB, TILE), 0)
    return row >= SUB - FAR if second else row < NEAR


def adjoint_kernel(
    row_b, row_a, visc, fric, driv, mask, obs, n2, n4, c, i, v0, v1, basis_p, basis_q, edge, turned,
    vel, wide, sides, seams,
    stack, plain, dens, total, *refs,
):
    rows = visc.shape[0]
    span = rows // SUB
    even = is_even(ROW_AXES)
    field = field_of(visc, fric, driv, mask, obs)
    for a in range(ARRAYS):
        at = slice(HALO * a, HALO * (a + 1))
        got_a, got_b = row_a[at, :], row_b[at, :]
        base = STRIP * a
        first = [field(a, slice(at, at + SUB)) for at in (0, SUB)]
        last = [field(a, slice(at, at + SUB)) for at in (rows - 2 * SUB, rows - SUB)]
        fill(stack, base, first, last)
        stack[base : base + LEAD, :] = jnp.where(even, got_b, got_a)[HALO - LEAD :]
        stack[base + STRIP - HALO : base + STRIP, :] = jnp.where(even, got_a, got_b)
    strips = Strips(refs[:STRIP_FIELDS], 0, STRIP // SUB, strided(stack, 0), lambda: visc[rows - KEPT - 1 : rows - KEPT, :])
    strips.prepare(False)
    run([strips])
    velocity(strips, plain, 0)
    for k in range(2):
        for e in range(2):
            out = HALO * (2 * k + e)
            vel[out : out + HALO, :] = plain[STRIP * k + OUTER[e] : STRIP * k + OUTER[e] + HALO, :]
    interior = Domain(
        (n2, n4, c, i, *refs[STRIP_FIELDS:]), 0, span, lambda a, j: field(a, pl.ds(j, SUB, stride=span))
    )
    strips.retarget(False)
    interior.retarget(False, (v0, v1))
    run([interior, strips])
    w0, w1 = interior.refs[6:8]
    for j in range(span):
        at = interior.at(j)
        value = -interior.source(FRIC, j) * (w0[at, :] * v0[at, :] + w1[at, :] * v1[at, :])
        dens[pl.ds(j, SUB, stride=span), :] = value
    density(strips, plain, 0, dens, rows)

    side = beside()
    for s in range(0, TILE, SUB):
        summed = jnp.zeros((SUB, TILE), F32)
        for row in range(s, rows, TILE):
            value = dens[row : row + SUB, :]
            if row in (0, rows - SUB):
                at = rows + OUTER[row > 0]
                value = jnp.where(ends(row > 0), dens[at : at + SUB, :], value)
            summed += value
        total[s : s + SUB, :] = jnp.where(side, 0.0, summed)
    exact = dict(precision=lax.Precision.HIGHEST, preferred_element_type=F32)
    half = jnp.dot(basis_p[...], total[...], **exact)
    wide[...] = jnp.dot(half, basis_q[...], **exact)

    corner = corners()
    for part in range(PARTS):
        for a in range(ARRAYS):
            columns = []
            for r in range(0, SLOT, SUB):
                value = edge[slot(part, a) + r : slot(part, a) + r + SUB, :]
                if part == 2:
                    moved = pltpu.roll(turned[r : r + SUB, :], (UPPER - HALO * a) % TILE, 1)
                    value = jnp.where(corner, moved, value)
                columns.append(value)
            fill(sides, strip(part, a), columns[2:], columns[:2])
            if a == VISC:
                seams[SUB * part : SUB * (part + 1), :] = columns[0]


def strip(part, a):
    return STRIP * (ARRAYS * part + a)


def corners():
    lane = lanes()
    above = (lane >= UPPER) & (lane < UPPER + HALO)
    return above | ((lane >= LOWER + INNER + HALO) & (lane < LOWER + SLOT))


def split(x, axis):
    high = x.astype(jnp.bfloat16)
    low = (x - high.astype(F32)).astype(jnp.bfloat16)
    return jnp.concatenate([high, high, low], axis=axis)


def split_constant(x, axis):
    x = np.asarray(x, np.float32)
    high = np.asarray(x, jnp.bfloat16)
    low = np.asarray(x - np.asarray(high, np.float32), jnp.bfloat16)
    return jnp.asarray(np.concatenate([high, low, high], axis=axis))


def left_right_kernel(
    _, seams, col_a, col_b, wide_in, block, basis_rows, basis_cols,
    stack, strips, coef,
    plain, *refs,
):
    even = is_even(COL_AXES)
    lane = lanes()
    row = lax.broadcasted_iota(jnp.int32, (SUB, TILE), 0)
    upper = (lane >= UPPER + HALO) & (lane < UPPER + SLOT)
    lower = (lane >= LOWER) & (lane < LOWER + INNER + HALO)
    seam_t0 = lane >= TILE - INNER - HALO
    seam_t1 = lane < INNER + HALO
    corner = corners()
    for from_left in (True, False):
        groups = []
        for g in range(2 * GROUPS + 1):
            got_a, got_b = col_a[HALO * g : HALO * (g + 1), :], col_b[HALO * g : HALO * (g + 1), :]
            groups.append(jnp.where(even, got_b, got_a) if from_left else jnp.where(even, got_a, got_b))
        tiles = []
        for part in range(2):
            tile = groups[GROUPS * part : GROUPS * (part + 1)]
            for k in range(2):
                g, h = tile[1 + 2 * k], tile[2 + 2 * k]
                if from_left:
                    tile.append(jnp.where(row >= 5, pltpu.roll(g, 6, 0), pltpu.roll(h, 4, 0)))
                else:
                    tile.append(jnp.where(row < 2, pltpu.roll(g, 2, 0), pltpu.roll(h, 4, 0)))
            tiles.append(tile)
        for a in range(ARRAYS):
            t0, t1 = tiles[0][a], tiles[1][a]
            third = jnp.where(corner, pltpu.roll(groups[-1], (UPPER - HALO * a) % TILE, 1), 0.0)
            third = jnp.where(upper, pltpu.roll(t0, UPPER + HALO, 1), third)
            third = jnp.where(lower, pltpu.roll(t1, LOWER + INNER + HALO, 1), third)
            third = jnp.where(seam_t0, t0, jnp.where(seam_t1, t1, third))
            for part, value in enumerate((t0, t1, third)):
                base = strip(part, a)
                if from_left:
                    stack[base : base + LEAD, :] = value[:LEAD]
                else:
                    stack[base + STRIP - HALO : base + STRIP, :] = value
    last = INNER - KEPT - 1
    before = [lambda at=SUB * part + last: seams[at : at + 1, :] for part in range(PARTS)]
    domains = [
        Strips(refs, STRIP * part, STRIP // SUB, strided(stack, strip(part, 0)), seam)
        for part, seam in enumerate(before)
    ]
    for domain in domains:
        domain.prepare(True)
    run(domains, True)
    for part, domain in enumerate(domains):
        velocity(domain, strips, 2 * STRIP * part)
        domain.retarget(True)
    run(domains, True)
    for part, domain in enumerate(domains):
        density(domain, strips, 2 * STRIP * part, plain, STRIP * part)

    def side(part):
        base = STRIP * part
        return jnp.concatenate(
            [plain[base + at : base + at + HALO, :] for at in OUTER], axis=0
        )

    lane = lax.broadcasted_iota(jnp.int32, (2 * HALO, TILE), 1)
    row = lax.broadcasted_iota(jnp.int32, (2 * HALO, TILE), 0)
    right = (row < NEAR) | (row >= 2 * HALO - FAR)
    straight = (lane >= HALO) & (lane < TILE - HALO)
    seam = (lane < HALO) | (lane >= TILE - HALO)
    top = (lane >= UPPER + HALO) & (lane < UPPER + 2 * HALO)
    bottom = (lane >= LOWER + INNER) & (lane < LOWER + INNER + HALO)
    dens = jnp.concatenate(
        [
            jnp.where(right & straight, side(0) + side(1), 0.0),
            jnp.where(right & (seam | top | bottom), side(2), 0.0),
        ],
        axis=1,
    )
    half = lax.dot_general(
        basis_rows[...], split(dens, 1), (((1,), (1,)), ((), ())), preferred_element_type=F32
    )
    high = half.astype(jnp.bfloat16)
    low = (half - high.astype(F32)).astype(jnp.bfloat16)
    both = jnp.dot(jnp.concatenate([high, low], axis=0), basis_cols[:INNER], preferred_element_type=F32)
    rest = jnp.dot(high, basis_cols[INNER:], preferred_element_type=F32)
    wide = wide_in[...] + (both[:MODES] + (both[MODES:] + rest))
    lane = lanes()
    which = lax.div(lane, MODES)
    flat = wide[:SUB]
    for j in range(1, MODES // SUB):
        flat = jnp.where(which == j, wide[SUB * j : SUB * (j + 1)], flat)
    mark = jnp.broadcast_to(block[:1, :].astype(F32), (SUB, TILE))
    row = lax.broadcasted_iota(jnp.int32, (SUB, TILE), 0)
    moved = [flat] + [pltpu.roll(flat, r, 0) for r in range(1, SUB)] + [flat]
    lines = [flat] + [
        jnp.where(row < r - 1, moved[r - 1], jnp.where(row == r - 1, mark, moved[r])) for r in range(1, SUB + 1)
    ]
    cycle = SUB * (SUB + 1)
    chunk = min(4, coef.shape[0] // cycle)

    def spread(d, carry):
        for e in range(chunk):
            for r, line in enumerate(lines):
                coef[pl.ds(pl.multiple_of((d * chunk + e) * cycle + SUB * r, SUB), SUB), :] = line
        return carry

    lax.fori_loop(0, coef.shape[0] // cycle // chunk, spread, 0)


def join_kernel(v0, v1, vel_ends, strips, vel, turned):
    rows = vel.shape[1]
    span = rows // SUB
    middle = jnp.zeros((TILE - 2 * HALO, TILE), F32)
    side = beside()
    for k, v in enumerate((v0, v1)):
        for part in range(PARTS):
            base = STRIP * (2 * part + 1 - k)
            first, last = (strips[base + at : base + at + HALO, :] for at in OUTER)
            at = TILE * (2 * part + k)
            turned[at : at + TILE, :] = jnp.concatenate([first, middle, last], axis=0).T
        for row in range(0, rows, SUB):
            value = v[pl.ds(SUB * (row % span) + row // span, SUB, stride=SUB), :]
            if row in (0, rows - SUB):
                at = HALO * (2 * k + (row > 0))
                value = jnp.where(ends(row > 0), vel_ends[at : at + HALO, :], value)
            part, lane = right_part(row)
            at = TILE * (2 * part + k) + lane
            vel[k, row : row + SUB, :] = jnp.where(side, turned[at : at + SUB, :], value)


def bases():
    places = np.arange(TILE) + 0.5
    basis = np.cos(math.pi * places[:, None] * np.arange(MODES)[None, :] / TILE)
    groups = MODES // SUB
    order = np.arange(MODES).reshape(SUB, groups).T.reshape(-1)
    rows = basis[:, order] / TILE
    cols = np.tile(basis, (1, groups))
    placed = np.zeros((2 * TILE, MODES))
    for row in range(0, 2 * TILE, SUB):
        part, lane = right_part(row)
        at = lane + (TILE if part == 2 else 0)
        placed[at : at + SUB] = rows[row % TILE : row % TILE + SUB]
    outer = np.concatenate([cols[:HALO], cols[TILE - HALO :]])
    return jnp.asarray(rows.T, F32), jnp.asarray(cols, F32), split_constant(placed.T, 1), split_constant(outer, 0)[: 2 * INNER]


def pick_kernel(owners, every, out):
    mine = out.shape[1]
    own = lax.axis_index("own")
    wanted = [owners[pl.ds(own, 1), k : k + 1].astype(F32) for k in range(mine)]
    lines = SUB + 1
    devices = every.shape[0] // lines
    chunk = min(4, devices // SUB)

    def body(d, sums):
        sums = list(sums)
        for e in range(chunk):
            base = (d * chunk + e) * SUB * lines
            mark = every[pl.ds(base + SUB, SUB, stride=lines), :]
            hits = [mark == wanted[k] for k in range(mine)]
            for r in range(SUB):
                part = every[pl.ds(base + r, SUB, stride=lines), :]
                for k in range(mine):
                    sums[SUB * k + r] += jnp.where(hits[k], part, 0.0)
        return tuple(sums)

    start = (jnp.zeros((SUB, TILE), F32),) * (mine * SUB)
    sums = lax.fori_loop(0, devices // SUB // chunk, body, start)
    for k in range(mine):
        for r in range(SUB):
            total = jnp.sum(sums[SUB * k + r], axis=0, keepdims=True)
            out[0, k : k + 1, TILE * r : TILE * (r + 1)] = total


def local(viscosity, friction, driving, observed, ice_mask, tile_block, owner_list):
    rows, cols = viscosity.shape
    assert (rows, cols) == (2 * TILE, TILE)
    inputs = (viscosity, friction, driving, ice_mask, observed)
    near = [pltpu.with_memory_space_constraint(x, pltpu.VMEM) for x in inputs]
    basis_p, basis_q, basis_rows, basis_cols = bases()
    to_b, to_a = call(
        ends_kernel,
        "ends",
        (vmem(EDGE, cols), vmem(EDGE, cols)),
        [
            vmem(2, 2, HALO, cols),
            vmem(2, 2, 2, HALO, cols),
            pltpu.VMEM((2, HALO, cols), jnp.int32),
            pltpu.SemaphoreType.DMA((2, 5)),
        ],
        10**6,
        *(pltpu.with_memory_space_constraint(x, pltpu.HBM) for x in inputs),
    )
    row_b = swap(to_b, 0, 1)
    row_a = swap(to_a, 0, 0)
    edge, *forward = call(
        interior_kernel,
        "interior",
        (vmem(2 * PARTS * TILE, TILE),) + (vmem(rows, cols),) * 6,
        [vmem(rows, cols)] * (FIELDS - 6),
        8 * 10**6,
        *near,
    )
    to_b, to_a, turned = call(
        columns_kernel,
        "columns",
        (vmem(SENT, TILE), vmem(SENT, TILE), vmem(SLOT, TILE)),
        [],
        10**5,
        row_b,
        row_a,
        edge,
    )
    col_b = swap(to_b, 1, 1)
    col_a = swap(to_a, 1, 0)
    vel_ends, wide, sides, seams = call(
        adjoint_kernel,
        "adjoint",
        (
            vmem(4 * HALO, cols),
            vmem(MODES, TILE),
            vmem(PARTS * ARRAYS * STRIP, TILE),
            vmem(PARTS * SUB, TILE),
        ),
        [vmem(ARRAYS * STRIP, cols), vmem(2 * STRIP, cols), vmem(rows + STRIP, cols), vmem(TILE, cols)]
        + [vmem(STRIP, cols)] * STRIP_FIELDS
        + [vmem(rows, cols)] * (FIELDS - 4),
        8 * 10**6,
        row_b,
        row_a,
        *near,
        *forward,
        basis_p,
        basis_q,
        edge,
        turned,
    )
    devices = lax.axis_size(ROW_AXES + COL_AXES)
    _, strips, coef = call(
        left_right_kernel,
        "left_right",
        (
            vmem(PARTS * ARRAYS * STRIP, TILE),
            vmem(PARTS * 2 * STRIP, TILE),
            vmem(devices * (SUB + 1), TILE),
        ),
        [vmem(PARTS * STRIP, TILE)] * (STRIP_FIELDS + 1),
        4 * 10**6,
        sides,
        seams,
        col_a,
        col_b,
        wide,
        tile_block,
        basis_rows,
        basis_cols,
        aliases={0: 0},
    )
    coef = coef.reshape(devices, 1, (SUB + 1) * TILE)
    sizes = [lax.axis_size(axis) for axis in ("col", "row", "own")]
    members = [
        (row * sizes[0] + col) * sizes[2] + own
        for col in range(sizes[0])
        for row in range(sizes[1])
        for own in range(sizes[2])
    ]
    parts = lax.all_to_all(coef, ("row", "col", "own"), 0, 0, axis_index_groups=[members], tiled=True)
    state = call(
        join_kernel,
        "join",
        jax.ShapeDtypeStruct((2, rows, cols), F32),
        [vmem(2 * PARTS * TILE, TILE)],
        4 * 10**6,
        *forward[4:],
        vel_ends,
        strips,
    )
    owners = owner_list.reshape(lax.axis_size("own"), -1)
    picked = call(
        pick_kernel,
        "pick",
        jax.ShapeDtypeStruct((1, owners.shape[1], MODES * MODES), F32),
        [],
        10**5,
        owners,
        parts.reshape(-1, TILE),
    )
    return (state, picked)


def solution(mesh):
    return jax.shard_map(
        local,
        mesh=mesh,
        in_specs=(
            P(("row", "own"), "col"),
            P(("row", "own"), "col"),
            P(None, ("row", "own"), "col"),
            P(None, ("row", "own"), "col"),
            P(("row", "own"), "col"),
            P(("row", "own"), "col"),
            P(),
        ),
        out_specs=(P(None, ("row", "own"), "col"), P("own", None, None)),
        check_vma=False,
    )
```
